32 devices in a mesh: ha: 8 (over z, x), wa: 4 (over y, core).
Axes of the slice: x: 2, y: 2, z: 4, core: 2. Of those that a mesh axis runs over, the one named last changes fastest.
Arguments:
- bottom: bfloat16 [24, 16, 32, 512], P(None, 'ha', 'wa'), may hold values from -6 to 6
- skipped: bfloat16 [24, 32, 64, 512], P(None, 'ha', 'wa'), may hold values from -6 to 6
- groups: int32 [24], replicated, may hold values from 0 to 4, never falling along the last dimension, each value on 1 to 8 neighbouring positions
- pixel_mask: int32 [24, 32, 64], P(None, 'ha', 'wa'), may hold values from 0 to 1
- labels: int32 [24, 32, 64], P(None, 'ha', 'wa'), may hold values 0 or 1
- conv1_weight: float32 [4608, 1024], P(('ha', 'wa')), may hold values from -0.09375 to 0.09375
- conv1_momentum: float32 [4608, 1024], P(('ha', 'wa')), may hold values from -0.00061035156 to 0.00061035156
- conv1_average: float32 [4608, 1024], P(('ha', 'wa')), may hold values from -0.09375 to 0.09375
- conv2_weight: float32 [9216, 1024], P(('ha', 'wa')), may hold values from -0.0625 to 0.0625
- conv2_momentum: float32 [9216, 1024], P(('ha', 'wa')), may hold values from -0.00061035156 to 0.00061035156
- conv2_average: float32 [9216, 1024], P(('ha', 'wa')), may hold values from -0.0625 to 0.0625
- up_weight: float32 [1024, 2048], P(('ha', 'wa')), may hold values from -0.1875 to 0.1875
- up_momentum: float32 [1024, 2048], P(('ha', 'wa')), may hold values from -0.00061035156 to 0.00061035156
- up_average: float32 [1024, 2048], P(('ha', 'wa')), may hold values from -0.1875 to 0.1875
- conv3_weight: float32 [9216, 512], P(('ha', 'wa')), may hold values from -0.0625 to 0.0625
- conv3_momentum: float32 [9216, 512], P(('ha', 'wa')), may hold values from -0.00061035156 to 0.00061035156
- conv3_average: float32 [9216, 512], P(('ha', 'wa')), may hold values from -0.0625 to 0.0625
- head_weight: float32 [512, 2], P(('ha', 'wa')), may hold values from -0.25 to 0.25
- head_momentum: float32 [512, 2], P(('ha', 'wa')), may hold values from -0.0234375 to 0.0234375
- head_average: float32 [512, 2], P(('ha', 'wa')), may hold values from -0.25 to 0.25
Outputs:
- loss_value: float32 [], replicated
- conv1_weight_new: float32 [4608, 1024], P(('ha', 'wa'))
- conv1_momentum_new: float32 [4608, 1024], P(('ha', 'wa'))
- conv1_average_new: float32 [4608, 1024], P(('ha', 'wa'))
- conv2_weight_new: float32 [9216, 1024], P(('ha', 'wa'))
- conv2_momentum_new: float32 [9216, 1024], P(('ha', 'wa'))
- conv2_average_new: float32 [9216, 1024], P(('ha', 'wa'))
- up_weight_new: float32 [1024, 2048], P(('ha', 'wa'))
- up_momentum_new: float32 [1024, 2048], P(('ha', 'wa'))
- up_average_new: float32 [1024, 2048], P(('ha', 'wa'))
- conv3_weight_new: float32 [9216, 512], P(('ha', 'wa'))
- conv3_momentum_new: float32 [9216, 512], P(('ha', 'wa'))
- conv3_average_new: float32 [9216, 512], P(('ha', 'wa'))
- head_weight_new: float32 [512, 2], P(('ha', 'wa'))
- head_momentum_new: float32 [512, 2], P(('ha', 'wa'))
- head_average_new: float32 [512, 2], P(('ha', 'wa'))
The draws below stay inside these ranges and needn't reach their ends.
Inputs may be any that keep to these rules, and one draw needn't show every extreme that they name: `groups`: never falls along the slices; every group has 1 to 8 slices, and one group has exactly 8.
All inputs are finite; a program needn't handle non-finite values. No bound on the sum of `labels` on one device may be relied on, other than what follows from the above.
Results may differ from the reference program's by a relative error of at most 0.0065.
Values may be sent and summed in bfloat16 or wider, within the bound.
A program may use at most 320 MiB of HBM per device.

```python
import math
import jax
import jax.numpy as jnp
import numpy as np
from jax import lax

CB = 512
CM = 1024
CU = 512
CLASSES = 2
GROUPS = 5
SLICES = 24
H = 16
W = 32


def draw_pixel_mask(key, part):
    key = jax.random.fold_in(key, 7)
    row_index = jnp.arange(2 * H, dtype=jnp.int32)[:, None]
    col_index = jnp.arange(2 * W, dtype=jnp.int32)[None, :]
    threshold = 50 + 450 * row_index // (2 * H) + 450 * col_index // (2 * W)
    drawn = jax.random.randint(key, (SLICES, 2 * H, 2 * W), 0, 1000, dtype=jnp.int32)
    return (drawn < threshold[None, :, :]).astype(jnp.int32)


def set_ends(entries, key, low, high):
    extent = entries.shape
    index_at = [jax.random.randint(jax.random.fold_in(key, axis), (), 0, extent[axis]) for axis in range(len(extent))]
    entries = entries.at[tuple(index_at)].set(low)
    longest = extent.index(max(extent))
    index_at[longest] = (index_at[longest] + 1) % extent[longest]
    return entries.at[tuple(index_at)].set(high)


def block_scale(own_key, shape, shards, smallest, high):
    gain = 1.0
    for dim, parts in shards:
        heights = jax.random.uniform(jax.random.fold_in(jax.random.fold_in(own_key, 6), dim), (parts,), jnp.float32, smallest / len(shards), high / len(shards))
        gain = gain * jnp.repeat(jnp.exp(heights), shape[dim] // parts).reshape((-1,) + (1,) * (len(shape) - 1 - dim))
    return gain


def length_profile(count, total, most, slope):
    loads = [(1 << 20) // math.isqrt(grade ** slope) + 1 for grade in range(2, count + 1)]
    surplus, counts = total - most - (count - 1), [1] * (count - 1)
    while surplus > 0:
        candidates = [i for i in range(count - 1) if counts[i] < most]
        mass, budget = sum([loads[i] for i in candidates]), surplus
        for i in candidates:
            addition = min(most - counts[i], max(1, budget * loads[i] // mass), surplus)
            counts[i] = counts[i] + addition
            surplus = surplus - addition
    return np.array([most] + counts)


def ragged(key, count, total, limit, slope):
    if count == 2:
        one = jax.random.randint(key, (), max(1, total - limit), min(limit, total - 1) + 1)
        return jnp.stack([one, total - one])
    tallies = jnp.asarray(length_profile(count, total, limit, slope), jnp.int32)
    couples = (count - 1) // 2
    giver, sink = tallies[1:1 + 2 * couples:2], tallies[2:2 + 2 * couples:2]
    room = jnp.minimum(giver - 1, limit - sink)
    moved = jax.random.randint(jax.random.fold_in(key, 1), (couples,), 0, 1 << 20) % (room + 1)
    tallies = tallies.at[1:1 + 2 * couples:2].set(giver - moved).at[2:2 + 2 * couples:2].set(sink + moved)
    return tallies[jax.random.permutation(jax.random.fold_in(key, 2), count)]


def gaussian(key, dims, width, bound, cuts=(), kind=jnp.bfloat16):
    entries = width * jax.random.normal(key, dims, jnp.float32)
    if cuts:
        entries = entries * block_scale(key, dims, cuts, -0.22, 0.18)
    return jnp.clip(entries, -bound, bound).astype(kind)


def setup_inputs(seed: int = 0) -> dict:
    keys = jax.random.split(jax.random.key(seed), 21)
    return {
        "bottom": gaussian(keys[0], (SLICES, H, W, CB), 1.0, 6.0, ((1, 8), (2, 4))),
        "skipped": gaussian(keys[1], (SLICES, 2 * H, 2 * W, CU), 1.0, 6.0, ((1, 8), (2, 4))),
        "groups": jnp.searchsorted(jnp.cumsum(ragged(keys[2], GROUPS, SLICES, SLICES // 3, 1)), jnp.arange(SLICES), side="right").astype(jnp.int32),
        "pixel_mask": draw_pixel_mask(jax.random.fold_in(keys[20], 71), 0),
        "labels": set_ends((jax.random.randint(keys[4], (SLICES, 2 * H, 2 * W), 0, 5) < 2).astype(jnp.int32), jax.random.fold_in(keys[4], 1), 0, 1),
        "conv1_weight": gaussian(keys[5], (9 * CB, CM), (9 * CB) ** -0.5, 0.09375, ((0, 32),), jnp.float32),
        "conv1_momentum": gaussian(keys[6], (9 * CB, CM), (0.01 / (4 * SLICES * H * W) ** 0.5), 0.00061035156, ((0, 32),), jnp.float32),
        "conv1_average": gaussian(keys[7], (9 * CB, CM), (9 * CB) ** -0.5, 0.09375, ((0, 32),), jnp.float32),
        "conv2_weight": gaussian(keys[8], (9 * CM, CM), (9 * CM) ** -0.5, 0.0625, ((0, 32),), jnp.float32),
        "conv2_momentum": gaussian(keys[9], (9 * CM, CM), (0.01 / (4 * SLICES * H * W) ** 0.5), 0.00061035156, ((0, 32),), jnp.float32),
        "conv2_average": gaussian(keys[10], (9 * CM, CM), (9 * CM) ** -0.5, 0.0625, ((0, 32),), jnp.float32),
        "up_weight": gaussian(keys[11], (CM, 4 * CU), CM ** -0.5, 0.1875, ((0, 32),), jnp.float32),
        "up_momentum": gaussian(keys[12], (CM, 4 * CU), (0.01 / (4 * SLICES * H * W) ** 0.5), 0.00061035156, ((0, 32),), jnp.float32),
        "up_average": gaussian(keys[13], (CM, 4 * CU), CM ** -0.5, 0.1875, ((0, 32),), jnp.float32),
        "conv3_weight": gaussian(keys[14], (18 * CU, CU), (18 * CU) ** -0.5, 0.0625, ((0, 32),), jnp.float32),
        "conv3_momentum": gaussian(keys[15], (18 * CU, CU), (0.01 / (4 * SLICES * H * W) ** 0.5), 0.00061035156, ((0, 32),), jnp.float32),
        "conv3_average": gaussian(keys[16], (18 * CU, CU), (18 * CU) ** -0.5, 0.0625, ((0, 32),), jnp.float32),
        "head_weight": gaussian(keys[17], (CU, CLASSES), CU ** -0.5, 0.25, ((0, 32),), jnp.float32),
        "head_momentum": gaussian(keys[18], (CU, CLASSES), (0.35 / (4 * SLICES * H * W) ** 0.5), 0.0234375, ((0, 32),), jnp.float32),
        "head_average": gaussian(keys[19], (CU, CLASSES), CU ** -0.5, 0.25, ((0, 32),), jnp.float32),
    }


MOMENTUM = 0.9
RATE_CONV = 600.0
RATE_HEAD = 25.0
AVERAGE_DECAY = 0.5
SMOOTHING = 1.0
HIGHEST = lax.Precision.HIGHEST

@jax.custom_vjp
def low(v):
    return lax.optimization_barrier(v.astype(jnp.bfloat16)).astype(jnp.float32)

@jax.custom_vjp
def low_back(v):
    return v

def low_keep(v):
    return (low(v), None)

def low_pass(kept, grad):
    return (grad,)

def back_keep(v):
    return (v, None)

def back_low(kept, grad):
    return (low(grad),)
low.defvjp(low_keep, low_pass)
low_back.defvjp(back_keep, back_low)

def smooth(source):
    return jax.nn.gelu(source, approximate=True)

def conv_same(source, weight):
    in_chan = source.shape[3]
    row_count, col_count = (source.shape[1], source.shape[2])
    padded = jnp.pad(source, ((0, 0), (1, 1), (1, 1), (0, 0)))
    running = jnp.zeros(source.shape[:3] + (weight.shape[1],), jnp.float32)
    for tap_index in range(9):
        row_off, col_off = (tap_index // 3, tap_index % 3)
        window = padded[:, row_off:row_off + row_count, col_off:col_off + col_count, :]
        taps = weight[tap_index * in_chan:(tap_index + 1) * in_chan]
        running = running + jnp.einsum('shwc,co->shwo', window, taps, precision=HIGHEST)
    return running

def upsample(source, weight):
    slices, row_count, col_count, _ = source.shape
    flattened = jnp.einsum('shwc,cq->shwq', source, weight, precision=HIGHEST)
    blocks = flattened.reshape(slices, row_count, col_count, 2, 2, -1).transpose(0, 1, 3, 2, 4, 5)
    return blocks.reshape(slices, 2 * row_count, 2 * col_count, -1)

def dice_loss(logits, pixel_mask, labels, groups):
    probability = jax.nn.softmax(logits, axis=-1)
    classes = jnp.arange(logits.shape[-1])
    target = (labels[..., None] == classes[None, None, None, :]).astype(jnp.float32)
    weighted = pixel_mask[..., None].astype(jnp.float32)
    member = (groups[:, None] == jnp.arange(GROUPS)[None, :]).astype(jnp.float32)
    per_slice = jnp.stack([lax.optimization_barrier(jnp.sum(weighted * probability * target, axis=(1, 2))), lax.optimization_barrier(jnp.sum(weighted * probability, axis=(1, 2))), lax.optimization_barrier(jnp.sum(weighted * target, axis=(1, 2)))], axis=-1)
    totals = jnp.einsum('skj,sg->gkj', per_slice, member, precision=HIGHEST)
    union_sum = totals[..., 1] + totals[..., 2] + SMOOTHING
    dice_score = (2.0 * totals[..., 0] + SMOOTHING) / union_sum
    return 1.0 - jnp.mean(dice_score)

def forward(weight_one, weight_two, weight_up, weight_three, weight_head, bottom, skipped, pixel_mask, labels, groups):
    pre_one = conv_same(bottom, low(weight_one))
    hidden_one = low(smooth(low_back(pre_one)))
    pre_two = conv_same(hidden_one, low(weight_two))
    hidden_two = low(smooth(low_back(pre_two)))
    upsampled = low(low_back(upsample(hidden_two, low(weight_up))))
    joined = jnp.concatenate([upsampled, skipped], axis=3)
    pre_three = conv_same(joined, low(weight_three))
    hidden_three = low(smooth(low_back(pre_three)))
    logits = low_back(jnp.einsum('shwc,ck->shwk', hidden_three, low(weight_head), precision=HIGHEST))
    return dice_loss(logits, pixel_mask, labels, groups)

def renew_state(weight, moment, average, gradient, rate):
    moment_new = MOMENTUM * moment + gradient
    weight_new = weight - rate * (gradient + MOMENTUM * moment_new)
    average_new = AVERAGE_DECAY * average + (1.0 - AVERAGE_DECAY) * weight_new
    return (weight_new, moment_new, average_new)

def reference(bottom, skipped, groups, pixel_mask, labels, conv1_weight, conv1_momentum, conv1_average, conv2_weight, conv2_momentum, conv2_average, up_weight, up_momentum, up_average, conv3_weight, conv3_momentum, conv3_average, head_weight, head_momentum, head_average):
    bottom_float = bottom.astype(jnp.float32)
    skipped_float = skipped.astype(jnp.float32)

    def loss_of(weight_one, weight_two, weight_up, weight_three, weight_head):
        return forward(weight_one, weight_two, weight_up, weight_three, weight_head, bottom_float, skipped_float, pixel_mask, labels, groups)
    loss_value, pull_back = jax.vjp(loss_of, conv1_weight, conv2_weight, up_weight, conv3_weight, head_weight)
    gradients = pull_back(jnp.ones_like(loss_value))
    first = renew_state(conv1_weight, conv1_momentum, conv1_average, gradients[0], RATE_CONV)
    second = renew_state(conv2_weight, conv2_momentum, conv2_average, gradients[1], RATE_CONV)
    upward = renew_state(up_weight, up_momentum, up_average, gradients[2], RATE_CONV)
    third = renew_state(conv3_weight, conv3_momentum, conv3_average, gradients[3], RATE_CONV)
    header = renew_state(head_weight, head_momentum, head_average, gradients[4], RATE_HEAD)
    return (loss_value, first[0], first[1], first[2], second[0], second[1], second[2], upward[0], upward[1], upward[2], third[0], third[1], third[2], header[0], header[1], header[2])
```

```python
import functools

import jax
import jax.numpy as jnp
from jax import lax
from jax.experimental import pallas as pl
from jax.experimental.pallas import tpu as pltpu
from jax.sharding import PartitionSpec as P

GROUPS = 5


MOMENTUM = 0.9
RATE_CONV = 600.0
RATE_HEAD = 25.0
AVERAGE_DECAY = 0.5
SMOOTHING = 1.0
HIGHEST = lax.Precision.HIGHEST


def with_halo(block, sides, width):
    for axis, dim in sides:
        count = lax.axis_size(axis)
        forward = [(i, i + 1) for i in range(count - 1)]
        backward = [(target, source) for source, target in forward]
        low = lax.ppermute(
            lax.slice_in_dim(block, block.shape[dim] - width, None, axis=dim), axis, forward
        )
        high = lax.ppermute(lax.slice_in_dim(block, 0, width, axis=dim), axis, backward)
        block = jnp.concatenate([low, block, high], axis=dim)
    return block


def smooth(source):
    return jax.nn.gelu(source, approximate=True)


def smooth_back(pre_value, gradient):
    _, pull_back = jax.vjp(smooth, pre_value)
    return pull_back(gradient)[0]


def widened_field(source):
    return with_halo(source, (("ha", 1), ("wa", 2)), 1)


def conv_taps(padded, weight):
    kernel = weight.reshape(3, 3, padded.shape[3], weight.shape[1])
    return lax.conv_general_dilated(
        padded,
        kernel,
        (1, 1),
        "VALID",
        dimension_numbers=("NHWC", "HWIO", "NHWC"),
        preferred_element_type=jnp.float32,
    )


def conv_back(padded, grad_out, weight, back_chan):
    in_chan = padded.shape[3]
    weight_grad = lax.conv_general_dilated(
        padded,
        grad_out,
        (1, 1),
        "VALID",
        dimension_numbers=("CHWN", "IHWO", "HWNC"),
        preferred_element_type=jnp.float32,
    ).reshape(9 * in_chan, grad_out.shape[3])
    if not back_chan:
        return (weight_grad, None)
    grad_padded = widened_field(grad_out)
    kernel = weight.reshape(3, 3, in_chan, weight.shape[1])[::-1, ::-1, :back_chan]
    source_grad = lax.conv_general_dilated(
        grad_padded,
        kernel,
        (1, 1),
        "VALID",
        dimension_numbers=("NHWC", "HWOI", "NHWC"),
        preferred_element_type=jnp.float32,
    )
    return (weight_grad, source_grad)


def upsample(source, weight):
    slices, row_count, col_count, _ = source.shape
    flattened = jnp.einsum("shwc,cq->shwq", source, weight, preferred_element_type=jnp.float32)
    blocks = flattened.reshape(slices, row_count, col_count, 2, 2, -1).transpose(0, 1, 3, 2, 4, 5)
    return blocks.reshape(slices, 2 * row_count, 2 * col_count, -1)


def upsample_back(source, grad_up, weight):
    slices, row_count, col_count, _ = source.shape
    blocks = grad_up.reshape(slices, row_count, 2, col_count, 2, -1).transpose(0, 1, 3, 2, 4, 5)
    flattened = blocks.reshape(slices, row_count, col_count, -1)
    weight_grad = jnp.einsum("shwc,shwq->cq", source, flattened, preferred_element_type=jnp.float32)
    source_grad = jnp.einsum("shwq,cq->shwc", flattened, weight, preferred_element_type=jnp.float32)
    return (weight_grad, source_grad)


def forward(gathered, bottom, skipped):
    weight_one, weight_two, weight_up, weight_three, weight_head = gathered
    pad_zero = widened_field(bottom)
    pre_one = conv_taps(pad_zero, weight_one)
    hidden_one = smooth(pre_one).astype(jnp.bfloat16)
    pad_one = widened_field(hidden_one)
    pre_two = conv_taps(pad_one, weight_two)
    hidden_two = smooth(pre_two).astype(jnp.bfloat16)
    upsampled = upsample(hidden_two, weight_up).astype(jnp.bfloat16)
    joined = jnp.concatenate([upsampled, skipped], axis=3)
    pad_two = widened_field(joined)
    pre_three = conv_taps(pad_two, weight_three)
    hidden_three = smooth(pre_three).astype(jnp.bfloat16)
    logits = jnp.einsum(
        "shwc,ck->shwk", hidden_three, weight_head, preferred_element_type=jnp.float32
    )
    return (
        pad_zero,
        pre_one,
        pad_one,
        pre_two,
        hidden_two,
        pad_two,
        pre_three,
        hidden_three,
        logits,
    )


def pixel_terms(logits, pixel_mask, labels):
    probability = jax.nn.softmax(logits, axis=-1)
    classes = jnp.arange(logits.shape[-1])
    target = (labels[..., None] == classes[None, None, None, :]).astype(jnp.float32)
    weighted = pixel_mask[..., None].astype(jnp.float32)
    return (probability, target, weighted)


def dice_terms(logits, pixel_mask, labels, member):
    probability, target, weighted = pixel_terms(logits, pixel_mask, labels)
    per_slice = jnp.stack(
        [
            jnp.sum(weighted * probability * target, axis=(1, 2)),
            jnp.sum(weighted * probability, axis=(1, 2)),
            jnp.sum(weighted * target, axis=(1, 2)),
        ],
        axis=-1,
    )
    return jnp.einsum("skj,sg->gkj", per_slice, member, precision=HIGHEST)


def dice_back(logits, pixel_mask, labels, member, totals):
    probability, target, weighted = pixel_terms(logits, pixel_mask, labels)
    union_sum = totals[..., 1] + totals[..., 2] + SMOOTHING
    numerator = 2.0 * totals[..., 0] + SMOOTHING
    dice_score = numerator / union_sum
    loss_value = 1.0 - jnp.mean(dice_score)
    entry_count = float(dice_score.size)
    coef_common = -2.0 / (entry_count * union_sum)
    coef_prob = numerator / (entry_count * union_sum * union_sum)
    slice_common = jnp.einsum("sg,gk->sk", member, coef_common, precision=HIGHEST)
    slice_prob = jnp.einsum("sg,gk->sk", member, coef_prob, precision=HIGHEST)
    grad_prob = weighted * (target * slice_common[:, None, None, :] + slice_prob[:, None, None, :])
    inner = jnp.sum(probability * grad_prob, axis=-1, keepdims=True)
    grad_logits = (probability * (grad_prob - inner)).astype(jnp.bfloat16)
    return (loss_value, grad_logits)


def renew_state(weight, moment, average, gradient, rate):
    moment_new = MOMENTUM * moment + gradient
    weight_new = weight - rate * (gradient + MOMENTUM * moment_new)
    average_new = AVERAGE_DECAY * average + (1.0 - AVERAGE_DECAY) * weight_new
    return (weight_new, moment_new, average_new)


def tiled_grads(
    bottom, skipped, groups, pixel_mask, labels, conv1_weight, conv2_weight, up_weight, conv3_weight,
    head_weight,
):
    gathered = (
        lax.all_gather(conv1_weight.astype(jnp.bfloat16), ("ha", "wa"), axis=0, tiled=True),
        lax.all_gather(conv2_weight.astype(jnp.bfloat16), ("ha", "wa"), axis=0, tiled=True),
        lax.all_gather(up_weight.astype(jnp.bfloat16), ("ha", "wa"), axis=0, tiled=True),
        lax.all_gather(conv3_weight.astype(jnp.bfloat16), ("ha", "wa"), axis=0, tiled=True),
        lax.all_gather(head_weight.astype(jnp.bfloat16), ("ha", "wa"), axis=0, tiled=True),
    )
    member = (groups[:, None] == jnp.arange(GROUPS)[None, :]).astype(jnp.float32)
    kept = forward(gathered, bottom, skipped)
    partial_sums = dice_terms(kept[8], pixel_mask, labels, member)
    totals = lax.psum(partial_sums, ("ha", "wa"))
    pad_zero, pre_one, pad_one, pre_two, hidden_two, pad_two, pre_three, hidden_three, logits = kept
    weight_one, weight_two, weight_up, weight_three, weight_head = gathered
    loss_value, grad_logits = dice_back(logits, pixel_mask, labels, member, totals)
    head_grad = jnp.einsum(
        "shwc,shwk->ck", hidden_three, grad_logits, preferred_element_type=jnp.float32
    )
    grad_hidden = jnp.einsum(
        "shwk,ck->shwc", grad_logits, weight_head, preferred_element_type=jnp.float32
    )
    grad_pre_three = smooth_back(pre_three, grad_hidden).astype(jnp.bfloat16)
    conv3_grad, grad_joined = conv_back(pad_two, grad_pre_three, weight_three, weight_up.shape[1] // 4)
    grad_upsampled = grad_joined.astype(jnp.bfloat16)
    up_grad, grad_hidden_two = upsample_back(hidden_two, grad_upsampled, weight_up)
    grad_pre_two = smooth_back(pre_two, grad_hidden_two).astype(jnp.bfloat16)
    conv2_grad, grad_hidden_one = conv_back(pad_one, grad_pre_two, weight_two, pad_one.shape[3])
    grad_pre_one = smooth_back(pre_one, grad_hidden_one).astype(jnp.bfloat16)
    conv1_grad, _ = conv_back(pad_zero, grad_pre_one, weight_one, 0)
    sums = (
        lax.psum_scatter(conv1_grad.astype(jnp.bfloat16), ("ha", "wa"), scatter_dimension=0, tiled=True),
        lax.psum_scatter(conv2_grad.astype(jnp.bfloat16), ("ha", "wa"), scatter_dimension=0, tiled=True),
        lax.psum_scatter(up_grad.astype(jnp.bfloat16), ("ha", "wa"), scatter_dimension=0, tiled=True),
        lax.psum_scatter(conv3_grad.astype(jnp.bfloat16), ("ha", "wa"), scatter_dimension=0, tiled=True),
        lax.psum_scatter(head_grad.astype(jnp.bfloat16), ("ha", "wa"), scatter_dimension=0, tiled=True),
    )
    return (loss_value, *[s.astype(jnp.float32) for s in sums])


MESH = pl.DeviceIdType.MESH
FLOAT = jnp.float32
HALF = jnp.bfloat16


def place():
    row, col = (lax.axis_index("ha"), lax.axis_index("wa"))
    return (row // 2, row % 2, col // 2, col % 2)


def spot(z, x, y, c):
    return (2 * z + x, 2 * y + c)


def greet_all():
    row, col = (lax.axis_index("ha"), lax.axis_index("wa"))
    rows, cols = (lax.axis_size("ha"), lax.axis_size("wa"))
    barrier = pltpu.get_barrier_semaphore()
    for step in range(1, rows * cols):
        other = lax.rem(row * cols + col + step, rows * cols)
        pl.semaphore_signal(
            barrier, inc=1, device_id=(other // cols, lax.rem(other, cols)), device_id_type=MESH
        )
    pl.semaphore_wait(barrier, rows * cols - 1)


def remote(source, target, send_sem, recv_sem, device):
    return pltpu.make_async_remote_copy(
        src_ref=source,
        dst_ref=target,
        send_sem=send_sem,
        recv_sem=recv_sem,
        device_id=device,
        device_id_type=MESH,
    )


def gelu_of(value):
    inner = 0.7978845608028654 * (value + 0.044715 * value * value * value)
    return 0.5 * value * (1.0 + jnp.tanh(inner))


def conv_slice(source, weight, parts, index, chan):
    parts[...] = jnp.zeros_like(parts)

    def row_tap(r, carry):
        window = source[index, pl.ds(r, 16)].reshape(512, chan)
        for c in range(3):
            start = pl.multiple_of((3 * r + c) * chan, chan)
            parts[c] += jnp.dot(
                window, weight[pl.ds(start, chan), :], preferred_element_type=FLOAT
            )
        return carry

    lax.fori_loop(0, 3, row_tap, 0)
    shape = (16, 32, 256)
    column = lax.broadcasted_iota(jnp.int32, shape, 1)
    low = jnp.where(column > 0, pltpu.roll(parts[0].reshape(shape), 1, 1), 0.0)
    high = jnp.where(column < 31, pltpu.roll(parts[2].reshape(shape), 31, 1), 0.0)
    return parts[1].reshape(shape) + low + high


def front_kernel(
    compute,
    bot, skip, w1, w2, wu, w3, wh,
    x0_out, h1_out, h2_out, sk_out, w2_out, wu_out, w3_out, wh_out, pre1_out, pre2_out,
    xr, x0, w1q, w2q, h1s, h1, parts, h2s,
    send, here, r_bot, r_grp, r_w1, r_w1x, r_w2, r_w2x, r_h1, r_h2, r_skip, r_wh, r_w3, r_wu,
):
    z, x, y, c = place()
    ha, wa = (2 * z + x, 2 * y + c)
    x_peer, y_peer, c_peer = (spot(z, 1 - x, y, c), spot(z, x, 1 - y, c), spot(z, x, y, 1 - c))
    mine = ha * 4 + wa
    greet_all()
    sends = []
    stays = []

    def go(source, target, recv_sem, device):
        copy = remote(source, target, send.at[len(sends)], recv_sem, device)
        copy.start()
        sends.append(copy)
        return copy

    def stay(source, target):
        copy = pltpu.make_async_copy(source, target, here.at[len(stays)])
        copy.start()
        stays.append([copy, False])
        return stays[-1]

    def settle(entry):
        entry[0].wait()
        entry[1] = True

    own_bot = stay(bot.at[ha], xr.at[ha, wa])
    bots = [
        go(bot.at[lax.rem(ha + d, 8)], xr.at[ha, wa], r_bot.at[d - 1], (lax.rem(ha + d, 8), wa))
        for d in range(1, 8)
    ]

    def spread(shard, whole, rows, recv):
        place_rows = whole.at[pl.ds(pl.multiple_of(mine * rows, rows), rows)]
        own = stay(shard.at[:, pl.ds(pl.multiple_of(wa * 256, 256), 256)], place_rows)
        copies = [[], [], [], []]
        for dz in range(4):
            for dw in range(4):
                if dz == 0 and dw == 0:
                    continue
                to = lax.rem(wa + dw, 4)
                copies[dz].append(
                    go(
                        shard.at[:, pl.ds(pl.multiple_of(to * 256, 256), 256)],
                        place_rows,
                        recv.at[dz, dw],
                        (lax.rem(z + dz, 4) * 2 + x, to),
                    )
                )
        return (own, copies)

    def pass_x(whole, rows, got, recv):
        own, copies = got
        settle(own)
        passed = []
        for dz in range(4):
            for copy in copies[dz]:
                copy.wait_recv()
            origin = lax.rem(z + 4 - dz, 4)
            block = whole.at[pl.ds(pl.multiple_of((origin * 2 + x) * 4 * rows, 4 * rows), 4 * rows)]
            passed.append(go(block, block, recv.at[dz], x_peer))
        return passed

    got_w1 = spread(w1, w1q, 144, r_w1)
    got_w2 = spread(w2, w2q, 288, r_w2)

    settle(own_bot)
    for copy in bots:
        copy.wait_recv()
    to_c = go(xr.at[:, wa], xr.at[:, wa], r_grp.at[0], c_peer)
    to_y = go(xr.at[:, wa], xr.at[:, wa], r_grp.at[1], y_peer)

    def spread_z(shard, whole, recv):
        own = stay(shard, whole.at[z, x, y, c])
        copies = [
            go(shard, whole.at[z, x, y, c], recv.at[d - 1], spot(lax.rem(z + d, 4), x, y, c))
            for d in range(1, 4)
        ]
        return (own, copies)

    def spread_two(whole, got, recv, half):
        own, copies = got
        settle(own)
        for copy in copies:
            copy.wait_recv()
        low, high = (pl.ds(0, half), pl.ds(half, half))
        part = whole.at[:, x, y, c]
        core = go(part, part, recv.at[3], c_peer)
        part = whole.at[:, x, y, c, :, low]
        first = go(part, part, recv.at[4], x_peer)
        part = whole.at[:, x, y, c, :, high]
        second = go(part, part, recv.at[5], y_peer)
        return (core, first, second)

    def spread_three(whole, got, recv, half):
        core, first, second = got
        low, high = (pl.ds(0, half), pl.ds(half, half))
        first.wait_recv()
        part = whole.at[:, :, y, c, :, low]
        third = go(part, part, recv.at[6], y_peer)
        part = whole.at[:, 1 - x, y, c, :, low]
        core_first = go(part, part, recv.at[8], c_peer)
        second.wait_recv()
        part = whole.at[:, x, :, c, :, high]
        fourth = go(part, part, recv.at[7], x_peer)
        part = whole.at[:, x, 1 - y, c, :, high]
        core_second = go(part, part, recv.at[9], c_peer)
        return (core, core_first, core_second, third, fourth)

    def spread_four(whole, got, recv, half):
        core, core_first, core_second, third, fourth = got
        low, high = (pl.ds(0, half), pl.ds(half, half))
        third.wait_recv()
        part = whole.at[:, :, 1 - y, c, :, low]
        core_third = go(part, part, recv.at[10], c_peer)
        fourth.wait_recv()
        part = whole.at[:, 1 - x, :, c, :, high]
        core_fourth = go(part, part, recv.at[11], c_peer)
        return (core, core_first, core_second, core_third, core_fourth)

    own_head = stay(wh, wh_out.at[mine])
    heads = []
    for step in range(1, 32):
        other = lax.rem(mine + step, 32)
        heads.append(go(wh, wh_out.at[mine], r_wh.at[step - 1], (other // 4, lax.rem(other, 4))))

    passed_w1 = pass_x(w1q, 144, got_w1, r_w1x)
    got_w3 = spread_z(w3, w3_out, r_w3)

    to_y.wait_recv()
    part = xr.at[:, 2 * (1 - y) + c]
    on_c = go(part, part, r_grp.at[2], c_peer)
    to_c.wait_recv()
    on_c.wait_recv()

    if compute:
        x0[:, 0] = jnp.zeros((3, 32, 512), HALF)
        x0[:, 17] = jnp.zeros((3, 32, 512), HALF)
        h1[:, 0] = jnp.zeros((3, 32, 1024), HALF)
        h1[:, 17] = jnp.zeros((3, 32, 1024), HALF)

        def reorder(h, carry):
            block = xr[h].astype(FLOAT).reshape(4, 3, 2, 8, 512)
            for s in range(3):
                for r in range(2):
                    row = jnp.concatenate([block[w, s, r] for w in range(4)], axis=0)
                    x0[s, 2 * h + 1 + r] = row.astype(HALF)
            return carry

        lax.fori_loop(0, 8, reorder, 0)
    stay(x0.at[:, pl.ds(1, 16)], x0_out)

    for copy in passed_w1:
        copy.wait_recv()
    if compute:

        def one(s, carry):
            value = conv_slice(x0, w1q, parts, s, 512)
            pre1_out[s] = value
            h1s[s] = gelu_of(value).astype(HALF)
            return carry

        lax.fori_loop(0, 3, one, 0)

    def lanes(col):
        return h1.at[:, pl.ds(1, 16), :, pl.ds(pl.multiple_of(col * 256, 256), 256)]

    own_h1 = stay(h1s, lanes(wa))
    h1_c = go(h1s, lanes(wa), r_h1.at[0], c_peer)
    h1_y = go(h1s, lanes(wa), r_h1.at[1], y_peer)

    passed_w2 = pass_x(w2q, 288, got_w2, r_w2x)
    got_wu = spread_z(wu, wu_out, r_wu)
    own_skip = stay(skip.at[ha], sk_out.at[ha])
    skips = [
        go(skip.at[lax.rem(ha + d, 8)], sk_out.at[ha], r_skip.at[d - 1], (lax.rem(ha + d, 8), wa))
        for d in range(1, 8)
    ]
    got_w3 = spread_two(w3_out, got_w3, r_w3, 256)

    h1_y.wait_recv()
    h1_on = go(lanes(2 * (1 - y) + c), lanes(2 * (1 - y) + c), r_h1.at[2], c_peer)
    settle(own_h1)
    h1_c.wait_recv()
    h1_on.wait_recv()
    stay(h1.at[:, pl.ds(1, 16)], h1_out)

    for copy in passed_w2:
        copy.wait_recv()
    stay(w2q, w2_out)
    if compute:

        def two(s, carry):
            value = conv_slice(h1, w2q, parts, s, 1024)
            pre2_out[s] = value
            hidden = gelu_of(value)
            for w in range(4):
                tile = hidden[:, 8 * w : 8 * w + 8].reshape(128, 256)
                h2s[w, pl.ds(pl.multiple_of(s * 128, 128), 128)] = tile.astype(HALF)
                left = hidden[:, 8 * w - 1] if w > 0 else jnp.zeros((16, 256), FLOAT)
                h2s[w, pl.ds(pl.multiple_of(384 + s * 16, 16), 16)] = left.astype(HALF)
                right = hidden[:, 8 * w + 8] if w < 3 else jnp.zeros((16, 256), FLOAT)
                h2s[w, pl.ds(pl.multiple_of(432 + s * 16, 16), 16)] = right.astype(HALF)
            return carry

        lax.fori_loop(0, 3, two, 0)
    h2_lanes = h2_out.at[:, pl.ds(pl.multiple_of(wa * 256, 256), 256)]
    stay(h2s.at[wa], h2_lanes)
    h2_got = [
        go(h2s.at[lax.rem(wa + d, 4)], h2_lanes, r_h2.at[d - 1], (ha, lax.rem(wa + d, 4)))
        for d in range(1, 4)
    ]

    got_wu = spread_two(wu_out, got_wu, r_wu, 1024)
    got_w3 = spread_three(w3_out, got_w3, r_w3, 256)
    got_wu = spread_three(wu_out, got_wu, r_wu, 1024)
    got_w3 = spread_four(w3_out, got_w3, r_w3, 256)
    got_wu = spread_four(wu_out, got_wu, r_wu, 1024)
    for copy in list(got_w3) + list(got_wu) + h2_got + skips + heads:
        copy.wait_recv()
    for entry in stays:
        if not entry[1]:
            settle(entry)
    for copy in sends:
        copy.wait_send()


def front(bot, skip, w1, w2, wu, w3, wh, compute=True):
    anywhere = pl.BlockSpec(memory_space=pl.ANY)
    inside = pl.BlockSpec(memory_space=pltpu.VMEM)
    shape = jax.ShapeDtypeStruct
    dma = pltpu.SemaphoreType.DMA
    return pl.pallas_call(
        functools.partial(front_kernel, compute),
        name="front",
        out_shape=(
            shape((3, 16, 32, 512), HALF),
            shape((3, 16, 32, 1024), HALF),
            shape((480, 1024), HALF),
            shape((8, 192, 512), HALF),
            shape((9216, 256), HALF),
            shape((4, 2, 2, 2, 32, 2048), HALF),
            shape((4, 2, 2, 2, 288, 512), HALF),
            shape((32, 16, 128), HALF),
            shape((3, 16, 32, 256), FLOAT),
            shape((3, 16, 32, 256), FLOAT),
        ),
        in_specs=[anywhere] * 7,
        out_specs=[anywhere] * 8 + [inside] * 2,
        scratch_shapes=[
            pltpu.VMEM((8, 4, 48, 512), HALF),
            pltpu.VMEM((3, 18, 32, 512), HALF),
            pltpu.VMEM((4608, 256), HALF),
            pltpu.VMEM((9216, 256), HALF),
            pltpu.VMEM((3, 16, 32, 256), HALF),
            pltpu.VMEM((3, 18, 32, 1024), HALF),
            pltpu.VMEM((3, 512, 256), FLOAT),
            pltpu.VMEM((4, 480, 256), HALF),
            dma((136,)),
            dma((16,)),
            dma((7,)),
            dma((3,)),
            dma((4, 4)),
            dma((4,)),
            dma((4, 4)),
            dma((4,)),
            dma((3,)),
            dma((3,)),
            dma((7,)),
            dma((31,)),
            dma((12,)),
            dma((12,)),
        ],
        compiler_params=pltpu.CompilerParams(
            collective_id=0, has_side_effects=True, vmem_limit_bytes=60 * 1024 * 1024
        ),
    )(bot, skip, w1, w2, wu, w3, wh)


def sum_kernel(part, out, got, send, recv):
    row, col = (lax.axis_index("ha"), lax.axis_index("wa"))
    mine = row * 4 + col
    greet_all()
    copies = []
    for step in range(1, 32):
        other = lax.rem(mine + step, 32)
        copy = remote(
            part,
            got.at[step],
            send.at[step - 1],
            recv.at[step - 1],
            (other // 4, lax.rem(other, 4)),
        )
        copy.start()
        copies.append(copy)
    total = part[...]
    for step in range(1, 32):
        copies[step - 1].wait_recv()
        total = total + got[step]
    out[...] = total
    for copy in copies:
        copy.wait_send()


def sum_all(part):
    inside = pl.BlockSpec(memory_space=pltpu.VMEM)
    return pl.pallas_call(
        sum_kernel,
        name="sum_all",
        out_shape=jax.ShapeDtypeStruct((8, 128), FLOAT),
        in_specs=[inside],
        out_specs=inside,
        scratch_shapes=[
            pltpu.VMEM((32, 8, 128), FLOAT),
            pltpu.SemaphoreType.DMA((31,)),
            pltpu.SemaphoreType.DMA((31,)),
        ],
        compiler_params=pltpu.CompilerParams(collective_id=1, has_side_effects=True),
    )(part)


def add_into(total, term, count, pick):
    def step(i, carry):
        at_total, at_term = pick(i)
        value = total[at_total].astype(FLOAT) + term[at_term].astype(FLOAT)
        total[at_total] = value.astype(HALF)
        return carry

    lax.fori_loop(0, count, step, 0)


def back_kernel(
    d3, du, d2, d1, dh,
    g3, gu, g2, g1, gh,
    l3, c3, y3, x3, z3, lu, cu, yu, xu, zu, m2, a2, b2, t2, m1, a1, b1, t1, hh,
    send, here, r_3, r_u, r_2, r_1, r_h,
):
    z, x, y, c = place()
    ha, wa = (2 * z + x, 2 * y + c)
    x_peer, y_peer, c_peer = (spot(z, 1 - x, y, c), spot(z, x, 1 - y, c), spot(z, x, y, 1 - c))
    mine = ha * 4 + wa
    greet_all()
    sends = []
    stays = []

    def go(source, target, recv_sem, device):
        copy = remote(source, target, send.at[len(sends)], recv_sem, device)
        copy.start()
        sends.append(copy)
        return copy

    def stay(source, target):
        copy = pltpu.make_async_copy(source, target, here.at[len(stays)])
        copy.start()
        stays.append([copy, False])
        return stays[-1]

    def settle(entry):
        entry[0].wait()
        entry[1] = True

    def all_core(grad, own, core, recv):
        return (stay(grad.at[:, :, :, c], own), go(grad.at[:, :, :, 1 - c], core, recv.at[0], c_peer))

    def all_y(own, core, along_y, recv, got):
        settle(got[0])
        got[1].wait_recv()
        add_into(own, core, 8, lambda i: ((i // 2, i % 2, 1 - y),) * 2)
        copy = go(own.at[:, :, 1 - y], along_y, recv.at[1], y_peer)
        add_into(own, core, 8, lambda i: ((i // 2, i % 2, y),) * 2)
        return copy

    def all_x(own, along_y, along_x, recv, got):
        got.wait_recv()
        add_into(own, along_y, 4, lambda i: ((i, 1 - x, y), (i, 1 - x)))
        copy = go(own.at[:, 1 - x, y], along_x, recv.at[2], x_peer)
        add_into(own, along_y, 4, lambda i: ((i, x, y), (i, x)))
        return copy

    def all_z(own, along_x, along_z, recv, got):
        got.wait_recv()
        add_into(own, along_x, 4, lambda i: ((i, x, y), (i,)))
        return [
            go(
                own.at[lax.rem(z + d, 4), x, y],
                along_z.at[d - 1],
                recv.at[2 + d],
                spot(lax.rem(z + d, 4), x, y, c),
            )
            for d in range(1, 4)
        ]

    def all_end(own, along_z, out, got):
        total = own[z, x, y].astype(FLOAT)
        for d in range(3):
            got[d].wait_recv()
            total = total + along_z[d].astype(FLOAT)
        out[...] = total

    def quarter_x(grad, own, along_x, recv):
        return (stay(grad.at[:, x], own), go(grad.at[:, 1 - x], along_x, recv.at[0], x_peer))

    def quarter_z(own, along_x, along_z, recv, got):
        settle(got[0])
        got[1].wait_recv()
        add_into(own, along_x, 16, lambda i: ((i // 4, i % 4),) * 2)
        return [
            go(
                own.at[lax.rem(z + d, 4)],
                along_z.at[d - 1],
                recv.at[d],
                spot(lax.rem(z + d, 4), x, y, c),
            )
            for d in range(1, 4)
        ]

    def quarter_w(own, along_z, total, out, recv, got):
        for copy in got:
            copy.wait_recv()

        def step(w, carry):
            value = own[z, w].astype(FLOAT)
            for d in range(3):
                value = value + along_z[d, w].astype(FLOAT)
            total[w] = value.astype(HALF)
            return carry

        lax.fori_loop(0, 4, step, 0)
        target = out.at[:, pl.ds(pl.multiple_of(wa * 256, 256), 256)]
        stay(total.at[wa], target)
        return [
            go(total.at[lax.rem(wa + d, 4)], target, recv.at[3 + d], (ha, lax.rem(wa + d, 4)))
            for d in range(1, 4)
        ]

    s3 = all_core(d3, l3, c3, r_3)
    su = all_core(du, lu, cu, r_u)
    s2 = quarter_x(d2, m2, a2, r_2)
    s1 = quarter_x(d1, m1, a1, r_1)
    own_head = stay(dh.at[mine], hh.at[0])
    heads = []
    for step in range(1, 32):
        other = lax.rem(mine + step, 32)
        heads.append(
            go(dh.at[other], hh.at[step], r_h.at[step - 1], (other // 4, lax.rem(other, 4)))
        )
    s3 = all_y(l3, c3, y3, r_3, s3)
    su = all_y(lu, cu, yu, r_u, su)
    s2 = quarter_z(m2, a2, b2, r_2, s2)
    s3 = all_x(l3, y3, x3, r_3, s3)
    su = all_x(lu, yu, xu, r_u, su)
    s1 = quarter_z(m1, a1, b1, r_1, s1)
    s3 = all_z(l3, x3, z3, r_3, s3)
    su = all_z(lu, xu, zu, r_u, su)
    s2 = quarter_w(m2, b2, t2, g2, r_2, s2)
    s1 = quarter_w(m1, b1, t1, g1, r_1, s1)
    settle(own_head)
    total = hh[0]
    for step in range(1, 32):
        heads[step - 1].wait_recv()
        total = total + hh[step]
    gh[...] = total
    all_end(l3, z3, g3, s3)
    all_end(lu, zu, gu, su)
    for copy in s2 + s1:
        copy.wait_recv()
    for entry in stays:
        if not entry[1]:
            settle(entry)
    for copy in sends:
        copy.wait_send()


def back(d3, du, d2, d1, dh):
    anywhere = pl.BlockSpec(memory_space=pl.ANY)
    inside = pl.BlockSpec(memory_space=pltpu.VMEM)
    shape = jax.ShapeDtypeStruct
    dma = pltpu.SemaphoreType.DMA

    def whole(rows, cols):
        return [
            pltpu.VMEM((4, 2, 2, rows, cols), HALF),
            pltpu.VMEM((4, 2, 2, rows, cols), HALF),
            pltpu.VMEM((4, 2, rows, cols), HALF),
            pltpu.VMEM((4, rows, cols), HALF),
            pltpu.VMEM((3, rows, cols), HALF),
        ]

    def quarter(rows):
        return [
            pltpu.VMEM((4, 4, rows, 256), HALF),
            pltpu.VMEM((4, 4, rows, 256), HALF),
            pltpu.VMEM((3, 4, rows, 256), HALF),
            pltpu.VMEM((4, rows, 256), HALF),
        ]

    return pl.pallas_call(
        back_kernel,
        name="back",
        out_shape=(
            shape((288, 512), FLOAT),
            shape((32, 2048), FLOAT),
            shape((288, 1024), HALF),
            shape((144, 1024), HALF),
            shape((16, 128), FLOAT),
        ),
        in_specs=[anywhere] * 5,
        out_specs=[inside] * 5,
        scratch_shapes=whole(288, 512)
        + whole(32, 2048)
        + quarter(288)
        + quarter(144)
        + [
            pltpu.VMEM((32, 16, 128), FLOAT),
            dma((64,)),
            dma((8,)),
            dma((6,)),
            dma((6,)),
            dma((7,)),
            dma((7,)),
            dma((31,)),
        ],
        compiler_params=pltpu.CompilerParams(
            collective_id=2, has_side_effects=True, vmem_limit_bytes=60 * 1024 * 1024
        ),
    )(d3, du, d2, d1, dh)


def conv_with(source, weight, col_rim):
    chan = source.shape[3]
    return lax.conv_general_dilated(
        source,
        weight.reshape(3, 3, chan, weight.shape[1]),
        (1, 1),
        ((1, 1), (col_rim, col_rim)),
        dimension_numbers=("NHWC", "HWIO", "NHWC"),
        preferred_element_type=FLOAT,
    )


def conv_weight_grad(source, grad, col_rim):
    return lax.conv_general_dilated(
        source,
        grad,
        (1, 1),
        ((1, 1), (col_rim, col_rim)),
        dimension_numbers=("CHWN", "IHWO", "HWNC"),
        preferred_element_type=FLOAT,
    ).reshape(9 * source.shape[3], grad.shape[3])


def conv_source_grad(grad, weight, chan, col_rim):
    kernel = weight.reshape(3, 3, -1, weight.shape[1])[::-1, ::-1, :chan]
    return lax.conv_general_dilated(
        grad,
        kernel,
        (1, 1),
        ((1, 1), (col_rim, col_rim)),
        dimension_numbers=("NHWC", "HWOI", "NHWC"),
        preferred_element_type=FLOAT,
    )


def with_cols(block):
    return with_halo(block, (("wa", 2),), 1)


def sliced_grads(
    bottom, skipped, groups, pixel_mask, labels, weight_one, weight_two, weight_up, weight_three,
    weight_head,
):
    ha = lax.axis_index("ha")
    code = lax.all_to_all(pixel_mask + 2 * labels, "ha", 0, 1, tiled=True)
    mask, label = (code % 2, code // 2)
    head_rows = jnp.pad(weight_head.astype(HALF), ((0, 0), (0, 126)))
    x0, h1, h2, skip, w2, wu, w3, wh, pre_one, pre_two = front(
        bottom.reshape(8, 48, 512),
        skipped.reshape(8, 192, 512),
        weight_one.astype(HALF),
        weight_two.astype(HALF),
        weight_up.astype(HALF),
        weight_three.astype(HALF),
        head_rows,
    )
    wu = wu.reshape(1024, 2048)
    w3 = w3.reshape(9216, 512)
    wh = wh.reshape(512, 128)[:, :2]
    skip = skip.reshape(8, 3, 4, 16, 512).transpose(1, 0, 2, 3, 4).reshape(3, 32, 16, 512)
    skip = with_cols(skip)
    hidden_two = h2[:384].reshape(3, 16, 8, 1024)
    ups = upsample(hidden_two, wu).astype(HALF)
    taps = wu.reshape(1024, 2, 2, 512)
    rims = [
        jnp.einsum(
            "pc,caq->paq",
            h2[384 + 48 * side : 432 + 48 * side],
            taps[:, :, 1 - side],
            preferred_element_type=FLOAT,
        )
        .astype(HALF)
        .reshape(3, 32, 1, 512)
        for side in range(2)
    ]
    joined = jnp.concatenate(
        [jnp.concatenate([rims[0], ups, rims[1]], axis=2), skip], axis=3
    )
    pre_three = conv_with(joined, w3, 0)
    hidden_three = smooth(pre_three).astype(HALF)
    logits = jnp.einsum("shwc,ck->shwk", hidden_three, wh, preferred_element_type=FLOAT)
    member = (groups[:, None] == jnp.arange(GROUPS)[None, :]).astype(FLOAT)
    member = lax.dynamic_slice_in_dim(member, 3 * ha, 3, axis=0)
    sums = dice_terms(logits, mask, label, member).reshape(1, 30)
    sums = sum_all(jnp.pad(sums, ((0, 7), (0, 98))))
    totals = sums[0, :30].reshape(GROUPS, 2, 3)
    loss_value, grad_logits = dice_back(logits, mask, label, member, totals)
    head_grad = jnp.einsum("shwc,shwk->ck", hidden_three, grad_logits, preferred_element_type=FLOAT)
    grad_hidden = jnp.einsum("shwk,ck->shwc", grad_logits, wh, preferred_element_type=FLOAT)
    grad_three = smooth_back(pre_three, grad_hidden).astype(HALF)
    grad_wide = with_cols(grad_three)
    d3 = conv_weight_grad(joined, grad_three, 0).astype(HALF)
    grad_ups = conv_source_grad(grad_wide, w3, 512, 0).astype(HALF)
    du, grad_hidden_two = upsample_back(hidden_two, grad_ups, wu)
    grad_hidden_two = lax.all_to_all(grad_hidden_two.astype(HALF), "wa", 3, 2, tiled=True)
    grad_two = smooth_back(pre_two, grad_hidden_two.astype(FLOAT)).astype(HALF)
    d2 = conv_weight_grad(h1, grad_two, 1).astype(HALF)
    grad_hidden_one = conv_source_grad(grad_two, w2, 1024, 1).astype(HALF)
    grad_hidden_one = lax.psum_scatter(grad_hidden_one, "wa", scatter_dimension=3, tiled=True)
    grad_one = smooth_back(pre_one, grad_hidden_one.astype(FLOAT)).astype(HALF)
    d1 = conv_weight_grad(x0, grad_one, 1).astype(HALF)
    g3, gu, g2, g1, gh = back(
        d3.reshape(4, 2, 2, 2, 288, 512),
        du.astype(HALF).reshape(4, 2, 2, 2, 32, 2048),
        d2.reshape(4, 2, 4, 288, 256),
        d1.reshape(4, 2, 4, 144, 256),
        jnp.pad(head_grad, ((0, 0), (0, 126))).reshape(32, 16, 128),
    )
    return (loss_value, g1.astype(FLOAT), g2.astype(FLOAT), gu, g3, gh[:, :2])


def body(
    bottom,
    skipped,
    groups,
    pixel_mask,
    labels,
    conv1_weight,
    conv1_momentum,
    conv1_average,
    conv2_weight,
    conv2_momentum,
    conv2_average,
    up_weight,
    up_momentum,
    up_average,
    conv3_weight,
    conv3_momentum,
    conv3_average,
    head_weight,
    head_momentum,
    head_average,
):
    split = bottom.shape[0] == 24 and bottom.shape[1:3] == (2, 8) and bottom.shape[3] == 512
    split = split and (lax.axis_size("ha"), lax.axis_size("wa")) == (8, 4)
    grads = sliced_grads if split else tiled_grads
    loss_value, conv1_grad, conv2_grad, up_grad, conv3_grad, head_grad = grads(
        bottom,
        skipped,
        groups,
        pixel_mask,
        labels,
        conv1_weight,
        conv2_weight,
        up_weight,
        conv3_weight,
        head_weight,
    )
    first = renew_state(conv1_weight, conv1_momentum, conv1_average, conv1_grad, RATE_CONV)
    second = renew_state(conv2_weight, conv2_momentum, conv2_average, conv2_grad, RATE_CONV)
    upward = renew_state(up_weight, up_momentum, up_average, up_grad, RATE_CONV)
    third = renew_state(conv3_weight, conv3_momentum, conv3_average, conv3_grad, RATE_CONV)
    header = renew_state(head_weight, head_momentum, head_average, head_grad, RATE_HEAD)
    return (
        loss_value,
        first[0],
        first[1],
        first[2],
        second[0],
        second[1],
        second[2],
        upward[0],
        upward[1],
        upward[2],
        third[0],
        third[1],
        third[2],
        header[0],
        header[1],
        header[2],
    )


def solution(mesh):
    in_specs = (
        P(None, "ha", "wa", None),
        P(None, "ha", "wa", None),
        P(),
        P(None, "ha", "wa"),
        P(None, "ha", "wa"),
        P(("ha", "wa"), None),
        P(("ha", "wa"), None),
        P(("ha", "wa"), None),
        P(("ha", "wa"), None),
        P(("ha", "wa"), None),
        P(("ha", "wa"), None),
        P(("ha", "wa"), None),
        P(("ha", "wa"), None),
        P(("ha", "wa"), None),
        P(("ha", "wa"), None),
        P(("ha", "wa"), None),
        P(("ha", "wa"), None),
        P(("ha", "wa"), None),
        P(("ha", "wa"), None),
        P(("ha", "wa"), None),
    )
    out_specs = (
        P(),
        P(("ha", "wa"), None),
        P(("ha", "wa"), None),
        P(("ha", "wa"), None),
        P(("ha", "wa"), None),
        P(("ha", "wa"), None),
        P(("ha", "wa"), None),
        P(("ha", "wa"), None),
        P(("ha", "wa"), None),
        P(("ha", "wa"), None),
        P(("ha", "wa"), None),
        P(("ha", "wa"), None),
        P(("ha", "wa"), None),
        P(("ha", "wa"), None),
        P(("ha", "wa"), None),
        P(("ha", "wa"), None),
    )
    return jax.shard_map(body, mesh=mesh, in_specs=in_specs, out_specs=out_specs, check_vma=False)
```

```python
import functools

import jax
import jax.numpy as jnp
from jax import lax
from jax.experimental import pallas as pl
from jax.experimental.pallas import tpu as pltpu
from jax.sharding import PartitionSpec as P

GROUPS = 5


MOMENTUM = 0.9
RATE_CONV = 600.0
RATE_HEAD = 25.0
AVERAGE_DECAY = 0.5
SMOOTHING = 1.0
HIGHEST = lax.Precision.HIGHEST


def with_halo(block, sides, width):
    for axis, dim in sides:
        count = lax.axis_size(axis)
        forward = [(i, i + 1) for i in range(count - 1)]
        backward = [(target, source) for source, target in forward]
        low = lax.ppermute(
            lax.slice_in_dim(block, block.shape[dim] - width, None, axis=dim), axis, forward
        )
        high = lax.ppermute(lax.slice_in_dim(block, 0, width, axis=dim), axis, backward)
        block = jnp.concatenate([low, block, high], axis=dim)
    return block


def smooth(source):
    return jax.nn.gelu(source, approximate=True)


def smooth_back(pre_value, gradient):
    _, pull_back = jax.vjp(smooth, pre_value)
    return pull_back(gradient)[0]


def widened_field(source):
    return with_halo(source, (("ha", 1), ("wa", 2)), 1)


def conv_taps(padded, weight):
    kernel = weight.reshape(3, 3, padded.shape[3], weight.shape[1])
    return lax.conv_general_dilated(
        padded,
        kernel,
        (1, 1),
        "VALID",
        dimension_numbers=("NHWC", "HWIO", "NHWC"),
        preferred_element_type=jnp.float32,
    )


def conv_back(padded, grad_out, weight, back_chan):
    in_chan = padded.shape[3]
    weight_grad = lax.conv_general_dilated(
        padded,
        grad_out,
        (1, 1),
        "VALID",
        dimension_numbers=("CHWN", "IHWO", "HWNC"),
        preferred_element_type=jnp.float32,
    ).reshape(9 * in_chan, grad_out.shape[3])
    if not back_chan:
        return (weight_grad, None)
    grad_padded = widened_field(grad_out)
    kernel = weight.reshape(3, 3, in_chan, weight.shape[1])[::-1, ::-1, :back_chan]
    source_grad = lax.conv_general_dilated(
        grad_padded,
        kernel,
        (1, 1),
        "VALID",
        dimension_numbers=("NHWC", "HWOI", "NHWC"),
        preferred_element_type=jnp.float32,
    )
    return (weight_grad, source_grad)


def upsample(source, weight):
    slices, row_count, col_count, _ = source.shape
    flattened = jnp.einsum("shwc,cq->shwq", source, weight, preferred_element_type=jnp.float32)
    blocks = flattened.reshape(slices, row_count, col_count, 2, 2, -1).transpose(0, 1, 3, 2, 4, 5)
    return blocks.reshape(slices, 2 * row_count, 2 * col_count, -1)


def upsample_back(source, grad_up, weight):
    slices, row_count, col_count, _ = source.shape
    blocks = grad_up.reshape(slices, row_count, 2, col_count, 2, -1).transpose(0, 1, 3, 2, 4, 5)
    flattened = blocks.reshape(slices, row_count, col_count, -1)
    weight_grad = jnp.einsum("shwc,shwq->cq", source, flattened, preferred_element_type=jnp.float32)
    source_grad = jnp.einsum("shwq,cq->shwc", flattened, weight, preferred_element_type=jnp.float32)
    return (weight_grad, source_grad)


def forward(gathered, bottom, skipped):
    weight_one, weight_two, weight_up, weight_three, weight_head = gathered
    pad_zero = widened_field(bottom)
    pre_one = conv_taps(pad_zero, weight_one)
    hidden_one = smooth(pre_one).astype(jnp.bfloat16)
    pad_one = widened_field(hidden_one)
    pre_two = conv_taps(pad_one, weight_two)
    hidden_two = smooth(pre_two).astype(jnp.bfloat16)
    upsampled = upsample(hidden_two, weight_up).astype(jnp.bfloat16)
    joined = jnp.concatenate([upsampled, skipped], axis=3)
    pad_two = widened_field(joined)
    pre_three = conv_taps(pad_two, weight_three)
    hidden_three = smooth(pre_three).astype(jnp.bfloat16)
    logits = jnp.einsum(
        "shwc,ck->shwk", hidden_three, weight_head, preferred_element_type=jnp.float32
    )
    return (
        pad_zero,
        pre_one,
        pad_one,
        pre_two,
        hidden_two,
        pad_two,
        pre_three,
        hidden_three,
        logits,
    )


def pixel_terms(logits, pixel_mask, labels):
    probability = jax.nn.softmax(logits, axis=-1)
    classes = jnp.arange(logits.shape[-1])
    target = (labels[..., None] == classes[None, None, None, :]).astype(jnp.float32)
    weighted = pixel_mask[..., None].astype(jnp.float32)
    return (probability, target, weighted)


def dice_terms(logits, pixel_mask, labels, member):
    probability, target, weighted = pixel_terms(logits, pixel_mask, labels)
    per_slice = jnp.stack(
        [
            jnp.sum(weighted * probability * target, axis=(1, 2)),
            jnp.sum(weighted * probability, axis=(1, 2)),
            jnp.sum(weighted * target, axis=(1, 2)),
        ],
        axis=-1,
    )
    return jnp.einsum("skj,sg->gkj", per_slice, member, precision=HIGHEST)


def dice_back(logits, pixel_mask, labels, member, totals):
    probability, target, weighted = pixel_terms(logits, pixel_mask, labels)
    union_sum = totals[..., 1] + totals[..., 2] + SMOOTHING
    numerator = 2.0 * totals[..., 0] + SMOOTHING
    dice_score = numerator / union_sum
    loss_value = 1.0 - jnp.mean(dice_score)
    entry_count = float(dice_score.size)
    coef_common = -2.0 / (entry_count * union_sum)
    coef_prob = numerator / (entry_count * union_sum * union_sum)
    slice_common = jnp.einsum("sg,gk->sk", member, coef_common, precision=HIGHEST)
    slice_prob = jnp.einsum("sg,gk->sk", member, coef_prob, precision=HIGHEST)
    grad_prob = weighted * (target * slice_common[:, None, None, :] + slice_prob[:, None, None, :])
    inner = jnp.sum(probability * grad_prob, axis=-1, keepdims=True)
    grad_logits = (probability * (grad_prob - inner)).astype(jnp.bfloat16)
    return (loss_value, grad_logits)


def renew_state(weight, moment, average, gradient, rate):
    moment_new = MOMENTUM * moment + gradient
    weight_new = weight - rate * (gradient + MOMENTUM * moment_new)
    average_new = AVERAGE_DECAY * average + (1.0 - AVERAGE_DECAY) * weight_new
    return (weight_new, moment_new, average_new)


def tiled_grads(
    bottom, skipped, groups, pixel_mask, labels, conv1_weight, conv2_weight, up_weight, conv3_weight,
    head_weight,
):
    gathered = (
        lax.all_gather(conv1_weight.astype(jnp.bfloat16), ("ha", "wa"), axis=0, tiled=True),
        lax.all_gather(conv2_weight.astype(jnp.bfloat16), ("ha", "wa"), axis=0, tiled=True),
        lax.all_gather(up_weight.astype(jnp.bfloat16), ("ha", "wa"), axis=0, tiled=True),
        lax.all_gather(conv3_weight.astype(jnp.bfloat16), ("ha", "wa"), axis=0, tiled=True),
        lax.all_gather(head_weight.astype(jnp.bfloat16), ("ha", "wa"), axis=0, tiled=True),
    )
    member = (groups[:, None] == jnp.arange(GROUPS)[None, :]).astype(jnp.float32)
    kept = forward(gathered, bottom, skipped)
    partial_sums = dice_terms(kept[8], pixel_mask, labels, member)
    totals = lax.psum(partial_sums, ("ha", "wa"))
    pad_zero, pre_one, pad_one, pre_two, hidden_two, pad_two, pre_three, hidden_three, logits = kept
    weight_one, weight_two, weight_up, weight_three, weight_head = gathered
    loss_value, grad_logits = dice_back(logits, pixel_mask, labels, member, totals)
    head_grad = jnp.einsum(
        "shwc,shwk->ck", hidden_three, grad_logits, preferred_element_type=jnp.float32
    )
    grad_hidden = jnp.einsum(
        "shwk,ck->shwc", grad_logits, weight_head, preferred_element_type=jnp.float32
    )
    grad_pre_three = smooth_back(pre_three, grad_hidden).astype(jnp.bfloat16)
    conv3_grad, grad_joined = conv_back(pad_two, grad_pre_three, weight_three, weight_up.shape[1] // 4)
    grad_upsampled = grad_joined.astype(jnp.bfloat16)
    up_grad, grad_hidden_two = upsample_back(hidden_two, grad_upsampled, weight_up)
    grad_pre_two = smooth_back(pre_two, grad_hidden_two).astype(jnp.bfloat16)
    conv2_grad, grad_hidden_one = conv_back(pad_one, grad_pre_two, weight_two, pad_one.shape[3])
    grad_pre_one = smooth_back(pre_one, grad_hidden_one).astype(jnp.bfloat16)
    conv1_grad, _ = conv_back(pad_zero, grad_pre_one, weight_one, 0)
    sums = (
        lax.psum_scatter(conv1_grad.astype(jnp.bfloat16), ("ha", "wa"), scatter_dimension=0, tiled=True),
        lax.psum_scatter(conv2_grad.astype(jnp.bfloat16), ("ha", "wa"), scatter_dimension=0, tiled=True),
        lax.psum_scatter(up_grad.astype(jnp.bfloat16), ("ha", "wa"), scatter_dimension=0, tiled=True),
        lax.psum_scatter(conv3_grad.astype(jnp.bfloat16), ("ha", "wa"), scatter_dimension=0, tiled=True),
        lax.psum_scatter(head_grad.astype(jnp.bfloat16), ("ha", "wa"), scatter_dimension=0, tiled=True),
    )
    return (loss_value, *[s.astype(jnp.float32) for s in sums])


MESH = pl.DeviceIdType.MESH
FLOAT = jnp.float32
HALF = jnp.bfloat16


def place():
    row, col = (lax.axis_index("ha"), lax.axis_index("wa"))
    return (row // 2, row % 2, col // 2, col % 2)


def spot(z, x, y, c):
    return (2 * z + x, 2 * y + c)


def greet_all():
    row, col = (lax.axis_index("ha"), lax.axis_index("wa"))
    rows, cols = (lax.axis_size("ha"), lax.axis_size("wa"))
    barrier = pltpu.get_barrier_semaphore()
    for step in range(1, rows * cols):
        other = lax.rem(row * cols + col + step, rows * cols)
        pl.semaphore_signal(
            barrier, inc=1, device_id=(other // cols, lax.rem(other, cols)), device_id_type=MESH
        )
    pl.semaphore_wait(barrier, rows * cols - 1)


def remote(source, target, send_sem, recv_sem, device):
    return pltpu.make_async_remote_copy(
        src_ref=source,
        dst_ref=target,
        send_sem=send_sem,
        recv_sem=recv_sem,
        device_id=device,
        device_id_type=MESH,
    )


def gelu_of(value):
    inner = 0.7978845608028654 * (value + 0.044715 * value * value * value)
    return 0.5 * value * (1.0 + jnp.tanh(inner))


def conv_slice(source, weight, parts, index, chan):
    parts[...] = jnp.zeros_like(parts)

    def row_tap(r, carry):
        window = source[index, pl.ds(r, 16)].reshape(512, chan)
        for c in range(3):
            start = pl.multiple_of((3 * r + c) * chan, chan)
            parts[c] += jnp.dot(
                window, weight[pl.ds(start, chan), :], preferred_element_type=FLOAT
            )
        return carry

    lax.fori_loop(0, 3, row_tap, 0)
    shape = (16, 32, 256)
    column = lax.broadcasted_iota(jnp.int32, shape, 1)
    low = jnp.where(column > 0, pltpu.roll(parts[0].reshape(shape), 1, 1), 0.0)
    high = jnp.where(column < 31, pltpu.roll(parts[2].reshape(shape), 31, 1), 0.0)
    return parts[1].reshape(shape) + low + high


def front_kernel(
    compute,
    bot, skip, w1, w2, wu, w3, wh,
    x0_out, h1_out, h2_out, sk_out, w2_out, wu_out, w3_out, wh_out, pre1_out, pre2_out,
    xr, x0, w1q, w2q, h1s, h1, parts, h2s,
    send, here, r_bot, r_grp, r_w1, r_w1x, r_w2, r_w2x, r_h1, r_h2, r_skip, r_wh, r_w3, r_wu,
):
    z, x, y, c = place()
    ha, wa = (2 * z + x, 2 * y + c)
    x_peer, y_peer, c_peer = (spot(z, 1 - x, y, c), spot(z, x, 1 - y, c), spot(z, x, y, 1 - c))
    mine = ha * 4 + wa
    greet_all()
    sends = []
    stays = []

    def go(source, target, recv_sem, device):
        copy = remote(source, target, send.at[len(sends)], recv_sem, device)
        copy.start()
        sends.append(copy)
        return copy

    def stay(source, target):
        copy = pltpu.make_async_copy(source, target, here.at[len(stays)])
        copy.start()
        stays.append([copy, False])
        return stays[-1]

    def settle(entry):
        entry[0].wait()
        entry[1] = True

    own_bot = stay(bot.at[ha], xr.at[ha, wa])
    bots = [
        go(bot.at[lax.rem(ha + d, 8)], xr.at[ha, wa], r_bot.at[d - 1], (lax.rem(ha + d, 8), wa))
        for d in range(1, 8)
    ]

    def spread(shard, whole, rows, recv):
        place_rows = whole.at[pl.ds(pl.multiple_of(mine * rows, rows), rows)]
        own = stay(shard.at[:, pl.ds(pl.multiple_of(wa * 256, 256), 256)], place_rows)
        copies = [[], [], [], []]
        for dz in range(4):
            for dw in range(4):
                if dz == 0 and dw == 0:
                    continue
                to = lax.rem(wa + dw, 4)
                copies[dz].append(
                    go(
                        shard.at[:, pl.ds(pl.multiple_of(to * 256, 256), 256)],
                        place_rows,
                        recv.at[dz, dw],
                        (lax.rem(z + dz, 4) * 2 + x, to),
                    )
                )
        return (own, copies)

    def pass_x(whole, rows, got, recv):
        own, copies = got
        settle(own)
        passed = []
        for dz in range(4):
            for copy in copies[dz]:
                copy.wait_recv()
            origin = lax.rem(z + 4 - dz, 4)
            block = whole.at[pl.ds(pl.multiple_of((origin * 2 + x) * 4 * rows, 4 * rows), 4 * rows)]
            passed.append(go(block, block, recv.at[dz], x_peer))
        return passed

    got_w1 = spread(w1, w1q, 144, r_w1)
    got_w2 = spread(w2, w2q, 288, r_w2)

    settle(own_bot)
    for copy in bots:
        copy.wait_recv()
    to_c = go(xr.at[:, wa], xr.at[:, wa], r_grp.at[0], c_peer)
    to_y = go(xr.at[:, wa], xr.at[:, wa], r_grp.at[1], y_peer)

    def spread_z(shard, whole, recv):
        own = stay(shard, whole.at[z, x, y, c])
        copies = [
            go(shard, whole.at[z, x, y, c], recv.at[d - 1], spot(lax.rem(z + d, 4), x, y, c))
            for d in range(1, 4)
        ]
        return (own, copies)

    def spread_two(whole, got, recv, half):
        own, copies = got
        settle(own)
        for copy in copies:
            copy.wait_recv()
        low, high = (pl.ds(0, half), pl.ds(half, half))
        part = whole.at[:, x, y, c]
        core = go(part, part, recv.at[3], c_peer)
        part = whole.at[:, x, y, c, :, low]
        first = go(part, part, recv.at[4], x_peer)
        part = whole.at[:, x, y, c, :, high]
        second = go(part, part, recv.at[5], y_peer)
        return (core, first, second)

    def spread_three(whole, got, recv, half):
        core, first, second = got
        low, high = (pl.ds(0, half), pl.ds(half, half))
        first.wait_recv()
        part = whole.at[:, :, y, c, :, low]
        third = go(part, part, recv.at[6], y_peer)
        part = whole.at[:, 1 - x, y, c, :, low]
        core_first = go(part, part, recv.at[8], c_peer)
        second.wait_recv()
        part = whole.at[:, x, :, c, :, high]
        fourth = go(part, part, recv.at[7], x_peer)
        part = whole.at[:, x, 1 - y, c, :, high]
        core_second = go(part, part, recv.at[9], c_peer)
        return (core, core_first, core_second, third, fourth)

    def spread_four(whole, got, recv, half):
        core, core_first, core_second, third, fourth = got
        low, high = (pl.ds(0, half), pl.ds(half, half))
        third.wait_recv()
        part = whole.at[:, :, 1 - y, c, :, low]
        core_third = go(part, part, recv.at[10], c_peer)
        fourth.wait_recv()
        part = whole.at[:, 1 - x, :, c, :, high]
        core_fourth = go(part, part, recv.at[11], c_peer)
        return (core, core_first, core_second, core_third, core_fourth)

    own_head = stay(wh, wh_out.at[mine])
    heads = []
    for step in range(1, 32):
        other = lax.rem(mine + step, 32)
        heads.append(go(wh, wh_out.at[mine], r_wh.at[step - 1], (other // 4, lax.rem(other, 4))))

    passed_w1 = pass_x(w1q, 144, got_w1, r_w1x)
    got_w3 = spread_z(w3, w3_out, r_w3)

    to_y.wait_recv()
    part = xr.at[:, 2 * (1 - y) + c]
    on_c = go(part, part, r_grp.at[2], c_peer)
    to_c.wait_recv()
    on_c.wait_recv()

    if compute:
        x0[:, 0] = jnp.zeros((3, 32, 512), HALF)
        x0[:, 17] = jnp.zeros((3, 32, 512), HALF)
        h1[:, 0] = jnp.zeros((3, 32, 1024), HALF)
        h1[:, 17] = jnp.zeros((3, 32, 1024), HALF)

        def reorder(h, carry):
            block = xr[h].astype(FLOAT).reshape(4, 3, 2, 8, 512)
            for s in range(3):
                for r in range(2):
                    row = jnp.concatenate([block[w, s, r] for w in range(4)], axis=0)
                    x0[s, 2 * h + 1 + r] = row.astype(HALF)
            return carry

        lax.fori_loop(0, 8, reorder, 0)
    stay(x0.at[:, pl.ds(1, 16)], x0_out)

    for copy in passed_w1:
        copy.wait_recv()
    if compute:

        def one(s, carry):
            value = conv_slice(x0, w1q, parts, s, 512)
            pre1_out[s] = value
            h1s[s] = gelu_of(value).astype(HALF)
            return carry

        lax.fori_loop(0, 3, one, 0)

    def lanes(col):
        return h1.at[:, pl.ds(1, 16), :, pl.ds(pl.multiple_of(col * 256, 256), 256)]

    own_h1 = stay(h1s, lanes(wa))
    h1_c = go(h1s, lanes(wa), r_h1.at[0], c_peer)
    h1_y = go(h1s, lanes(wa), r_h1.at[1], y_peer)

    passed_w2 = pass_x(w2q, 288, got_w2, r_w2x)
    got_wu = spread_z(wu, wu_out, r_wu)
    own_skip = stay(skip.at[ha], sk_out.at[ha])
    skips = [
        go(skip.at[lax.rem(ha + d, 8)], sk_out.at[ha], r_skip.at[d - 1], (lax.rem(ha + d, 8), wa))
        for d in range(1, 8)
    ]
    got_w3 = spread_two(w3_out, got_w3, r_w3, 256)

    h1_y.wait_recv()
    h1_on = go(lanes(2 * (1 - y) + c), lanes(2 * (1 - y) + c), r_h1.at[2], c_peer)
    settle(own_h1)
    h1_c.wait_recv()
    h1_on.wait_recv()
    stay(h1.at[:, pl.ds(1, 16)], h1_out)

    for copy in passed_w2:
        copy.wait_recv()
    stay(w2q, w2_out)
    if compute:

        def two(s, carry):
            value = conv_slice(h1, w2q, parts, s, 1024)
            pre2_out[s] = value
            hidden = gelu_of(value)
            for w in range(4):
                tile = hidden[:, 8 * w : 8 * w + 8].reshape(128, 256)
                h2s[w, pl.ds(pl.multiple_of(s * 128, 128), 128)] = tile.astype(HALF)
                left = hidden[:, 8 * w - 1] if w > 0 else jnp.zeros((16, 256), FLOAT)
                h2s[w, pl.ds(pl.multiple_of(384 + s * 16, 16), 16)] = left.astype(HALF)
                right = hidden[:, 8 * w + 8] if w < 3 else jnp.zeros((16, 256), FLOAT)
                h2s[w, pl.ds(pl.multiple_of(432 + s * 16, 16), 16)] = right.astype(HALF)
            return carry

        lax.fori_loop(0, 3, two, 0)
    h2_lanes = h2_out.at[:, pl.ds(pl.multiple_of(wa * 256, 256), 256)]
    stay(h2s.at[wa], h2_lanes)
    h2_got = [
        go(h2s.at[lax.rem(wa + d, 4)], h2_lanes, r_h2.at[d - 1], (ha, lax.rem(wa + d, 4)))
        for d in range(1, 4)
    ]

    got_wu = spread_two(wu_out, got_wu, r_wu, 1024)
    got_w3 = spread_three(w3_out, got_w3, r_w3, 256)
    got_wu = spread_three(wu_out, got_wu, r_wu, 1024)
    got_w3 = spread_four(w3_out, got_w3, r_w3, 256)
    got_wu = spread_four(wu_out, got_wu, r_wu, 1024)
    for copy in list(got_w3) + list(got_wu) + h2_got + skips + heads:
        copy.wait_recv()
    for entry in stays:
        if not entry[1]:
            settle(entry)
    for copy in sends:
        copy.wait_send()


def front(bot, skip, w1, w2, wu, w3, wh, compute=True):
    anywhere = pl.BlockSpec(memory_space=pl.ANY)
    inside = pl.BlockSpec(memory_space=pltpu.VMEM)
    shape = jax.ShapeDtypeStruct
    dma = pltpu.SemaphoreType.DMA
    return pl.pallas_call(
        functools.partial(front_kernel, compute),
        name="front",
        out_shape=(
            shape((3, 16, 32, 512), HALF),
            shape((3, 16, 32, 1024), HALF),
            shape((480, 1024), HALF),
            shape((8, 192, 512), HALF),
            shape((9216, 256), HALF),
            shape((4, 2, 2, 2, 32, 2048), HALF),
            shape((4, 2, 2, 2, 288, 512), HALF),
            shape((32, 16, 128), HALF),
            shape((3, 16, 32, 256), FLOAT),
            shape((3, 16, 32, 256), FLOAT),
        ),
        in_specs=[anywhere] * 7,
        out_specs=[anywhere] * 8 + [inside] * 2,
        scratch_shapes=[
            pltpu.VMEM((8, 4, 48, 512), HALF),
            pltpu.VMEM((3, 18, 32, 512), HALF),
            pltpu.VMEM((4608, 256), HALF),
            pltpu.VMEM((9216, 256), HALF),
            pltpu.VMEM((3, 16, 32, 256), HALF),
            pltpu.VMEM((3, 18, 32, 1024), HALF),
            pltpu.VMEM((3, 512, 256), FLOAT),
            pltpu.VMEM((4, 480, 256), HALF),
            dma((136,)),
            dma((16,)),
            dma((7,)),
            dma((3,)),
            dma((4, 4)),
            dma((4,)),
            dma((4, 4)),
            dma((4,)),
            dma((3,)),
            dma((3,)),
            dma((7,)),
            dma((31,)),
            dma((12,)),
            dma((12,)),
        ],
        compiler_params=pltpu.CompilerParams(
            collective_id=0, has_side_effects=True, vmem_limit_bytes=60 * 1024 * 1024
        ),
    )(bot, skip, w1, w2, wu, w3, wh)


def sum_kernel(part, out, got, send, recv):
    row, col = (lax.axis_index("ha"), lax.axis_index("wa"))
    mine = row * 4 + col
    greet_all()
    copies = []
    for step in range(1, 32):
        other = lax.rem(mine + step, 32)
        copy = remote(
            part,
            got.at[step],
            send.at[step - 1],
            recv.at[step - 1],
            (other // 4, lax.rem(other, 4)),
        )
        copy.start()
        copies.append(copy)
    total = part[...]
    for step in range(1, 32):
        copies[step - 1].wait_recv()
        total = total + got[step]
    out[...] = total
    for copy in copies:
        copy.wait_send()


def sum_all(part):
    inside = pl.BlockSpec(memory_space=pltpu.VMEM)
    return pl.pallas_call(
        sum_kernel,
        name="sum_all",
        out_shape=jax.ShapeDtypeStruct((8, 128), FLOAT),
        in_specs=[inside],
        out_specs=inside,
        scratch_shapes=[
            pltpu.VMEM((32, 8, 128), FLOAT),
            pltpu.SemaphoreType.DMA((31,)),
            pltpu.SemaphoreType.DMA((31,)),
        ],
        compiler_params=pltpu.CompilerParams(collective_id=1, has_side_effects=True),
    )(part)


def gelu_slope(value):
    square = value * value
    bend = jnp.tanh(0.7978845608028654 * value * (1.0 + 0.044715 * square))
    rise = 0.7978845608028654 * (1.0 + 3.0 * 0.044715 * square)
    return 0.5 * (1.0 + bend) + 0.5 * value * (1.0 - bend * bend) * rise


def across(source, window):
    return lax.dot_general(source, window, (((0,), (0,)), ((), ())), preferred_element_type=FLOAT)


def against(window, weight):
    return lax.dot_general(window, weight, (((1,), (1,)), ((), ())), preferred_element_type=FLOAT)


def add_rows(total, start, term, rows):
    where = pl.ds(pl.multiple_of(start, 16), rows)
    total[where] = (total[where].astype(FLOAT) + term.astype(FLOAT)).astype(HALF)


def back_kernel(
    gs_in, w3_in, wu_in, w2_in, joined_in, h2_in, h1_in, x0_in, pre1_in, pre2_in, dh,
    g3, gu, g2, g1, gh,
    gs3, joined, slot, acc, flat, wu, h2, gh2, from_wa, pre, gs2, d_core, d_y,
    du_c, du_y, du_x, du_z, d3, d3_c, d3_y, d3_x, d3_z, d2, d2_x, d2_z, d1_x, d1_z, hh,
    send, here, r_wa, r_d, r_u, r_3, r_2, r_1, r_h, free,
):
    z, x, y, c = place()
    ha, wa = (2 * z + x, 2 * y + c)
    x_peer, y_peer, c_peer = (spot(z, 1 - x, y, c), spot(z, x, 1 - y, c), spot(z, x, y, 1 - c))
    mine = ha * 4 + wa
    sends = []
    stays = []

    def go(source, target, recv_sem, device):
        copy = remote(source, target, send.at[len(sends)], recv_sem, device)
        copy.start()
        sends.append(copy)
        return copy

    def stay(source, target):
        copy = pltpu.make_async_copy(source, target, here.at[len(stays)])
        copy.start()
        stays.append([copy, False])
        return stays[-1]

    def settle(*entries):
        for entry in entries:
            entry[0].wait()
            entry[1] = True

    got_gs = stay(gs_in, gs3)
    got_w3 = [
        stay(
            w3_in.at[pl.ds(1024 * t, 512), pl.ds(256 * half, 256)],
            slot.at[pl.ds(4608 * half + 512 * t, 512)],
        )
        for half in range(2)
        for t in range(9)
    ]
    got_wu = stay(wu_in, wu)
    got_h2 = stay(h2_in.at[pl.ds(0, 384)], h2)
    got_joined = stay(joined_in, joined)
    greet_all()
    own_head = stay(dh.at[mine], hh.at[0])
    heads = []
    for step in range(1, 32):
        other = lax.rem(mine + step, 32)
        heads.append(
            go(dh.at[other], hh.at[step], r_h.at[step - 1], (other // 4, lax.rem(other, 4)))
        )

    order = lax.broadcasted_iota(jnp.int32, (256, 256), 0)
    inner = order % 128
    pick = (inner // 8) * 16 + (inner % 8) * 2 + order // 128
    apart = jnp.where(lax.broadcasted_iota(jnp.int32, (256, 256), 1) == pick, 1.0, 0.0).astype(HALF)
    settle(got_gs, *got_w3)

    def three_source(s, carry):
        acc[...] = jnp.zeros_like(acc)

        def tap(t, inner_carry):
            window = gs3[2 - t % 3, s, pl.ds(2 - t // 3, 32)].reshape(512, 512)
            for half in range(2):
                rows = pl.ds(pl.multiple_of(4608 * half + 512 * t, 512), 512)
                acc[...] += against(window[:, 256 * half : 256 * half + 256], slot[rows])
            return inner_carry

        lax.fori_loop(0, 9, tap, 0)
        fine = acc[...].astype(HALF).reshape(16, 2, 16, 512)
        for a in range(2):
            parted = jnp.dot(
                apart, fine[:, a].reshape(256, 512), preferred_element_type=FLOAT
            ).astype(HALF)
            for b in range(2):
                rows = pl.ds(pl.multiple_of(128 * s, 128), 128)
                flat[rows, pl.ds(512 * (2 * a + b), 512)] = parted[128 * b : 128 * b + 128]
        return carry

    lax.fori_loop(0, 3, three_source, 0)
    got_w2 = stay(w2_in, slot)
    settle(got_wu, got_h2)
    for part in range(4):
        lanes = slice(256 * part, 256 * part + 256)
        gh2[:, lanes] = against(flat[...], wu[lanes, :]).astype(HALF)

    def wa_lanes(col):
        return gh2.at[:, pl.ds(pl.multiple_of(col * 256, 256), 256)]

    own_wa = stay(wa_lanes(wa), from_wa.at[wa])
    got_wa = [
        go(
            wa_lanes(lax.rem(wa + d, 4)),
            from_wa.at[wa],
            r_wa.at[d - 1],
            (ha, lax.rem(wa + d, 4)),
        )
        for d in range(1, 4)
    ]
    for part in range(4):
        lanes = slice(512 * part, 512 * part + 512)
        wu[:, lanes] = across(h2[...], flat[:, lanes]).astype(HALF)

    def block(grad, rows, bz, bx, by, bc):
        number = ((bz * 2 + bx) * 2 + by) * 2 + bc
        return grad.at[pl.ds(pl.multiple_of(number * rows, 16), rows)]

    def all_core(grad, rows, core, recv, some):
        return [
            go(
                block(grad, rows, bz, bx, by, 1 - c),
                core.at[((bz - some[0]) * 2 + bx) * 2 + by],
                recv.at[((bz - some[0]) * 2 + bx) * 2 + by],
                c_peer,
            )
            for bz in some
            for bx in range(2)
            for by in range(2)
        ]

    def all_y(grad, rows, core, along_y, recv, some, got):
        for copy in got:
            copy.wait_recv()

        def step(by):
            def add(i, carry):
                number = (((some[0] * 2 + i) * 2) + by) * 2 + c
                add_rows(grad, number * rows, core[i * 2 + by], rows)
                return carry

            lax.fori_loop(0, 2 * len(some), add, 0)

        step(1 - y)
        copies = [
            go(
                block(grad, rows, bz, bx, 1 - y, c),
                along_y.at[bz * 2 + bx],
                recv.at[16 + bz * 2 + bx],
                y_peer,
            )
            for bz in some
            for bx in range(2)
        ]
        step(y)
        return copies

    def all_x(grad, rows, along_y, along_x, recv, got):
        for copy in got:
            copy.wait_recv()

        def step(bx):
            def add(bz, carry):
                number = ((bz * 2 + bx) * 2 + y) * 2 + c
                add_rows(grad, number * rows, along_y[bz * 2 + bx], rows)
                return carry

            lax.fori_loop(0, 4, add, 0)

        step(1 - x)
        copies = [
            go(block(grad, rows, bz, 1 - x, y, c), along_x.at[bz], recv.at[24 + bz], x_peer)
            for bz in range(4)
        ]
        step(x)
        return copies

    def all_z(grad, rows, along_x, along_z, recv, got):
        for copy in got:
            copy.wait_recv()

        def add(bz, carry):
            number = ((bz * 2 + x) * 2 + y) * 2 + c
            add_rows(grad, number * rows, along_x[bz], rows)
            return carry

        lax.fori_loop(0, 4, add, 0)
        return [
            go(
                block(grad, rows, lax.rem(z + d, 4), x, y, c),
                along_z.at[d - 1],
                recv.at[27 + d],
                spot(lax.rem(z + d, 4), x, y, c),
            )
            for d in range(1, 4)
        ]

    def all_end(grad, rows, along_z, out, got):
        total = grad[pl.ds(pl.multiple_of(mine * rows, 16), rows)].astype(FLOAT)
        for d in range(3):
            got[d].wait_recv()
            total = total + along_z[d].astype(FLOAT)
        out[...] = total

    def quarter_x(grad, rows, along_x, recv, bz):
        source = grad.at[pl.ds(pl.multiple_of((bz * 2 + 1 - x) * 4 * rows, 16), 4 * rows)]
        return go(source, along_x.at[bz], recv.at[bz], x_peer)

    def quarter_z(grad, rows, along_x, along_z, recv, got):
        for copy in got:
            copy.wait_recv()

        def add(d, carry):
            bz = lax.rem(z + d, 4)
            add_rows(grad, (bz * 2 + x) * 4 * rows, along_x[bz], 4 * rows)
            return carry

        lax.fori_loop(0, 4, add, 0)
        return [
            go(
                grad.at[
                    pl.ds(pl.multiple_of((lax.rem(z + d, 4) * 2 + x) * 4 * rows, 16), 4 * rows)
                ],
                along_z.at[d - 1],
                recv.at[3 + d],
                spot(lax.rem(z + d, 4), x, y, c),
            )
            for d in range(1, 4)
        ]

    def quarter_w(grad, rows, along_z, out, recv, got):
        for copy in got:
            copy.wait_recv()

        own = pl.ds(pl.multiple_of(ha * 4 * rows, 16), 4 * rows)
        value = grad[own].astype(FLOAT)
        for d in range(3):
            value = value + along_z[d].astype(FLOAT)
        grad[own] = value.astype(HALF)
        target = out.at[:, pl.ds(pl.multiple_of(wa * 256, 256), 256)]

        def piece(col):
            return grad.at[pl.ds(pl.multiple_of((ha * 4 + col) * rows, 16), rows)]

        stay(piece(wa), target)
        return [
            go(
                piece(lax.rem(wa + d, 4)),
                target,
                recv.at[6 + d],
                (ha, lax.rem(wa + d, 4)),
            )
            for d in range(1, 4)
        ]

    su = all_core(wu, 32, du_c, r_u, (0, 1, 2, 3))
    settle(got_joined)

    def three_weight(t, carry):
        window = gs3[2 - t % 3, :, pl.ds(2 - t // 3, 32)].reshape(1536, 512)
        rows = pl.ds(pl.multiple_of(1024 * t, 1024), 1024)
        d3[rows] = across(joined[...], window).astype(HALF)
        return carry

    lax.fori_loop(0, 5, three_weight, 0)
    s3 = all_core(d3, 288, d3_c, r_3, (0, 1))
    su = all_y(wu, 32, du_c, du_y, r_u, (0, 1, 2, 3), su)
    s3_low = all_y(d3, 288, d3_c, d3_y, r_3, (0, 1), s3)
    pl.semaphore_signal(free, inc=1, device_id=c_peer, device_id_type=MESH)
    lax.fori_loop(5, 9, three_weight, 0)
    pl.semaphore_wait(free, 1)
    s3 = all_core(d3, 288, d3_c, r_3, (2, 3))
    got_h1 = stay(h1_in, joined)

    settle(own_wa)
    for copy in got_wa:
        copy.wait_recv()

    def put_columns(target, s, value):
        column = lax.broadcasted_iota(jnp.int32, (16, 32, 256), 1)
        target[0, s, pl.ds(1, 16)] = jnp.where(column > 0, pltpu.roll(value, 1, 1), 0.0).astype(HALF)
        target[1, s, pl.ds(1, 16)] = value.astype(HALF)
        target[2, s, pl.ds(1, 16)] = jnp.where(column < 31, pltpu.roll(value, 31, 1), 0.0).astype(
            HALF
        )

    for e in range(3):
        gs2[e, :, 0] = jnp.zeros((3, 32, 256), HALF)
        gs2[e, :, 17] = jnp.zeros((3, 32, 256), HALF)
    settle(stay(pre2_in, pre))

    def two_grad(s, carry):
        rows = pl.ds(pl.multiple_of(128 * s, 128), 128)
        parts = [from_wa[w, rows].astype(FLOAT).reshape(16, 8, 256) for w in range(4)]
        put_columns(gs2, s, jnp.concatenate(parts, axis=1) * gelu_slope(pre[s]))
        return carry

    lax.fori_loop(0, 3, two_grad, 0)
    got_pre1 = stay(pre1_in, pre)
    settle(got_h1)

    def two_weight(t, carry):
        window = gs2[2 - t % 3, :, pl.ds(2 - t // 3, 16)].reshape(1536, 256)
        rows = pl.ds(pl.multiple_of(1024 * t, 1024), 1024)
        d2[rows] = across(joined[...], window).astype(HALF)
        return carry

    s2 = []
    for bz, (first, last) in enumerate(((0, 3), (3, 5), (5, 7), (7, 9))):
        lax.fori_loop(first, last, two_weight, 0)
        s2.append(quarter_x(d2, 288, d2_x, r_2, bz))

    s3_high = all_y(d3, 288, d3_c, d3_y, r_3, (2, 3), s3)
    got_x0 = stay(x0_in, joined.at[:, pl.ds(0, 512)])
    settle(got_w2)

    def source_two(s):
        for half in range(2):
            acc[...] = jnp.zeros_like(acc)

            def tap(t, inner_carry):
                window = gs2[2 - t % 3, s, pl.ds(2 - t // 3, 16)].reshape(512, 256)
                rows = pl.ds(pl.multiple_of(1024 * t + 512 * half, 512), 512)
                acc[...] += against(window, slot[rows])
                return inner_carry

            lax.fori_loop(0, 9, tap, 0)
            gs3[half, s, pl.ds(0, 32)] = acc[...].astype(HALF).reshape(32, 16, 512)

    def d_lanes(halves, s, core):
        return gs3.at[halves, s, pl.ds(0, 32), :, pl.ds(pl.multiple_of(256 * core, 256), 256)]

    sd = []
    for s in range(3):
        source_two(s)
        sd.append(go(d_lanes(pl.ds(0, 2), s, 1 - c), d_core.at[s], r_d.at[s], c_peer))
        if s == 0:
            su = all_x(wu, 32, du_y, du_x, r_u, su)
    sy = []
    own_lanes = pl.ds(pl.multiple_of(256 * c, 256), 256)
    for s in range(3):
        sd[s].wait_recv()
        for half in range(2):
            value = gs3[half, s, pl.ds(0, 32), :, own_lanes].astype(FLOAT)
            value = value + d_core[s, half].astype(FLOAT)
            gs3[half, s, pl.ds(0, 32), :, own_lanes] = value.astype(HALF)
        sy.append(go(d_lanes(1 - y, s, c), d_y.at[s], r_d.at[3 + s], y_peer))
    s2 = quarter_z(d2, 288, d2_x, d2_z, r_2, s2)
    settle(got_pre1)
    for s in range(3):
        sy[s].wait_recv()
        value = gs3[y, s, pl.ds(0, 32), :, own_lanes].astype(FLOAT) + d_y[s].astype(FLOAT)
        put_columns(gs2, s, value.reshape(16, 32, 256) * gelu_slope(pre[s]))
    settle(got_x0)

    def one_weight(t, carry):
        window = gs2[2 - t % 3, :, pl.ds(2 - t // 3, 16)].reshape(1536, 256)
        rows = pl.ds(pl.multiple_of(512 * t, 512), 512)
        slot[rows] = across(joined[:, 0:512], window).astype(HALF)
        return carry

    s1 = []
    for bz, (first, last) in enumerate(((0, 3), (3, 5), (5, 7), (7, 9))):
        lax.fori_loop(first, last, one_weight, 0)
        s1.append(quarter_x(slot, 144, d1_x, r_1, bz))

    s3 = all_x(d3, 288, d3_y, d3_x, r_3, s3_low + s3_high)
    su = all_z(wu, 32, du_x, du_z, r_u, su)
    s2 = quarter_w(d2, 288, d2_z, g2, r_2, s2)
    s1 = quarter_z(slot, 144, d1_x, d1_z, r_1, s1)
    s3 = all_z(d3, 288, d3_x, d3_z, r_3, s3)
    settle(own_head)
    total = hh[0]
    for step in range(1, 32):
        heads[step - 1].wait_recv()
        total = total + hh[step]
    gh[...] = total
    all_end(wu, 32, du_z, gu, su)
    s1 = quarter_w(slot, 144, d1_z, g1, r_1, s1)
    all_end(d3, 288, d3_z, g3, s3)
    for copy in s2 + s1:
        copy.wait_recv()
    for entry in stays:
        if not entry[1]:
            settle(entry)
    for copy in sends:
        copy.wait_send()


def back(gs, w3, wu, w2, joined, h2, h1, x0, pre1, pre2, dh):
    anywhere = pl.BlockSpec(memory_space=pl.ANY)
    inside = pl.BlockSpec(memory_space=pltpu.VMEM)
    shape = jax.ShapeDtypeStruct
    dma = pltpu.SemaphoreType.DMA

    def room(*dims):
        return pltpu.VMEM(dims, HALF)

    return pl.pallas_call(
        back_kernel,
        name="back",
        out_shape=(
            shape((288, 512), FLOAT),
            shape((32, 2048), FLOAT),
            shape((288, 1024), HALF),
            shape((144, 1024), HALF),
            shape((16, 128), FLOAT),
        ),
        in_specs=[anywhere] * 11,
        out_specs=[inside, inside, anywhere, anywhere, inside],
        scratch_shapes=[
            room(3, 3, 34, 16, 512),
            room(1536, 1024),
            room(9216, 256),
            pltpu.VMEM((512, 512), FLOAT),
            room(384, 2048),
            room(1024, 2048),
            room(384, 1024),
            room(384, 1024),
            room(4, 384, 256),
            pltpu.VMEM((3, 16, 32, 256), FLOAT),
            room(3, 3, 18, 32, 256),
            room(3, 2, 32, 16, 256),
            room(3, 32, 16, 256),
            room(16, 32, 2048),
            room(8, 32, 2048),
            room(4, 32, 2048),
            room(3, 32, 2048),
            room(9216, 512),
            room(8, 288, 512),
            room(8, 288, 512),
            room(4, 288, 512),
            room(3, 288, 512),
            room(9216, 256),
            room(4, 1152, 256),
            room(3, 1152, 256),
            room(4, 576, 256),
            room(3, 576, 256),
            pltpu.VMEM((32, 16, 128), FLOAT),
            dma((144,)),
            dma((40,)),
            dma((3,)),
            dma((6,)),
            dma((31,)),
            dma((31,)),
            dma((10,)),
            dma((10,)),
            dma((31,)),
            pltpu.SemaphoreType.REGULAR,
        ],
        compiler_params=pltpu.CompilerParams(
            collective_id=2, has_side_effects=True, vmem_limit_bytes=64 * 1024 * 1024
        ),
    )(gs, w3, wu, w2, joined, h2, h1, x0, pre1, pre2, dh)


def conv_with(source, weight, col_rim):
    chan = source.shape[3]
    return lax.conv_general_dilated(
        source,
        weight.reshape(3, 3, chan, weight.shape[1]),
        (1, 1),
        ((1, 1), (col_rim, col_rim)),
        dimension_numbers=("NHWC", "HWIO", "NHWC"),
        preferred_element_type=FLOAT,
    )


def with_cols(block):
    return with_halo(block, (("wa", 2),), 1)


def sliced_grads(
    bottom, skipped, groups, pixel_mask, labels, weight_one, weight_two, weight_up, weight_three,
    weight_head,
):
    ha = lax.axis_index("ha")
    code = lax.all_to_all(pixel_mask + 2 * labels, "ha", 0, 1, tiled=True)
    mask, label = (code % 2, code // 2)
    head_rows = jnp.pad(weight_head.astype(HALF), ((0, 0), (0, 126)))
    x0, h1, h2, skip, w2, wu, w3, wh, pre_one, pre_two = front(
        bottom.reshape(8, 48, 512),
        skipped.reshape(8, 192, 512),
        weight_one.astype(HALF),
        weight_two.astype(HALF),
        weight_up.astype(HALF),
        weight_three.astype(HALF),
        head_rows,
    )
    wu = wu.reshape(1024, 2048)
    w3 = w3.reshape(9216, 512)
    wh = wh.reshape(512, 128)[:, :2]
    skip = skip.reshape(8, 3, 4, 16, 512).transpose(1, 0, 2, 3, 4).reshape(3, 32, 16, 512)
    skip = with_cols(skip)
    hidden_two = h2[:384].reshape(3, 16, 8, 1024)
    ups = upsample(hidden_two, wu).astype(HALF)
    taps = wu.reshape(1024, 2, 2, 512)
    rims = [
        jnp.einsum(
            "pc,caq->paq",
            h2[384 + 48 * side : 432 + 48 * side],
            taps[:, :, 1 - side],
            preferred_element_type=FLOAT,
        )
        .astype(HALF)
        .reshape(3, 32, 1, 512)
        for side in range(2)
    ]
    joined = jnp.concatenate(
        [jnp.concatenate([rims[0], ups, rims[1]], axis=2), skip], axis=3
    )
    pre_three = conv_with(joined, w3, 0)
    hidden_three = smooth(pre_three).astype(HALF)
    logits = jnp.einsum("shwc,ck->shwk", hidden_three, wh, preferred_element_type=FLOAT)
    member = (groups[:, None] == jnp.arange(GROUPS)[None, :]).astype(FLOAT)
    member = lax.dynamic_slice_in_dim(member, 3 * ha, 3, axis=0)
    sums = dice_terms(logits, mask, label, member).reshape(1, 30)
    sums = sum_all(jnp.pad(sums, ((0, 7), (0, 98))))
    totals = sums[0, :30].reshape(GROUPS, 2, 3)
    loss_value, grad_logits = dice_back(logits, mask, label, member, totals)
    head_grad = jnp.einsum("shwc,shwk->ck", hidden_three, grad_logits, preferred_element_type=FLOAT)
    grad_hidden = jnp.einsum("shwk,ck->shwc", grad_logits, wh, preferred_element_type=FLOAT)
    grad_three = smooth_back(pre_three, grad_hidden).astype(HALF)
    grad_wide = with_cols(grad_three)
    grad_rows = jnp.pad(grad_wide, ((0, 0), (1, 1), (0, 0), (0, 0)))
    shifts = jnp.stack([grad_rows[:, :, e : e + 16] for e in range(3)])
    g3, gu, g2, g1, gh = back(
        shifts,
        w3,
        wu,
        w2,
        joined[:, :, 1:17].reshape(1536, 1024),
        h2,
        h1.reshape(1536, 1024),
        x0.reshape(1536, 512),
        pre_one,
        pre_two,
        jnp.pad(head_grad, ((0, 0), (0, 126))).reshape(32, 16, 128),
    )
    return (loss_value, g1.astype(FLOAT), g2.astype(FLOAT), gu, g3, gh[:, :2])


def body(
    bottom,
    skipped,
    groups,
    pixel_mask,
    labels,
    conv1_weight,
    conv1_momentum,
    conv1_average,
    conv2_weight,
    conv2_momentum,
    conv2_average,
    up_weight,
    up_momentum,
    up_average,
    conv3_weight,
    conv3_momentum,
    conv3_average,
    head_weight,
    head_momentum,
    head_average,
):
    split = bottom.shape[0] == 24 and bottom.shape[1:3] == (2, 8) and bottom.shape[3] == 512
    split = split and (lax.axis_size("ha"), lax.axis_size("wa")) == (8, 4)
    grads = sliced_grads if split else tiled_grads
    loss_value, conv1_grad, conv2_grad, up_grad, conv3_grad, head_grad = grads(
        bottom,
        skipped,
        groups,
        pixel_mask,
        labels,
        conv1_weight,
        conv2_weight,
        up_weight,
        conv3_weight,
        head_weight,
    )
    first = renew_state(conv1_weight, conv1_momentum, conv1_average, conv1_grad, RATE_CONV)
    second = renew_state(conv2_weight, conv2_momentum, conv2_average, conv2_grad, RATE_CONV)
    upward = renew_state(up_weight, up_momentum, up_average, up_grad, RATE_CONV)
    third = renew_state(conv3_weight, conv3_momentum, conv3_average, conv3_grad, RATE_CONV)
    header = renew_state(head_weight, head_momentum, head_average, head_grad, RATE_HEAD)
    return (
        loss_value,
        first[0],
        first[1],
        first[2],
        second[0],
        second[1],
        second[2],
        upward[0],
        upward[1],
        upward[2],
        third[0],
        third[1],
        third[2],
        header[0],
        header[1],
        header[2],
    )


def solution(mesh):
    in_specs = (
        P(None, "ha", "wa", None),
        P(None, "ha", "wa", None),
        P(),
        P(None, "ha", "wa"),
        P(None, "ha", "wa"),
        P(("ha", "wa"), None),
        P(("ha", "wa"), None),
        P(("ha", "wa"), None),
        P(("ha", "wa"), None),
        P(("ha", "wa"), None),
        P(("ha", "wa"), None),
        P(("ha", "wa"), None),
        P(("ha", "wa"), None),
        P(("ha", "wa"), None),
        P(("ha", "wa"), None),
        P(("ha", "wa"), None),
        P(("ha", "wa"), None),
        P(("ha", "wa"), None),
        P(("ha", "wa"), None),
        P(("ha", "wa"), None),
    )
    out_specs = (
        P(),
        P(("ha", "wa"), None),
        P(("ha", "wa"), None),
        P(("ha", "wa"), None),
        P(("ha", "wa"), None),
        P(("ha", "wa"), None),
        P(("ha", "wa"), None),
        P(("ha", "wa"), None),
        P(("ha", "wa"), None),
        P(("ha", "wa"), None),
        P(("ha", "wa"), None),
        P(("ha", "wa"), None),
        P(("ha", "wa"), None),
        P(("ha", "wa"), None),
        P(("ha", "wa"), None),
        P(("ha", "wa"), None),
    )
    return jax.shard_map(body, mesh=mesh, in_specs=in_specs, out_specs=out_specs, check_vma=False)
```

```python
import functools

import jax
import jax.numpy as jnp
from jax import lax
from jax.experimental import pallas as pl
from jax.experimental.pallas import tpu as pltpu
from jax.sharding import PartitionSpec as P

GROUPS = 5


MOMENTUM = 0.9
RATE_CONV = 600.0
RATE_HEAD = 25.0
AVERAGE_DECAY = 0.5
SMOOTHING = 1.0
HIGHEST = lax.Precision.HIGHEST


def with_halo(block, sides, width):
    for axis, dim in sides:
        count = lax.axis_size(axis)
        forward = [(i, i + 1) for i in range(count - 1)]
        backward = [(target, source) for source, target in forward]
        low = lax.ppermute(
            lax.slice_in_dim(block, block.shape[dim] - width, None, axis=dim), axis, forward
        )
        high = lax.ppermute(lax.slice_in_dim(block, 0, width, axis=dim), axis, backward)
        block = jnp.concatenate([low, block, high], axis=dim)
    return block


def smooth(source):
    return jax.nn.gelu(source, approximate=True)


def smooth_back(pre_value, gradient):
    _, pull_back = jax.vjp(smooth, pre_value)
    return pull_back(gradient)[0]


def widened_field(source):
    return with_halo(source, (("ha", 1), ("wa", 2)), 1)


def conv_taps(padded, weight):
    kernel = weight.reshape(3, 3, padded.shape[3], weight.shape[1])
    return lax.conv_general_dilated(
        padded,
        kernel,
        (1, 1),
        "VALID",
        dimension_numbers=("NHWC", "HWIO", "NHWC"),
        preferred_element_type=jnp.float32,
    )


def conv_back(padded, grad_out, weight, back_chan):
    in_chan = padded.shape[3]
    weight_grad = lax.conv_general_dilated(
        padded,
        grad_out,
        (1, 1),
        "VALID",
        dimension_numbers=("CHWN", "IHWO", "HWNC"),
        preferred_element_type=jnp.float32,
    ).reshape(9 * in_chan, grad_out.shape[3])
    if not back_chan:
        return (weight_grad, None)
    grad_padded = widened_field(grad_out)
    kernel = weight.reshape(3, 3, in_chan, weight.shape[1])[::-1, ::-1, :back_chan]
    source_grad = lax.conv_general_dilated(
        grad_padded,
        kernel,
        (1, 1),
        "VALID",
        dimension_numbers=("NHWC", "HWOI", "NHWC"),
        preferred_element_type=jnp.float32,
    )
    return (weight_grad, source_grad)


def upsample(source, weight):
    slices, row_count, col_count, _ = source.shape
    flattened = jnp.einsum("shwc,cq->shwq", source, weight, preferred_element_type=jnp.float32)
    blocks = flattened.reshape(slices, row_count, col_count, 2, 2, -1).transpose(0, 1, 3, 2, 4, 5)
    return blocks.reshape(slices, 2 * row_count, 2 * col_count, -1)


def upsample_back(source, grad_up, weight):
    slices, row_count, col_count, _ = source.shape
    blocks = grad_up.reshape(slices, row_count, 2, col_count, 2, -1).transpose(0, 1, 3, 2, 4, 5)
    flattened = blocks.reshape(slices, row_count, col_count, -1)
    weight_grad = jnp.einsum("shwc,shwq->cq", source, flattened, preferred_element_type=jnp.float32)
    source_grad = jnp.einsum("shwq,cq->shwc", flattened, weight, preferred_element_type=jnp.float32)
    return (weight_grad, source_grad)


def forward(gathered, bottom, skipped):
    weight_one, weight_two, weight_up, weight_three, weight_head = gathered
    pad_zero = widened_field(bottom)
    pre_one = conv_taps(pad_zero, weight_one)
    hidden_one = smooth(pre_one).astype(jnp.bfloat16)
    pad_one = widened_field(hidden_one)
    pre_two = conv_taps(pad_one, weight_two)
    hidden_two = smooth(pre_two).astype(jnp.bfloat16)
    upsampled = upsample(hidden_two, weight_up).astype(jnp.bfloat16)
    joined = jnp.concatenate([upsampled, skipped], axis=3)
    pad_two = widened_field(joined)
    pre_three = conv_taps(pad_two, weight_three)
    hidden_three = smooth(pre_three).astype(jnp.bfloat16)
    logits = jnp.einsum(
        "shwc,ck->shwk", hidden_three, weight_head, preferred_element_type=jnp.float32
    )
    return (
        pad_zero,
        pre_one,
        pad_one,
        pre_two,
        hidden_two,
        pad_two,
        pre_three,
        hidden_three,
        logits,
    )


def pixel_terms(logits, pixel_mask, labels):
    probability = jax.nn.softmax(logits, axis=-1)
    classes = jnp.arange(logits.shape[-1])
    target = (labels[..., None] == classes[None, None, None, :]).astype(jnp.float32)
    weighted = pixel_mask[..., None].astype(jnp.float32)
    return (probability, target, weighted)


def dice_terms(logits, pixel_mask, labels, member):
    probability, target, weighted = pixel_terms(logits, pixel_mask, labels)
    per_slice = jnp.stack(
        [
            jnp.sum(weighted * probability * target, axis=(1, 2)),
            jnp.sum(weighted * probability, axis=(1, 2)),
            jnp.sum(weighted * target, axis=(1, 2)),
        ],
        axis=-1,
    )
    return jnp.einsum("skj,sg->gkj", per_slice, member, precision=HIGHEST)


def dice_back(logits, pixel_mask, labels, member, totals):
    probability, target, weighted = pixel_terms(logits, pixel_mask, labels)
    union_sum = totals[..., 1] + totals[..., 2] + SMOOTHING
    numerator = 2.0 * totals[..., 0] + SMOOTHING
    dice_score = numerator / union_sum
    loss_value = 1.0 - jnp.mean(dice_score)
    entry_count = float(dice_score.size)
    coef_common = -2.0 / (entry_count * union_sum)
    coef_prob = numerator / (entry_count * union_sum * union_sum)
    slice_common = jnp.einsum("sg,gk->sk", member, coef_common, precision=HIGHEST)
    slice_prob = jnp.einsum("sg,gk->sk", member, coef_prob, precision=HIGHEST)
    grad_prob = weighted * (target * slice_common[:, None, None, :] + slice_prob[:, None, None, :])
    inner = jnp.sum(probability * grad_prob, axis=-1, keepdims=True)
    grad_logits = (probability * (grad_prob - inner)).astype(jnp.bfloat16)
    return (loss_value, grad_logits)


def renew_state(weight, moment, average, gradient, rate):
    moment_new = MOMENTUM * moment + gradient
    weight_new = weight - rate * (gradient + MOMENTUM * moment_new)
    average_new = AVERAGE_DECAY * average + (1.0 - AVERAGE_DECAY) * weight_new
    return (weight_new, moment_new, average_new)


def tiled_grads(
    bottom, skipped, groups, pixel_mask, labels, conv1_weight, conv2_weight, up_weight, conv3_weight,
    head_weight,
):
    gathered = (
        lax.all_gather(conv1_weight.astype(jnp.bfloat16), ("ha", "wa"), axis=0, tiled=True),
        lax.all_gather(conv2_weight.astype(jnp.bfloat16), ("ha", "wa"), axis=0, tiled=True),
        lax.all_gather(up_weight.astype(jnp.bfloat16), ("ha", "wa"), axis=0, tiled=True),
        lax.all_gather(conv3_weight.astype(jnp.bfloat16), ("ha", "wa"), axis=0, tiled=True),
        lax.all_gather(head_weight.astype(jnp.bfloat16), ("ha", "wa"), axis=0, tiled=True),
    )
    member = (groups[:, None] == jnp.arange(GROUPS)[None, :]).astype(jnp.float32)
    kept = forward(gathered, bottom, skipped)
    partial_sums = dice_terms(kept[8], pixel_mask, labels, member)
    totals = lax.psum(partial_sums, ("ha", "wa"))
    pad_zero, pre_one, pad_one, pre_two, hidden_two, pad_two, pre_three, hidden_three, logits = kept
    weight_one, weight_two, weight_up, weight_three, weight_head = gathered
    loss_value, grad_logits = dice_back(logits, pixel_mask, labels, member, totals)
    head_grad = jnp.einsum(
        "shwc,shwk->ck", hidden_three, grad_logits, preferred_element_type=jnp.float32
    )
    grad_hidden = jnp.einsum(
        "shwk,ck->shwc", grad_logits, weight_head, preferred_element_type=jnp.float32
    )
    grad_pre_three = smooth_back(pre_three, grad_hidden).astype(jnp.bfloat16)
    conv3_grad, grad_joined = conv_back(pad_two, grad_pre_three, weight_three, weight_up.shape[1] // 4)
    grad_upsampled = grad_joined.astype(jnp.bfloat16)
    up_grad, grad_hidden_two = upsample_back(hidden_two, grad_upsampled, weight_up)
    grad_pre_two = smooth_back(pre_two, grad_hidden_two).astype(jnp.bfloat16)
    conv2_grad, grad_hidden_one = conv_back(pad_one, grad_pre_two, weight_two, pad_one.shape[3])
    grad_pre_one = smooth_back(pre_one, grad_hidden_one).astype(jnp.bfloat16)
    conv1_grad, _ = conv_back(pad_zero, grad_pre_one, weight_one, 0)
    sums = (
        lax.psum_scatter(conv1_grad.astype(jnp.bfloat16), ("ha", "wa"), scatter_dimension=0, tiled=True),
        lax.psum_scatter(conv2_grad.astype(jnp.bfloat16), ("ha", "wa"), scatter_dimension=0, tiled=True),
        lax.psum_scatter(up_grad.astype(jnp.bfloat16), ("ha", "wa"), scatter_dimension=0, tiled=True),
        lax.psum_scatter(conv3_grad.astype(jnp.bfloat16), ("ha", "wa"), scatter_dimension=0, tiled=True),
        lax.psum_scatter(head_grad.astype(jnp.bfloat16), ("ha", "wa"), scatter_dimension=0, tiled=True),
    )
    return (loss_value, *[s.astype(jnp.float32) for s in sums])


MESH = pl.DeviceIdType.MESH
FLOAT = jnp.float32
HALF = jnp.bfloat16


def place():
    row, col = (lax.axis_index("ha"), lax.axis_index("wa"))
    return (row // 2, row % 2, col // 2, col % 2)


def spot(z, x, y, c):
    return (2 * z + x, 2 * y + c)


def greet_all():
    row, col = (lax.axis_index("ha"), lax.axis_index("wa"))
    rows, cols = (lax.axis_size("ha"), lax.axis_size("wa"))
    barrier = pltpu.get_barrier_semaphore()
    for step in range(1, rows * cols):
        other = lax.rem(row * cols + col + step, rows * cols)
        pl.semaphore_signal(
            barrier, inc=1, device_id=(other // cols, lax.rem(other, cols)), device_id_type=MESH
        )
    pl.semaphore_wait(barrier, rows * cols - 1)


def remote(source, target, send_sem, recv_sem, device):
    return pltpu.make_async_remote_copy(
        src_ref=source,
        dst_ref=target,
        send_sem=send_sem,
        recv_sem=recv_sem,
        device_id=device,
        device_id_type=MESH,
    )


def gelu_of(value):
    inner = 0.7978845608028654 * (value + 0.044715 * value * value * value)
    return 0.5 * value * (1.0 + jnp.tanh(inner))


def conv_slice(source, weight, parts, index, chan):
    parts[...] = jnp.zeros_like(parts)

    def row_tap(r, carry):
        window = source[index, pl.ds(r, 16)].reshape(512, chan)
        for c in range(3):
            start = pl.multiple_of((3 * r + c) * chan, chan)
            parts[c] += jnp.dot(
                window, weight[pl.ds(start, chan), :], preferred_element_type=FLOAT
            )
        return carry

    lax.fori_loop(0, 3, row_tap, 0)
    shape = (16, 32, 256)
    column = lax.broadcasted_iota(jnp.int32, shape, 1)
    low = jnp.where(column > 0, pltpu.roll(parts[0].reshape(shape), 1, 1), 0.0)
    high = jnp.where(column < 31, pltpu.roll(parts[2].reshape(shape), 31, 1), 0.0)
    return parts[1].reshape(shape) + low + high


def put_shifts(target, lanes, s, value, left, right):
    column = lax.broadcasted_iota(jnp.int32, value.shape, 1)
    last = value.shape[1] - 1
    rows = pl.ds(1, value.shape[0])
    low = jnp.where(column > 0, pltpu.roll(value, 1, 1), left)
    target[0, s, rows, :, lanes] = low.astype(HALF)
    target[1, s, rows, :, lanes] = value.astype(HALF)
    high = jnp.where(column < last, pltpu.roll(value, last, 1), right)
    target[2, s, rows, :, lanes] = high.astype(HALF)


def front_kernel(
    compute,
    bot, skip, code, w1, w2, wu, w3, wh,
    x0_out, h1_out, h2_out, joined_out, w2_out, wu_out, w3_out, pre1_out, pre2_out, pre3_out,
    hidden_out, logit_out, code_out, sums_out, head_out,
    xr, x0, w1q, w2q, h1s, h1, parts, h2s, h2v, wuv, w3v, skv, rims, rims_got, tiles, whv,
    send, here, r_bot, r_grp, r_w1, r_w1x, r_w2, r_w2x, r_h1, r_h2, r_skip, r_wh, r_w3, r_wu,
    r_code, r_rim, r_sum,
):
    z, x, y, c = place()
    ha, wa = (2 * z + x, 2 * y + c)
    x_peer, y_peer, c_peer = (spot(z, 1 - x, y, c), spot(z, x, 1 - y, c), spot(z, x, y, 1 - c))
    mine = ha * 4 + wa
    greet_all()
    sends = []
    stays = []

    def go(source, target, recv_sem, device):
        copy = remote(source, target, send.at[len(sends)], recv_sem, device)
        copy.start()
        sends.append(copy)
        return copy

    def stay(source, target):
        copy = pltpu.make_async_copy(source, target, here.at[len(stays)])
        copy.start()
        stays.append([copy, False])
        return stays[-1]

    def settle(*entries):
        for entry in entries:
            entry[0].wait()
            entry[1] = True

    def arrive(*copies):
        for copy in copies:
            copy.wait_recv()

    def spread(shard, whole, rows, first, count, recv):
        start = pl.multiple_of(mine * rows + first, 16)
        place_rows = whole.at[pl.ds(start, count)]
        source_rows = pl.ds(first, count)
        lanes = [pl.ds(pl.multiple_of(lax.rem(wa + dw, 4) * 256, 256), 256) for dw in range(4)]
        own = stay(shard.at[source_rows, lanes[0]], place_rows)
        copies = [
            go(
                shard.at[source_rows, lanes[dw]],
                place_rows,
                recv.at[dz, dw],
                (lax.rem(z + dz, 4) * 2 + x, lax.rem(wa + dw, 4)),
            )
            for dz in (1, 2, 3, 0)
            for dw in range(4)
            if dz + dw > 0
        ]
        return (own, copies)

    def pass_x(whole, rows, first, count, got, recv):
        own, copies = got
        settle(own)
        arrive(*copies)
        if count == rows:
            spans = [(dz, 0, 4 * rows) for dz in range(4)]
        else:
            spans = [(dz, w * rows + first, count) for dz in range(4) for w in range(4)]
        passed = []
        for number, (dz, offset, length) in enumerate(spans):
            start = (lax.rem(z + 4 - dz, 4) * 2 + x) * 4 * rows + offset
            block = whole.at[pl.ds(pl.multiple_of(start, 16), length)]
            passed.append(go(block, block, recv.at[number], x_peer))
        return passed

    def spread_z(shard, whole, recv):
        own = stay(shard, whole.at[z, x, y, c])
        copies = [
            go(shard, whole.at[z, x, y, c], recv.at[d - 1], spot(lax.rem(z + d, 4), x, y, c))
            for d in range(1, 4)
        ]
        return (own, copies)

    def spread_two(whole, got, recv, half, width):
        settle(got[0])
        arrive(*got[1])
        low, high = (pl.ds(0, half), pl.ds(half, width - half))
        part = whole.at[:, x, y, c, :, low]
        first = go(part, part, recv.at[4], x_peer)
        part = whole.at[:, x, y, c, :, high]
        second = go(part, part, recv.at[5], y_peer)
        part = whole.at[:, x, y, c]
        core = go(part, part, recv.at[3], c_peer)
        return (core, first, second)

    def spread_three(whole, got, recv, half, width):
        core, first, second = got
        low, high = (pl.ds(0, half), pl.ds(half, width - half))
        arrive(first)
        part = whole.at[:, :, y, c, :, low]
        third = go(part, part, recv.at[6], y_peer)
        part = whole.at[:, 1 - x, y, c, :, low]
        core_first = go(part, part, recv.at[8], c_peer)
        arrive(second)
        part = whole.at[:, x, :, c, :, high]
        fourth = go(part, part, recv.at[7], x_peer)
        part = whole.at[:, x, 1 - y, c, :, high]
        core_second = go(part, part, recv.at[9], c_peer)
        return (core, core_first, core_second, third, fourth)

    def spread_four(whole, got, recv, half, width):
        core, core_first, core_second, third, fourth = got
        low, high = (pl.ds(0, half), pl.ds(half, width - half))
        arrive(third)
        part = whole.at[:, :, 1 - y, c, :, low]
        core_third = go(part, part, recv.at[10], c_peer)
        arrive(fourth)
        part = whole.at[:, 1 - x, :, c, :, high]
        core_fourth = go(part, part, recv.at[11], c_peer)
        arrive(core, core_first, core_second, core_third, core_fourth)

    own_bot = stay(bot.at[ha], xr.at[ha, wa])
    bots = [
        go(bot.at[lax.rem(ha + d, 8)], xr.at[ha, wa], r_bot.at[d - 1], (lax.rem(ha + d, 8), wa))
        for d in range(1, 8)
    ]
    got_w1 = spread(w1, w1q, 144, 0, 144, r_w1)
    own_code = stay(code.at[ha], code_out.at[ha])
    codes = [
        go(code.at[lax.rem(ha + d, 8)], code_out.at[ha], r_code.at[d - 1], (lax.rem(ha + d, 8), wa))
        for d in range(1, 8)
    ]
    own_head = stay(wh, whv.at[mine])
    heads = []
    for step in range(1, 32):
        other = lax.rem(mine + step, 32)
        heads.append(go(wh, whv.at[mine], r_wh.at[step - 1], (other // 4, lax.rem(other, 4))))
    settle(own_bot)
    arrive(*bots)
    to_c = go(xr.at[:, wa], xr.at[:, wa], r_grp.at[0], c_peer)
    to_y = go(xr.at[:, wa], xr.at[:, wa], r_grp.at[1], y_peer)
    if compute:
        x0[:, 0] = jnp.zeros((3, 32, 512), HALF)
        x0[:, 17] = jnp.zeros((3, 32, 512), HALF)
        h1[:, 0] = jnp.zeros((3, 32, 1024), HALF)
        h1[:, 17] = jnp.zeros((3, 32, 1024), HALF)
        for shift in range(3):
            tiles[shift, :, 0] = jnp.zeros((3, 16, 1024), HALF)
            tiles[shift, :, 33] = jnp.zeros((3, 16, 1024), HALF)
    passed_w1 = pass_x(w1q, 144, 0, 144, got_w1, r_w1x)
    got_w2a = spread(w2, w2q, 288, 0, 144, r_w2.at[0])
    arrive(to_y)
    part = xr.at[:, 2 * (1 - y) + c]
    on_c = go(part, part, r_grp.at[2], c_peer)
    arrive(to_c, on_c)

    if compute:

        def reorder(h, carry):
            block = xr[h].astype(FLOAT).reshape(4, 3, 2, 8, 512)
            for s in range(3):
                for r in range(2):
                    row = jnp.concatenate([block[w, s, r] for w in range(4)], axis=0)
                    x0[s, 2 * h + 1 + r] = row.astype(HALF)
            return carry

        lax.fori_loop(0, 8, reorder, 0)
    stay(x0.at[:, pl.ds(1, 16)], x0_out)
    passed_w2a = pass_x(w2q, 288, 0, 144, got_w2a, r_w2x.at[0])
    got_w2b = spread(w2, w2q, 288, 144, 144, r_w2.at[1])
    arrive(*passed_w1)
    if compute:

        def one(s, carry):
            value = conv_slice(x0, w1q, parts, s, 512)
            pre1_out[s] = value
            h1s[s] = gelu_of(value).astype(HALF)
            return carry

        lax.fori_loop(0, 3, one, 0)

    def lanes(col):
        return h1.at[:, pl.ds(1, 16), :, pl.ds(pl.multiple_of(col * 256, 256), 256)]

    own_h1 = stay(h1s, lanes(wa))
    h1_c = go(h1s, lanes(wa), r_h1.at[0], c_peer)
    h1_y = go(h1s, lanes(wa), r_h1.at[1], y_peer)

    passed_w2b = pass_x(w2q, 288, 144, 144, got_w2b, r_w2x.at[1])
    got_wu = spread_z(wu, wuv, r_wu)
    got_w3 = spread_z(w3, w3v, r_w3)
    own_skip = stay(skip.at[ha], skv.at[ha])
    skips = [
        go(skip.at[lax.rem(ha + d, 8)], skv.at[ha], r_skip.at[d - 1], (lax.rem(ha + d, 8), wa))
        for d in range(1, 8)
    ]
    arrive(h1_y)
    h1_on = go(lanes(2 * (1 - y) + c), lanes(2 * (1 - y) + c), r_h1.at[2], c_peer)
    settle(own_h1)
    arrive(h1_c, h1_on)
    stay(h1.at[:, pl.ds(1, 16)], h1_out)
    got_wu = spread_two(wuv, got_wu, r_wu, 1536, 2048)
    arrive(*passed_w2a, *passed_w2b)
    stay(w2q, w2_out)
    if compute:

        def two(s, carry):
            value = conv_slice(h1, w2q, parts, s, 1024)
            pre2_out[s] = value
            hidden = gelu_of(value)
            for w in range(4):
                tile = hidden[:, 8 * w : 8 * w + 8].reshape(128, 256)
                h2s[w, pl.ds(pl.multiple_of(s * 128, 128), 128)] = tile.astype(HALF)
                left = hidden[:, 8 * w - 1] if w > 0 else jnp.zeros((16, 256), FLOAT)
                h2s[w, pl.ds(pl.multiple_of(384 + s * 16, 16), 16)] = left.astype(HALF)
                right = hidden[:, 8 * w + 8] if w < 3 else jnp.zeros((16, 256), FLOAT)
                h2s[w, pl.ds(pl.multiple_of(432 + s * 16, 16), 16)] = right.astype(HALF)
            return carry

        lax.fori_loop(0, 3, two, 0)
    h2_lanes = h2v.at[:, pl.ds(pl.multiple_of(wa * 256, 256), 256)]
    own_h2 = stay(h2s.at[wa], h2_lanes)
    h2_got = [
        go(h2s.at[lax.rem(wa + d, 4)], h2_lanes, r_h2.at[d - 1], (ha, lax.rem(wa + d, 4)))
        for d in range(1, 4)
    ]
    got_w3 = spread_two(w3v, got_w3, r_w3, 384, 512)
    got_wu = spread_three(wuv, got_wu, r_wu, 1536, 2048)

    settle(own_skip)
    arrive(*skips)

    def skip_slice(s):
        return skv[:, 64 * s : 64 * s + 64].astype(FLOAT).reshape(32, 16, 512)

    if compute:
        for s in range(3):
            value = skip_slice(s)
            rims[0, s] = value[:, 0].astype(HALF)
            rims[1, s] = value[:, 15].astype(HALF)
    before = (ha, lax.rem(wa + 3, 4))
    after = (ha, lax.rem(wa + 1, 4))
    rim_right = go(rims.at[0], rims_got.at[1], r_rim.at[1], before)
    rim_left = go(rims.at[1], rims_got.at[0], r_rim.at[0], after)
    got_w3 = spread_three(w3v, got_w3, r_w3, 384, 512)
    arrive(rim_right, rim_left)
    if compute:
        for s in range(3):
            left = jnp.where(wa > 0, rims_got[0, s].astype(FLOAT), 0.0)
            right = jnp.where(wa < 3, rims_got[1, s].astype(FLOAT), 0.0)
            put_shifts(
                tiles, pl.ds(512, 512), s, skip_slice(s), left[:, None, :], right[:, None, :]
            )
    spread_four(wuv, got_wu, r_wu, 1536, 2048)
    stay(wuv, wu_out)
    settle(own_h2)
    arrive(*h2_got)
    stay(h2v, h2_out)
    if compute:
        order = lax.broadcasted_iota(jnp.int32, (256, 256), 1)
        inner = order % 128
        pick = (inner // 8) * 16 + (inner % 8) * 2 + order // 128
        woven = jnp.where(lax.broadcasted_iota(jnp.int32, (256, 256), 0) == pick, 1.0, 0.0)
        woven = woven.astype(HALF)
        wide = wuv.reshape(1024, 2048)
        for s in range(3):
            fine, sides = ([], ([], []))
            for a in range(2):
                weight = wide[:, 1024 * a : 1024 * a + 1024]
                flat = jnp.dot(
                    h2v[128 * s : 128 * s + 128], weight, preferred_element_type=FLOAT
                ).astype(HALF)
                flat = jnp.concatenate([flat[:, :512], flat[:, 512:]], axis=0)
                flat = jnp.dot(woven, flat, preferred_element_type=FLOAT)
                fine.append(flat.reshape(16, 16, 512))
                for side in range(2):
                    start = 384 + 48 * side + 16 * s
                    rim = jnp.dot(
                        h2v[start : start + 16],
                        weight[:, 512 * (1 - side) : 512 * (1 - side) + 512],
                        preferred_element_type=FLOAT,
                    )
                    sides[side].append(rim.astype(HALF).astype(FLOAT)[:, None, :])
            value = jnp.stack(fine, axis=1).reshape(32, 16, 512)
            left, right = [jnp.stack(side, axis=1).reshape(32, 1, 512) for side in sides]
            put_shifts(tiles, pl.ds(0, 512), s, value, left, right)
    stay(tiles.at[1, :, pl.ds(1, 32)], joined_out)
    settle(own_head)
    arrive(*heads)
    settle(own_code)
    arrive(*codes)
    spread_four(w3v, got_w3, r_w3, 384, 512)
    stay(w3v, w3_out)
    if compute:
        head = whv.reshape(512, 128)[...].astype(FLOAT).T[:16].astype(HALF)
        head_out[...] = head
        rows = w3v.reshape(9216, 512)
        row = lax.broadcasted_iota(jnp.int32, (8, 128), 0)
        lane = lax.broadcasted_iota(jnp.int32, (8, 128), 1)
        sums_out[0] = jnp.zeros((8, 128), FLOAT)

        def three(s, carry):
            pre3_out[s] = jnp.zeros((512, 512), FLOAT)

            def tap(t, inner_carry):
                window = tiles[t % 3, s, pl.ds(t // 3, 32)].reshape(512, 1024)
                start = pl.multiple_of(1024 * t, 1024)
                pre3_out[s] += jnp.dot(
                    window, rows[pl.ds(start, 1024), :], preferred_element_type=FLOAT
                )
                return inner_carry

            lax.fori_loop(0, 9, tap, 0)
            hidden = gelu_of(pre3_out[s]).astype(HALF)
            hidden_out[s] = hidden
            logits = lax.dot_general(
                head, hidden, (((1,), (1,)), ((), ())), preferred_element_type=FLOAT
            )
            logit_out[s] = logits
            return carry

        lax.fori_loop(0, 3, three, 0)
        total = jnp.zeros((8, 128), FLOAT)
        for s in range(3):
            probability, target, weighted = class_terms(logit_out, code_out, s)
            for k in range(2):
                terms = (
                    weighted * probability[k] * target[k],
                    weighted * probability[k],
                    weighted * target[k],
                )
                for j, term in enumerate(terms):
                    value = jnp.sum(term, axis=1, keepdims=True)
                    here_is = jnp.logical_and(row == s, lane == 3 * k + j)
                    total = total + jnp.where(here_is, value, 0.0)
        sums_out[0] = total
    sums = []
    for step in range(1, 32):
        other = lax.rem(mine + step, 32)
        sums.append(
            go(
                sums_out.at[0],
                sums_out.at[step],
                r_sum.at[step - 1],
                (other // 4, lax.rem(other, 4)),
            )
        )
    arrive(*sums)
    for entry in stays:
        if not entry[1]:
            settle(entry)
    for copy in sends:
        copy.wait_send()


def class_terms(logits, codes, s):
    pieces = [codes[2 * q, s : s + 1] + codes[2 * q + 1, s : s + 1] for q in range(4)]
    both = jnp.concatenate(pieces, axis=1)
    label = jnp.where(both >= 2.0, 1.0, 0.0)
    weighted = both - 2.0 * label
    first, second = (logits[s, 0:1], logits[s, 1:2])
    top = jnp.maximum(first, second)
    first, second = (jnp.exp(first - top), jnp.exp(second - top))
    scale = 1.0 / (first + second)
    return ((first * scale, second * scale), (1.0 - label, label), weighted)


def front(bot, skip, code, w1, w2, wu, w3, wh, compute=True):
    anywhere = pl.BlockSpec(memory_space=pl.ANY)
    inside = pl.BlockSpec(memory_space=pltpu.VMEM)
    shape = jax.ShapeDtypeStruct
    dma = pltpu.SemaphoreType.DMA

    def room(*dims):
        return pltpu.VMEM(dims, HALF)

    return pl.pallas_call(
        functools.partial(front_kernel, compute),
        name="front",
        out_shape=(
            shape((3, 16, 32, 512), HALF),
            shape((3, 16, 32, 1024), HALF),
            shape((480, 1024), HALF),
            shape((3, 32, 16, 1024), HALF),
            shape((9216, 256), HALF),
            shape((4, 2, 2, 2, 32, 2048), HALF),
            shape((4, 2, 2, 2, 288, 512), HALF),
            shape((3, 16, 32, 256), FLOAT),
            shape((3, 16, 32, 256), FLOAT),
            shape((3, 512, 512), FLOAT),
            shape((3, 512, 512), HALF),
            shape((3, 16, 512), FLOAT),
            shape((8, 8, 128), FLOAT),
            shape((32, 8, 128), FLOAT),
            shape((16, 512), HALF),
        ),
        in_specs=[anywhere] * 8,
        out_specs=[anywhere] * 7 + [inside] * 8,
        scratch_shapes=[
            room(8, 4, 48, 512),
            room(3, 18, 32, 512),
            room(4608, 256),
            room(9216, 256),
            room(3, 16, 32, 256),
            room(3, 18, 32, 1024),
            pltpu.VMEM((3, 512, 256), FLOAT),
            room(4, 480, 256),
            room(480, 1024),
            room(4, 2, 2, 2, 32, 2048),
            room(4, 2, 2, 2, 288, 512),
            room(8, 192, 512),
            room(2, 3, 32, 512),
            room(2, 3, 32, 512),
            room(3, 3, 34, 16, 1024),
            room(32, 16, 128),
            dma((220,)),
            dma((24,)),
            dma((7,)),
            dma((3,)),
            dma((4, 4)),
            dma((4,)),
            dma((2, 4, 4)),
            dma((2, 16)),
            dma((3,)),
            dma((3,)),
            dma((7,)),
            dma((31,)),
            dma((12,)),
            dma((12,)),
            dma((7,)),
            dma((2,)),
            dma((31,)),
        ],
        compiler_params=pltpu.CompilerParams(
            collective_id=0, has_side_effects=True, vmem_limit_bytes=64 * 1024 * 1024
        ),
    )(bot, skip, code, w1, w2, wu, w3, wh)


def gelu_slope(value):
    square = value * value
    bend = jnp.tanh(0.7978845608028654 * value * (1.0 + 0.044715 * square))
    rise = 0.7978845608028654 * (1.0 + 3.0 * 0.044715 * square)
    return 0.5 * (1.0 + bend) + 0.5 * value * (1.0 - bend * bend) * rise


def across(source, window):
    return lax.dot_general(source, window, (((0,), (0,)), ((), ())), preferred_element_type=FLOAT)


def against(window, weight):
    return lax.dot_general(window, weight, (((1,), (1,)), ((), ())), preferred_element_type=FLOAT)


def add_rows(total, start, term, rows):
    where = pl.ds(pl.multiple_of(start, 16), rows)
    total[where] = (total[where].astype(FLOAT) + term.astype(FLOAT)).astype(HALF)


def back_kernel(
    w3_in, wu_in, w2_in, joined_in, h2_in, h1_in, x0_in, pre1_in, pre2_in, pre3_in, hidden_in,
    logits, codes, slopes, head,
    g3, gu, g2, g1, gh,
    gs3, rims, rims_got, dh, joined, slot, acc, flat, wu, h2, gh2, from_wa, pre, gs2, d_core, d_y,
    du_c, du_y, du_x, du_z, d3, d3_c, d3_y, d3_x, d3_z, d2, d2_x, d2_z, d1_x, d1_z, hh,
    send, here, r_rim, r_wa, r_d, r_u, r_3, r_2, r_1, r_h, free,
):
    z, x, y, c = place()
    ha, wa = (2 * z + x, 2 * y + c)
    x_peer, y_peer, c_peer = (spot(z, 1 - x, y, c), spot(z, x, 1 - y, c), spot(z, x, y, 1 - c))
    mine = ha * 4 + wa
    sends = []
    stays = []

    def go(source, target, recv_sem, device):
        copy = remote(source, target, send.at[len(sends)], recv_sem, device)
        copy.start()
        sends.append(copy)
        return copy

    def stay(source, target):
        copy = pltpu.make_async_copy(source, target, here.at[len(stays)])
        copy.start()
        stays.append([copy, False])
        return stays[-1]

    def settle(*entries):
        for entry in entries:
            entry[0].wait()
            entry[1] = True

    got_hidden = stay(hidden_in, d3.at[pl.ds(0, 1536)])
    got_pre3 = stay(pre3_in.at[0], acc)
    got_w3 = [
        stay(
            w3_in.at[pl.ds(1024 * t, 512), pl.ds(256 * half, 256)],
            slot.at[pl.ds(4608 * half + 512 * t, 512)],
        )
        for half in range(2)
        for t in range(9)
    ]
    got_wu = stay(wu_in, wu)
    got_h2 = stay(h2_in.at[pl.ds(0, 384)], h2)
    got_joined = stay(joined_in, joined)
    greet_all()

    settle(got_hidden)
    head_sum = jnp.zeros((16, 512), FLOAT)
    class_row = lax.broadcasted_iota(jnp.int32, (16, 512), 0)
    for e in range(3):
        gs3[e, :, 0] = jnp.zeros((3, 16, 512), HALF)
        gs3[e, :, 33] = jnp.zeros((3, 16, 512), HALF)
    for s in range(3):
        probability, target, weighted = class_terms(logits, codes, s)
        grads = [
            weighted * (target[k] * slopes[s : s + 1, k : k + 1] + slopes[s : s + 1, 2 + k : 3 + k])
            for k in range(2)
        ]
        inner = probability[0] * grads[0] + probability[1] * grads[1]
        grads = [probability[k] * (grads[k] - inner) for k in range(2)]
        grads = jnp.where(class_row == 0, grads[0], jnp.where(class_row == 1, grads[1], 0.0))
        grads = grads.astype(HALF)
        hidden = d3[512 * s : 512 * s + 512]
        head_sum = head_sum + jnp.dot(grads, hidden, preferred_element_type=FLOAT)
        settle(got_pre3)
        value = (across(grads, head[...]) * gelu_slope(acc[...])).astype(HALF)
        if s < 2:
            got_pre3 = stay(pre3_in.at[s + 1], acc)
        gs3[1, s, 1:33] = value.reshape(32, 16, 512)
        value = value.astype(FLOAT).reshape(32, 16, 512)
        rims[0, s] = value[:, 0].astype(HALF)
        rims[1, s] = value[:, 15].astype(HALF)
    before = (ha, lax.rem(wa + 3, 4))
    after = (ha, lax.rem(wa + 1, 4))
    rim_right = go(rims.at[0], rims_got.at[1], r_rim.at[1], before)
    rim_left = go(rims.at[1], rims_got.at[0], r_rim.at[0], after)
    rows = jnp.concatenate([head_sum, jnp.zeros((112, 512), FLOAT)], axis=0)
    dh[...] = rows.T.reshape(32, 16, 128)
    own_head = stay(dh.at[mine], hh.at[0])
    heads = []
    for step in range(1, 32):
        other = lax.rem(mine + step, 32)
        heads.append(
            go(dh.at[other], hh.at[step], r_h.at[step - 1], (other // 4, lax.rem(other, 4)))
        )
    rim_right.wait_recv()
    rim_left.wait_recv()
    for s in range(3):
        left = jnp.where(wa > 0, rims_got[0, s].astype(FLOAT), 0.0)
        right = jnp.where(wa < 3, rims_got[1, s].astype(FLOAT), 0.0)
        value = gs3[1, s, 1:33].astype(FLOAT)
        put_shifts(gs3, pl.ds(0, 512), s, value, left[:, None, :], right[:, None, :])

    order = lax.broadcasted_iota(jnp.int32, (256, 256), 0)
    inner = order % 128
    pick = (inner // 8) * 16 + (inner % 8) * 2 + order // 128
    apart = jnp.where(lax.broadcasted_iota(jnp.int32, (256, 256), 1) == pick, 1.0, 0.0).astype(HALF)
    settle(*got_w3)

    def three_source(s, carry):
        acc[...] = jnp.zeros_like(acc)

        def tap(t, inner_carry):
            window = gs3[2 - t % 3, s, pl.ds(2 - t // 3, 32)].reshape(512, 512)
            for half in range(2):
                rows = pl.ds(pl.multiple_of(4608 * half + 512 * t, 512), 512)
                acc[...] += against(window[:, 256 * half : 256 * half + 256], slot[rows])
            return inner_carry

        lax.fori_loop(0, 9, tap, 0)
        fine = acc[...].astype(HALF).reshape(16, 2, 16, 512)
        for a in range(2):
            parted = jnp.dot(
                apart, fine[:, a].reshape(256, 512), preferred_element_type=FLOAT
            ).astype(HALF)
            for b in range(2):
                rows = pl.ds(pl.multiple_of(128 * s, 128), 128)
                flat[rows, pl.ds(512 * (2 * a + b), 512)] = parted[128 * b : 128 * b + 128]
        return carry

    lax.fori_loop(0, 3, three_source, 0)
    got_w2 = stay(w2_in, slot)
    settle(got_wu, got_h2)
    for part in range(4):
        lanes = slice(256 * part, 256 * part + 256)
        gh2[:, lanes] = against(flat[...], wu[lanes, :]).astype(HALF)

    def wa_lanes(col):
        return gh2.at[:, pl.ds(pl.multiple_of(col * 256, 256), 256)]

    own_wa = stay(wa_lanes(wa), from_wa.at[wa])
    got_wa = [
        go(
            wa_lanes(lax.rem(wa + d, 4)),
            from_wa.at[wa],
            r_wa.at[d - 1],
            (ha, lax.rem(wa + d, 4)),
        )
        for d in range(1, 4)
    ]
    for part in range(4):
        lanes = slice(512 * part, 512 * part + 512)
        wu[:, lanes] = across(h2[...], flat[:, lanes]).astype(HALF)

    def block(grad, rows, bz, bx, by, bc):
        number = ((bz * 2 + bx) * 2 + by) * 2 + bc
        return grad.at[pl.ds(pl.multiple_of(number * rows, 16), rows)]

    def all_core(grad, rows, core, recv, some):
        return [
            go(
                block(grad, rows, bz, bx, by, 1 - c),
                core.at[((bz - some[0]) * 2 + bx) * 2 + by],
                recv.at[((bz - some[0]) * 2 + bx) * 2 + by],
                c_peer,
            )
            for bz in some
            for bx in range(2)
            for by in range(2)
        ]

    def all_y(grad, rows, core, along_y, recv, some, got):
        for copy in got:
            copy.wait_recv()

        def step(by):
            def add(i, carry):
                number = (((some[0] * 2 + i) * 2) + by) * 2 + c
                add_rows(grad, number * rows, core[i * 2 + by], rows)
                return carry

            lax.fori_loop(0, 2 * len(some), add, 0)

        step(1 - y)
        copies = [
            go(
                block(grad, rows, bz, bx, 1 - y, c),
                along_y.at[bz * 2 + bx],
                recv.at[16 + bz * 2 + bx],
                y_peer,
            )
            for bz in some
            for bx in range(2)
        ]
        step(y)
        return copies

    def all_x(grad, rows, along_y, along_x, recv, got):
        for copy in got:
            copy.wait_recv()

        def step(bx):
            def add(bz, carry):
                number = ((bz * 2 + bx) * 2 + y) * 2 + c
                add_rows(grad, number * rows, along_y[bz * 2 + bx], rows)
                return carry

            lax.fori_loop(0, 4, add, 0)

        step(1 - x)
        copies = [
            go(block(grad, rows, bz, 1 - x, y, c), along_x.at[bz], recv.at[24 + bz], x_peer)
            for bz in range(4)
        ]
        step(x)
        return copies

    def all_z(grad, rows, along_x, along_z, recv, got):
        for copy in got:
            copy.wait_recv()

        def add(bz, carry):
            number = ((bz * 2 + x) * 2 + y) * 2 + c
            add_rows(grad, number * rows, along_x[bz], rows)
            return carry

        lax.fori_loop(0, 4, add, 0)
        return [
            go(
                block(grad, rows, lax.rem(z + d, 4), x, y, c),
                along_z.at[d - 1],
                recv.at[27 + d],
                spot(lax.rem(z + d, 4), x, y, c),
            )
            for d in range(1, 4)
        ]

    def all_end(grad, rows, along_z, out, got):
        total = grad[pl.ds(pl.multiple_of(mine * rows, 16), rows)].astype(FLOAT)
        for d in range(3):
            got[d].wait_recv()
            total = total + along_z[d].astype(FLOAT)
        out[...] = total

    def quarter_x(grad, rows, along_x, recv, bz):
        source = grad.at[pl.ds(pl.multiple_of((bz * 2 + 1 - x) * 4 * rows, 16), 4 * rows)]
        return go(source, along_x.at[bz], recv.at[bz], x_peer)

    def quarter_z(grad, rows, along_x, along_z, recv, got):
        for copy in got:
            copy.wait_recv()

        def add(d, carry):
            bz = lax.rem(z + d, 4)
            add_rows(grad, (bz * 2 + x) * 4 * rows, along_x[bz], 4 * rows)
            return carry

        lax.fori_loop(0, 4, add, 0)
        return [
            go(
                grad.at[
                    pl.ds(pl.multiple_of((lax.rem(z + d, 4) * 2 + x) * 4 * rows, 16), 4 * rows)
                ],
                along_z.at[d - 1],
                recv.at[3 + d],
                spot(lax.rem(z + d, 4), x, y, c),
            )
            for d in range(1, 4)
        ]

    def quarter_w(grad, rows, along_z, out, recv, got):
        for copy in got:
            copy.wait_recv()

        own = pl.ds(pl.multiple_of(ha * 4 * rows, 16), 4 * rows)
        value = grad[own].astype(FLOAT)
        for d in range(3):
            value = value + along_z[d].astype(FLOAT)
        grad[own] = value.astype(HALF)
        target = out.at[:, pl.ds(pl.multiple_of(wa * 256, 256), 256)]

        def piece(col):
            return grad.at[pl.ds(pl.multiple_of((ha * 4 + col) * rows, 16), rows)]

        stay(piece(wa), target)
        return [
            go(
                piece(lax.rem(wa + d, 4)),
                target,
                recv.at[6 + d],
                (ha, lax.rem(wa + d, 4)),
            )
            for d in range(1, 4)
        ]

    su = all_core(wu, 32, du_c, r_u, (0, 1, 2, 3))
    settle(got_joined)

    def three_weight(t, carry):
        window = gs3[2 - t % 3, :, pl.ds(2 - t // 3, 32)].reshape(1536, 512)
        rows = pl.ds(pl.multiple_of(1024 * t, 1024), 1024)
        d3[rows] = across(joined[...], window).astype(HALF)
        return carry

    lax.fori_loop(0, 5, three_weight, 0)
    s3 = all_core(d3, 288, d3_c, r_3, (0, 1))
    su = all_y(wu, 32, du_c, du_y, r_u, (0, 1, 2, 3), su)
    s3_low = all_y(d3, 288, d3_c, d3_y, r_3, (0, 1), s3)
    pl.semaphore_signal(free, inc=1, device_id=c_peer, device_id_type=MESH)
    lax.fori_loop(5, 9, three_weight, 0)
    pl.semaphore_wait(free, 1)
    s3 = all_core(d3, 288, d3_c, r_3, (2, 3))
    got_h1 = stay(h1_in, joined)

    settle(own_wa)
    for copy in got_wa:
        copy.wait_recv()

    def put_columns(target, s, value):
        column = lax.broadcasted_iota(jnp.int32, (16, 32, 256), 1)
        target[0, s, pl.ds(1, 16)] = jnp.where(column > 0, pltpu.roll(value, 1, 1), 0.0).astype(HALF)
        target[1, s, pl.ds(1, 16)] = value.astype(HALF)
        target[2, s, pl.ds(1, 16)] = jnp.where(column < 31, pltpu.roll(value, 31, 1), 0.0).astype(
            HALF
        )

    for e in range(3):
        gs2[e, :, 0] = jnp.zeros((3, 32, 256), HALF)
        gs2[e, :, 17] = jnp.zeros((3, 32, 256), HALF)
    settle(stay(pre2_in, pre))

    def two_grad(s, carry):
        rows = pl.ds(pl.multiple_of(128 * s, 128), 128)
        parts = [from_wa[w, rows].astype(FLOAT).reshape(16, 8, 256) for w in range(4)]
        put_columns(gs2, s, jnp.concatenate(parts, axis=1) * gelu_slope(pre[s]))
        return carry

    lax.fori_loop(0, 3, two_grad, 0)
    got_pre1 = stay(pre1_in, pre)
    settle(got_h1)

    def two_weight(t, carry):
        window = gs2[2 - t % 3, :, pl.ds(2 - t // 3, 16)].reshape(1536, 256)
        rows = pl.ds(pl.multiple_of(1024 * t, 1024), 1024)
        d2[rows] = across(joined[...], window).astype(HALF)
        return carry

    s2 = []
    for bz, (first, last) in enumerate(((0, 3), (3, 5), (5, 7), (7, 9))):
        lax.fori_loop(first, last, two_weight, 0)
        s2.append(quarter_x(d2, 288, d2_x, r_2, bz))

    s3_high = all_y(d3, 288, d3_c, d3_y, r_3, (2, 3), s3)
    got_x0 = stay(x0_in, joined.at[:, pl.ds(0, 512)])
    settle(got_w2)

    def source_two(s):
        for half in range(2):
            acc[...] = jnp.zeros_like(acc)

            def tap(t, inner_carry):
                window = gs2[2 - t % 3, s, pl.ds(2 - t // 3, 16)].reshape(512, 256)
                rows = pl.ds(pl.multiple_of(1024 * t + 512 * half, 512), 512)
                acc[...] += against(window, slot[rows])
                return inner_carry

            lax.fori_loop(0, 9, tap, 0)
            gs3[half, s, pl.ds(0, 32)] = acc[...].astype(HALF).reshape(32, 16, 512)

    def d_lanes(halves, s, core):
        return gs3.at[halves, s, pl.ds(0, 32), :, pl.ds(pl.multiple_of(256 * core, 256), 256)]

    sd = []
    for s in range(3):
        source_two(s)
        sd.append(go(d_lanes(pl.ds(0, 2), s, 1 - c), d_core.at[s], r_d.at[s], c_peer))
        if s == 0:
            su = all_x(wu, 32, du_y, du_x, r_u, su)
    sy = []
    own_lanes = pl.ds(pl.multiple_of(256 * c, 256), 256)
    for s in range(3):
        sd[s].wait_recv()
        for half in range(2):
            value = gs3[half, s, pl.ds(0, 32), :, own_lanes].astype(FLOAT)
            value = value + d_core[s, half].astype(FLOAT)
            gs3[half, s, pl.ds(0, 32), :, own_lanes] = value.astype(HALF)
        sy.append(go(d_lanes(1 - y, s, c), d_y.at[s], r_d.at[3 + s], y_peer))
    s2 = quarter_z(d2, 288, d2_x, d2_z, r_2, s2)
    settle(got_pre1)
    for s in range(3):
        sy[s].wait_recv()
        value = gs3[y, s, pl.ds(0, 32), :, own_lanes].astype(FLOAT) + d_y[s].astype(FLOAT)
        put_columns(gs2, s, value.reshape(16, 32, 256) * gelu_slope(pre[s]))
    settle(got_x0)

    def one_weight(t, carry):
        window = gs2[2 - t % 3, :, pl.ds(2 - t // 3, 16)].reshape(1536, 256)
        rows = pl.ds(pl.multiple_of(512 * t, 512), 512)
        slot[rows] = across(joined[:, 0:512], window).astype(HALF)
        return carry

    s1 = []
    for bz, (first, last) in enumerate(((0, 3), (3, 5), (5, 7), (7, 9))):
        lax.fori_loop(first, last, one_weight, 0)
        s1.append(quarter_x(slot, 144, d1_x, r_1, bz))

    s3 = all_x(d3, 288, d3_y, d3_x, r_3, s3_low + s3_high)
    su = all_z(wu, 32, du_x, du_z, r_u, su)
    s2 = quarter_w(d2, 288, d2_z, g2, r_2, s2)
    s1 = quarter_z(slot, 144, d1_x, d1_z, r_1, s1)
    s3 = all_z(d3, 288, d3_x, d3_z, r_3, s3)
    settle(own_head)
    total = hh[0]
    for step in range(1, 32):
        heads[step - 1].wait_recv()
        total = total + hh[step]
    gh[...] = total
    all_end(wu, 32, du_z, gu, su)
    s1 = quarter_w(slot, 144, d1_z, g1, r_1, s1)
    all_end(d3, 288, d3_z, g3, s3)
    for copy in s2 + s1:
        copy.wait_recv()
    for entry in stays:
        if not entry[1]:
            settle(entry)
    for copy in sends:
        copy.wait_send()


def back(*args):
    anywhere = pl.BlockSpec(memory_space=pl.ANY)
    inside = pl.BlockSpec(memory_space=pltpu.VMEM)
    shape = jax.ShapeDtypeStruct
    dma = pltpu.SemaphoreType.DMA

    def room(*dims):
        return pltpu.VMEM(dims, HALF)

    return pl.pallas_call(
        back_kernel,
        name="back",
        out_shape=(
            shape((288, 512), FLOAT),
            shape((32, 2048), FLOAT),
            shape((288, 1024), HALF),
            shape((144, 1024), HALF),
            shape((16, 128), FLOAT),
        ),
        in_specs=[anywhere] * 11 + [inside] * 4,
        out_specs=[inside, inside, anywhere, anywhere, inside],
        scratch_shapes=[
            room(3, 3, 34, 16, 512),
            room(2, 3, 32, 512),
            room(2, 3, 32, 512),
            pltpu.VMEM((32, 16, 128), FLOAT),
            room(1536, 1024),
            room(9216, 256),
            pltpu.VMEM((512, 512), FLOAT),
            room(384, 2048),
            room(1024, 2048),
            room(384, 1024),
            room(384, 1024),
            room(4, 384, 256),
            pltpu.VMEM((3, 16, 32, 256), FLOAT),
            room(3, 3, 18, 32, 256),
            room(3, 2, 32, 16, 256),
            room(3, 32, 16, 256),
            room(16, 32, 2048),
            room(8, 32, 2048),
            room(4, 32, 2048),
            room(3, 32, 2048),
            room(9216, 512),
            room(8, 288, 512),
            room(8, 288, 512),
            room(4, 288, 512),
            room(3, 288, 512),
            room(9216, 256),
            room(4, 1152, 256),
            room(3, 1152, 256),
            room(4, 576, 256),
            room(3, 576, 256),
            pltpu.VMEM((32, 16, 128), FLOAT),
            dma((144,)),
            dma((40,)),
            dma((2,)),
            dma((3,)),
            dma((6,)),
            dma((31,)),
            dma((31,)),
            dma((10,)),
            dma((10,)),
            dma((31,)),
            pltpu.SemaphoreType.REGULAR,
        ],
        compiler_params=pltpu.CompilerParams(
            collective_id=2, has_side_effects=True, vmem_limit_bytes=64 * 1024 * 1024
        ),
    )(*args)


def dice_slopes(totals):
    union_sum = totals[..., 1] + totals[..., 2] + SMOOTHING
    numerator = 2.0 * totals[..., 0] + SMOOTHING
    dice_score = numerator / union_sum
    loss_value = 1.0 - jnp.mean(dice_score)
    entry_count = float(dice_score.size)
    common = -2.0 / (entry_count * union_sum)
    return (loss_value, jnp.concatenate([common, numerator / (entry_count * union_sum**2)], axis=1))


def sliced_grads(
    bottom, skipped, groups, pixel_mask, labels, weight_one, weight_two, weight_up, weight_three,
    weight_head,
):
    ha = lax.axis_index("ha")
    code = (pixel_mask + 2 * labels).astype(FLOAT).reshape(8, 3, 64)
    pads = [jnp.pad(code, ((0, 0), (0, 5), (64 * odd, 64 - 64 * odd))) for odd in range(2)]
    code = jnp.where(ha % 2 == 0, *pads)
    head_rows = jnp.pad(weight_head.astype(HALF), ((0, 0), (0, 126)))
    x0, h1, h2, joined, w2, wu, w3, pre_one, pre_two, pre_three, hidden_three, logits, code, sums, head = front(
        bottom.reshape(8, 48, 512),
        skipped.reshape(8, 192, 512),
        code,
        weight_one.astype(HALF),
        weight_two.astype(HALF),
        weight_up.astype(HALF),
        weight_three.astype(HALF),
        head_rows,
    )
    wu = wu.reshape(1024, 2048)
    w3 = w3.reshape(9216, 512)
    member = (groups[:, None] == jnp.arange(GROUPS)[None, :]).astype(FLOAT)
    step = lax.axis_index("ha") * 4 + lax.axis_index("wa")
    origin = (step - jnp.arange(32)) % 32
    at_group = jnp.einsum(
        "dh,hsg->dsg",
        (origin[:, None] // 4 == jnp.arange(8)[None, :]).astype(FLOAT),
        member.reshape(8, 3, GROUPS),
        precision=HIGHEST,
    )
    totals = jnp.einsum("dsg,dsq->gq", at_group, sums[:, :3, :6], precision=HIGHEST)
    totals = totals.reshape(GROUPS, 2, 3)
    loss_value, slopes = dice_slopes(totals)
    member = lax.dynamic_slice_in_dim(member, 3 * ha, 3, axis=0)
    slopes = jnp.einsum("sg,gq->sq", member, slopes, precision=HIGHEST)
    g3, gu, g2, g1, gh = back(
        w3,
        wu,
        w2,
        joined.reshape(1536, 1024),
        h2,
        h1.reshape(1536, 1024),
        x0.reshape(1536, 512),
        pre_one,
        pre_two,
        pre_three,
        hidden_three.reshape(1536, 512),
        logits,
        code,
        jnp.pad(slopes, ((0, 5), (0, 124))),
        head,
    )
    return (loss_value, g1.astype(FLOAT), g2.astype(FLOAT), gu, g3, gh[:, :2])


def body(
    bottom,
    skipped,
    groups,
    pixel_mask,
    labels,
    conv1_weight,
    conv1_momentum,
    conv1_average,
    conv2_weight,
    conv2_momentum,
    conv2_average,
    up_weight,
    up_momentum,
    up_average,
    conv3_weight,
    conv3_momentum,
    conv3_average,
    head_weight,
    head_momentum,
    head_average,
):
    split = bottom.shape[0] == 24 and bottom.shape[1:3] == (2, 8) and bottom.shape[3] == 512
    split = split and (lax.axis_size("ha"), lax.axis_size("wa")) == (8, 4)
    grads = sliced_grads if split else tiled_grads
    loss_value, conv1_grad, conv2_grad, up_grad, conv3_grad, head_grad = grads(
        bottom,
        skipped,
        groups,
        pixel_mask,
        labels,
        conv1_weight,
        conv2_weight,
        up_weight,
        conv3_weight,
        head_weight,
    )
    first = renew_state(conv1_weight, conv1_momentum, conv1_average, conv1_grad, RATE_CONV)
    second = renew_state(conv2_weight, conv2_momentum, conv2_average, conv2_grad, RATE_CONV)
    upward = renew_state(up_weight, up_momentum, up_average, up_grad, RATE_CONV)
    third = renew_state(conv3_weight, conv3_momentum, conv3_average, conv3_grad, RATE_CONV)
    header = renew_state(head_weight, head_momentum, head_average, head_grad, RATE_HEAD)
    return (
        loss_value,
        first[0],
        first[1],
        first[2],
        second[0],
        second[1],
        second[2],
        upward[0],
        upward[1],
        upward[2],
        third[0],
        third[1],
        third[2],
        header[0],
        header[1],
        header[2],
    )


def solution(mesh):
    in_specs = (
        P(None, "ha", "wa", None),
        P(None, "ha", "wa", None),
        P(),
        P(None, "ha", "wa"),
        P(None, "ha", "wa"),
        P(("ha", "wa"), None),
        P(("ha", "wa"), None),
        P(("ha", "wa"), None),
        P(("ha", "wa"), None),
        P(("ha", "wa"), None),
        P(("ha", "wa"), None),
        P(("ha", "wa"), None),
        P(("ha", "wa"), None),
        P(("ha", "wa"), None),
        P(("ha", "wa"), None),
        P(("ha", "wa"), None),
        P(("ha", "wa"), None),
        P(("ha", "wa"), None),
        P(("ha", "wa"), None),
        P(("ha", "wa"), None),
    )
    out_specs = (
        P(),
        P(("ha", "wa"), None),
        P(("ha", "wa"), None),
        P(("ha", "wa"), None),
        P(("ha", "wa"), None),
        P(("ha", "wa"), None),
        P(("ha", "wa"), None),
        P(("ha", "wa"), None),
        P(("ha", "wa"), None),
        P(("ha", "wa"), None),
        P(("ha", "wa"), None),
        P(("ha", "wa"), None),
        P(("ha", "wa"), None),
        P(("ha", "wa"), None),
        P(("ha", "wa"), None),
        P(("ha", "wa"), None),
    )
    return jax.shard_map(body, mesh=mesh, in_specs=in_specs, out_specs=out_specs, check_vma=False)
```

```python
import functools

import jax
import jax.numpy as jnp
from jax import lax
from jax.experimental import pallas as pl
from jax.experimental.pallas import tpu as pltpu
from jax.sharding import PartitionSpec as P

GROUPS = 5


MOMENTUM = 0.9
RATE_CONV = 600.0
RATE_HEAD = 25.0
AVERAGE_DECAY = 0.5
SMOOTHING = 1.0
HIGHEST = lax.Precision.HIGHEST


def with_halo(block, sides, width):
    for axis, dim in sides:
        count = lax.axis_size(axis)
        forward = [(i, i + 1) for i in range(count - 1)]
        backward = [(target, source) for source, target in forward]
        low = lax.ppermute(
            lax.slice_in_dim(block, block.shape[dim] - width, None, axis=dim), axis, forward
        )
        high = lax.ppermute(lax.slice_in_dim(block, 0, width, axis=dim), axis, backward)
        block = jnp.concatenate([low, block, high], axis=dim)
    return block


def smooth(source):
    return jax.nn.gelu(source, approximate=True)


def smooth_back(pre_value, gradient):
    _, pull_back = jax.vjp(smooth, pre_value)
    return pull_back(gradient)[0]


def widened_field(source):
    return with_halo(source, (("ha", 1), ("wa", 2)), 1)


def conv_taps(padded, weight):
    kernel = weight.reshape(3, 3, padded.shape[3], weight.shape[1])
    return lax.conv_general_dilated(
        padded,
        kernel,
        (1, 1),
        "VALID",
        dimension_numbers=("NHWC", "HWIO", "NHWC"),
        preferred_element_type=jnp.float32,
    )


def conv_back(padded, grad_out, weight, back_chan):
    in_chan = padded.shape[3]
    weight_grad = lax.conv_general_dilated(
        padded,
        grad_out,
        (1, 1),
        "VALID",
        dimension_numbers=("CHWN", "IHWO", "HWNC"),
        preferred_element_type=jnp.float32,
    ).reshape(9 * in_chan, grad_out.shape[3])
    if not back_chan:
        return (weight_grad, None)
    grad_padded = widened_field(grad_out)
    kernel = weight.reshape(3, 3, in_chan, weight.shape[1])[::-1, ::-1, :back_chan]
    source_grad = lax.conv_general_dilated(
        grad_padded,
        kernel,
        (1, 1),
        "VALID",
        dimension_numbers=("NHWC", "HWOI", "NHWC"),
        preferred_element_type=jnp.float32,
    )
    return (weight_grad, source_grad)


def upsample(source, weight):
    slices, row_count, col_count, _ = source.shape
    flattened = jnp.einsum("shwc,cq->shwq", source, weight, preferred_element_type=jnp.float32)
    blocks = flattened.reshape(slices, row_count, col_count, 2, 2, -1).transpose(0, 1, 3, 2, 4, 5)
    return blocks.reshape(slices, 2 * row_count, 2 * col_count, -1)


def upsample_back(source, grad_up, weight):
    slices, row_count, col_count, _ = source.shape
    blocks = grad_up.reshape(slices, row_count, 2, col_count, 2, -1).transpose(0, 1, 3, 2, 4, 5)
    flattened = blocks.reshape(slices, row_count, col_count, -1)
    weight_grad = jnp.einsum("shwc,shwq->cq", source, flattened, preferred_element_type=jnp.float32)
    source_grad = jnp.einsum("shwq,cq->shwc", flattened, weight, preferred_element_type=jnp.float32)
    return (weight_grad, source_grad)


def forward(gathered, bottom, skipped):
    weight_one, weight_two, weight_up, weight_three, weight_head = gathered
    pad_zero = widened_field(bottom)
    pre_one = conv_taps(pad_zero, weight_one)
    hidden_one = smooth(pre_one).astype(jnp.bfloat16)
    pad_one = widened_field(hidden_one)
    pre_two = conv_taps(pad_one, weight_two)
    hidden_two = smooth(pre_two).astype(jnp.bfloat16)
    upsampled = upsample(hidden_two, weight_up).astype(jnp.bfloat16)
    joined = jnp.concatenate([upsampled, skipped], axis=3)
    pad_two = widened_field(joined)
    pre_three = conv_taps(pad_two, weight_three)
    hidden_three = smooth(pre_three).astype(jnp.bfloat16)
    logits = jnp.einsum(
        "shwc,ck->shwk", hidden_three, weight_head, preferred_element_type=jnp.float32
    )
    return (
        pad_zero,
        pre_one,
        pad_one,
        pre_two,
        hidden_two,
        pad_two,
        pre_three,
        hidden_three,
        logits,
    )


def pixel_terms(logits, pixel_mask, labels):
    probability = jax.nn.softmax(logits, axis=-1)
    classes = jnp.arange(logits.shape[-1])
    target = (labels[..., None] == classes[None, None, None, :]).astype(jnp.float32)
    weighted = pixel_mask[..., None].astype(jnp.float32)
    return (probability, target, weighted)


def dice_terms(logits, pixel_mask, labels, member):
    probability, target, weighted = pixel_terms(logits, pixel_mask, labels)
    per_slice = jnp.stack(
        [
            jnp.sum(weighted * probability * target, axis=(1, 2)),
            jnp.sum(weighted * probability, axis=(1, 2)),
            jnp.sum(weighted * target, axis=(1, 2)),
        ],
        axis=-1,
    )
    return jnp.einsum("skj,sg->gkj", per_slice, member, precision=HIGHEST)


def dice_back(logits, pixel_mask, labels, member, totals):
    probability, target, weighted = pixel_terms(logits, pixel_mask, labels)
    union_sum = totals[..., 1] + totals[..., 2] + SMOOTHING
    numerator = 2.0 * totals[..., 0] + SMOOTHING
    dice_score = numerator / union_sum
    loss_value = 1.0 - jnp.mean(dice_score)
    entry_count = float(dice_score.size)
    coef_common = -2.0 / (entry_count * union_sum)
    coef_prob = numerator / (entry_count * union_sum * union_sum)
    slice_common = jnp.einsum("sg,gk->sk", member, coef_common, precision=HIGHEST)
    slice_prob = jnp.einsum("sg,gk->sk", member, coef_prob, precision=HIGHEST)
    grad_prob = weighted * (target * slice_common[:, None, None, :] + slice_prob[:, None, None, :])
    inner = jnp.sum(probability * grad_prob, axis=-1, keepdims=True)
    grad_logits = (probability * (grad_prob - inner)).astype(jnp.bfloat16)
    return (loss_value, grad_logits)


def renew_state(weight, moment, average, gradient, rate):
    moment_new = MOMENTUM * moment + gradient
    weight_new = weight - rate * (gradient + MOMENTUM * moment_new)
    average_new = AVERAGE_DECAY * average + (1.0 - AVERAGE_DECAY) * weight_new
    return (weight_new, moment_new, average_new)


def tiled_grads(
    bottom, skipped, groups, pixel_mask, labels, conv1_weight, conv2_weight, up_weight, conv3_weight,
    head_weight,
):
    gathered = (
        lax.all_gather(conv1_weight.astype(jnp.bfloat16), ("ha", "wa"), axis=0, tiled=True),
        lax.all_gather(conv2_weight.astype(jnp.bfloat16), ("ha", "wa"), axis=0, tiled=True),
        lax.all_gather(up_weight.astype(jnp.bfloat16), ("ha", "wa"), axis=0, tiled=True),
        lax.all_gather(conv3_weight.astype(jnp.bfloat16), ("ha", "wa"), axis=0, tiled=True),
        lax.all_gather(head_weight.astype(jnp.bfloat16), ("ha", "wa"), axis=0, tiled=True),
    )
    member = (groups[:, None] == jnp.arange(GROUPS)[None, :]).astype(jnp.float32)
    kept = forward(gathered, bottom, skipped)
    partial_sums = dice_terms(kept[8], pixel_mask, labels, member)
    totals = lax.psum(partial_sums, ("ha", "wa"))
    pad_zero, pre_one, pad_one, pre_two, hidden_two, pad_two, pre_three, hidden_three, logits = kept
    weight_one, weight_two, weight_up, weight_three, weight_head = gathered
    loss_value, grad_logits = dice_back(logits, pixel_mask, labels, member, totals)
    head_grad = jnp.einsum(
        "shwc,shwk->ck", hidden_three, grad_logits, preferred_element_type=jnp.float32
    )
    grad_hidden = jnp.einsum(
        "shwk,ck->shwc", grad_logits, weight_head, preferred_element_type=jnp.float32
    )
    grad_pre_three = smooth_back(pre_three, grad_hidden).astype(jnp.bfloat16)
    conv3_grad, grad_joined = conv_back(pad_two, grad_pre_three, weight_three, weight_up.shape[1] // 4)
    grad_upsampled = grad_joined.astype(jnp.bfloat16)
    up_grad, grad_hidden_two = upsample_back(hidden_two, grad_upsampled, weight_up)
    grad_pre_two = smooth_back(pre_two, grad_hidden_two).astype(jnp.bfloat16)
    conv2_grad, grad_hidden_one = conv_back(pad_one, grad_pre_two, weight_two, pad_one.shape[3])
    grad_pre_one = smooth_back(pre_one, grad_hidden_one).astype(jnp.bfloat16)
    conv1_grad, _ = conv_back(pad_zero, grad_pre_one, weight_one, 0)
    sums = (
        lax.psum_scatter(conv1_grad.astype(jnp.bfloat16), ("ha", "wa"), scatter_dimension=0, tiled=True),
        lax.psum_scatter(conv2_grad.astype(jnp.bfloat16), ("ha", "wa"), scatter_dimension=0, tiled=True),
        lax.psum_scatter(up_grad.astype(jnp.bfloat16), ("ha", "wa"), scatter_dimension=0, tiled=True),
        lax.psum_scatter(conv3_grad.astype(jnp.bfloat16), ("ha", "wa"), scatter_dimension=0, tiled=True),
        lax.psum_scatter(head_grad.astype(jnp.bfloat16), ("ha", "wa"), scatter_dimension=0, tiled=True),
    )
    return (loss_value, *[s.astype(jnp.float32) for s in sums])


MESH = pl.DeviceIdType.MESH
FLOAT = jnp.float32
HALF = jnp.bfloat16


def place():
    row, col = (lax.axis_index("ha"), lax.axis_index("wa"))
    return (row // 2, row % 2, col // 2, col % 2)


def spot(z, x, y, c):
    return (2 * z + x, 2 * y + c)


def greet_all():
    row, col = (lax.axis_index("ha"), lax.axis_index("wa"))
    rows, cols = (lax.axis_size("ha"), lax.axis_size("wa"))
    barrier = pltpu.get_barrier_semaphore()
    for step in range(1, rows * cols):
        other = lax.rem(row * cols + col + step, rows * cols)
        pl.semaphore_signal(
            barrier, inc=1, device_id=(other // cols, lax.rem(other, cols)), device_id_type=MESH
        )
    pl.semaphore_wait(barrier, rows * cols - 1)


def remote(source, target, send_sem, recv_sem, device):
    return pltpu.make_async_remote_copy(
        src_ref=source,
        dst_ref=target,
        send_sem=send_sem,
        recv_sem=recv_sem,
        device_id=device,
        device_id_type=MESH,
    )


def gelu_of(value):
    inner = 0.7978845608028654 * (value + 0.044715 * value * value * value)
    return 0.5 * value * (1.0 + jnp.tanh(inner))


def conv_slice(source, weight, parts, index, chan):
    parts[...] = jnp.zeros_like(parts)

    def row_tap(r, carry):
        window = source[index, pl.ds(r, 16)].reshape(512, chan)
        for c in range(3):
            start = pl.multiple_of((3 * r + c) * chan, chan)
            parts[c] += jnp.dot(
                window, weight[pl.ds(start, chan), :], preferred_element_type=FLOAT
            )
        return carry

    lax.fori_loop(0, 3, row_tap, 0)
    shape = (16, 32, 256)
    column = lax.broadcasted_iota(jnp.int32, shape, 1)
    low = jnp.where(column > 0, pltpu.roll(parts[0].reshape(shape), 1, 1), 0.0)
    high = jnp.where(column < 31, pltpu.roll(parts[2].reshape(shape), 31, 1), 0.0)
    return parts[1].reshape(shape) + low + high


def put_shifts(target, lanes, s, value, left, right):
    column = lax.broadcasted_iota(jnp.int32, value.shape, 1)
    last = value.shape[1] - 1
    rows = pl.ds(1, value.shape[0])
    low = jnp.where(column > 0, pltpu.roll(value, 1, 1), left)
    target[0, s, rows, :, lanes] = low.astype(HALF)
    target[1, s, rows, :, lanes] = value.astype(HALF)
    high = jnp.where(column < last, pltpu.roll(value, last, 1), right)
    target[2, s, rows, :, lanes] = high.astype(HALF)


def front_kernel(
    compute,
    bot, skip, code, w1, w2, wu, w3, wh,
    x0_out, h1_out, h2_out, joined_out, w2_out, wu_out, w3_out, pre1_out, pre2_out, pre3_out,
    hidden_out, logit_out, code_out, sums_out, head_out,
    xr, x0, w1q, w2q, h1s, h1, parts, h2s, h2v, wuv, w3v, skv, rims, rims_got, tiles, whv,
    send, here, r_bot, r_grp, r_w1, r_w1x, r_w2, r_w2x, r_h1, r_h2, r_skip, r_wh, r_w3, r_wu,
    r_code, r_rim, r_sum,
):
    z, x, y, c = place()
    ha, wa = (2 * z + x, 2 * y + c)
    x_peer, y_peer, c_peer = (spot(z, 1 - x, y, c), spot(z, x, 1 - y, c), spot(z, x, y, 1 - c))
    mine = ha * 4 + wa
    greet_all()
    sends = []
    stays = []

    def go(source, target, recv_sem, device):
        copy = remote(source, target, send.at[len(sends)], recv_sem, device)
        copy.start()
        sends.append(copy)
        return copy

    def stay(source, target):
        copy = pltpu.make_async_copy(source, target, here.at[len(stays)])
        copy.start()
        stays.append([copy, False])
        return stays[-1]

    def settle(*entries):
        for entry in entries:
            entry[0].wait()
            entry[1] = True

    def arrive(*copies):
        for copy in copies:
            copy.wait_recv()

    def spread(shard, whole, rows, first, count, recv):
        start = pl.multiple_of(mine * rows + first, 16)
        place_rows = whole.at[pl.ds(start, count)]
        source_rows = pl.ds(first, count)
        lanes = [pl.ds(pl.multiple_of(lax.rem(wa + dw, 4) * 256, 256), 256) for dw in range(4)]
        own = stay(shard.at[source_rows, lanes[0]], place_rows)
        copies = [
            go(
                shard.at[source_rows, lanes[dw]],
                place_rows,
                recv.at[dz, dw],
                (lax.rem(z + dz, 4) * 2 + x, lax.rem(wa + dw, 4)),
            )
            for dz in (1, 2, 3, 0)
            for dw in range(4)
            if dz + dw > 0
        ]
        return (own, copies)

    def pass_x(whole, rows, first, count, got, recv):
        own, copies = got
        settle(own)
        arrive(*copies)
        if count == rows:
            spans = [(dz, 0, 4 * rows) for dz in range(4)]
        else:
            spans = [(dz, w * rows + first, count) for dz in range(4) for w in range(4)]
        passed = []
        for number, (dz, offset, length) in enumerate(spans):
            start = (lax.rem(z + 4 - dz, 4) * 2 + x) * 4 * rows + offset
            block = whole.at[pl.ds(pl.multiple_of(start, 16), length)]
            passed.append(go(block, block, recv.at[number], x_peer))
        return passed

    def spread_z(shard, whole, recv):
        own = stay(shard, whole.at[z, x, y, c])
        copies = [
            go(shard, whole.at[z, x, y, c], recv.at[d - 1], spot(lax.rem(z + d, 4), x, y, c))
            for d in range(1, 4)
        ]
        return (own, copies)

    def spread_two(whole, got, recv, half, width):
        settle(got[0])
        arrive(*got[1])
        low, high = (pl.ds(0, half), pl.ds(half, width - half))
        part = whole.at[:, x, y, c, :, low]
        first = go(part, part, recv.at[4], x_peer)
        part = whole.at[:, x, y, c, :, high]
        second = go(part, part, recv.at[5], y_peer)
        part = whole.at[:, x, y, c]
        core = go(part, part, recv.at[3], c_peer)
        return (core, first, second)

    def spread_three(whole, got, recv, half, width):
        core, first, second = got
        low, high = (pl.ds(0, half), pl.ds(half, width - half))
        arrive(first)
        part = whole.at[:, :, y, c, :, low]
        third = go(part, part, recv.at[6], y_peer)
        part = whole.at[:, 1 - x, y, c, :, low]
        core_first = go(part, part, recv.at[8], c_peer)
        arrive(second)
        part = whole.at[:, x, :, c, :, high]
        fourth = go(part, part, recv.at[7], x_peer)
        part = whole.at[:, x, 1 - y, c, :, high]
        core_second = go(part, part, recv.at[9], c_peer)
        return (core, core_first, core_second, third, fourth)

    def spread_four(whole, got, recv, half, width):
        core, core_first, core_second, third, fourth = got
        low, high = (pl.ds(0, half), pl.ds(half, width - half))
        arrive(third)
        part = whole.at[:, :, 1 - y, c, :, low]
        core_third = go(part, part, recv.at[10], c_peer)
        arrive(fourth)
        part = whole.at[:, 1 - x, :, c, :, high]
        core_fourth = go(part, part, recv.at[11], c_peer)
        arrive(core, core_first, core_second, core_third, core_fourth)

    own_bot = stay(bot.at[ha], xr.at[ha, wa])
    bots = [
        go(bot.at[lax.rem(ha + d, 8)], xr.at[ha, wa], r_bot.at[d - 1], (lax.rem(ha + d, 8), wa))
        for d in range(1, 8)
    ]
    got_w3 = spread_z(w3, w3v, r_w3)
    got_wu = spread_z(wu, wuv, r_wu)
    got_w1 = spread(w1, w1q, 144, 0, 144, r_w1)
    settle(own_bot)
    arrive(*bots)
    to_c = go(xr.at[:, wa], xr.at[:, wa], r_grp.at[0], c_peer)
    to_y = go(xr.at[:, wa], xr.at[:, wa], r_grp.at[1], y_peer)
    got_w2a = spread(w2, w2q, 288, 0, 144, r_w2.at[0])
    got_w2b = spread(w2, w2q, 288, 144, 144, r_w2.at[1])
    own_skip = stay(skip.at[ha], skv.at[ha])
    skips = [
        go(skip.at[lax.rem(ha + d, 8)], skv.at[ha], r_skip.at[d - 1], (lax.rem(ha + d, 8), wa))
        for d in range(1, 8)
    ]
    own_code = stay(code.at[ha], code_out.at[ha])
    codes = [
        go(code.at[lax.rem(ha + d, 8)], code_out.at[ha], r_code.at[d - 1], (lax.rem(ha + d, 8), wa))
        for d in range(1, 8)
    ]
    own_head = stay(wh, whv.at[mine])
    heads = []
    for step in range(1, 32):
        other = lax.rem(mine + step, 32)
        heads.append(go(wh, whv.at[mine], r_wh.at[step - 1], (other // 4, lax.rem(other, 4))))
    if compute:
        x0[:, 0] = jnp.zeros((3, 32, 512), HALF)
        x0[:, 17] = jnp.zeros((3, 32, 512), HALF)
        h1[:, 0] = jnp.zeros((3, 32, 1024), HALF)
        h1[:, 17] = jnp.zeros((3, 32, 1024), HALF)
        for shift in range(3):
            tiles[shift, :, 0] = jnp.zeros((3, 16, 1024), HALF)
            tiles[shift, :, 33] = jnp.zeros((3, 16, 1024), HALF)
    arrive(to_y)
    part = xr.at[:, 2 * (1 - y) + c]
    on_c = go(part, part, r_grp.at[2], c_peer)
    arrive(to_c, on_c)

    if compute:

        def reorder(h, carry):
            block = xr[h].astype(FLOAT).reshape(4, 3, 2, 8, 512)
            for s in range(3):
                for r in range(2):
                    row = jnp.concatenate([block[w, s, r] for w in range(4)], axis=0)
                    x0[s, 2 * h + 1 + r] = row.astype(HALF)
            return carry

        lax.fori_loop(0, 8, reorder, 0)
    stay(x0.at[:, pl.ds(1, 16)], x0_out)
    got_w3 = spread_two(w3v, got_w3, r_w3, 384, 512)
    got_wu = spread_two(wuv, got_wu, r_wu, 1536, 2048)
    got_w3 = spread_three(w3v, got_w3, r_w3, 384, 512)
    got_wu = spread_three(wuv, got_wu, r_wu, 1536, 2048)
    passed_w1 = pass_x(w1q, 144, 0, 144, got_w1, r_w1x)
    spread_four(w3v, got_w3, r_w3, 384, 512)
    stay(w3v, w3_out)
    passed_w2a = pass_x(w2q, 288, 0, 144, got_w2a, r_w2x.at[0])
    arrive(*passed_w1)
    if compute:

        def one(s, carry):
            value = conv_slice(x0, w1q, parts, s, 512)
            pre1_out[s] = value
            h1s[s] = gelu_of(value).astype(HALF)
            return carry

        lax.fori_loop(0, 3, one, 0)

    def lanes(col):
        return h1.at[:, pl.ds(1, 16), :, pl.ds(pl.multiple_of(col * 256, 256), 256)]

    own_h1 = stay(h1s, lanes(wa))
    h1_c = go(h1s, lanes(wa), r_h1.at[0], c_peer)
    h1_y = go(h1s, lanes(wa), r_h1.at[1], y_peer)

    spread_four(wuv, got_wu, r_wu, 1536, 2048)
    stay(wuv, wu_out)
    passed_w2b = pass_x(w2q, 288, 144, 144, got_w2b, r_w2x.at[1])
    arrive(h1_y)
    h1_on = go(lanes(2 * (1 - y) + c), lanes(2 * (1 - y) + c), r_h1.at[2], c_peer)
    settle(own_h1)
    arrive(h1_c, h1_on)
    stay(h1.at[:, pl.ds(1, 16)], h1_out)
    settle(own_skip)
    arrive(*skips)

    def skip_slice(s):
        return skv[:, 64 * s : 64 * s + 64].astype(FLOAT).reshape(32, 16, 512)

    if compute:
        for s in range(3):
            value = skip_slice(s)
            rims[0, s] = value[:, 0].astype(HALF)
            rims[1, s] = value[:, 15].astype(HALF)
    before = (ha, lax.rem(wa + 3, 4))
    after = (ha, lax.rem(wa + 1, 4))
    rim_right = go(rims.at[0], rims_got.at[1], r_rim.at[1], before)
    rim_left = go(rims.at[1], rims_got.at[0], r_rim.at[0], after)
    arrive(*passed_w2a, *passed_w2b)
    stay(w2q, w2_out)
    if compute:

        def two(s, carry):
            value = conv_slice(h1, w2q, parts, s, 1024)
            pre2_out[s] = value
            hidden = gelu_of(value)
            for w in range(4):
                tile = hidden[:, 8 * w : 8 * w + 8].reshape(128, 256)
                h2s[w, pl.ds(pl.multiple_of(s * 128, 128), 128)] = tile.astype(HALF)
                left = hidden[:, 8 * w - 1] if w > 0 else jnp.zeros((16, 256), FLOAT)
                h2s[w, pl.ds(pl.multiple_of(384 + s * 16, 16), 16)] = left.astype(HALF)
                right = hidden[:, 8 * w + 8] if w < 3 else jnp.zeros((16, 256), FLOAT)
                h2s[w, pl.ds(pl.multiple_of(432 + s * 16, 16), 16)] = right.astype(HALF)
            return carry

        lax.fori_loop(0, 3, two, 0)
    h2_lanes = h2v.at[:, pl.ds(pl.multiple_of(wa * 256, 256), 256)]
    own_h2 = stay(h2s.at[wa], h2_lanes)
    h2_got = [
        go(h2s.at[lax.rem(wa + d, 4)], h2_lanes, r_h2.at[d - 1], (ha, lax.rem(wa + d, 4)))
        for d in range(1, 4)
    ]

    arrive(rim_right, rim_left)
    if compute:
        for s in range(3):
            left = jnp.where(wa > 0, rims_got[0, s].astype(FLOAT), 0.0)
            right = jnp.where(wa < 3, rims_got[1, s].astype(FLOAT), 0.0)
            put_shifts(
                tiles, pl.ds(512, 512), s, skip_slice(s), left[:, None, :], right[:, None, :]
            )
    def half_conv(first, fresh):
        rows = w3v.reshape(9216, 512)

        def one_slice(s, carry):
            if fresh:
                pre3_out[s] = jnp.zeros((512, 512), FLOAT)

            def tap(t, inner_carry):
                window = tiles[t % 3, s, pl.ds(t // 3, 32), :, pl.ds(first, 512)].reshape(512, 512)
                start = pl.multiple_of(1024 * t + first, 512)
                pre3_out[s] += jnp.dot(
                    window, rows[pl.ds(start, 512), :], preferred_element_type=FLOAT
                )
                return inner_carry

            lax.fori_loop(0, 9, tap, 0)
            return carry

        lax.fori_loop(0, 3, one_slice, 0)

    if compute:
        half_conv(512, True)
    settle(own_h2)
    arrive(*h2_got)
    stay(h2v, h2_out)
    if compute:
        order = lax.broadcasted_iota(jnp.int32, (256, 256), 1)
        inner = order % 128
        pick = (inner // 8) * 16 + (inner % 8) * 2 + order // 128
        woven = jnp.where(lax.broadcasted_iota(jnp.int32, (256, 256), 0) == pick, 1.0, 0.0)
        woven = woven.astype(HALF)
        wide = wuv.reshape(1024, 2048)
        for s in range(3):
            fine, sides = ([], ([], []))
            for a in range(2):
                weight = wide[:, 1024 * a : 1024 * a + 1024]
                flat = jnp.dot(
                    h2v[128 * s : 128 * s + 128], weight, preferred_element_type=FLOAT
                ).astype(HALF)
                flat = jnp.concatenate([flat[:, :512], flat[:, 512:]], axis=0)
                flat = jnp.dot(woven, flat, preferred_element_type=FLOAT)
                fine.append(flat.reshape(16, 16, 512))
                for side in range(2):
                    start = 384 + 48 * side + 16 * s
                    rim = jnp.dot(
                        h2v[start : start + 16],
                        weight[:, 512 * (1 - side) : 512 * (1 - side) + 512],
                        preferred_element_type=FLOAT,
                    )
                    sides[side].append(rim.astype(HALF).astype(FLOAT)[:, None, :])
            value = jnp.stack(fine, axis=1).reshape(32, 16, 512)
            left, right = [jnp.stack(side, axis=1).reshape(32, 1, 512) for side in sides]
            put_shifts(tiles, pl.ds(0, 512), s, value, left, right)

    stay(tiles.at[1, :, pl.ds(1, 32)], joined_out)
    settle(own_head)
    arrive(*heads)
    settle(own_code)
    arrive(*codes)
    if compute:
        head = whv.reshape(512, 128)[...].astype(FLOAT).T[:16].astype(HALF)
        head_out[...] = head
        row = lax.broadcasted_iota(jnp.int32, (8, 128), 0)
        lane = lax.broadcasted_iota(jnp.int32, (8, 128), 1)
        sums_out[0] = jnp.zeros((8, 128), FLOAT)

        half_conv(0, False)

        def three(s, carry):
            hidden = gelu_of(pre3_out[s]).astype(HALF)
            hidden_out[s] = hidden
            logits = lax.dot_general(
                head, hidden, (((1,), (1,)), ((), ())), preferred_element_type=FLOAT
            )
            logit_out[s] = logits
            return carry

        lax.fori_loop(0, 3, three, 0)
        total = jnp.zeros((8, 128), FLOAT)
        for s in range(3):
            probability, target, weighted = class_terms(logit_out, code_out, s)
            for k in range(2):
                terms = (
                    weighted * probability[k] * target[k],
                    weighted * probability[k],
                    weighted * target[k],
                )
                for j, term in enumerate(terms):
                    value = jnp.sum(term, axis=1, keepdims=True)
                    here_is = jnp.logical_and(row == s, lane == 3 * k + j)
                    total = total + jnp.where(here_is, value, 0.0)
        sums_out[0] = total
    sums = []
    for step in range(1, 32):
        other = lax.rem(mine + step, 32)
        sums.append(
            go(
                sums_out.at[0],
                sums_out.at[step],
                r_sum.at[step - 1],
                (other // 4, lax.rem(other, 4)),
            )
        )
    arrive(*sums)
    for entry in stays:
        if not entry[1]:
            settle(entry)
    for copy in sends:
        copy.wait_send()


def class_terms(logits, codes, s):
    pieces = [codes[2 * q, s : s + 1] + codes[2 * q + 1, s : s + 1] for q in range(4)]
    both = jnp.concatenate(pieces, axis=1)
    label = jnp.where(both >= 2.0, 1.0, 0.0)
    weighted = both - 2.0 * label
    first, second = (logits[s, 0:1], logits[s, 1:2])
    top = jnp.maximum(first, second)
    first, second = (jnp.exp(first - top), jnp.exp(second - top))
    scale = 1.0 / (first + second)
    return ((first * scale, second * scale), (1.0 - label, label), weighted)


def front(bot, skip, code, w1, w2, wu, w3, wh, compute=True):
    anywhere = pl.BlockSpec(memory_space=pl.ANY)
    inside = pl.BlockSpec(memory_space=pltpu.VMEM)
    shape = jax.ShapeDtypeStruct
    dma = pltpu.SemaphoreType.DMA

    def room(*dims):
        return pltpu.VMEM(dims, HALF)

    return pl.pallas_call(
        functools.partial(front_kernel, compute),
        name="front",
        out_shape=(
            shape((3, 16, 32, 512), HALF),
            shape((3, 16, 32, 1024), HALF),
            shape((480, 1024), HALF),
            shape((3, 32, 16, 1024), HALF),
            shape((9216, 256), HALF),
            shape((4, 2, 2, 2, 32, 2048), HALF),
            shape((4, 2, 2, 2, 288, 512), HALF),
            shape((3, 16, 32, 256), FLOAT),
            shape((3, 16, 32, 256), FLOAT),
            shape((3, 512, 512), FLOAT),
            shape((3, 512, 512), HALF),
            shape((3, 16, 512), FLOAT),
            shape((8, 8, 128), FLOAT),
            shape((32, 8, 128), FLOAT),
            shape((16, 512), HALF),
        ),
        in_specs=[anywhere] * 8,
        out_specs=[anywhere] * 7 + [inside] * 8,
        scratch_shapes=[
            room(8, 4, 48, 512),
            room(3, 18, 32, 512),
            room(4608, 256),
            room(9216, 256),
            room(3, 16, 32, 256),
            room(3, 18, 32, 1024),
            pltpu.VMEM((3, 512, 256), FLOAT),
            room(4, 480, 256),
            room(480, 1024),
            room(4, 2, 2, 2, 32, 2048),
            room(4, 2, 2, 2, 288, 512),
            room(8, 192, 512),
            room(2, 3, 32, 512),
            room(2, 3, 32, 512),
            room(3, 3, 34, 16, 1024),
            room(32, 16, 128),
            dma((220,)),
            dma((24,)),
            dma((7,)),
            dma((3,)),
            dma((4, 4)),
            dma((4,)),
            dma((2, 4, 4)),
            dma((2, 16)),
            dma((3,)),
            dma((3,)),
            dma((7,)),
            dma((31,)),
            dma((12,)),
            dma((12,)),
            dma((7,)),
            dma((2,)),
            dma((31,)),
        ],
        compiler_params=pltpu.CompilerParams(
            collective_id=0, has_side_effects=True, vmem_limit_bytes=64 * 1024 * 1024
        ),
    )(bot, skip, code, w1, w2, wu, w3, wh)


def gelu_slope(value):
    square = value * value
    bend = jnp.tanh(0.7978845608028654 * value * (1.0 + 0.044715 * square))
    rise = 0.7978845608028654 * (1.0 + 3.0 * 0.044715 * square)
    return 0.5 * (1.0 + bend) + 0.5 * value * (1.0 - bend * bend) * rise


def across(source, window):
    return lax.dot_general(source, window, (((0,), (0,)), ((), ())), preferred_element_type=FLOAT)


def against(window, weight):
    return lax.dot_general(window, weight, (((1,), (1,)), ((), ())), preferred_element_type=FLOAT)


def add_rows(total, start, term, rows):
    where = pl.ds(pl.multiple_of(start, 16), rows)
    total[where] = (total[where].astype(FLOAT) + term.astype(FLOAT)).astype(HALF)


def back_kernel(
    w3_in, wu_in, w2_in, joined_in, h2_in, h1_in, x0_in, pre1_in, pre2_in, pre3_in, hidden_in,
    logits, codes, slopes, head,
    g3, gu, g2, g1, gh,
    gs3, rims, rims_got, dh, joined, slot, acc, flat, wu, h2, gh2, from_wa, pre, gs2, d_core, d_y,
    du_c, du_y, du_x, du_z, d3, d3_c, d3_y, d3_x, d3_z, d2, d2_x, d2_z, d1_x, d1_z, hh,
    send, here, r_rim, r_wa, r_d, r_u, r_3, r_2, r_1, r_h, free,
):
    z, x, y, c = place()
    ha, wa = (2 * z + x, 2 * y + c)
    x_peer, y_peer, c_peer = (spot(z, 1 - x, y, c), spot(z, x, 1 - y, c), spot(z, x, y, 1 - c))
    mine = ha * 4 + wa
    sends = []
    stays = []

    def go(source, target, recv_sem, device):
        copy = remote(source, target, send.at[len(sends)], recv_sem, device)
        copy.start()
        sends.append(copy)
        return copy

    def stay(source, target):
        copy = pltpu.make_async_copy(source, target, here.at[len(stays)])
        copy.start()
        stays.append([copy, False])
        return stays[-1]

    def settle(*entries):
        for entry in entries:
            entry[0].wait()
            entry[1] = True

    got_hidden = stay(hidden_in, d3.at[pl.ds(0, 1536)])
    got_pre3 = stay(pre3_in.at[0], acc)
    got_w3 = [
        stay(
            w3_in.at[pl.ds(1024 * t, 512), pl.ds(256 * half, 256)],
            slot.at[pl.ds(4608 * half + 512 * t, 512)],
        )
        for half in range(2)
        for t in range(9)
    ]
    got_wu = stay(wu_in, wu)
    got_h2 = stay(h2_in.at[pl.ds(0, 384)], h2)
    got_h1 = stay(h1_in, joined)
    greet_all()

    settle(got_hidden)
    head_sum = jnp.zeros((16, 512), FLOAT)
    class_row = lax.broadcasted_iota(jnp.int32, (16, 512), 0)
    for e in range(3):
        gs3[e, :, 0] = jnp.zeros((3, 16, 512), HALF)
        gs3[e, :, 33] = jnp.zeros((3, 16, 512), HALF)
    for s in range(3):
        probability, target, weighted = class_terms(logits, codes, s)
        grads = [
            weighted * (target[k] * slopes[s : s + 1, k : k + 1] + slopes[s : s + 1, 2 + k : 3 + k])
            for k in range(2)
        ]
        inner = probability[0] * grads[0] + probability[1] * grads[1]
        grads = [probability[k] * (grads[k] - inner) for k in range(2)]
        grads = jnp.where(class_row == 0, grads[0], jnp.where(class_row == 1, grads[1], 0.0))
        grads = grads.astype(HALF)
        hidden = d3[512 * s : 512 * s + 512]
        head_sum = head_sum + jnp.dot(grads, hidden, preferred_element_type=FLOAT)
        settle(got_pre3)
        value = (across(grads, head[...]) * gelu_slope(acc[...])).astype(HALF)
        if s < 2:
            got_pre3 = stay(pre3_in.at[s + 1], acc)
        gs3[1, s, 1:33] = value.reshape(32, 16, 512)
        value = value.astype(FLOAT).reshape(32, 16, 512)
        rims[0, s] = value[:, 0].astype(HALF)
        rims[1, s] = value[:, 15].astype(HALF)
    before = (ha, lax.rem(wa + 3, 4))
    after = (ha, lax.rem(wa + 1, 4))
    rim_right = go(rims.at[0], rims_got.at[1], r_rim.at[1], before)
    rim_left = go(rims.at[1], rims_got.at[0], r_rim.at[0], after)
    rows = jnp.concatenate([head_sum, jnp.zeros((112, 512), FLOAT)], axis=0)
    dh[...] = rows.T.reshape(32, 16, 128)
    own_head = stay(dh.at[mine], hh.at[0])
    heads = []
    for step in range(1, 32):
        other = lax.rem(mine + step, 32)
        heads.append(
            go(dh.at[other], hh.at[step], r_h.at[step - 1], (other // 4, lax.rem(other, 4)))
        )
    rim_right.wait_recv()
    rim_left.wait_recv()
    for s in range(3):
        left = jnp.where(wa > 0, rims_got[0, s].astype(FLOAT), 0.0)
        right = jnp.where(wa < 3, rims_got[1, s].astype(FLOAT), 0.0)
        value = gs3[1, s, 1:33].astype(FLOAT)
        put_shifts(gs3, pl.ds(0, 512), s, value, left[:, None, :], right[:, None, :])

    order = lax.broadcasted_iota(jnp.int32, (256, 256), 0)
    inner = order % 128
    pick = (inner // 8) * 16 + (inner % 8) * 2 + order // 128
    apart = jnp.where(lax.broadcasted_iota(jnp.int32, (256, 256), 1) == pick, 1.0, 0.0).astype(HALF)
    settle(*got_w3)

    def three_source(s, carry):
        acc[...] = jnp.zeros_like(acc)

        def tap(t, inner_carry):
            window = gs3[2 - t % 3, s, pl.ds(2 - t // 3, 32)].reshape(512, 512)
            for half in range(2):
                rows = pl.ds(pl.multiple_of(4608 * half + 512 * t, 512), 512)
                acc[...] += against(window[:, 256 * half : 256 * half + 256], slot[rows])
            return inner_carry

        lax.fori_loop(0, 9, tap, 0)
        fine = acc[...].astype(HALF).reshape(16, 2, 16, 512)
        for a in range(2):
            parted = jnp.dot(
                apart, fine[:, a].reshape(256, 512), preferred_element_type=FLOAT
            ).astype(HALF)
            for b in range(2):
                rows = pl.ds(pl.multiple_of(128 * s, 128), 128)
                flat[rows, pl.ds(512 * (2 * a + b), 512)] = parted[128 * b : 128 * b + 128]
        return carry

    lax.fori_loop(0, 3, three_source, 0)
    got_w2 = stay(w2_in, slot)
    settle(got_wu, got_h2)
    for part in range(4):
        lanes = slice(256 * part, 256 * part + 256)
        gh2[:, lanes] = against(flat[...], wu[lanes, :]).astype(HALF)

    def wa_lanes(col):
        return gh2.at[:, pl.ds(pl.multiple_of(col * 256, 256), 256)]

    own_wa = stay(wa_lanes(wa), from_wa.at[wa])
    got_wa = [
        go(
            wa_lanes(lax.rem(wa + d, 4)),
            from_wa.at[wa],
            r_wa.at[d - 1],
            (ha, lax.rem(wa + d, 4)),
        )
        for d in range(1, 4)
    ]
    for part in range(4):
        lanes = slice(512 * part, 512 * part + 512)
        wu[:, lanes] = across(h2[...], flat[:, lanes]).astype(HALF)

    def block(grad, rows, bz, bx, by, bc):
        number = ((bz * 2 + bx) * 2 + by) * 2 + bc
        return grad.at[pl.ds(pl.multiple_of(number * rows, 16), rows)]

    def all_core(grad, rows, core, recv, some):
        return [
            go(
                block(grad, rows, bz, bx, by, 1 - c),
                core.at[((bz - some[0]) * 2 + bx) * 2 + by],
                recv.at[((bz - some[0]) * 2 + bx) * 2 + by],
                c_peer,
            )
            for bz in some
            for bx in range(2)
            for by in range(2)
        ]

    def all_y(grad, rows, core, along_y, recv, some, got):
        for copy in got:
            copy.wait_recv()

        def step(by):
            def add(i, carry):
                number = (((some[0] * 2 + i) * 2) + by) * 2 + c
                add_rows(grad, number * rows, core[i * 2 + by], rows)
                return carry

            lax.fori_loop(0, 2 * len(some), add, 0)

        step(1 - y)
        copies = [
            go(
                block(grad, rows, bz, bx, 1 - y, c),
                along_y.at[bz * 2 + bx],
                recv.at[16 + bz * 2 + bx],
                y_peer,
            )
            for bz in some
            for bx in range(2)
        ]
        step(y)
        return copies

    def all_x(grad, rows, along_y, along_x, recv, some, got):
        for copy in got:
            copy.wait_recv()

        def step(bx):
            def add(bz, carry):
                number = ((bz * 2 + bx) * 2 + y) * 2 + c
                add_rows(grad, number * rows, along_y[bz * 2 + bx], rows)
                return carry

            lax.fori_loop(some[0], some[-1] + 1, add, 0)

        step(1 - x)
        copies = [
            go(block(grad, rows, bz, 1 - x, y, c), along_x.at[bz], recv.at[24 + bz], x_peer)
            for bz in some
        ]
        step(x)
        return copies

    def all_z(grad, rows, along_x, along_z, recv, got):
        for copy in got:
            copy.wait_recv()

        def add(bz, carry):
            number = ((bz * 2 + x) * 2 + y) * 2 + c
            add_rows(grad, number * rows, along_x[bz], rows)
            return carry

        lax.fori_loop(0, 4, add, 0)
        return [
            go(
                block(grad, rows, lax.rem(z + d, 4), x, y, c),
                along_z.at[d - 1],
                recv.at[27 + d],
                spot(lax.rem(z + d, 4), x, y, c),
            )
            for d in range(1, 4)
        ]

    def all_end(grad, rows, along_z, out, got):
        total = grad[pl.ds(pl.multiple_of(mine * rows, 16), rows)].astype(FLOAT)
        for d in range(3):
            got[d].wait_recv()
            total = total + along_z[d].astype(FLOAT)
        out[...] = total

    def quarter_rows(rows, bz, bx):
        return pl.ds(pl.multiple_of((bz * 2 + bx) * 4 * rows, 16), 4 * rows)

    def quarter_x(grad, rows, along_x, recv, d):
        bz = lax.rem(z + d, 4)
        return go(grad.at[quarter_rows(rows, bz, 1 - x)], along_x.at[d - 1], recv.at[d - 1], x_peer)

    def quarter_z(grad, rows, along_x, along_z, recv, got, d):
        got[d - 1].wait_recv()
        bz = lax.rem(z + d, 4)
        add_rows(grad, (bz * 2 + x) * 4 * rows, along_x[d - 1], 4 * rows)
        if d == 4:
            return None
        return go(
            grad.at[quarter_rows(rows, bz, x)],
            along_z.at[d - 1],
            recv.at[3 + d],
            spot(bz, x, y, c),
        )

    def quarter_taps(taps):
        first = 2 * lax.rem(z + 1, 4)
        return [
            (d + 1, span, lambda i, carry: taps(lax.rem(first + i, 9), carry))
            for d, span in enumerate(((0, 3), (3, 6), (6, 8), (8, 9)))
        ]

    def quarter_w(grad, rows, along_z, out, recv, got):
        for copy in got:
            copy.wait_recv()

        own = pl.ds(pl.multiple_of(ha * 4 * rows, 16), 4 * rows)
        value = grad[own].astype(FLOAT)
        for d in range(3):
            value = value + along_z[d].astype(FLOAT)
        grad[own] = value.astype(HALF)
        target = out.at[:, pl.ds(pl.multiple_of(wa * 256, 256), 256)]

        def piece(col):
            return grad.at[pl.ds(pl.multiple_of((ha * 4 + col) * rows, 16), rows)]

        stay(piece(wa), target)
        return [
            go(
                piece(lax.rem(wa + d, 4)),
                target,
                recv.at[6 + d],
                (ha, lax.rem(wa + d, 4)),
            )
            for d in range(1, 4)
        ]

    su = all_core(wu, 32, du_c, r_u, (0, 1, 2, 3))
    su = all_y(wu, 32, du_c, du_y, r_u, (0, 1, 2, 3), su)

    def put_columns(target, s, value):
        put_shifts(target, pl.ds(0, 256), s, value, 0.0, 0.0)

    for e in range(3):
        gs2[e, :, 0] = jnp.zeros((3, 32, 256), HALF)
        gs2[e, :, 17] = jnp.zeros((3, 32, 256), HALF)
    settle(stay(pre2_in, pre))
    settle(own_wa)
    for copy in got_wa:
        copy.wait_recv()

    def two_grad(s, carry):
        rows = pl.ds(pl.multiple_of(128 * s, 128), 128)
        parts = [from_wa[w, rows].astype(FLOAT).reshape(16, 8, 256) for w in range(4)]
        put_columns(gs2, s, jnp.concatenate(parts, axis=1) * gelu_slope(pre[s]))
        return carry

    lax.fori_loop(0, 3, two_grad, 0)
    got_pre1 = stay(pre1_in, pre)
    settle(got_h1)

    def two_weight(t, carry):
        window = gs2[2 - t % 3, :, pl.ds(2 - t // 3, 16)].reshape(1536, 256)
        rows = pl.ds(pl.multiple_of(1024 * t, 1024), 1024)
        d2[rows] = across(joined[...], window).astype(HALF)
        return carry

    s2 = []
    for d, (first, last), taps in quarter_taps(two_weight):
        lax.fori_loop(first, last, taps, 0)
        s2.append(quarter_x(d2, 288, d2_x, r_2, d))
    settle(stay(joined_in, joined))

    def three_weight(t, carry):
        window = gs3[2 - t % 3, :, pl.ds(2 - t // 3, 32)].reshape(1536, 512)
        rows = pl.ds(pl.multiple_of(1024 * t, 1024), 1024)
        d3[rows] = across(joined[...], window).astype(HALF)
        return carry

    lax.fori_loop(0, 5, three_weight, 0)
    s3 = all_core(d3, 288, d3_c, r_3, (0, 1))
    z2 = [quarter_z(d2, 288, d2_x, d2_z, r_2, s2, 1)]
    s3_low = all_y(d3, 288, d3_c, d3_y, r_3, (0, 1), s3)
    pl.semaphore_signal(free, inc=1, device_id=c_peer, device_id_type=MESH)
    lax.fori_loop(5, 9, three_weight, 0)
    pl.semaphore_wait(free, 1)
    s3 = all_core(d3, 288, d3_c, r_3, (2, 3))
    got_x0 = stay(x0_in, joined.at[:, pl.ds(0, 512)])
    z2.append(quarter_z(d2, 288, d2_x, d2_z, r_2, s2, 2))
    settle(got_w2)

    def source_two(s):
        for half in range(2):
            acc[...] = jnp.zeros_like(acc)

            def tap(t, inner_carry):
                window = gs2[2 - t % 3, s, pl.ds(2 - t // 3, 16)].reshape(512, 256)
                rows = pl.ds(pl.multiple_of(1024 * t + 512 * half, 512), 512)
                acc[...] += against(window, slot[rows])
                return inner_carry

            lax.fori_loop(0, 9, tap, 0)
            gs3[half, s, pl.ds(0, 32)] = acc[...].astype(HALF).reshape(32, 16, 512)

    def d_lanes(halves, s, core):
        return gs3.at[halves, s, pl.ds(0, 32), :, pl.ds(pl.multiple_of(256 * core, 256), 256)]

    own_lanes = pl.ds(pl.multiple_of(256 * c, 256), 256)

    def d_pass(s):
        sd[s].wait_recv()
        for half in range(2):
            value = gs3[half, s, pl.ds(0, 32), :, own_lanes].astype(FLOAT)
            value = value + d_core[s, half].astype(FLOAT)
            gs3[half, s, pl.ds(0, 32), :, own_lanes] = value.astype(HALF)
        return go(d_lanes(1 - y, s, c), d_y.at[s], r_d.at[3 + s], y_peer)

    sd = []
    sy = []
    for s in range(3):
        source_two(s)
        sd.append(go(d_lanes(pl.ds(0, 2), s, 1 - c), d_core.at[s], r_d.at[s], c_peer))
        if s > 0:
            sy.append(d_pass(s - 1))
    sy.append(d_pass(2))
    s3_high = all_y(d3, 288, d3_c, d3_y, r_3, (2, 3), s3)
    z2.append(quarter_z(d2, 288, d2_x, d2_z, r_2, s2, 3))
    su = all_x(wu, 32, du_y, du_x, r_u, (0, 1, 2, 3), su)
    settle(got_pre1)
    for s in range(3):
        sy[s].wait_recv()
        value = gs3[y, s, pl.ds(0, 32), :, own_lanes].astype(FLOAT) + d_y[s].astype(FLOAT)
        put_columns(gs2, s, value.reshape(16, 32, 256) * gelu_slope(pre[s]))
    settle(got_x0)

    def one_weight(t, carry):
        window = gs2[2 - t % 3, :, pl.ds(2 - t // 3, 16)].reshape(1536, 256)
        rows = pl.ds(pl.multiple_of(512 * t, 512), 512)
        slot[rows] = across(joined[:, 0:512], window).astype(HALF)
        return carry

    s1 = []
    for d, (first, last), taps in quarter_taps(one_weight):
        lax.fori_loop(first, last, taps, 0)
        s1.append(quarter_x(slot, 144, d1_x, r_1, d))

    quarter_z(d2, 288, d2_x, d2_z, r_2, s2, 4)
    x3 = all_x(d3, 288, d3_y, d3_x, r_3, (0, 1), s3_low)
    su = all_z(wu, 32, du_x, du_z, r_u, su)
    z1 = [quarter_z(slot, 144, d1_x, d1_z, r_1, s1, d) for d in range(1, 4)]
    x3 += all_x(d3, 288, d3_y, d3_x, r_3, (2, 3), s3_high)
    s2 = quarter_w(d2, 288, d2_z, g2, r_2, z2)
    quarter_z(slot, 144, d1_x, d1_z, r_1, s1, 4)
    settle(own_head)
    total = hh[0]
    for step in range(1, 32):
        heads[step - 1].wait_recv()
        total = total + hh[step]
    gh[...] = total
    s3 = all_z(d3, 288, d3_x, d3_z, r_3, x3)
    all_end(wu, 32, du_z, gu, su)
    s1 = quarter_w(slot, 144, d1_z, g1, r_1, z1)
    all_end(d3, 288, d3_z, g3, s3)
    for copy in s2 + s1:
        copy.wait_recv()
    for entry in stays:
        if not entry[1]:
            settle(entry)
    for copy in sends:
        copy.wait_send()


def back(*args):
    anywhere = pl.BlockSpec(memory_space=pl.ANY)
    inside = pl.BlockSpec(memory_space=pltpu.VMEM)
    shape = jax.ShapeDtypeStruct
    dma = pltpu.SemaphoreType.DMA

    def room(*dims):
        return pltpu.VMEM(dims, HALF)

    return pl.pallas_call(
        back_kernel,
        name="back",
        out_shape=(
            shape((288, 512), FLOAT),
            shape((32, 2048), FLOAT),
            shape((288, 1024), HALF),
            shape((144, 1024), HALF),
            shape((16, 128), FLOAT),
        ),
        in_specs=[anywhere] * 11 + [inside] * 4,
        out_specs=[inside, inside, anywhere, anywhere, inside],
        scratch_shapes=[
            room(3, 3, 34, 16, 512),
            room(2, 3, 32, 512),
            room(2, 3, 32, 512),
            pltpu.VMEM((32, 16, 128), FLOAT),
            room(1536, 1024),
            room(9216, 256),
            pltpu.VMEM((512, 512), FLOAT),
            room(384, 2048),
            room(1024, 2048),
            room(384, 1024),
            room(384, 1024),
            room(4, 384, 256),
            pltpu.VMEM((3, 16, 32, 256), FLOAT),
            room(3, 3, 18, 32, 256),
            room(3, 2, 32, 16, 256),
            room(3, 32, 16, 256),
            room(16, 32, 2048),
            room(8, 32, 2048),
            room(4, 32, 2048),
            room(3, 32, 2048),
            room(9216, 512),
            room(8, 288, 512),
            room(8, 288, 512),
            room(4, 288, 512),
            room(3, 288, 512),
            room(9216, 256),
            room(4, 1152, 256),
            room(3, 1152, 256),
            room(4, 576, 256),
            room(3, 576, 256),
            pltpu.VMEM((32, 16, 128), FLOAT),
            dma((144,)),
            dma((40,)),
            dma((2,)),
            dma((3,)),
            dma((6,)),
            dma((31,)),
            dma((31,)),
            dma((10,)),
            dma((10,)),
            dma((31,)),
            pltpu.SemaphoreType.REGULAR,
        ],
        compiler_params=pltpu.CompilerParams(
            collective_id=2, has_side_effects=True, vmem_limit_bytes=64 * 1024 * 1024
        ),
    )(*args)


def dice_slopes(totals):
    union_sum = totals[..., 1] + totals[..., 2] + SMOOTHING
    numerator = 2.0 * totals[..., 0] + SMOOTHING
    dice_score = numerator / union_sum
    loss_value = 1.0 - jnp.mean(dice_score)
    entry_count = float(dice_score.size)
    common = -2.0 / (entry_count * union_sum)
    return (loss_value, jnp.concatenate([common, numerator / (entry_count * union_sum**2)], axis=1))


def sliced_grads(
    bottom, skipped, groups, pixel_mask, labels, weight_one, weight_two, weight_up, weight_three,
    weight_head,
):
    ha = lax.axis_index("ha")
    code = (pixel_mask + 2 * labels).astype(FLOAT).reshape(8, 3, 64)
    pads = [jnp.pad(code, ((0, 0), (0, 5), (64 * odd, 64 - 64 * odd))) for odd in range(2)]
    code = jnp.where(ha % 2 == 0, *pads)
    head_rows = jnp.pad(weight_head.astype(HALF), ((0, 0), (0, 126)))
    x0, h1, h2, joined, w2, wu, w3, pre_one, pre_two, pre_three, hidden_three, logits, code, sums, head = front(
        bottom.reshape(8, 48, 512),
        skipped.reshape(8, 192, 512),
        code,
        weight_one.astype(HALF),
        weight_two.astype(HALF),
        weight_up.astype(HALF),
        weight_three.astype(HALF),
        head_rows,
    )
    wu = wu.reshape(1024, 2048)
    w3 = w3.reshape(9216, 512)
    member = (groups[:, None] == jnp.arange(GROUPS)[None, :]).astype(FLOAT)
    step = lax.axis_index("ha") * 4 + lax.axis_index("wa")
    origin = (step - jnp.arange(32)) % 32
    at_group = jnp.einsum(
        "dh,hsg->dsg",
        (origin[:, None] // 4 == jnp.arange(8)[None, :]).astype(FLOAT),
        member.reshape(8, 3, GROUPS),
        precision=HIGHEST,
    )
    totals = jnp.einsum("dsg,dsq->gq", at_group, sums[:, :3, :6], precision=HIGHEST)
    totals = totals.reshape(GROUPS, 2, 3)
    loss_value, slopes = dice_slopes(totals)
    member = lax.dynamic_slice_in_dim(member, 3 * ha, 3, axis=0)
    slopes = jnp.einsum("sg,gq->sq", member, slopes, precision=HIGHEST)
    g3, gu, g2, g1, gh = back(
        w3,
        wu,
        w2,
        joined.reshape(1536, 1024),
        h2,
        h1.reshape(1536, 1024),
        x0.reshape(1536, 512),
        pre_one,
        pre_two,
        pre_three,
        hidden_three.reshape(1536, 512),
        logits,
        code,
        jnp.pad(slopes, ((0, 5), (0, 124))),
        head,
    )
    return (loss_value, g1.astype(FLOAT), g2.astype(FLOAT), gu, g3, gh[:, :2])


def body(
    bottom,
    skipped,
    groups,
    pixel_mask,
    labels,
    conv1_weight,
    conv1_momentum,
    conv1_average,
    conv2_weight,
    conv2_momentum,
    conv2_average,
    up_weight,
    up_momentum,
    up_average,
    conv3_weight,
    conv3_momentum,
    conv3_average,
    head_weight,
    head_momentum,
    head_average,
):
    split = bottom.shape[0] == 24 and bottom.shape[1:3] == (2, 8) and bottom.shape[3] == 512
    split = split and (lax.axis_size("ha"), lax.axis_size("wa")) == (8, 4)
    grads = sliced_grads if split else tiled_grads
    loss_value, conv1_grad, conv2_grad, up_grad, conv3_grad, head_grad = grads(
        bottom,
        skipped,
        groups,
        pixel_mask,
        labels,
        conv1_weight,
        conv2_weight,
        up_weight,
        conv3_weight,
        head_weight,
    )
    first = renew_state(conv1_weight, conv1_momentum, conv1_average, conv1_grad, RATE_CONV)
    second = renew_state(conv2_weight, conv2_momentum, conv2_average, conv2_grad, RATE_CONV)
    upward = renew_state(up_weight, up_momentum, up_average, up_grad, RATE_CONV)
    third = renew_state(conv3_weight, conv3_momentum, conv3_average, conv3_grad, RATE_CONV)
    header = renew_state(head_weight, head_momentum, head_average, head_grad, RATE_HEAD)
    return (
        loss_value,
        first[0],
        first[1],
        first[2],
        second[0],
        second[1],
        second[2],
        upward[0],
        upward[1],
        upward[2],
        third[0],
        third[1],
        third[2],
        header[0],
        header[1],
        header[2],
    )


def solution(mesh):
    in_specs = (
        P(None, "ha", "wa", None),
        P(None, "ha", "wa", None),
        P(),
        P(None, "ha", "wa"),
        P(None, "ha", "wa"),
        P(("ha", "wa"), None),
        P(("ha", "wa"), None),
        P(("ha", "wa"), None),
        P(("ha", "wa"), None),
        P(("ha", "wa"), None),
        P(("ha", "wa"), None),
        P(("ha", "wa"), None),
        P(("ha", "wa"), None),
        P(("ha", "wa"), None),
        P(("ha", "wa"), None),
        P(("ha", "wa"), None),
        P(("ha", "wa"), None),
        P(("ha", "wa"), None),
        P(("ha", "wa"), None),
        P(("ha", "wa"), None),
    )
    out_specs = (
        P(),
        P(("ha", "wa"), None),
        P(("ha", "wa"), None),
        P(("ha", "wa"), None),
        P(("ha", "wa"), None),
        P(("ha", "wa"), None),
        P(("ha", "wa"), None),
        P(("ha", "wa"), None),
        P(("ha", "wa"), None),
        P(("ha", "wa"), None),
        P(("ha", "wa"), None),
        P(("ha", "wa"), None),
        P(("ha", "wa"), None),
        P(("ha", "wa"), None),
        P(("ha", "wa"), None),
        P(("ha", "wa"), None),
    )
    return jax.shard_map(body, mesh=mesh, in_specs=in_specs, out_specs=out_specs, check_vma=False)
```

```python
import functools

import jax
import jax.numpy as jnp
from jax import lax
from jax.experimental import pallas as pl
from jax.experimental.pallas import tpu as pltpu
from jax.sharding import PartitionSpec as P

GROUPS = 5


MOMENTUM = 0.9
RATE_CONV = 600.0
RATE_HEAD = 25.0
AVERAGE_DECAY = 0.5
SMOOTHING = 1.0
HIGHEST = lax.Precision.HIGHEST


def with_halo(block, sides, width):
    for axis, dim in sides:
        count = lax.axis_size(axis)
        forward = [(i, i + 1) for i in range(count - 1)]
        backward = [(target, source) for source, target in forward]
        low = lax.ppermute(
            lax.slice_in_dim(block, block.shape[dim] - width, None, axis=dim), axis, forward
        )
        high = lax.ppermute(lax.slice_in_dim(block, 0, width, axis=dim), axis, backward)
        block = jnp.concatenate([low, block, high], axis=dim)
    return block


def smooth(source):
    return jax.nn.gelu(source, approximate=True)


def smooth_back(pre_value, gradient):
    _, pull_back = jax.vjp(smooth, pre_value)
    return pull_back(gradient)[0]


def widened_field(source):
    return with_halo(source, (("ha", 1), ("wa", 2)), 1)


def conv_taps(padded, weight):
    kernel = weight.reshape(3, 3, padded.shape[3], weight.shape[1])
    return lax.conv_general_dilated(
        padded,
        kernel,
        (1, 1),
        "VALID",
        dimension_numbers=("NHWC", "HWIO", "NHWC"),
        preferred_element_type=jnp.float32,
    )


def conv_back(padded, grad_out, weight, back_chan):
    in_chan = padded.shape[3]
    weight_grad = lax.conv_general_dilated(
        padded,
        grad_out,
        (1, 1),
        "VALID",
        dimension_numbers=("CHWN", "IHWO", "HWNC"),
        preferred_element_type=jnp.float32,
    ).reshape(9 * in_chan, grad_out.shape[3])
    if not back_chan:
        return (weight_grad, None)
    grad_padded = widened_field(grad_out)
    kernel = weight.reshape(3, 3, in_chan, weight.shape[1])[::-1, ::-1, :back_chan]
    source_grad = lax.conv_general_dilated(
        grad_padded,
        kernel,
        (1, 1),
        "VALID",
        dimension_numbers=("NHWC", "HWOI", "NHWC"),
        preferred_element_type=jnp.float32,
    )
    return (weight_grad, source_grad)


def upsample(source, weight):
    slices, row_count, col_count, _ = source.shape
    flattened = jnp.einsum("shwc,cq->shwq", source, weight, preferred_element_type=jnp.float32)
    blocks = flattened.reshape(slices, row_count, col_count, 2, 2, -1).transpose(0, 1, 3, 2, 4, 5)
    return blocks.reshape(slices, 2 * row_count, 2 * col_count, -1)


def upsample_back(source, grad_up, weight):
    slices, row_count, col_count, _ = source.shape
    blocks = grad_up.reshape(slices, row_count, 2, col_count, 2, -1).transpose(0, 1, 3, 2, 4, 5)
    flattened = blocks.reshape(slices, row_count, col_count, -1)
    weight_grad = jnp.einsum("shwc,shwq->cq", source, flattened, preferred_element_type=jnp.float32)
    source_grad = jnp.einsum("shwq,cq->shwc", flattened, weight, preferred_element_type=jnp.float32)
    return (weight_grad, source_grad)


def forward(gathered, bottom, skipped):
    weight_one, weight_two, weight_up, weight_three, weight_head = gathered
    pad_zero = widened_field(bottom)
    pre_one = conv_taps(pad_zero, weight_one)
    hidden_one = smooth(pre_one).astype(jnp.bfloat16)
    pad_one = widened_field(hidden_one)
    pre_two = conv_taps(pad_one, weight_two)
    hidden_two = smooth(pre_two).astype(jnp.bfloat16)
    upsampled = upsample(hidden_two, weight_up).astype(jnp.bfloat16)
    joined = jnp.concatenate([upsampled, skipped], axis=3)
    pad_two = widened_field(joined)
    pre_three = conv_taps(pad_two, weight_three)
    hidden_three = smooth(pre_three).astype(jnp.bfloat16)
    logits = jnp.einsum(
        "shwc,ck->shwk", hidden_three, weight_head, preferred_element_type=jnp.float32
    )
    return (
        pad_zero,
        pre_one,
        pad_one,
        pre_two,
        hidden_two,
        pad_two,
        pre_three,
        hidden_three,
        logits,
    )


def pixel_terms(logits, pixel_mask, labels):
    probability = jax.nn.softmax(logits, axis=-1)
    classes = jnp.arange(logits.shape[-1])
    target = (labels[..., None] == classes[None, None, None, :]).astype(jnp.float32)
    weighted = pixel_mask[..., None].astype(jnp.float32)
    return (probability, target, weighted)


def dice_terms(logits, pixel_mask, labels, member):
    probability, target, weighted = pixel_terms(logits, pixel_mask, labels)
    per_slice = jnp.stack(
        [
            jnp.sum(weighted * probability * target, axis=(1, 2)),
            jnp.sum(weighted * probability, axis=(1, 2)),
            jnp.sum(weighted * target, axis=(1, 2)),
        ],
        axis=-1,
    )
    return jnp.einsum("skj,sg->gkj", per_slice, member, precision=HIGHEST)


def dice_back(logits, pixel_mask, labels, member, totals):
    probability, target, weighted = pixel_terms(logits, pixel_mask, labels)
    union_sum = totals[..., 1] + totals[..., 2] + SMOOTHING
    numerator = 2.0 * totals[..., 0] + SMOOTHING
    dice_score = numerator / union_sum
    loss_value = 1.0 - jnp.mean(dice_score)
    entry_count = float(dice_score.size)
    coef_common = -2.0 / (entry_count * union_sum)
    coef_prob = numerator / (entry_count * union_sum * union_sum)
    slice_common = jnp.einsum("sg,gk->sk", member, coef_common, precision=HIGHEST)
    slice_prob = jnp.einsum("sg,gk->sk", member, coef_prob, precision=HIGHEST)
    grad_prob = weighted * (target * slice_common[:, None, None, :] + slice_prob[:, None, None, :])
    inner = jnp.sum(probability * grad_prob, axis=-1, keepdims=True)
    grad_logits = (probability * (grad_prob - inner)).astype(jnp.bfloat16)
    return (loss_value, grad_logits)


def renew_state(weight, moment, average, gradient, rate):
    moment_new = MOMENTUM * moment + gradient
    weight_new = weight - rate * (gradient + MOMENTUM * moment_new)
    average_new = AVERAGE_DECAY * average + (1.0 - AVERAGE_DECAY) * weight_new
    return (weight_new, moment_new, average_new)


def tiled_grads(
    bottom, skipped, groups, pixel_mask, labels, conv1_weight, conv2_weight, up_weight, conv3_weight,
    head_weight,
):
    gathered = (
        lax.all_gather(conv1_weight.astype(jnp.bfloat16), ("ha", "wa"), axis=0, tiled=True),
        lax.all_gather(conv2_weight.astype(jnp.bfloat16), ("ha", "wa"), axis=0, tiled=True),
        lax.all_gather(up_weight.astype(jnp.bfloat16), ("ha", "wa"), axis=0, tiled=True),
        lax.all_gather(conv3_weight.astype(jnp.bfloat16), ("ha", "wa"), axis=0, tiled=True),
        lax.all_gather(head_weight.astype(jnp.bfloat16), ("ha", "wa"), axis=0, tiled=True),
    )
    member = (groups[:, None] == jnp.arange(GROUPS)[None, :]).astype(jnp.float32)
    kept = forward(gathered, bottom, skipped)
    partial_sums = dice_terms(kept[8], pixel_mask, labels, member)
    totals = lax.psum(partial_sums, ("ha", "wa"))
    pad_zero, pre_one, pad_one, pre_two, hidden_two, pad_two, pre_three, hidden_three, logits = kept
    weight_one, weight_two, weight_up, weight_three, weight_head = gathered
    loss_value, grad_logits = dice_back(logits, pixel_mask, labels, member, totals)
    head_grad = jnp.einsum(
        "shwc,shwk->ck", hidden_three, grad_logits, preferred_element_type=jnp.float32
    )
    grad_hidden = jnp.einsum(
        "shwk,ck->shwc", grad_logits, weight_head, preferred_element_type=jnp.float32
    )
    grad_pre_three = smooth_back(pre_three, grad_hidden).astype(jnp.bfloat16)
    conv3_grad, grad_joined = conv_back(pad_two, grad_pre_three, weight_three, weight_up.shape[1] // 4)
    grad_upsampled = grad_joined.astype(jnp.bfloat16)
    up_grad, grad_hidden_two = upsample_back(hidden_two, grad_upsampled, weight_up)
    grad_pre_two = smooth_back(pre_two, grad_hidden_two).astype(jnp.bfloat16)
    conv2_grad, grad_hidden_one = conv_back(pad_one, grad_pre_two, weight_two, pad_one.shape[3])
    grad_pre_one = smooth_back(pre_one, grad_hidden_one).astype(jnp.bfloat16)
    conv1_grad, _ = conv_back(pad_zero, grad_pre_one, weight_one, 0)
    sums = (
        lax.psum_scatter(conv1_grad.astype(jnp.bfloat16), ("ha", "wa"), scatter_dimension=0, tiled=True),
        lax.psum_scatter(conv2_grad.astype(jnp.bfloat16), ("ha", "wa"), scatter_dimension=0, tiled=True),
        lax.psum_scatter(up_grad.astype(jnp.bfloat16), ("ha", "wa"), scatter_dimension=0, tiled=True),
        lax.psum_scatter(conv3_grad.astype(jnp.bfloat16), ("ha", "wa"), scatter_dimension=0, tiled=True),
        lax.psum_scatter(head_grad.astype(jnp.bfloat16), ("ha", "wa"), scatter_dimension=0, tiled=True),
    )
    return (loss_value, *[s.astype(jnp.float32) for s in sums])


MESH = pl.DeviceIdType.MESH
FLOAT = jnp.float32
HALF = jnp.bfloat16


def place():
    row, col = (lax.axis_index("ha"), lax.axis_index("wa"))
    return (row // 2, row % 2, col // 2, col % 2)


def spot(z, x, y, c):
    return (2 * z + x, 2 * y + c)


def greet_all():
    row, col = (lax.axis_index("ha"), lax.axis_index("wa"))
    rows, cols = (lax.axis_size("ha"), lax.axis_size("wa"))
    barrier = pltpu.get_barrier_semaphore()
    for step in range(1, rows * cols):
        other = lax.rem(row * cols + col + step, rows * cols)
        pl.semaphore_signal(
            barrier, inc=1, device_id=(other // cols, lax.rem(other, cols)), device_id_type=MESH
        )
    pl.semaphore_wait(barrier, rows * cols - 1)


def remote(source, target, send_sem, recv_sem, device):
    return pltpu.make_async_remote_copy(
        src_ref=source,
        dst_ref=target,
        send_sem=send_sem,
        recv_sem=recv_sem,
        device_id=device,
        device_id_type=MESH,
    )


def gelu_of(value):
    inner = 0.7978845608028654 * (value + 0.044715 * value * value * value)
    return 0.5 * value * (1.0 + jnp.tanh(inner))


def conv_slice(source, weight, parts, index, chan):
    parts[...] = jnp.zeros_like(parts)

    def row_tap(r, carry):
        window = source[index, pl.ds(r, 16)].reshape(512, chan)
        for c in range(3):
            start = pl.multiple_of((3 * r + c) * chan, chan)
            parts[c] += jnp.dot(
                window, weight[pl.ds(start, chan), :], preferred_element_type=FLOAT
            )
        return carry

    lax.fori_loop(0, 3, row_tap, 0)
    shape = (16, 32, 256)
    column = lax.broadcasted_iota(jnp.int32, shape, 1)
    low = jnp.where(column > 0, pltpu.roll(parts[0].reshape(shape), 1, 1), 0.0)
    high = jnp.where(column < 31, pltpu.roll(parts[2].reshape(shape), 31, 1), 0.0)
    return parts[1].reshape(shape) + low + high


def put_shifts(target, lanes, s, value, left, right):
    column = lax.broadcasted_iota(jnp.int32, value.shape, 1)
    last = value.shape[1] - 1
    rows = pl.ds(1, value.shape[0])
    low = jnp.where(column > 0, pltpu.roll(value, 1, 1), left)
    target[0, s, rows, :, lanes] = low.astype(HALF)
    target[1, s, rows, :, lanes] = value.astype(HALF)
    high = jnp.where(column < last, pltpu.roll(value, last, 1), right)
    target[2, s, rows, :, lanes] = high.astype(HALF)


def front_kernel(
    compute,
    bot, skip, code, w1, w2, wu, w3, wh,
    x0_out, h1_out, h2_out, joined_out, w2_out, wu_out, w3_out, pre1_out, pre2_out, pre3_out,
    hidden_out, logit_out, code_out, sums_out, head_out,
    xr, x0, w1q, w2q, h1s, h1, parts, h2s, h2v, wuv, w3v, skv, rims, rims_got, tiles, whv,
    send, here, r_bot, r_grp, r_w1, r_w2, r_h1, r_h2, r_skip, r_wh, r_w3, r_wu,
    r_code, r_rim, r_sum,
):
    z, x, y, c = place()
    ha, wa = (2 * z + x, 2 * y + c)
    x_peer, y_peer, c_peer = (spot(z, 1 - x, y, c), spot(z, x, 1 - y, c), spot(z, x, y, 1 - c))
    mine = ha * 4 + wa
    greet_all()
    sends = []
    stays = []

    def go(source, target, recv_sem, device):
        copy = remote(source, target, send.at[len(sends)], recv_sem, device)
        copy.start()
        sends.append((copy, None))
        return copy

    def stay(source, target):
        copy = pltpu.make_async_copy(source, target, here.at[len(stays)])
        copy.start()
        stays.append([copy, False])
        return stays[-1]

    def settle(*entries):
        for entry in entries:
            entry[0].wait()
            entry[1] = True

    def arrive(*copies):
        for copy in copies:
            copy.wait_recv()

    def go_if(when, source, target, recv_sem, device):
        copy = remote(source, target, send.at[len(sends)], recv_sem, device)
        pl.when(when)(lambda: copy.start())
        sends.append((copy, when))
        return (copy, when)

    def arrive_if(copy, when):
        pl.when(when)(lambda: copy.wait_recv())

    above, below = (spot(lax.rem(z + 1, 4), x, y, c), spot(lax.rem(z + 3, 4), x, y, c))

    def line_start(part, line):
        go_if(z < 3, part(z), part(z), line.at[0], above)
        go_if(z > 0, part(z), part(z), line.at[3], below)

    def line_hop(part, line, j, passes):
        for first, other, more, last, neighbour in (
            (0, lax.rem(z + 3 - j, 4), z >= j + 1, z < 3, above),
            (3, lax.rem(z + 1 + j, 4), z <= 2 - j, z > 0, below),
        ):
            piece = part(other)
            arrive_if(remote(piece, piece, send.at[0], line.at[first + j], x_peer), more)
            if j < 2:
                go_if(
                    jnp.logical_and(more, last), piece, piece, line.at[first + j + 1], neighbour
                )
            for recv, got, device in passes:
                got.append(go_if(more, piece, piece, recv.at[1 + first + j], device))

    def swap(shard, whole, first, count, recv):
        source_rows = pl.ds(first, count)
        target = whole.at[ha, wa, source_rows]
        lanes = [pl.ds(pl.multiple_of(lax.rem(wa + dw, 4) * 256, 256), 256) for dw in range(4)]
        own = stay(shard.at[source_rows, lanes[0]], target)
        copies = [
            go(shard.at[source_rows, lanes[dw]], target, recv.at[dw], (ha, lax.rem(wa + dw, 4)))
            for dw in range(1, 4)
        ]
        return (own, copies)

    class Quarter:
        def __init__(self, shard, whole, first, count, line, recv):
            self.line, self.recv, self.got = (line, recv, [])
            self.part = lambda bz: whole.at[bz * 2 + x, :, pl.ds(first, count)]
            self.swapped = swap(shard, whole, first, count, recv.at[1])

        def start(self):
            settle(self.swapped[0])
            arrive(*self.swapped[1])
            line_start(self.part, self.line)
            own = self.part(z)
            self.got.append((go(own, own, self.recv.at[0, 0], x_peer), None))

        def hop(self, j):
            line_hop(self.part, self.line, j, [(self.recv.at[0], self.got, x_peer)])

        def done(self):
            for copy, when in self.got:
                if when is None:
                    copy.wait_recv()
                else:
                    arrive_if(copy, when)

    class Whole:
        def __init__(self, shard, whole, line, recv):
            self.whole, self.line, self.recv = (whole, line, recv)
            self.part = lambda bz: whole.at[bz, x, y, c]
            self.own = stay(shard, self.part(z))
            self.along_x, self.along_y, self.core = ([], [], [])

        def start(self):
            settle(self.own)
            line_start(self.part, self.line)
            own = self.part(z)
            self.along_x.append((go(own, own, self.recv.at[0, 0], x_peer), None))
            self.along_y.append((go(own, own, self.recv.at[1, 0], y_peer), None))
            self.core.append((go(own, own, self.recv.at[2, 0], c_peer), None))

        def hop(self, j):
            passes = [
                (self.recv.at[0], self.along_x, x_peer),
                (self.recv.at[1], self.along_y, y_peer),
                (self.recv.at[2], self.core, c_peer),
            ]
            line_hop(self.part, self.line, j, passes)

        def wait(self, got):
            for copy, when in got:
                if when is None:
                    copy.wait_recv()
                else:
                    arrive_if(copy, when)

        def turn(self):
            self.wait(self.along_x)
            part = self.whole.at[:, 1 - x, y, c]
            self.last = go(part, part, self.recv.at[1, 7], y_peer)
            self.core.append((go(part, part, self.recv.at[2, 7], c_peer), None))

        def finish(self):
            self.wait(self.along_y)
            part = self.whole.at[:, x, 1 - y, c]
            self.core.append((go(part, part, self.recv.at[0, 7], c_peer), None))
            arrive(self.last)
            part = self.whole.at[:, 1 - x, 1 - y, c]
            self.core.append((go(part, part, self.recv.at[3, 0], c_peer), None))

        def done(self):
            self.wait(self.core)

    own_bot = stay(bot.at[ha], xr.at[ha, wa])
    bots = [
        go(bot.at[lax.rem(ha + d, 8)], xr.at[ha, wa], r_bot.at[d - 1], (lax.rem(ha + d, 8), wa))
        for d in range(1, 8)
    ]
    whole_three = Whole(w3, w3v, r_w3.at[4, pl.ds(0, 6)], r_w3)
    whole_up = Whole(wu, wuv, r_wu.at[4, pl.ds(0, 6)], r_wu)
    one_part = Quarter(w1, w1q, 0, 144, r_w1.at[2], r_w1)
    two_low = Quarter(w2, w2q, 0, 144, r_w2.at[0, 2], r_w2.at[0])
    two_high = Quarter(w2, w2q, 144, 144, r_w2.at[1, 2], r_w2.at[1])
    whole_three.start()
    whole_up.start()
    settle(own_bot)
    arrive(*bots)
    to_c = go(xr.at[:, wa], xr.at[:, wa], r_grp.at[0], c_peer)
    to_y = go(xr.at[:, wa], xr.at[:, wa], r_grp.at[1], y_peer)
    whole_three.hop(0)
    whole_up.hop(0)
    one_part.start()
    whole_three.hop(1)
    whole_up.hop(1)
    own_code = stay(code.at[ha], code_out.at[ha])
    codes = [
        go(code.at[lax.rem(ha + d, 8)], code_out.at[ha], r_code.at[d - 1], (lax.rem(ha + d, 8), wa))
        for d in range(1, 8)
    ]
    own_head = stay(wh, whv.at[mine])
    heads = []
    for step in range(1, 32):
        other = lax.rem(mine + step, 32)
        heads.append(go(wh, whv.at[mine], r_wh.at[step - 1], (other // 4, lax.rem(other, 4))))
    if compute:
        x0[:, 0] = jnp.zeros((3, 32, 512), HALF)
        x0[:, 17] = jnp.zeros((3, 32, 512), HALF)
        h1[:, 0] = jnp.zeros((3, 32, 1024), HALF)
        h1[:, 17] = jnp.zeros((3, 32, 1024), HALF)
        for shift in range(3):
            tiles[shift, :, 0] = jnp.zeros((3, 16, 1024), HALF)
            tiles[shift, :, 33] = jnp.zeros((3, 16, 1024), HALF)
    whole_three.hop(2)
    two_low.start()
    whole_up.hop(2)
    one_part.hop(0)
    two_high.start()
    arrive(to_y)
    part = xr.at[:, 2 * (1 - y) + c]
    on_c = go(part, part, r_grp.at[2], c_peer)
    arrive(to_c, on_c)

    if compute:

        def reorder(h, carry):
            block = xr[h].astype(FLOAT).reshape(4, 3, 2, 8, 512)
            for s in range(3):
                for r in range(2):
                    row = jnp.concatenate([block[w, s, r] for w in range(4)], axis=0)
                    x0[s, 2 * h + 1 + r] = row.astype(HALF)
            return carry

        lax.fori_loop(0, 8, reorder, 0)
    stay(x0.at[:, pl.ds(1, 16)], x0_out)
    one_part.hop(1)
    two_low.hop(0)
    one_part.hop(2)
    two_high.hop(0)
    whole_three.turn()
    two_low.hop(1)
    two_high.hop(1)
    whole_up.turn()
    own_skip = stay(skip.at[ha], skv.at[ha])
    skips = [
        go(skip.at[lax.rem(ha + d, 8)], skv.at[ha], r_skip.at[d - 1], (lax.rem(ha + d, 8), wa))
        for d in range(1, 8)
    ]
    two_low.hop(2)
    one_part.done()
    if compute:

        def one(s, carry):
            value = conv_slice(x0, w1q.reshape(4608, 256), parts, s, 512)
            pre1_out[s] = value
            h1s[s] = gelu_of(value).astype(HALF)
            return carry

        lax.fori_loop(0, 3, one, 0)

    def lanes(col):
        return h1.at[:, pl.ds(1, 16), :, pl.ds(pl.multiple_of(col * 256, 256), 256)]

    own_h1 = stay(h1s, lanes(wa))
    h1_c = go(h1s, lanes(wa), r_h1.at[0], c_peer)
    h1_y = go(h1s, lanes(wa), r_h1.at[1], y_peer)

    two_high.hop(2)
    whole_three.finish()
    whole_up.finish()
    arrive(h1_y)
    h1_on = go(lanes(2 * (1 - y) + c), lanes(2 * (1 - y) + c), r_h1.at[2], c_peer)
    settle(own_h1)
    arrive(h1_c, h1_on)
    stay(h1.at[:, pl.ds(1, 16)], h1_out)
    two_low.done()
    two_high.done()
    stay(w2q, w2_out)
    if compute:

        def two(s, carry):
            value = conv_slice(h1, w2q.reshape(9216, 256), parts, s, 1024)
            pre2_out[s] = value
            hidden = gelu_of(value)
            for w in range(4):
                tile = hidden[:, 8 * w : 8 * w + 8].reshape(128, 256)
                h2s[w, pl.ds(pl.multiple_of(s * 128, 128), 128)] = tile.astype(HALF)
                left = hidden[:, 8 * w - 1] if w > 0 else jnp.zeros((16, 256), FLOAT)
                h2s[w, pl.ds(pl.multiple_of(384 + s * 16, 16), 16)] = left.astype(HALF)
                right = hidden[:, 8 * w + 8] if w < 3 else jnp.zeros((16, 256), FLOAT)
                h2s[w, pl.ds(pl.multiple_of(432 + s * 16, 16), 16)] = right.astype(HALF)
            return carry

        lax.fori_loop(0, 3, two, 0)
    h2_lanes = h2v.at[:, pl.ds(pl.multiple_of(wa * 256, 256), 256)]
    own_h2 = stay(h2s.at[wa], h2_lanes)
    h2_got = [
        go(h2s.at[lax.rem(wa + d, 4)], h2_lanes, r_h2.at[d - 1], (ha, lax.rem(wa + d, 4)))
        for d in range(1, 4)
    ]

    settle(own_skip)
    arrive(*skips)

    def skip_slice(s):
        return skv[:, 64 * s : 64 * s + 64].astype(FLOAT).reshape(32, 16, 512)

    if compute:
        for s in range(3):
            value = skip_slice(s)
            rims[0, s] = value[:, 0].astype(HALF)
            rims[1, s] = value[:, 15].astype(HALF)
    before = (ha, lax.rem(wa + 3, 4))
    after = (ha, lax.rem(wa + 1, 4))
    rim_right = go(rims.at[0], rims_got.at[1], r_rim.at[1], before)
    rim_left = go(rims.at[1], rims_got.at[0], r_rim.at[0], after)
    arrive(rim_right, rim_left)
    if compute:
        for s in range(3):
            left = jnp.where(wa > 0, rims_got[0, s].astype(FLOAT), 0.0)
            right = jnp.where(wa < 3, rims_got[1, s].astype(FLOAT), 0.0)
            put_shifts(
                tiles, pl.ds(512, 512), s, skip_slice(s), left[:, None, :], right[:, None, :]
            )
    def half_conv(first, fresh):
        rows = w3v.reshape(9216, 512)

        def one_slice(s, carry):
            if fresh:
                pre3_out[s] = jnp.zeros((512, 512), FLOAT)

            def tap(t, inner_carry):
                window = tiles[t % 3, s, pl.ds(t // 3, 32), :, pl.ds(first, 512)].reshape(512, 512)
                start = pl.multiple_of(1024 * t + first, 512)
                pre3_out[s] += jnp.dot(
                    window, rows[pl.ds(start, 512), :], preferred_element_type=FLOAT
                )
                return inner_carry

            lax.fori_loop(0, 9, tap, 0)
            return carry

        lax.fori_loop(0, 3, one_slice, 0)

    whole_three.done()
    stay(w3v, w3_out)
    if compute:
        half_conv(512, True)
    settle(own_h2)
    arrive(*h2_got)
    stay(h2v, h2_out)
    whole_up.done()
    stay(wuv, wu_out)
    if compute:
        order = lax.broadcasted_iota(jnp.int32, (256, 256), 1)
        inner = order % 128
        pick = (inner // 8) * 16 + (inner % 8) * 2 + order // 128
        woven = jnp.where(lax.broadcasted_iota(jnp.int32, (256, 256), 0) == pick, 1.0, 0.0)
        woven = woven.astype(HALF)
        wide = wuv.reshape(1024, 2048)
        for s in range(3):
            fine, sides = ([], ([], []))
            for a in range(2):
                weight = wide[:, 1024 * a : 1024 * a + 1024]
                flat = jnp.dot(
                    h2v[128 * s : 128 * s + 128], weight, preferred_element_type=FLOAT
                ).astype(HALF)
                flat = jnp.concatenate([flat[:, :512], flat[:, 512:]], axis=0)
                flat = jnp.dot(woven, flat, preferred_element_type=FLOAT)
                fine.append(flat.reshape(16, 16, 512))
                for side in range(2):
                    start = 384 + 48 * side + 16 * s
                    rim = jnp.dot(
                        h2v[start : start + 16],
                        weight[:, 512 * (1 - side) : 512 * (1 - side) + 512],
                        preferred_element_type=FLOAT,
                    )
                    sides[side].append(rim.astype(HALF).astype(FLOAT)[:, None, :])
            value = jnp.stack(fine, axis=1).reshape(32, 16, 512)
            left, right = [jnp.stack(side, axis=1).reshape(32, 1, 512) for side in sides]
            put_shifts(tiles, pl.ds(0, 512), s, value, left, right)

    stay(tiles.at[1, :, pl.ds(1, 32)], joined_out)
    settle(own_head)
    arrive(*heads)
    settle(own_code)
    arrive(*codes)
    if compute:
        head = whv.reshape(512, 128)[...].astype(FLOAT).T[:16].astype(HALF)
        head_out[...] = head
        row = lax.broadcasted_iota(jnp.int32, (8, 128), 0)
        lane = lax.broadcasted_iota(jnp.int32, (8, 128), 1)
        sums_out[0] = jnp.zeros((8, 128), FLOAT)

        half_conv(0, False)

        def three(s, carry):
            hidden = gelu_of(pre3_out[s]).astype(HALF)
            hidden_out[s] = hidden
            logits = lax.dot_general(
                head, hidden, (((1,), (1,)), ((), ())), preferred_element_type=FLOAT
            )
            logit_out[s] = logits
            return carry

        lax.fori_loop(0, 3, three, 0)
        total = jnp.zeros((8, 128), FLOAT)
        for s in range(3):
            probability, target, weighted = class_terms(logit_out, code_out, s)
            for k in range(2):
                terms = (
                    weighted * probability[k] * target[k],
                    weighted * probability[k],
                    weighted * target[k],
                )
                for j, term in enumerate(terms):
                    value = jnp.sum(term, axis=1, keepdims=True)
                    here_is = jnp.logical_and(row == s, lane == 3 * k + j)
                    total = total + jnp.where(here_is, value, 0.0)
        sums_out[0] = total
    sums = []
    for step in range(1, 32):
        other = lax.rem(mine + step, 32)
        sums.append(
            go(
                sums_out.at[0],
                sums_out.at[step],
                r_sum.at[step - 1],
                (other // 4, lax.rem(other, 4)),
            )
        )
    arrive(*sums)
    for entry in stays:
        if not entry[1]:
            settle(entry)
    for copy, when in sends:
        if when is None:
            copy.wait_send()
        else:
            pl.when(when)(copy.wait_send)


def class_terms(logits, codes, s):
    pieces = [codes[2 * q, s : s + 1] + codes[2 * q + 1, s : s + 1] for q in range(4)]
    both = jnp.concatenate(pieces, axis=1)
    label = jnp.where(both >= 2.0, 1.0, 0.0)
    weighted = both - 2.0 * label
    first, second = (logits[s, 0:1], logits[s, 1:2])
    top = jnp.maximum(first, second)
    first, second = (jnp.exp(first - top), jnp.exp(second - top))
    scale = 1.0 / (first + second)
    return ((first * scale, second * scale), (1.0 - label, label), weighted)


def front(bot, skip, code, w1, w2, wu, w3, wh, compute=True):
    anywhere = pl.BlockSpec(memory_space=pl.ANY)
    inside = pl.BlockSpec(memory_space=pltpu.VMEM)
    shape = jax.ShapeDtypeStruct
    dma = pltpu.SemaphoreType.DMA

    def room(*dims):
        return pltpu.VMEM(dims, HALF)

    return pl.pallas_call(
        functools.partial(front_kernel, compute),
        name="front",
        out_shape=(
            shape((3, 16, 32, 512), HALF),
            shape((3, 16, 32, 1024), HALF),
            shape((480, 1024), HALF),
            shape((3, 32, 16, 1024), HALF),
            shape((8, 4, 288, 256), HALF),
            shape((4, 2, 2, 2, 32, 2048), HALF),
            shape((4, 2, 2, 2, 288, 512), HALF),
            shape((3, 16, 32, 256), FLOAT),
            shape((3, 16, 32, 256), FLOAT),
            shape((3, 512, 512), FLOAT),
            shape((3, 512, 512), HALF),
            shape((3, 16, 512), FLOAT),
            shape((8, 8, 128), FLOAT),
            shape((32, 8, 128), FLOAT),
            shape((16, 512), HALF),
        ),
        in_specs=[anywhere] * 8,
        out_specs=[anywhere] * 7 + [inside] * 8,
        scratch_shapes=[
            room(8, 4, 48, 512),
            room(3, 18, 32, 512),
            room(8, 4, 144, 256),
            room(8, 4, 288, 256),
            room(3, 16, 32, 256),
            room(3, 18, 32, 1024),
            pltpu.VMEM((3, 512, 256), FLOAT),
            room(4, 480, 256),
            room(480, 1024),
            room(4, 2, 2, 2, 32, 2048),
            room(4, 2, 2, 2, 288, 512),
            room(8, 192, 512),
            room(2, 3, 32, 512),
            room(2, 3, 32, 512),
            room(3, 3, 34, 16, 1024),
            room(32, 16, 128),
            dma((256,)),
            dma((24,)),
            dma((7,)),
            dma((3,)),
            dma((3, 8)),
            dma((2, 3, 8)),
            dma((3,)),
            dma((3,)),
            dma((7,)),
            dma((31,)),
            dma((5, 8)),
            dma((5, 8)),
            dma((7,)),
            dma((2,)),
            dma((31,)),
        ],
        compiler_params=pltpu.CompilerParams(
            collective_id=0, has_side_effects=True, vmem_limit_bytes=64 * 1024 * 1024
        ),
    )(bot, skip, code, w1, w2, wu, w3, wh)


def gelu_slope(value):
    square = value * value
    bend = jnp.tanh(0.7978845608028654 * value * (1.0 + 0.044715 * square))
    rise = 0.7978845608028654 * (1.0 + 3.0 * 0.044715 * square)
    return 0.5 * (1.0 + bend) + 0.5 * value * (1.0 - bend * bend) * rise


def across(source, window):
    return lax.dot_general(source, window, (((0,), (0,)), ((), ())), preferred_element_type=FLOAT)


def against(window, weight):
    return lax.dot_general(window, weight, (((1,), (1,)), ((), ())), preferred_element_type=FLOAT)


def add_rows(total, start, term, rows):
    where = pl.ds(pl.multiple_of(start, 16), rows)
    total[where] = (total[where].astype(FLOAT) + term.astype(FLOAT)).astype(HALF)


def back_kernel(
    w3_in, wu_in, w2_in, joined_in, h2_in, h1_in, x0_in, pre1_in, pre2_in, pre3_in, hidden_in,
    logits, codes, slopes, head,
    g3, gu, g2, g1, gh,
    gs3, rims, rims_got, dh, joined, slot, acc, flat, wu, h2, gh2, from_wa, pre, gs2, d_core, d_y,
    du_c, du_y, du_x, du_z, d3, d3_c, d3_y, d3_x, d3_z, d2, d2_x, d2_z, d1_x, d1_z, hh,
    send, here, r_rim, r_wa, r_d, r_u, r_3, r_2, r_1, r_h, free,
):
    z, x, y, c = place()
    ha, wa = (2 * z + x, 2 * y + c)
    x_peer, y_peer, c_peer = (spot(z, 1 - x, y, c), spot(z, x, 1 - y, c), spot(z, x, y, 1 - c))
    mine = ha * 4 + wa
    sends = []
    stays = []

    def go(source, target, recv_sem, device):
        copy = remote(source, target, send.at[len(sends)], recv_sem, device)
        copy.start()
        sends.append(copy)
        return copy

    def stay(source, target):
        copy = pltpu.make_async_copy(source, target, here.at[len(stays)])
        copy.start()
        stays.append([copy, False])
        return stays[-1]

    def settle(*entries):
        for entry in entries:
            entry[0].wait()
            entry[1] = True

    got_hidden = stay(hidden_in, d3.at[pl.ds(0, 1536)])
    got_pre3 = stay(pre3_in.at[0], acc)
    got_w3 = [
        stay(
            w3_in.at[pl.ds(1024 * t, 512), pl.ds(256 * half, 256)],
            slot.at[pl.ds(4608 * half + 512 * t, 512)],
        )
        for half in range(2)
        for t in range(9)
    ]
    got_wu = stay(wu_in, wu)
    got_h2 = stay(h2_in.at[pl.ds(0, 384)], h2)
    got_h1 = stay(h1_in, joined)
    greet_all()

    settle(got_hidden)
    head_sum = jnp.zeros((16, 512), FLOAT)
    class_row = lax.broadcasted_iota(jnp.int32, (16, 512), 0)
    for e in range(3):
        gs3[e, :, 0] = jnp.zeros((3, 16, 512), HALF)
        gs3[e, :, 33] = jnp.zeros((3, 16, 512), HALF)
    for s in range(3):
        probability, target, weighted = class_terms(logits, codes, s)
        grads = [
            weighted * (target[k] * slopes[s : s + 1, k : k + 1] + slopes[s : s + 1, 2 + k : 3 + k])
            for k in range(2)
        ]
        inner = probability[0] * grads[0] + probability[1] * grads[1]
        grads = [probability[k] * (grads[k] - inner) for k in range(2)]
        grads = jnp.where(class_row == 0, grads[0], jnp.where(class_row == 1, grads[1], 0.0))
        grads = grads.astype(HALF)
        hidden = d3[512 * s : 512 * s + 512]
        head_sum = head_sum + jnp.dot(grads, hidden, preferred_element_type=FLOAT)
        settle(got_pre3)
        value = (across(grads, head[...]) * gelu_slope(acc[...])).astype(HALF)
        if s < 2:
            got_pre3 = stay(pre3_in.at[s + 1], acc)
        gs3[1, s, 1:33] = value.reshape(32, 16, 512)
        value = value.astype(FLOAT).reshape(32, 16, 512)
        rims[0, s] = value[:, 0].astype(HALF)
        rims[1, s] = value[:, 15].astype(HALF)
    before = (ha, lax.rem(wa + 3, 4))
    after = (ha, lax.rem(wa + 1, 4))
    rim_right = go(rims.at[0], rims_got.at[1], r_rim.at[1], before)
    rim_left = go(rims.at[1], rims_got.at[0], r_rim.at[0], after)
    rows = jnp.concatenate([head_sum, jnp.zeros((112, 512), FLOAT)], axis=0)
    dh[...] = rows.T.reshape(32, 16, 128)
    own_head = stay(dh.at[mine], hh.at[0])
    heads = []
    for step in range(1, 32):
        other = lax.rem(mine + step, 32)
        heads.append(
            go(dh.at[other], hh.at[step], r_h.at[step - 1], (other // 4, lax.rem(other, 4)))
        )
    rim_right.wait_recv()
    rim_left.wait_recv()
    for s in range(3):
        left = jnp.where(wa > 0, rims_got[0, s].astype(FLOAT), 0.0)
        right = jnp.where(wa < 3, rims_got[1, s].astype(FLOAT), 0.0)
        value = gs3[1, s, 1:33].astype(FLOAT)
        put_shifts(gs3, pl.ds(0, 512), s, value, left[:, None, :], right[:, None, :])

    order = lax.broadcasted_iota(jnp.int32, (256, 256), 0)
    inner = order % 128
    pick = (inner // 8) * 16 + (inner % 8) * 2 + order // 128
    apart = jnp.where(lax.broadcasted_iota(jnp.int32, (256, 256), 1) == pick, 1.0, 0.0).astype(HALF)
    settle(*got_w3)

    def three_source(s, carry):
        acc[...] = jnp.zeros_like(acc)

        def tap(t, inner_carry):
            window = gs3[2 - t % 3, s, pl.ds(2 - t // 3, 32)].reshape(512, 512)
            for half in range(2):
                rows = pl.ds(pl.multiple_of(4608 * half + 512 * t, 512), 512)
                acc[...] += against(window[:, 256 * half : 256 * half + 256], slot[rows])
            return inner_carry

        lax.fori_loop(0, 9, tap, 0)
        fine = acc[...].astype(HALF).reshape(16, 2, 16, 512)
        for a in range(2):
            parted = jnp.dot(
                apart, fine[:, a].reshape(256, 512), preferred_element_type=FLOAT
            ).astype(HALF)
            for b in range(2):
                rows = pl.ds(pl.multiple_of(128 * s, 128), 128)
                flat[rows, pl.ds(512 * (2 * a + b), 512)] = parted[128 * b : 128 * b + 128]
        return carry

    lax.fori_loop(0, 3, three_source, 0)
    got_w2 = stay(w2_in, slot)
    settle(got_wu, got_h2)
    for part in range(4):
        lanes = slice(256 * part, 256 * part + 256)
        gh2[:, lanes] = against(flat[...], wu[lanes, :]).astype(HALF)

    def wa_lanes(col):
        return gh2.at[:, pl.ds(pl.multiple_of(col * 256, 256), 256)]

    own_wa = stay(wa_lanes(wa), from_wa.at[wa])
    got_wa = [
        go(
            wa_lanes(lax.rem(wa + d, 4)),
            from_wa.at[wa],
            r_wa.at[d - 1],
            (ha, lax.rem(wa + d, 4)),
        )
        for d in range(1, 4)
    ]
    for part in range(4):
        lanes = slice(512 * part, 512 * part + 512)
        wu[:, lanes] = across(h2[...], flat[:, lanes]).astype(HALF)

    def block(grad, rows, bz, bx, by, bc):
        number = ((bz * 2 + bx) * 2 + by) * 2 + bc
        return grad.at[pl.ds(pl.multiple_of(number * rows, 16), rows)]

    def all_core(grad, rows, core, recv, some):
        return [
            go(
                block(grad, rows, bz, bx, by, 1 - c),
                core.at[((bz - some[0]) * 2 + bx) * 2 + by],
                recv.at[((bz - some[0]) * 2 + bx) * 2 + by],
                c_peer,
            )
            for bz in some
            for bx in range(2)
            for by in range(2)
        ]

    def all_y(grad, rows, core, along_y, recv, some, got):
        for copy in got:
            copy.wait_recv()

        def step(by):
            def add(i, carry):
                number = (((some[0] * 2 + i) * 2) + by) * 2 + c
                add_rows(grad, number * rows, core[i * 2 + by], rows)
                return carry

            lax.fori_loop(0, 2 * len(some), add, 0)

        step(1 - y)
        copies = [
            go(
                block(grad, rows, bz, bx, 1 - y, c),
                along_y.at[bz * 2 + bx],
                recv.at[16 + bz * 2 + bx],
                y_peer,
            )
            for bz in some
            for bx in range(2)
        ]
        step(y)
        return copies

    def all_x(grad, rows, along_y, along_x, recv, some, got):
        for copy in got:
            copy.wait_recv()

        def step(bx):
            def add(bz, carry):
                number = ((bz * 2 + bx) * 2 + y) * 2 + c
                add_rows(grad, number * rows, along_y[bz * 2 + bx], rows)
                return carry

            lax.fori_loop(some[0], some[-1] + 1, add, 0)

        step(1 - x)
        copies = [
            go(block(grad, rows, bz, 1 - x, y, c), along_x.at[bz], recv.at[24 + bz], x_peer)
            for bz in some
        ]
        step(x)
        return copies

    def all_z(grad, rows, along_x, along_z, recv, got):
        for copy in got:
            copy.wait_recv()

        def add(bz, carry):
            number = ((bz * 2 + x) * 2 + y) * 2 + c
            add_rows(grad, number * rows, along_x[bz], rows)
            return carry

        lax.fori_loop(0, 4, add, 0)
        return [
            go(
                block(grad, rows, lax.rem(z + d, 4), x, y, c),
                along_z.at[d - 1],
                recv.at[27 + d],
                spot(lax.rem(z + d, 4), x, y, c),
            )
            for d in range(1, 4)
        ]

    def all_end(grad, rows, along_z, out, got):
        total = grad[pl.ds(pl.multiple_of(mine * rows, 16), rows)].astype(FLOAT)
        for d in range(3):
            got[d].wait_recv()
            total = total + along_z[d].astype(FLOAT)
        out[...] = total

    def quarter_rows(rows, bz, bx):
        return pl.ds(pl.multiple_of((bz * 2 + bx) * 4 * rows, 16), 4 * rows)

    def quarter_x(grad, rows, along_x, recv, d):
        bz = lax.rem(z + d, 4)
        return go(grad.at[quarter_rows(rows, bz, 1 - x)], along_x.at[d - 1], recv.at[d - 1], x_peer)

    def quarter_z(grad, rows, along_x, along_z, recv, got, d):
        got[d - 1].wait_recv()
        bz = lax.rem(z + d, 4)
        add_rows(grad, (bz * 2 + x) * 4 * rows, along_x[d - 1], 4 * rows)
        if d == 4:
            return None
        return go(
            grad.at[quarter_rows(rows, bz, x)],
            along_z.at[d - 1],
            recv.at[3 + d],
            spot(bz, x, y, c),
        )

    def quarter_taps(taps):
        first = 2 * lax.rem(z + 1, 4)
        return [
            (d + 1, span, lambda i, carry: taps(lax.rem(first + i, 9), carry))
            for d, span in enumerate(((0, 3), (3, 6), (6, 8), (8, 9)))
        ]

    def quarter_w(grad, rows, along_z, out, recv, got):
        for copy in got:
            copy.wait_recv()

        own = pl.ds(pl.multiple_of(ha * 4 * rows, 16), 4 * rows)
        value = grad[own].astype(FLOAT)
        for d in range(3):
            value = value + along_z[d].astype(FLOAT)
        grad[own] = value.astype(HALF)
        target = out.at[:, pl.ds(pl.multiple_of(wa * 256, 256), 256)]

        def piece(col):
            return grad.at[pl.ds(pl.multiple_of((ha * 4 + col) * rows, 16), rows)]

        stay(piece(wa), target)
        return [
            go(
                piece(lax.rem(wa + d, 4)),
                target,
                recv.at[6 + d],
                (ha, lax.rem(wa + d, 4)),
            )
            for d in range(1, 4)
        ]

    su = all_core(wu, 32, du_c, r_u, (0, 1, 2, 3))
    su = all_y(wu, 32, du_c, du_y, r_u, (0, 1, 2, 3), su)

    def put_columns(target, s, value):
        put_shifts(target, pl.ds(0, 256), s, value, 0.0, 0.0)

    for e in range(3):
        gs2[e, :, 0] = jnp.zeros((3, 32, 256), HALF)
        gs2[e, :, 17] = jnp.zeros((3, 32, 256), HALF)
    settle(stay(pre2_in, pre))
    settle(own_wa)
    for copy in got_wa:
        copy.wait_recv()

    def two_grad(s, carry):
        rows = pl.ds(pl.multiple_of(128 * s, 128), 128)
        parts = [from_wa[w, rows].astype(FLOAT).reshape(16, 8, 256) for w in range(4)]
        put_columns(gs2, s, jnp.concatenate(parts, axis=1) * gelu_slope(pre[s]))
        return carry

    lax.fori_loop(0, 3, two_grad, 0)
    got_pre1 = stay(pre1_in, pre)
    settle(got_h1)

    def two_weight(t, carry):
        window = gs2[2 - t % 3, :, pl.ds(2 - t // 3, 16)].reshape(1536, 256)
        rows = pl.ds(pl.multiple_of(1024 * t, 1024), 1024)
        d2[rows] = across(joined[...], window).astype(HALF)
        return carry

    s2 = []
    for d, (first, last), taps in quarter_taps(two_weight):
        lax.fori_loop(first, last, taps, 0)
        s2.append(quarter_x(d2, 288, d2_x, r_2, d))
    settle(stay(joined_in, joined))

    def three_weight(t, carry):
        window = gs3[2 - t % 3, :, pl.ds(2 - t // 3, 32)].reshape(1536, 512)
        rows = pl.ds(pl.multiple_of(1024 * t, 1024), 1024)
        d3[rows] = across(joined[...], window).astype(HALF)
        return carry

    lax.fori_loop(0, 5, three_weight, 0)
    s3 = all_core(d3, 288, d3_c, r_3, (0, 1))
    z2 = [quarter_z(d2, 288, d2_x, d2_z, r_2, s2, 1)]
    s3_low = all_y(d3, 288, d3_c, d3_y, r_3, (0, 1), s3)
    pl.semaphore_signal(free, inc=1, device_id=c_peer, device_id_type=MESH)
    lax.fori_loop(5, 9, three_weight, 0)
    pl.semaphore_wait(free, 1)
    s3 = all_core(d3, 288, d3_c, r_3, (2, 3))
    got_x0 = stay(x0_in, joined.at[:, pl.ds(0, 512)])
    z2.append(quarter_z(d2, 288, d2_x, d2_z, r_2, s2, 2))
    settle(got_w2)

    def source_two(s):
        for half in range(2):
            acc[...] = jnp.zeros_like(acc)

            def tap(t, inner_carry):
                window = gs2[2 - t % 3, s, pl.ds(2 - t // 3, 16)].reshape(512, 256)
                rows = pl.ds(pl.multiple_of(1024 * t + 512 * half, 512), 512)
                acc[...] += against(window, slot[rows])
                return inner_carry

            lax.fori_loop(0, 9, tap, 0)
            gs3[half, s, pl.ds(0, 32)] = acc[...].astype(HALF).reshape(32, 16, 512)

    def d_lanes(halves, s, core):
        return gs3.at[halves, s, pl.ds(0, 32), :, pl.ds(pl.multiple_of(256 * core, 256), 256)]

    own_lanes = pl.ds(pl.multiple_of(256 * c, 256), 256)

    def d_pass(s):
        sd[s].wait_recv()
        for half in range(2):
            value = gs3[half, s, pl.ds(0, 32), :, own_lanes].astype(FLOAT)
            value = value + d_core[s, half].astype(FLOAT)
            gs3[half, s, pl.ds(0, 32), :, own_lanes] = value.astype(HALF)
        return go(d_lanes(1 - y, s, c), d_y.at[s], r_d.at[3 + s], y_peer)

    sd = []
    sy = []
    for s in range(3):
        source_two(s)
        sd.append(go(d_lanes(pl.ds(0, 2), s, 1 - c), d_core.at[s], r_d.at[s], c_peer))
        if s > 0:
            sy.append(d_pass(s - 1))
    sy.append(d_pass(2))
    s3_high = all_y(d3, 288, d3_c, d3_y, r_3, (2, 3), s3)
    z2.append(quarter_z(d2, 288, d2_x, d2_z, r_2, s2, 3))
    su = all_x(wu, 32, du_y, du_x, r_u, (0, 1, 2, 3), su)
    settle(got_pre1)
    for s in range(3):
        sy[s].wait_recv()
        value = gs3[y, s, pl.ds(0, 32), :, own_lanes].astype(FLOAT) + d_y[s].astype(FLOAT)
        put_columns(gs2, s, value.reshape(16, 32, 256) * gelu_slope(pre[s]))
    settle(got_x0)

    def one_weight(t, carry):
        window = gs2[2 - t % 3, :, pl.ds(2 - t // 3, 16)].reshape(1536, 256)
        rows = pl.ds(pl.multiple_of(512 * t, 512), 512)
        slot[rows] = across(joined[:, 0:512], window).astype(HALF)
        return carry

    s1 = []
    for d, (first, last), taps in quarter_taps(one_weight):
        lax.fori_loop(first, last, taps, 0)
        s1.append(quarter_x(slot, 144, d1_x, r_1, d))

    quarter_z(d2, 288, d2_x, d2_z, r_2, s2, 4)
    x3 = all_x(d3, 288, d3_y, d3_x, r_3, (0, 1), s3_low)
    su = all_z(wu, 32, du_x, du_z, r_u, su)
    z1 = [quarter_z(slot, 144, d1_x, d1_z, r_1, s1, d) for d in range(1, 4)]
    x3 += all_x(d3, 288, d3_y, d3_x, r_3, (2, 3), s3_high)
    s2 = quarter_w(d2, 288, d2_z, g2, r_2, z2)
    quarter_z(slot, 144, d1_x, d1_z, r_1, s1, 4)
    settle(own_head)
    total = hh[0]
    for step in range(1, 32):
        heads[step - 1].wait_recv()
        total = total + hh[step]
    gh[...] = total
    s3 = all_z(d3, 288, d3_x, d3_z, r_3, x3)
    all_end(wu, 32, du_z, gu, su)
    s1 = quarter_w(slot, 144, d1_z, g1, r_1, z1)
    all_end(d3, 288, d3_z, g3, s3)
    for copy in s2 + s1:
        copy.wait_recv()
    for entry in stays:
        if not entry[1]:
            settle(entry)
    for copy in sends:
        copy.wait_send()


def back(*args):
    anywhere = pl.BlockSpec(memory_space=pl.ANY)
    inside = pl.BlockSpec(memory_space=pltpu.VMEM)
    shape = jax.ShapeDtypeStruct
    dma = pltpu.SemaphoreType.DMA

    def room(*dims):
        return pltpu.VMEM(dims, HALF)

    return pl.pallas_call(
        back_kernel,
        name="back",
        out_shape=(
            shape((288, 512), FLOAT),
            shape((32, 2048), FLOAT),
            shape((288, 1024), HALF),
            shape((144, 1024), HALF),
            shape((16, 128), FLOAT),
        ),
        in_specs=[anywhere] * 11 + [inside] * 4,
        out_specs=[inside, inside, anywhere, anywhere, inside],
        scratch_shapes=[
            room(3, 3, 34, 16, 512),
            room(2, 3, 32, 512),
            room(2, 3, 32, 512),
            pltpu.VMEM((32, 16, 128), FLOAT),
            room(1536, 1024),
            room(9216, 256),
            pltpu.VMEM((512, 512), FLOAT),
            room(384, 2048),
            room(1024, 2048),
            room(384, 1024),
            room(384, 1024),
            room(4, 384, 256),
            pltpu.VMEM((3, 16, 32, 256), FLOAT),
            room(3, 3, 18, 32, 256),
            room(3, 2, 32, 16, 256),
            room(3, 32, 16, 256),
            room(16, 32, 2048),
            room(8, 32, 2048),
            room(4, 32, 2048),
            room(3, 32, 2048),
            room(9216, 512),
            room(8, 288, 512),
            room(8, 288, 512),
            room(4, 288, 512),
            room(3, 288, 512),
            room(9216, 256),
            room(4, 1152, 256),
            room(3, 1152, 256),
            room(4, 576, 256),
            room(3, 576, 256),
            pltpu.VMEM((32, 16, 128), FLOAT),
            dma((144,)),
            dma((40,)),
            dma((2,)),
            dma((3,)),
            dma((6,)),
            dma((31,)),
            dma((31,)),
            dma((10,)),
            dma((10,)),
            dma((31,)),
            pltpu.SemaphoreType.REGULAR,
        ],
        compiler_params=pltpu.CompilerParams(
            collective_id=2, has_side_effects=True, vmem_limit_bytes=64 * 1024 * 1024
        ),
    )(*args)


def dice_slopes(totals):
    union_sum = totals[..., 1] + totals[..., 2] + SMOOTHING
    numerator = 2.0 * totals[..., 0] + SMOOTHING
    dice_score = numerator / union_sum
    loss_value = 1.0 - jnp.mean(dice_score)
    entry_count = float(dice_score.size)
    common = -2.0 / (entry_count * union_sum)
    return (loss_value, jnp.concatenate([common, numerator / (entry_count * union_sum**2)], axis=1))


def sliced_grads(
    bottom, skipped, groups, pixel_mask, labels, weight_one, weight_two, weight_up, weight_three,
    weight_head,
):
    ha = lax.axis_index("ha")
    code = (pixel_mask + 2 * labels).astype(FLOAT).reshape(8, 3, 64)
    pads = [jnp.pad(code, ((0, 0), (0, 5), (64 * odd, 64 - 64 * odd))) for odd in range(2)]
    code = jnp.where(ha % 2 == 0, *pads)
    head_rows = jnp.pad(weight_head.astype(HALF), ((0, 0), (0, 126)))
    x0, h1, h2, joined, w2, wu, w3, pre_one, pre_two, pre_three, hidden_three, logits, code, sums, head = front(
        bottom.reshape(8, 48, 512),
        skipped.reshape(8, 192, 512),
        code,
        weight_one.astype(HALF),
        weight_two.astype(HALF),
        weight_up.astype(HALF),
        weight_three.astype(HALF),
        head_rows,
    )
    wu = wu.reshape(1024, 2048)
    w3 = w3.reshape(9216, 512)
    w2 = w2.reshape(9216, 256)
    member = (groups[:, None] == jnp.arange(GROUPS)[None, :]).astype(FLOAT)
    step = lax.axis_index("ha") * 4 + lax.axis_index("wa")
    origin = (step - jnp.arange(32)) % 32
    at_group = jnp.einsum(
        "dh,hsg->dsg",
        (origin[:, None] // 4 == jnp.arange(8)[None, :]).astype(FLOAT),
        member.reshape(8, 3, GROUPS),
        precision=HIGHEST,
    )
    totals = jnp.einsum("dsg,dsq->gq", at_group, sums[:, :3, :6], precision=HIGHEST)
    totals = totals.reshape(GROUPS, 2, 3)
    loss_value, slopes = dice_slopes(totals)
    member = lax.dynamic_slice_in_dim(member, 3 * ha, 3, axis=0)
    slopes = jnp.einsum("sg,gq->sq", member, slopes, precision=HIGHEST)
    g3, gu, g2, g1, gh = back(
        w3,
        wu,
        w2,
        joined.reshape(1536, 1024),
        h2,
        h1.reshape(1536, 1024),
        x0.reshape(1536, 512),
        pre_one,
        pre_two,
        pre_three,
        hidden_three.reshape(1536, 512),
        logits,
        code,
        jnp.pad(slopes, ((0, 5), (0, 124))),
        head,
    )
    return (loss_value, g1.astype(FLOAT), g2.astype(FLOAT), gu, g3, gh[:, :2])


def body(
    bottom,
    skipped,
    groups,
    pixel_mask,
    labels,
    conv1_weight,
    conv1_momentum,
    conv1_average,
    conv2_weight,
    conv2_momentum,
    conv2_average,
    up_weight,
    up_momentum,
    up_average,
    conv3_weight,
    conv3_momentum,
    conv3_average,
    head_weight,
    head_momentum,
    head_average,
):
    split = bottom.shape[0] == 24 and bottom.shape[1:3] == (2, 8) and bottom.shape[3] == 512
    split = split and (lax.axis_size("ha"), lax.axis_size("wa")) == (8, 4)
    grads = sliced_grads if split else tiled_grads
    loss_value, conv1_grad, conv2_grad, up_grad, conv3_grad, head_grad = grads(
        bottom,
        skipped,
        groups,
        pixel_mask,
        labels,
        conv1_weight,
        conv2_weight,
        up_weight,
        conv3_weight,
        head_weight,
    )
    first = renew_state(conv1_weight, conv1_momentum, conv1_average, conv1_grad, RATE_CONV)
    second = renew_state(conv2_weight, conv2_momentum, conv2_average, conv2_grad, RATE_CONV)
    upward = renew_state(up_weight, up_momentum, up_average, up_grad, RATE_CONV)
    third = renew_state(conv3_weight, conv3_momentum, conv3_average, conv3_grad, RATE_CONV)
    header = renew_state(head_weight, head_momentum, head_average, head_grad, RATE_HEAD)
    return (
        loss_value,
        first[0],
        first[1],
        first[2],
        second[0],
        second[1],
        second[2],
        upward[0],
        upward[1],
        upward[2],
        third[0],
        third[1],
        third[2],
        header[0],
        header[1],
        header[2],
    )


def solution(mesh):
    in_specs = (
        P(None, "ha", "wa", None),
        P(None, "ha", "wa", None),
        P(),
        P(None, "ha", "wa"),
        P(None, "ha", "wa"),
        P(("ha", "wa"), None),
        P(("ha", "wa"), None),
        P(("ha", "wa"), None),
        P(("ha", "wa"), None),
        P(("ha", "wa"), None),
        P(("ha", "wa"), None),
        P(("ha", "wa"), None),
        P(("ha", "wa"), None),
        P(("ha", "wa"), None),
        P(("ha", "wa"), None),
        P(("ha", "wa"), None),
        P(("ha", "wa"), None),
        P(("ha", "wa"), None),
        P(("ha", "wa"), None),
        P(("ha", "wa"), None),
    )
    out_specs = (
        P(),
        P(("ha", "wa"), None),
        P(("ha", "wa"), None),
        P(("ha", "wa"), None),
        P(("ha", "wa"), None),
        P(("ha", "wa"), None),
        P(("ha", "wa"), None),
        P(("ha", "wa"), None),
        P(("ha", "wa"), None),
        P(("ha", "wa"), None),
        P(("ha", "wa"), None),
        P(("ha", "wa"), None),
        P(("ha", "wa"), None),
        P(("ha", "wa"), None),
        P(("ha", "wa"), None),
        P(("ha", "wa"), None),
    )
    return jax.shard_map(body, mesh=mesh, in_specs=in_specs, out_specs=out_specs, check_vma=False)
```

```python
import functools

import jax
import jax.numpy as jnp
from jax import lax
from jax.experimental import pallas as pl
from jax.experimental.pallas import tpu as pltpu
from jax.sharding import PartitionSpec as P

GROUPS = 5


MOMENTUM = 0.9
RATE_CONV = 600.0
RATE_HEAD = 25.0
AVERAGE_DECAY = 0.5
SMOOTHING = 1.0
HIGHEST = lax.Precision.HIGHEST


def with_halo(block, sides, width):
    for axis, dim in sides:
        count = lax.axis_size(axis)
        forward = [(i, i + 1) for i in range(count - 1)]
        backward = [(target, source) for source, target in forward]
        low = lax.ppermute(
            lax.slice_in_dim(block, block.shape[dim] - width, None, axis=dim), axis, forward
        )
        high = lax.ppermute(lax.slice_in_dim(block, 0, width, axis=dim), axis, backward)
        block = jnp.concatenate([low, block, high], axis=dim)
    return block


def smooth(source):
    return jax.nn.gelu(source, approximate=True)


def smooth_back(pre_value, gradient):
    _, pull_back = jax.vjp(smooth, pre_value)
    return pull_back(gradient)[0]


def widened_field(source):
    return with_halo(source, (("ha", 1), ("wa", 2)), 1)


def conv_taps(padded, weight):
    kernel = weight.reshape(3, 3, padded.shape[3], weight.shape[1])
    return lax.conv_general_dilated(
        padded,
        kernel,
        (1, 1),
        "VALID",
        dimension_numbers=("NHWC", "HWIO", "NHWC"),
        preferred_element_type=jnp.float32,
    )


def conv_back(padded, grad_out, weight, back_chan):
    in_chan = padded.shape[3]
    weight_grad = lax.conv_general_dilated(
        padded,
        grad_out,
        (1, 1),
        "VALID",
        dimension_numbers=("CHWN", "IHWO", "HWNC"),
        preferred_element_type=jnp.float32,
    ).reshape(9 * in_chan, grad_out.shape[3])
    if not back_chan:
        return (weight_grad, None)
    grad_padded = widened_field(grad_out)
    kernel = weight.reshape(3, 3, in_chan, weight.shape[1])[::-1, ::-1, :back_chan]
    source_grad = lax.conv_general_dilated(
        grad_padded,
        kernel,
        (1, 1),
        "VALID",
        dimension_numbers=("NHWC", "HWOI", "NHWC"),
        preferred_element_type=jnp.float32,
    )
    return (weight_grad, source_grad)


def upsample(source, weight):
    slices, row_count, col_count, _ = source.shape
    flattened = jnp.einsum("shwc,cq->shwq", source, weight, preferred_element_type=jnp.float32)
    blocks = flattened.reshape(slices, row_count, col_count, 2, 2, -1).transpose(0, 1, 3, 2, 4, 5)
    return blocks.reshape(slices, 2 * row_count, 2 * col_count, -1)


def upsample_back(source, grad_up, weight):
    slices, row_count, col_count, _ = source.shape
    blocks = grad_up.reshape(slices, row_count, 2, col_count, 2, -1).transpose(0, 1, 3, 2, 4, 5)
    flattened = blocks.reshape(slices, row_count, col_count, -1)
    weight_grad = jnp.einsum("shwc,shwq->cq", source, flattened, preferred_element_type=jnp.float32)
    source_grad = jnp.einsum("shwq,cq->shwc", flattened, weight, preferred_element_type=jnp.float32)
    return (weight_grad, source_grad)


def forward(gathered, bottom, skipped):
    weight_one, weight_two, weight_up, weight_three, weight_head = gathered
    pad_zero = widened_field(bottom)
    pre_one = conv_taps(pad_zero, weight_one)
    hidden_one = smooth(pre_one).astype(jnp.bfloat16)
    pad_one = widened_field(hidden_one)
    pre_two = conv_taps(pad_one, weight_two)
    hidden_two = smooth(pre_two).astype(jnp.bfloat16)
    upsampled = upsample(hidden_two, weight_up).astype(jnp.bfloat16)
    joined = jnp.concatenate([upsampled, skipped], axis=3)
    pad_two = widened_field(joined)
    pre_three = conv_taps(pad_two, weight_three)
    hidden_three = smooth(pre_three).astype(jnp.bfloat16)
    logits = jnp.einsum(
        "shwc,ck->shwk", hidden_three, weight_head, preferred_element_type=jnp.float32
    )
    return (
        pad_zero,
        pre_one,
        pad_one,
        pre_two,
        hidden_two,
        pad_two,
        pre_three,
        hidden_three,
        logits,
    )


def pixel_terms(logits, pixel_mask, labels):
    probability = jax.nn.softmax(logits, axis=-1)
    classes = jnp.arange(logits.shape[-1])
    target = (labels[..., None] == classes[None, None, None, :]).astype(jnp.float32)
    weighted = pixel_mask[..., None].astype(jnp.float32)
    return (probability, target, weighted)


def dice_terms(logits, pixel_mask, labels, member):
    probability, target, weighted = pixel_terms(logits, pixel_mask, labels)
    per_slice = jnp.stack(
        [
            jnp.sum(weighted * probability * target, axis=(1, 2)),
            jnp.sum(weighted * probability, axis=(1, 2)),
            jnp.sum(weighted * target, axis=(1, 2)),
        ],
        axis=-1,
    )
    return jnp.einsum("skj,sg->gkj", per_slice, member, precision=HIGHEST)


def dice_back(logits, pixel_mask, labels, member, totals):
    probability, target, weighted = pixel_terms(logits, pixel_mask, labels)
    union_sum = totals[..., 1] + totals[..., 2] + SMOOTHING
    numerator = 2.0 * totals[..., 0] + SMOOTHING
    dice_score = numerator / union_sum
    loss_value = 1.0 - jnp.mean(dice_score)
    entry_count = float(dice_score.size)
    coef_common = -2.0 / (entry_count * union_sum)
    coef_prob = numerator / (entry_count * union_sum * union_sum)
    slice_common = jnp.einsum("sg,gk->sk", member, coef_common, precision=HIGHEST)
    slice_prob = jnp.einsum("sg,gk->sk", member, coef_prob, precision=HIGHEST)
    grad_prob = weighted * (target * slice_common[:, None, None, :] + slice_prob[:, None, None, :])
    inner = jnp.sum(probability * grad_prob, axis=-1, keepdims=True)
    grad_logits = (probability * (grad_prob - inner)).astype(jnp.bfloat16)
    return (loss_value, grad_logits)


def renew_state(weight, moment, average, gradient, rate):
    moment_new = MOMENTUM * moment + gradient
    weight_new = weight - rate * (gradient + MOMENTUM * moment_new)
    average_new = AVERAGE_DECAY * average + (1.0 - AVERAGE_DECAY) * weight_new
    return (weight_new, moment_new, average_new)


def tiled_grads(
    bottom, skipped, groups, pixel_mask, labels, conv1_weight, conv2_weight, up_weight, conv3_weight,
    head_weight,
):
    gathered = (
        lax.all_gather(conv1_weight.astype(jnp.bfloat16), ("ha", "wa"), axis=0, tiled=True),
        lax.all_gather(conv2_weight.astype(jnp.bfloat16), ("ha", "wa"), axis=0, tiled=True),
        lax.all_gather(up_weight.astype(jnp.bfloat16), ("ha", "wa"), axis=0, tiled=True),
        lax.all_gather(conv3_weight.astype(jnp.bfloat16), ("ha", "wa"), axis=0, tiled=True),
        lax.all_gather(head_weight.astype(jnp.bfloat16), ("ha", "wa"), axis=0, tiled=True),
    )
    member = (groups[:, None] == jnp.arange(GROUPS)[None, :]).astype(jnp.float32)
    kept = forward(gathered, bottom, skipped)
    partial_sums = dice_terms(kept[8], pixel_mask, labels, member)
    totals = lax.psum(partial_sums, ("ha", "wa"))
    pad_zero, pre_one, pad_one, pre_two, hidden_two, pad_two, pre_three, hidden_three, logits = kept
    weight_one, weight_two, weight_up, weight_three, weight_head = gathered
    loss_value, grad_logits = dice_back(logits, pixel_mask, labels, member, totals)
    head_grad = jnp.einsum(
        "shwc,shwk->ck", hidden_three, grad_logits, preferred_element_type=jnp.float32
    )
    grad_hidden = jnp.einsum(
        "shwk,ck->shwc", grad_logits, weight_head, preferred_element_type=jnp.float32
    )
    grad_pre_three = smooth_back(pre_three, grad_hidden).astype(jnp.bfloat16)
    conv3_grad, grad_joined = conv_back(pad_two, grad_pre_three, weight_three, weight_up.shape[1] // 4)
    grad_upsampled = grad_joined.astype(jnp.bfloat16)
    up_grad, grad_hidden_two = upsample_back(hidden_two, grad_upsampled, weight_up)
    grad_pre_two = smooth_back(pre_two, grad_hidden_two).astype(jnp.bfloat16)
    conv2_grad, grad_hidden_one = conv_back(pad_one, grad_pre_two, weight_two, pad_one.shape[3])
    grad_pre_one = smooth_back(pre_one, grad_hidden_one).astype(jnp.bfloat16)
    conv1_grad, _ = conv_back(pad_zero, grad_pre_one, weight_one, 0)
    sums = (
        lax.psum_scatter(conv1_grad.astype(jnp.bfloat16), ("ha", "wa"), scatter_dimension=0, tiled=True),
        lax.psum_scatter(conv2_grad.astype(jnp.bfloat16), ("ha", "wa"), scatter_dimension=0, tiled=True),
        lax.psum_scatter(up_grad.astype(jnp.bfloat16), ("ha", "wa"), scatter_dimension=0, tiled=True),
        lax.psum_scatter(conv3_grad.astype(jnp.bfloat16), ("ha", "wa"), scatter_dimension=0, tiled=True),
        lax.psum_scatter(head_grad.astype(jnp.bfloat16), ("ha", "wa"), scatter_dimension=0, tiled=True),
    )
    return (loss_value, *[s.astype(jnp.float32) for s in sums])


MESH = pl.DeviceIdType.MESH
FLOAT = jnp.float32
HALF = jnp.bfloat16


def place():
    row, col = (lax.axis_index("ha"), lax.axis_index("wa"))
    return (row // 2, row % 2, col // 2, col % 2)


def spot(z, x, y, c):
    return (2 * z + x, 2 * y + c)


def greet_all():
    row, col = (lax.axis_index("ha"), lax.axis_index("wa"))
    rows, cols = (lax.axis_size("ha"), lax.axis_size("wa"))
    barrier = pltpu.get_barrier_semaphore()
    for step in range(1, rows * cols):
        other = lax.rem(row * cols + col + step, rows * cols)
        pl.semaphore_signal(
            barrier, inc=1, device_id=(other // cols, lax.rem(other, cols)), device_id_type=MESH
        )
    pl.semaphore_wait(barrier, rows * cols - 1)


def remote(source, target, send_sem, recv_sem, device):
    return pltpu.make_async_remote_copy(
        src_ref=source,
        dst_ref=target,
        send_sem=send_sem,
        recv_sem=recv_sem,
        device_id=device,
        device_id_type=MESH,
    )


def gelu_of(value):
    inner = 0.7978845608028654 * (value + 0.044715 * value * value * value)
    return 0.5 * value * (1.0 + jnp.tanh(inner))


def conv_slice(source, weight, parts, index, chan):
    parts[...] = jnp.zeros_like(parts)

    def row_tap(r, carry):
        window = source[index, pl.ds(r, 16)].reshape(512, chan)
        for c in range(3):
            start = pl.multiple_of((3 * r + c) * chan, chan)
            parts[c] += jnp.dot(
                window, weight[pl.ds(start, chan), :], preferred_element_type=FLOAT
            )
        return carry

    lax.fori_loop(0, 3, row_tap, 0)
    shape = (16, 32, 256)
    column = lax.broadcasted_iota(jnp.int32, shape, 1)
    low = jnp.where(column > 0, pltpu.roll(parts[0].reshape(shape), 1, 1), 0.0)
    high = jnp.where(column < 31, pltpu.roll(parts[2].reshape(shape), 31, 1), 0.0)
    return parts[1].reshape(shape) + low + high


def put_shifts(target, lanes, s, value, left, right):
    column = lax.broadcasted_iota(jnp.int32, value.shape, 1)
    last = value.shape[1] - 1
    rows = pl.ds(1, value.shape[0])
    low = jnp.where(column > 0, pltpu.roll(value, 1, 1), left)
    target[0, s, rows, :, lanes] = low.astype(HALF)
    target[1, s, rows, :, lanes] = value.astype(HALF)
    high = jnp.where(column < last, pltpu.roll(value, last, 1), right)
    target[2, s, rows, :, lanes] = high.astype(HALF)


def put_tile(target, first, s, value, left, right):
    column = lax.broadcasted_iota(jnp.int32, value.shape, 1)
    last = value.shape[1] - 1
    rows = pl.ds(1, value.shape[0])
    low = jnp.where(column > 0, pltpu.roll(value, 1, 1), left)
    high = jnp.where(column < last, pltpu.roll(value, last, 1), right)
    for shift, part in enumerate((low, value, high)):
        target[s, rows, :, pl.ds(1024 * shift + first, 512)] = part.astype(HALF)


def front_kernel(
    compute,
    bot, skip, code, w1, w2, wu, w3, wh,
    x0_out, h1_out, h2_out, joined_out, w2_out, wu_out, w3_out, pre1_out, pre2_out, pre3_out,
    hidden_out, logit_out, code_out, sums_out, head_out,
    xr, x0, w1q, w2q, h1s, h1, parts, h2s, h2v, wuv, w3v, skv, rims, rims_got, tiles, whv,
    send, here, r_bot, r_grp, r_w1, r_w2, r_h1, r_h2, r_skip, r_wh, r_w3, r_wu,
    r_code, r_rim, r_sum,
):
    z, x, y, c = place()
    ha, wa = (2 * z + x, 2 * y + c)
    x_peer, y_peer, c_peer = (spot(z, 1 - x, y, c), spot(z, x, 1 - y, c), spot(z, x, y, 1 - c))
    mine = ha * 4 + wa
    greet_all()
    sends = []
    stays = []

    def go(source, target, recv_sem, device):
        copy = remote(source, target, send.at[len(sends)], recv_sem, device)
        copy.start()
        sends.append((copy, None))
        return copy

    def stay(source, target):
        copy = pltpu.make_async_copy(source, target, here.at[len(stays)])
        copy.start()
        stays.append([copy, False])
        return stays[-1]

    def settle(*entries):
        for entry in entries:
            entry[0].wait()
            entry[1] = True

    def arrive(*copies):
        for copy in copies:
            copy.wait_recv()

    def go_if(when, source, target, recv_sem, device):
        copy = remote(source, target, send.at[len(sends)], recv_sem, device)
        pl.when(when)(lambda: copy.start())
        sends.append((copy, when))
        return (copy, when)

    def arrive_if(copy, when):
        pl.when(when)(lambda: copy.wait_recv())

    above, below = (spot(lax.rem(z + 1, 4), x, y, c), spot(lax.rem(z + 3, 4), x, y, c))

    def line_start(part, line):
        go_if(z < 3, part(z), part(z), line.at[0], above)
        go_if(z > 0, part(z), part(z), line.at[3], below)

    def line_hop(part, line, j, passes):
        for first, other, more, last, neighbour in (
            (0, lax.rem(z + 3 - j, 4), z >= j + 1, z < 3, above),
            (3, lax.rem(z + 1 + j, 4), z <= 2 - j, z > 0, below),
        ):
            piece = part(other)
            arrive_if(remote(piece, piece, send.at[0], line.at[first + j], x_peer), more)
            if j < 2:
                go_if(
                    jnp.logical_and(more, last), piece, piece, line.at[first + j + 1], neighbour
                )
            for recv, got, device in passes:
                got.append(go_if(more, piece, piece, recv.at[1 + first + j], device))

    def swap(shard, whole, first, count, recv):
        source_rows = pl.ds(first, count)
        target = whole.at[ha, wa, source_rows]
        lanes = [pl.ds(pl.multiple_of(lax.rem(wa + dw, 4) * 256, 256), 256) for dw in range(4)]
        own = stay(shard.at[source_rows, lanes[0]], target)
        copies = [
            go(shard.at[source_rows, lanes[dw]], target, recv.at[dw], (ha, lax.rem(wa + dw, 4)))
            for dw in range(1, 4)
        ]
        return (own, copies)

    class Quarter:
        def __init__(self, shard, whole, first, count, line, recv):
            self.line, self.recv, self.got = (line, recv, [])
            self.part = lambda bz: whole.at[bz * 2 + x, :, pl.ds(first, count)]
            self.swapped = swap(shard, whole, first, count, recv.at[1])

        def start(self):
            settle(self.swapped[0])
            arrive(*self.swapped[1])
            line_start(self.part, self.line)
            own = self.part(z)
            self.got.append((go(own, own, self.recv.at[0, 0], x_peer), None))

        def hop(self, j):
            line_hop(self.part, self.line, j, [(self.recv.at[0], self.got, x_peer)])

        def done(self):
            for copy, when in self.got:
                if when is None:
                    copy.wait_recv()
                else:
                    arrive_if(copy, when)

    class Whole:
        def __init__(self, shard, whole, line, recv):
            self.whole, self.line, self.recv = (whole, line, recv)
            self.part = lambda bz: whole.at[bz, x, y, c]
            self.own = stay(shard, self.part(z))
            self.along_x, self.along_y, self.core = ([], [], [])

        def start(self):
            settle(self.own)
            line_start(self.part, self.line)
            own = self.part(z)
            self.along_x.append((go(own, own, self.recv.at[0, 0], x_peer), None))
            self.along_y.append((go(own, own, self.recv.at[1, 0], y_peer), None))
            self.core.append((go(own, own, self.recv.at[2, 0], c_peer), None))

        def hop(self, j):
            passes = [
                (self.recv.at[0], self.along_x, x_peer),
                (self.recv.at[1], self.along_y, y_peer),
                (self.recv.at[2], self.core, c_peer),
            ]
            line_hop(self.part, self.line, j, passes)

        def wait(self, got):
            for copy, when in got:
                if when is None:
                    copy.wait_recv()
                else:
                    arrive_if(copy, when)

        def turn(self):
            self.wait(self.along_x)
            part = self.whole.at[:, 1 - x, y, c]
            self.last = go(part, part, self.recv.at[1, 7], y_peer)
            self.core.append((go(part, part, self.recv.at[2, 7], c_peer), None))

        def finish(self):
            self.wait(self.along_y)
            part = self.whole.at[:, x, 1 - y, c]
            self.core.append((go(part, part, self.recv.at[0, 7], c_peer), None))
            arrive(self.last)
            part = self.whole.at[:, 1 - x, 1 - y, c]
            self.core.append((go(part, part, self.recv.at[3, 0], c_peer), None))

        def done(self):
            self.wait(self.core)

    own_bot = stay(bot.at[ha], xr.at[ha, wa])
    bots = [
        go(bot.at[lax.rem(ha + d, 8)], xr.at[ha, wa], r_bot.at[d - 1], (lax.rem(ha + d, 8), wa))
        for d in range(1, 8)
    ]
    whole_three = Whole(w3, w3v, r_w3.at[4, pl.ds(0, 6)], r_w3)
    whole_up = Whole(wu, wuv, r_wu.at[4, pl.ds(0, 6)], r_wu)
    one_part = Quarter(w1, w1q, 0, 144, r_w1.at[2], r_w1)
    two_low = Quarter(w2, w2q, 0, 144, r_w2.at[0, 2], r_w2.at[0])
    two_high = Quarter(w2, w2q, 144, 144, r_w2.at[1, 2], r_w2.at[1])
    whole_three.start()
    whole_up.start()
    settle(own_bot)
    arrive(*bots)
    to_c = go(xr.at[:, wa], xr.at[:, wa], r_grp.at[0], c_peer)
    to_y = go(xr.at[:, wa], xr.at[:, wa], r_grp.at[1], y_peer)
    whole_three.hop(0)
    whole_up.hop(0)
    one_part.start()
    whole_three.hop(1)
    whole_up.hop(1)
    own_code = stay(code.at[ha], code_out.at[ha])
    codes = [
        go(code.at[lax.rem(ha + d, 8)], code_out.at[ha], r_code.at[d - 1], (lax.rem(ha + d, 8), wa))
        for d in range(1, 8)
    ]
    own_head = stay(wh, whv.at[mine])
    heads = []
    for step in range(1, 32):
        other = lax.rem(mine + step, 32)
        heads.append(go(wh, whv.at[mine], r_wh.at[step - 1], (other // 4, lax.rem(other, 4))))
    if compute:
        x0[:, 0] = jnp.zeros((3, 32, 512), HALF)
        x0[:, 17] = jnp.zeros((3, 32, 512), HALF)
        h1[:, 0] = jnp.zeros((3, 32, 1024), HALF)
        h1[:, 17] = jnp.zeros((3, 32, 1024), HALF)
        tiles[:, 0] = jnp.zeros((3, 16, 3072), HALF)
        tiles[:, 33] = jnp.zeros((3, 16, 3072), HALF)
    whole_three.hop(2)
    two_low.start()
    whole_up.hop(2)
    one_part.hop(0)
    two_high.start()
    arrive(to_y)
    part = xr.at[:, 2 * (1 - y) + c]
    on_c = go(part, part, r_grp.at[2], c_peer)
    arrive(to_c, on_c)

    if compute:

        def reorder(h, carry):
            block = xr[h].astype(FLOAT).reshape(4, 3, 2, 8, 512)
            for s in range(3):
                for r in range(2):
                    row = jnp.concatenate([block[w, s, r] for w in range(4)], axis=0)
                    x0[s, 2 * h + 1 + r] = row.astype(HALF)
            return carry

        lax.fori_loop(0, 8, reorder, 0)
    stay(x0.at[:, pl.ds(1, 16)], x0_out)
    one_part.hop(1)
    two_low.hop(0)
    one_part.hop(2)
    two_high.hop(0)
    whole_three.turn()
    two_low.hop(1)
    two_high.hop(1)
    whole_up.turn()
    own_skip = stay(skip.at[ha], skv.at[ha])
    skips = [
        go(skip.at[lax.rem(ha + d, 8)], skv.at[ha], r_skip.at[d - 1], (lax.rem(ha + d, 8), wa))
        for d in range(1, 8)
    ]
    two_low.hop(2)
    one_part.done()
    if compute:

        def one(s, carry):
            value = conv_slice(x0, w1q.reshape(4608, 256), parts, s, 512)
            pre1_out[s] = value
            h1s[s] = gelu_of(value).astype(HALF)
            return carry

        lax.fori_loop(0, 3, one, 0)

    def lanes(col):
        return h1.at[:, pl.ds(1, 16), :, pl.ds(pl.multiple_of(col * 256, 256), 256)]

    own_h1 = stay(h1s, lanes(wa))
    h1_c = go(h1s, lanes(wa), r_h1.at[0], c_peer)
    h1_y = go(h1s, lanes(wa), r_h1.at[1], y_peer)

    two_high.hop(2)
    whole_three.finish()
    whole_up.finish()
    arrive(h1_y)
    h1_on = go(lanes(2 * (1 - y) + c), lanes(2 * (1 - y) + c), r_h1.at[2], c_peer)
    settle(own_h1)
    arrive(h1_c, h1_on)
    stay(h1.at[:, pl.ds(1, 16)], h1_out)
    two_low.done()
    two_high.done()
    stay(w2q, w2_out)
    if compute:

        def two(s, carry):
            value = conv_slice(h1, w2q.reshape(9216, 256), parts, s, 1024)
            pre2_out[s] = value
            hidden = gelu_of(value)
            for w in range(4):
                tile = hidden[:, 8 * w : 8 * w + 8].reshape(128, 256)
                h2s[w, pl.ds(pl.multiple_of(s * 128, 128), 128)] = tile.astype(HALF)
                left = hidden[:, 8 * w - 1] if w > 0 else jnp.zeros((16, 256), FLOAT)
                h2s[w, pl.ds(pl.multiple_of(384 + s * 16, 16), 16)] = left.astype(HALF)
                right = hidden[:, 8 * w + 8] if w < 3 else jnp.zeros((16, 256), FLOAT)
                h2s[w, pl.ds(pl.multiple_of(432 + s * 16, 16), 16)] = right.astype(HALF)
            return carry

        lax.fori_loop(0, 3, two, 0)
    h2_lanes = h2v.at[:, pl.ds(pl.multiple_of(wa * 256, 256), 256)]
    own_h2 = stay(h2s.at[wa], h2_lanes)
    h2_got = [
        go(h2s.at[lax.rem(wa + d, 4)], h2_lanes, r_h2.at[d - 1], (ha, lax.rem(wa + d, 4)))
        for d in range(1, 4)
    ]

    settle(own_skip)
    arrive(*skips)

    def skip_slice(s):
        return skv[:, 64 * s : 64 * s + 64].astype(FLOAT).reshape(32, 16, 512)

    if compute:
        for s in range(3):
            value = skip_slice(s)
            rims[0, s] = value[:, 0].astype(HALF)
            rims[1, s] = value[:, 15].astype(HALF)
    before = (ha, lax.rem(wa + 3, 4))
    after = (ha, lax.rem(wa + 1, 4))
    rim_right = go(rims.at[0], rims_got.at[1], r_rim.at[1], before)
    rim_left = go(rims.at[1], rims_got.at[0], r_rim.at[0], after)
    arrive(rim_right, rim_left)
    if compute:
        for s in range(3):
            left = jnp.where(wa > 0, rims_got[0, s].astype(FLOAT), 0.0)
            right = jnp.where(wa < 3, rims_got[1, s].astype(FLOAT), 0.0)
            put_tile(tiles, 512, s, skip_slice(s), left[:, None, :], right[:, None, :])
    whole_three.done()
    stay(w3v, w3_out)
    settle(own_h2)
    arrive(*h2_got)
    stay(h2v, h2_out)
    whole_up.done()
    stay(wuv, wu_out)
    if compute:
        order = lax.broadcasted_iota(jnp.int32, (256, 256), 1)
        inner = order % 128
        pick = (inner // 8) * 16 + (inner % 8) * 2 + order // 128
        woven = jnp.where(lax.broadcasted_iota(jnp.int32, (256, 256), 0) == pick, 1.0, 0.0)
        woven = woven.astype(HALF)
        wide = wuv.reshape(1024, 2048)
        for s in range(3):
            fine, sides = ([], ([], []))
            for a in range(2):
                weight = wide[:, 1024 * a : 1024 * a + 1024]
                flat = jnp.dot(
                    h2v[128 * s : 128 * s + 128], weight, preferred_element_type=FLOAT
                ).astype(HALF)
                flat = jnp.concatenate([flat[:, :512], flat[:, 512:]], axis=0)
                flat = jnp.dot(woven, flat, preferred_element_type=FLOAT)
                fine.append(flat.reshape(16, 16, 512))
                for side in range(2):
                    start = 384 + 48 * side + 16 * s
                    rim = jnp.dot(
                        h2v[start : start + 16],
                        weight[:, 512 * (1 - side) : 512 * (1 - side) + 512],
                        preferred_element_type=FLOAT,
                    )
                    sides[side].append(rim.astype(HALF).astype(FLOAT)[:, None, :])
            value = jnp.stack(fine, axis=1).reshape(32, 16, 512)
            left, right = [jnp.stack(side, axis=1).reshape(32, 1, 512) for side in sides]
            put_tile(tiles, 0, s, value, left, right)

    stay(tiles.at[:, pl.ds(1, 32), :, pl.ds(1024, 1024)], joined_out)
    settle(own_head)
    arrive(*heads)
    settle(own_code)
    arrive(*codes)
    if compute:
        head = whv.reshape(512, 128)[...].astype(FLOAT).T[:16].astype(HALF)
        head_out[...] = head
        row = lax.broadcasted_iota(jnp.int32, (8, 128), 0)
        lane = lax.broadcasted_iota(jnp.int32, (8, 128), 1)
        sums_out[0] = jnp.zeros((8, 128), FLOAT)

        rows = w3v.reshape(9216, 512)

        def three(s, carry):
            for r in range(3):
                window = tiles[s, r : r + 32].reshape(512, 3072)
                value = jnp.dot(
                    window, rows[3072 * r : 3072 * r + 3072, :], preferred_element_type=FLOAT
                )
                if r == 0:
                    pre3_out[s] = value
                else:
                    pre3_out[s] += value
            hidden = gelu_of(pre3_out[s]).astype(HALF)
            hidden_out[s] = hidden
            logits = lax.dot_general(
                head, hidden, (((1,), (1,)), ((), ())), preferred_element_type=FLOAT
            )
            logit_out[s] = logits
            return carry

        lax.fori_loop(0, 3, three, 0)
        total = jnp.zeros((8, 128), FLOAT)
        for s in range(3):
            probability, target, weighted = class_terms(logit_out, code_out, s)
            for k in range(2):
                terms = (
                    weighted * probability[k] * target[k],
                    weighted * probability[k],
                    weighted * target[k],
                )
                for j, term in enumerate(terms):
                    value = jnp.sum(term, axis=1, keepdims=True)
                    here_is = jnp.logical_and(row == s, lane == 3 * k + j)
                    total = total + jnp.where(here_is, value, 0.0)
        sums_out[0] = total
    sums = []
    for step in range(1, 32):
        other = lax.rem(mine + step, 32)
        sums.append(
            go(
                sums_out.at[0],
                sums_out.at[step],
                r_sum.at[step - 1],
                (other // 4, lax.rem(other, 4)),
            )
        )
    arrive(*sums)
    for entry in stays:
        if not entry[1]:
            settle(entry)
    for copy, when in sends:
        if when is None:
            copy.wait_send()
        else:
            pl.when(when)(copy.wait_send)


def class_terms(logits, codes, s):
    pieces = [codes[2 * q, s : s + 1] + codes[2 * q + 1, s : s + 1] for q in range(4)]
    both = jnp.concatenate(pieces, axis=1)
    label = jnp.where(both >= 2.0, 1.0, 0.0)
    weighted = both - 2.0 * label
    first, second = (logits[s, 0:1], logits[s, 1:2])
    top = jnp.maximum(first, second)
    first, second = (jnp.exp(first - top), jnp.exp(second - top))
    scale = 1.0 / (first + second)
    return ((first * scale, second * scale), (1.0 - label, label), weighted)


def front(bot, skip, code, w1, w2, wu, w3, wh, compute=True):
    anywhere = pl.BlockSpec(memory_space=pl.ANY)
    inside = pl.BlockSpec(memory_space=pltpu.VMEM)
    shape = jax.ShapeDtypeStruct
    dma = pltpu.SemaphoreType.DMA

    def room(*dims):
        return pltpu.VMEM(dims, HALF)

    return pl.pallas_call(
        functools.partial(front_kernel, compute),
        name="front",
        out_shape=(
            shape((3, 16, 32, 512), HALF),
            shape((3, 16, 32, 1024), HALF),
            shape((480, 1024), HALF),
            shape((3, 32, 16, 1024), HALF),
            shape((8, 4, 288, 256), HALF),
            shape((4, 2, 2, 2, 32, 2048), HALF),
            shape((4, 2, 2, 2, 288, 512), HALF),
            shape((3, 16, 32, 256), FLOAT),
            shape((3, 16, 32, 256), FLOAT),
            shape((3, 512, 512), FLOAT),
            shape((3, 512, 512), HALF),
            shape((3, 16, 512), FLOAT),
            shape((8, 8, 128), FLOAT),
            shape((32, 8, 128), FLOAT),
            shape((16, 512), HALF),
        ),
        in_specs=[anywhere] * 8,
        out_specs=[anywhere] * 7 + [inside] * 8,
        scratch_shapes=[
            room(8, 4, 48, 512),
            room(3, 18, 32, 512),
            room(8, 4, 144, 256),
            room(8, 4, 288, 256),
            room(3, 16, 32, 256),
            room(3, 18, 32, 1024),
            pltpu.VMEM((3, 512, 256), FLOAT),
            room(4, 480, 256),
            room(480, 1024),
            room(4, 2, 2, 2, 32, 2048),
            room(4, 2, 2, 2, 288, 512),
            room(8, 192, 512),
            room(2, 3, 32, 512),
            room(2, 3, 32, 512),
            room(3, 34, 16, 3072),
            room(32, 16, 128),
            dma((256,)),
            dma((24,)),
            dma((7,)),
            dma((3,)),
            dma((3, 8)),
            dma((2, 3, 8)),
            dma((3,)),
            dma((3,)),
            dma((7,)),
            dma((31,)),
            dma((5, 8)),
            dma((5, 8)),
            dma((7,)),
            dma((2,)),
            dma((31,)),
        ],
        compiler_params=pltpu.CompilerParams(
            collective_id=0, has_side_effects=True, vmem_limit_bytes=64 * 1024 * 1024
        ),
    )(bot, skip, code, w1, w2, wu, w3, wh)


def gelu_slope(value):
    square = value * value
    bend = jnp.tanh(0.7978845608028654 * value * (1.0 + 0.044715 * square))
    rise = 0.7978845608028654 * (1.0 + 3.0 * 0.044715 * square)
    return 0.5 * (1.0 + bend) + 0.5 * value * (1.0 - bend * bend) * rise


def across(source, window):
    return lax.dot_general(source, window, (((0,), (0,)), ((), ())), preferred_element_type=FLOAT)


def against(window, weight):
    return lax.dot_general(window, weight, (((1,), (1,)), ((), ())), preferred_element_type=FLOAT)


def add_rows(total, start, term, rows):
    where = pl.ds(pl.multiple_of(start, 16), rows)
    total[where] = (total[where].astype(FLOAT) + term.astype(FLOAT)).astype(HALF)


def back_kernel(
    w3_in, wu_in, w2_in, joined_in, h2_in, h1_in, x0_in, pre1_in, pre2_in, pre3_in, hidden_in,
    logits, codes, slopes, head,
    g3, gu, g2, g1, gh,
    gs3, rims, rims_got, dh, joined, slot, acc, flat, wu, h2, gh2, from_wa, pre, gs2, d_core, d_y,
    du_c, du_y, du_x, du_z, d3, d3_c, d3_y, d3_x, d3_z, d2, d2_x, d2_z, d1_x, d1_z, hh,
    send, here, r_rim, r_wa, r_d, r_u, r_3, r_2, r_1, r_h, free,
):
    z, x, y, c = place()
    ha, wa = (2 * z + x, 2 * y + c)
    x_peer, y_peer, c_peer = (spot(z, 1 - x, y, c), spot(z, x, 1 - y, c), spot(z, x, y, 1 - c))
    mine = ha * 4 + wa
    sends = []
    stays = []

    def go(source, target, recv_sem, device):
        copy = remote(source, target, send.at[len(sends)], recv_sem, device)
        copy.start()
        sends.append(copy)
        return copy

    def stay(source, target):
        copy = pltpu.make_async_copy(source, target, here.at[len(stays)])
        copy.start()
        stays.append([copy, False])
        return stays[-1]

    def settle(*entries):
        for entry in entries:
            entry[0].wait()
            entry[1] = True

    got_hidden = stay(hidden_in, d3.at[pl.ds(0, 1536)])
    got_pre3 = stay(pre3_in.at[0], acc)
    got_w3 = [
        stay(w3_in.at[pl.ds(1024 * t, 512)], d3.at[pl.ds(4608 + 512 * t, 512)]) for t in range(9)
    ]
    got_w2 = stay(w2_in, slot)
    got_wu = stay(wu_in, wu)
    got_h2 = stay(h2_in.at[pl.ds(0, 384)], h2)
    got_h1 = stay(h1_in, joined)
    greet_all()

    settle(got_hidden)
    head_sum = jnp.zeros((16, 512), FLOAT)
    class_row = lax.broadcasted_iota(jnp.int32, (16, 512), 0)
    for e in range(3):
        gs3[e, :, 0] = jnp.zeros((3, 16, 512), HALF)
        gs3[e, :, 33] = jnp.zeros((3, 16, 512), HALF)
    for s in range(3):
        probability, target, weighted = class_terms(logits, codes, s)
        grads = [
            weighted * (target[k] * slopes[s : s + 1, k : k + 1] + slopes[s : s + 1, 2 + k : 3 + k])
            for k in range(2)
        ]
        inner = probability[0] * grads[0] + probability[1] * grads[1]
        grads = [probability[k] * (grads[k] - inner) for k in range(2)]
        grads = jnp.where(class_row == 0, grads[0], jnp.where(class_row == 1, grads[1], 0.0))
        grads = grads.astype(HALF)
        hidden = d3[512 * s : 512 * s + 512]
        head_sum = head_sum + jnp.dot(grads, hidden, preferred_element_type=FLOAT)
        settle(got_pre3)
        value = (across(grads, head[...]) * gelu_slope(acc[...])).astype(HALF)
        if s < 2:
            got_pre3 = stay(pre3_in.at[s + 1], acc)
        gs3[1, s, 1:33] = value.reshape(32, 16, 512)
        value = value.astype(FLOAT).reshape(32, 16, 512)
        rims[0, s] = value[:, 0].astype(HALF)
        rims[1, s] = value[:, 15].astype(HALF)
    before = (ha, lax.rem(wa + 3, 4))
    after = (ha, lax.rem(wa + 1, 4))
    rim_right = go(rims.at[0], rims_got.at[1], r_rim.at[1], before)
    rim_left = go(rims.at[1], rims_got.at[0], r_rim.at[0], after)
    rows = jnp.concatenate([head_sum, jnp.zeros((112, 512), FLOAT)], axis=0)
    dh[...] = rows.T.reshape(32, 16, 128)
    own_head = stay(dh.at[mine], hh.at[0])
    heads = []
    for step in range(1, 32):
        other = lax.rem(mine + step, 32)
        heads.append(
            go(dh.at[other], hh.at[step], r_h.at[step - 1], (other // 4, lax.rem(other, 4)))
        )
    rim_right.wait_recv()
    rim_left.wait_recv()
    for s in range(3):
        left = jnp.where(wa > 0, rims_got[0, s].astype(FLOAT), 0.0)
        right = jnp.where(wa < 3, rims_got[1, s].astype(FLOAT), 0.0)
        value = gs3[1, s, 1:33].astype(FLOAT)
        put_shifts(gs3, pl.ds(0, 512), s, value, left[:, None, :], right[:, None, :])

    order = lax.broadcasted_iota(jnp.int32, (256, 256), 0)
    inner = order % 128
    pick = (inner // 8) * 16 + (inner % 8) * 2 + order // 128
    apart = jnp.where(lax.broadcasted_iota(jnp.int32, (256, 256), 1) == pick, 1.0, 0.0).astype(HALF)
    settle(*got_w3)

    def three_source(s, carry):
        acc[...] = jnp.zeros_like(acc)

        def tap(t, inner_carry):
            window = gs3[2 - t % 3, s, pl.ds(2 - t // 3, 32)].reshape(512, 512)
            acc[...] += against(window, d3[pl.ds(pl.multiple_of(4608 + 512 * t, 512), 512)])
            return inner_carry

        lax.fori_loop(0, 9, tap, 0)
        fine = acc[...].astype(HALF).reshape(16, 2, 16, 512)
        for a in range(2):
            parted = jnp.dot(
                apart, fine[:, a].reshape(256, 512), preferred_element_type=FLOAT
            ).astype(HALF)
            for b in range(2):
                rows = pl.ds(pl.multiple_of(128 * s, 128), 128)
                flat[rows, pl.ds(512 * (2 * a + b), 512)] = parted[128 * b : 128 * b + 128]
        return carry

    lax.fori_loop(0, 3, three_source, 0)
    settle(got_wu, got_h2)
    for part in range(4):
        lanes = slice(256 * part, 256 * part + 256)
        gh2[:, lanes] = against(flat[...], wu[lanes, :]).astype(HALF)

    def wa_lanes(col):
        return gh2.at[:, pl.ds(pl.multiple_of(col * 256, 256), 256)]

    own_wa = stay(wa_lanes(wa), from_wa.at[wa])
    got_wa = [
        go(
            wa_lanes(lax.rem(wa + d, 4)),
            from_wa.at[wa],
            r_wa.at[d - 1],
            (ha, lax.rem(wa + d, 4)),
        )
        for d in range(1, 4)
    ]
    for part in range(4):
        lanes = slice(512 * part, 512 * part + 512)
        wu[:, lanes] = across(h2[...], flat[:, lanes]).astype(HALF)

    def block(grad, rows, bz, bx, by, bc):
        number = ((bz * 2 + bx) * 2 + by) * 2 + bc
        return grad.at[pl.ds(pl.multiple_of(number * rows, 16), rows)]

    def all_core(grad, rows, core, recv, some):
        return [
            go(
                block(grad, rows, bz, bx, by, 1 - c),
                core.at[((bz - some[0]) * 2 + bx) * 2 + by],
                recv.at[((bz - some[0]) * 2 + bx) * 2 + by],
                c_peer,
            )
            for bz in some
            for bx in range(2)
            for by in range(2)
        ]

    def all_y(grad, rows, core, along_y, recv, some, got):
        for copy in got:
            copy.wait_recv()

        def step(by):
            def add(i, carry):
                number = (((some[0] * 2 + i) * 2) + by) * 2 + c
                add_rows(grad, number * rows, core[i * 2 + by], rows)
                return carry

            lax.fori_loop(0, 2 * len(some), add, 0)

        step(1 - y)
        copies = [
            go(
                block(grad, rows, bz, bx, 1 - y, c),
                along_y.at[bz * 2 + bx],
                recv.at[16 + bz * 2 + bx],
                y_peer,
            )
            for bz in some
            for bx in range(2)
        ]
        step(y)
        return copies

    def all_x(grad, rows, along_y, along_x, recv, some, got):
        for copy in got:
            copy.wait_recv()

        def step(bx):
            def add(bz, carry):
                number = ((bz * 2 + bx) * 2 + y) * 2 + c
                add_rows(grad, number * rows, along_y[bz * 2 + bx], rows)
                return carry

            lax.fori_loop(some[0], some[-1] + 1, add, 0)

        step(1 - x)
        copies = [
            go(block(grad, rows, bz, 1 - x, y, c), along_x.at[bz], recv.at[24 + bz], x_peer)
            for bz in some
        ]
        step(x)
        return copies

    def all_z(grad, rows, along_x, along_z, recv, got):
        for copy in got:
            copy.wait_recv()

        def add(bz, carry):
            number = ((bz * 2 + x) * 2 + y) * 2 + c
            add_rows(grad, number * rows, along_x[bz], rows)
            return carry

        lax.fori_loop(0, 4, add, 0)
        return [
            go(
                block(grad, rows, lax.rem(z + d, 4), x, y, c),
                along_z.at[d - 1],
                recv.at[27 + d],
                spot(lax.rem(z + d, 4), x, y, c),
            )
            for d in range(1, 4)
        ]

    def all_end(grad, rows, along_z, out, got):
        total = grad[pl.ds(pl.multiple_of(mine * rows, 16), rows)].astype(FLOAT)
        for d in range(3):
            got[d].wait_recv()
            total = total + along_z[d].astype(FLOAT)
        out[...] = total

    def quarter_rows(rows, bz, bx):
        return pl.ds(pl.multiple_of((bz * 2 + bx) * 4 * rows, 16), 4 * rows)

    def quarter_x(grad, rows, along_x, recv, d):
        bz = lax.rem(z + d, 4)
        return go(grad.at[quarter_rows(rows, bz, 1 - x)], along_x.at[d - 1], recv.at[d - 1], x_peer)

    def quarter_z(grad, rows, along_x, along_z, recv, got, d):
        got[d - 1].wait_recv()
        bz = lax.rem(z + d, 4)
        add_rows(grad, (bz * 2 + x) * 4 * rows, along_x[d - 1], 4 * rows)
        if d == 4:
            return None
        return go(
            grad.at[quarter_rows(rows, bz, x)],
            along_z.at[d - 1],
            recv.at[3 + d],
            spot(bz, x, y, c),
        )

    def quarter_taps(taps):
        first = 2 * lax.rem(z + 1, 4)
        return [
            (d + 1, span, lambda i, carry: taps(lax.rem(first + i, 9), carry))
            for d, span in enumerate(((0, 3), (3, 6), (6, 8), (8, 9)))
        ]

    def quarter_w(grad, rows, along_z, out, recv, got):
        for copy in got:
            copy.wait_recv()

        own = pl.ds(pl.multiple_of(ha * 4 * rows, 16), 4 * rows)
        value = grad[own].astype(FLOAT)
        for d in range(3):
            value = value + along_z[d].astype(FLOAT)
        grad[own] = value.astype(HALF)
        target = out.at[:, pl.ds(pl.multiple_of(wa * 256, 256), 256)]

        def piece(col):
            return grad.at[pl.ds(pl.multiple_of((ha * 4 + col) * rows, 16), rows)]

        stay(piece(wa), target)
        return [
            go(
                piece(lax.rem(wa + d, 4)),
                target,
                recv.at[6 + d],
                (ha, lax.rem(wa + d, 4)),
            )
            for d in range(1, 4)
        ]

    su = all_core(wu, 32, du_c, r_u, (0, 1, 2, 3))
    su = all_y(wu, 32, du_c, du_y, r_u, (0, 1, 2, 3), su)

    def put_columns(target, s, value):
        put_shifts(target, pl.ds(0, 256), s, value, 0.0, 0.0)

    for e in range(3):
        gs2[e, :, 0] = jnp.zeros((3, 32, 256), HALF)
        gs2[e, :, 17] = jnp.zeros((3, 32, 256), HALF)
    settle(stay(pre2_in, pre))
    settle(own_wa)
    for copy in got_wa:
        copy.wait_recv()

    def two_grad(s, carry):
        rows = pl.ds(pl.multiple_of(128 * s, 128), 128)
        parts = [from_wa[w, rows].astype(FLOAT).reshape(16, 8, 256) for w in range(4)]
        put_columns(gs2, s, jnp.concatenate(parts, axis=1) * gelu_slope(pre[s]))
        return carry

    lax.fori_loop(0, 3, two_grad, 0)
    got_pre1 = stay(pre1_in, pre)
    settle(got_h1)

    def two_weight(t, carry):
        window = gs2[2 - t % 3, :, pl.ds(2 - t // 3, 16)].reshape(1536, 256)
        rows = pl.ds(pl.multiple_of(1024 * t, 1024), 1024)
        d2[rows] = across(joined[...], window).astype(HALF)
        return carry

    s2 = []
    for d, (first, last), taps in quarter_taps(two_weight):
        lax.fori_loop(first, last, taps, 0)
        s2.append(quarter_x(d2, 288, d2_x, r_2, d))
    settle(stay(joined_in, joined))

    def three_weight(t, carry):
        window = gs3[2 - t % 3, :, pl.ds(2 - t // 3, 32)].reshape(1536, 512)
        rows = pl.ds(pl.multiple_of(1024 * t, 1024), 1024)
        d3[rows] = across(joined[...], window).astype(HALF)
        return carry

    lax.fori_loop(0, 5, three_weight, 0)
    s3 = all_core(d3, 288, d3_c, r_3, (0, 1))
    z2 = [quarter_z(d2, 288, d2_x, d2_z, r_2, s2, 1)]
    s3_low = all_y(d3, 288, d3_c, d3_y, r_3, (0, 1), s3)
    pl.semaphore_signal(free, inc=1, device_id=c_peer, device_id_type=MESH)
    lax.fori_loop(5, 9, three_weight, 0)
    pl.semaphore_wait(free, 1)
    s3 = all_core(d3, 288, d3_c, r_3, (2, 3))
    got_x0 = stay(x0_in, joined.at[:, pl.ds(0, 512)])
    z2.append(quarter_z(d2, 288, d2_x, d2_z, r_2, s2, 2))
    settle(got_w2)

    def source_two(s):
        for half in range(2):
            acc[...] = jnp.zeros_like(acc)

            def tap(t, inner_carry):
                window = gs2[2 - t % 3, s, pl.ds(2 - t // 3, 16)].reshape(512, 256)
                rows = pl.ds(pl.multiple_of(1024 * t + 512 * half, 512), 512)
                acc[...] += against(window, slot[rows])
                return inner_carry

            lax.fori_loop(0, 9, tap, 0)
            gs3[half, s, pl.ds(0, 32)] = acc[...].astype(HALF).reshape(32, 16, 512)

    def d_lanes(halves, s, core):
        return gs3.at[halves, s, pl.ds(0, 32), :, pl.ds(pl.multiple_of(256 * core, 256), 256)]

    own_lanes = pl.ds(pl.multiple_of(256 * c, 256), 256)

    def d_pass(s):
        sd[s].wait_recv()
        for half in range(2):
            value = gs3[half, s, pl.ds(0, 32), :, own_lanes].astype(FLOAT)
            value = value + d_core[s, half].astype(FLOAT)
            gs3[half, s, pl.ds(0, 32), :, own_lanes] = value.astype(HALF)
        return go(d_lanes(1 - y, s, c), d_y.at[s], r_d.at[3 + s], y_peer)

    sd = []
    sy = []
    for s in range(3):
        source_two(s)
        sd.append(go(d_lanes(pl.ds(0, 2), s, 1 - c), d_core.at[s], r_d.at[s], c_peer))
        if s > 0:
            sy.append(d_pass(s - 1))
    sy.append(d_pass(2))
    s3_high = all_y(d3, 288, d3_c, d3_y, r_3, (2, 3), s3)
    z2.append(quarter_z(d2, 288, d2_x, d2_z, r_2, s2, 3))
    su = all_x(wu, 32, du_y, du_x, r_u, (0, 1, 2, 3), su)
    settle(got_pre1)
    for s in range(3):
        sy[s].wait_recv()
        value = gs3[y, s, pl.ds(0, 32), :, own_lanes].astype(FLOAT) + d_y[s].astype(FLOAT)
        put_columns(gs2, s, value.reshape(16, 32, 256) * gelu_slope(pre[s]))
    settle(got_x0)

    def one_weight(t, carry):
        window = gs2[2 - t % 3, :, pl.ds(2 - t // 3, 16)].reshape(1536, 256)
        rows = pl.ds(pl.multiple_of(512 * t, 512), 512)
        slot[rows] = across(joined[:, 0:512], window).astype(HALF)
        return carry

    s1 = []
    for d, (first, last), taps in quarter_taps(one_weight):
        lax.fori_loop(first, last, taps, 0)
        s1.append(quarter_x(slot, 144, d1_x, r_1, d))

    quarter_z(d2, 288, d2_x, d2_z, r_2, s2, 4)
    x3 = all_x(d3, 288, d3_y, d3_x, r_3, (0, 1), s3_low)
    su = all_z(wu, 32, du_x, du_z, r_u, su)
    z1 = [quarter_z(slot, 144, d1_x, d1_z, r_1, s1, d) for d in range(1, 4)]
    x3 += all_x(d3, 288, d3_y, d3_x, r_3, (2, 3), s3_high)
    s2 = quarter_w(d2, 288, d2_z, g2, r_2, z2)
    quarter_z(slot, 144, d1_x, d1_z, r_1, s1, 4)
    settle(own_head)
    total = hh[0]
    for step in range(1, 32):
        heads[step - 1].wait_recv()
        total = total + hh[step]
    gh[...] = total
    s3 = all_z(d3, 288, d3_x, d3_z, r_3, x3)
    all_end(wu, 32, du_z, gu, su)
    s1 = quarter_w(slot, 144, d1_z, g1, r_1, z1)
    all_end(d3, 288, d3_z, g3, s3)
    for copy in s2 + s1:
        copy.wait_recv()
    for entry in stays:
        if not entry[1]:
            settle(entry)
    for copy in sends:
        copy.wait_send()


def back(*args):
    anywhere = pl.BlockSpec(memory_space=pl.ANY)
    inside = pl.BlockSpec(memory_space=pltpu.VMEM)
    shape = jax.ShapeDtypeStruct
    dma = pltpu.SemaphoreType.DMA

    def room(*dims):
        return pltpu.VMEM(dims, HALF)

    return pl.pallas_call(
        back_kernel,
        name="back",
        out_shape=(
            shape((288, 512), FLOAT),
            shape((32, 2048), FLOAT),
            shape((288, 1024), HALF),
            shape((144, 1024), HALF),
            shape((16, 128), FLOAT),
        ),
        in_specs=[anywhere] * 11 + [inside] * 4,
        out_specs=[inside, inside, anywhere, anywhere, inside],
        scratch_shapes=[
            room(3, 3, 34, 16, 512),
            room(2, 3, 32, 512),
            room(2, 3, 32, 512),
            pltpu.VMEM((32, 16, 128), FLOAT),
            room(1536, 1024),
            room(9216, 256),
            pltpu.VMEM((512, 512), FLOAT),
            room(384, 2048),
            room(1024, 2048),
            room(384, 1024),
            room(384, 1024),
            room(4, 384, 256),
            pltpu.VMEM((3, 16, 32, 256), FLOAT),
            room(3, 3, 18, 32, 256),
            room(3, 2, 32, 16, 256),
            room(3, 32, 16, 256),
            room(16, 32, 2048),
            room(8, 32, 2048),
            room(4, 32, 2048),
            room(3, 32, 2048),
            room(9216, 512),
            room(8, 288, 512),
            room(8, 288, 512),
            room(4, 288, 512),
            room(3, 288, 512),
            room(9216, 256),
            room(4, 1152, 256),
            room(3, 1152, 256),
            room(4, 576, 256),
            room(3, 576, 256),
            pltpu.VMEM((32, 16, 128), FLOAT),
            dma((144,)),
            dma((40,)),
            dma((2,)),
            dma((3,)),
            dma((6,)),
            dma((31,)),
            dma((31,)),
            dma((10,)),
            dma((10,)),
            dma((31,)),
            pltpu.SemaphoreType.REGULAR,
        ],
        compiler_params=pltpu.CompilerParams(
            collective_id=2, has_side_effects=True, vmem_limit_bytes=64 * 1024 * 1024
        ),
    )(*args)


def dice_slopes(totals):
    union_sum = totals[..., 1] + totals[..., 2] + SMOOTHING
    numerator = 2.0 * totals[..., 0] + SMOOTHING
    dice_score = numerator / union_sum
    loss_value = 1.0 - jnp.mean(dice_score)
    entry_count = float(dice_score.size)
    common = -2.0 / (entry_count * union_sum)
    return (loss_value, jnp.concatenate([common, numerator / (entry_count * union_sum**2)], axis=1))


def sliced_grads(
    bottom, skipped, groups, pixel_mask, labels, weight_one, weight_two, weight_up, weight_three,
    weight_head,
):
    ha = lax.axis_index("ha")
    code = (pixel_mask + 2 * labels).astype(FLOAT).reshape(8, 3, 64)
    pads = [jnp.pad(code, ((0, 0), (0, 5), (64 * odd, 64 - 64 * odd))) for odd in range(2)]
    code = jnp.where(ha % 2 == 0, *pads)
    head_rows = jnp.pad(weight_head.astype(HALF), ((0, 0), (0, 126)))
    x0, h1, h2, joined, w2, wu, w3, pre_one, pre_two, pre_three, hidden_three, logits, code, sums, head = front(
        bottom.reshape(8, 48, 512),
        skipped.reshape(8, 192, 512),
        code,
        weight_one.astype(HALF),
        weight_two.astype(HALF),
        weight_up.astype(HALF),
        weight_three.astype(HALF),
        head_rows,
    )
    wu = wu.reshape(1024, 2048)
    w3 = w3.reshape(9216, 512)
    w2 = w2.reshape(9216, 256)
    member = (groups[:, None] == jnp.arange(GROUPS)[None, :]).astype(FLOAT)
    step = lax.axis_index("ha") * 4 + lax.axis_index("wa")
    origin = (step - jnp.arange(32)) % 32
    at_group = jnp.einsum(
        "dh,hsg->dsg",
        (origin[:, None] // 4 == jnp.arange(8)[None, :]).astype(FLOAT),
        member.reshape(8, 3, GROUPS),
        precision=HIGHEST,
    )
    totals = jnp.einsum("dsg,dsq->gq", at_group, sums[:, :3, :6], precision=HIGHEST)
    totals = totals.reshape(GROUPS, 2, 3)
    loss_value, slopes = dice_slopes(totals)
    member = lax.dynamic_slice_in_dim(member, 3 * ha, 3, axis=0)
    slopes = jnp.einsum("sg,gq->sq", member, slopes, precision=HIGHEST)
    g3, gu, g2, g1, gh = back(
        w3,
        wu,
        w2,
        joined.reshape(1536, 1024),
        h2,
        h1.reshape(1536, 1024),
        x0.reshape(1536, 512),
        pre_one,
        pre_two,
        pre_three,
        hidden_three.reshape(1536, 512),
        logits,
        code,
        jnp.pad(slopes, ((0, 5), (0, 124))),
        head,
    )
    return (loss_value, g1.astype(FLOAT), g2.astype(FLOAT), gu, g3, gh[:, :2])


def body(
    bottom,
    skipped,
    groups,
    pixel_mask,
    labels,
    conv1_weight,
    conv1_momentum,
    conv1_average,
    conv2_weight,
    conv2_momentum,
    conv2_average,
    up_weight,
    up_momentum,
    up_average,
    conv3_weight,
    conv3_momentum,
    conv3_average,
    head_weight,
    head_momentum,
    head_average,
):
    split = bottom.shape[0] == 24 and bottom.shape[1:3] == (2, 8) and bottom.shape[3] == 512
    split = split and (lax.axis_size("ha"), lax.axis_size("wa")) == (8, 4)
    grads = sliced_grads if split else tiled_grads
    loss_value, conv1_grad, conv2_grad, up_grad, conv3_grad, head_grad = grads(
        bottom,
        skipped,
        groups,
        pixel_mask,
        labels,
        conv1_weight,
        conv2_weight,
        up_weight,
        conv3_weight,
        head_weight,
    )
    first = renew_state(conv1_weight, conv1_momentum, conv1_average, conv1_grad, RATE_CONV)
    second = renew_state(conv2_weight, conv2_momentum, conv2_average, conv2_grad, RATE_CONV)
    upward = renew_state(up_weight, up_momentum, up_average, up_grad, RATE_CONV)
    third = renew_state(conv3_weight, conv3_momentum, conv3_average, conv3_grad, RATE_CONV)
    header = renew_state(head_weight, head_momentum, head_average, head_grad, RATE_HEAD)
    return (
        loss_value,
        first[0],
        first[1],
        first[2],
        second[0],
        second[1],
        second[2],
        upward[0],
        upward[1],
        upward[2],
        third[0],
        third[1],
        third[2],
        header[0],
        header[1],
        header[2],
    )


def solution(mesh):
    in_specs = (
        P(None, "ha", "wa", None),
        P(None, "ha", "wa", None),
        P(),
        P(None, "ha", "wa"),
        P(None, "ha", "wa"),
        P(("ha", "wa"), None),
        P(("ha", "wa"), None),
        P(("ha", "wa"), None),
        P(("ha", "wa"), None),
        P(("ha", "wa"), None),
        P(("ha", "wa"), None),
        P(("ha", "wa"), None),
        P(("ha", "wa"), None),
        P(("ha", "wa"), None),
        P(("ha", "wa"), None),
        P(("ha", "wa"), None),
        P(("ha", "wa"), None),
        P(("ha", "wa"), None),
        P(("ha", "wa"), None),
        P(("ha", "wa"), None),
    )
    out_specs = (
        P(),
        P(("ha", "wa"), None),
        P(("ha", "wa"), None),
        P(("ha", "wa"), None),
        P(("ha", "wa"), None),
        P(("ha", "wa"), None),
        P(("ha", "wa"), None),
        P(("ha", "wa"), None),
        P(("ha", "wa"), None),
        P(("ha", "wa"), None),
        P(("ha", "wa"), None),
        P(("ha", "wa"), None),
        P(("ha", "wa"), None),
        P(("ha", "wa"), None),
        P(("ha", "wa"), None),
        P(("ha", "wa"), None),
    )
    return jax.shard_map(body, mesh=mesh, in_specs=in_specs, out_specs=out_specs, check_vma=False)
```

```python
import functools

import jax
import jax.numpy as jnp
from jax import lax
from jax.experimental import pallas as pl
from jax.experimental.pallas import tpu as pltpu
from jax.sharding import PartitionSpec as P

GROUPS = 5


MOMENTUM = 0.9
RATE_CONV = 600.0
RATE_HEAD = 25.0
AVERAGE_DECAY = 0.5
SMOOTHING = 1.0
HIGHEST = lax.Precision.HIGHEST


def with_halo(block, sides, width):
    for axis, dim in sides:
        count = lax.axis_size(axis)
        forward = [(i, i + 1) for i in range(count - 1)]
        backward = [(target, source) for source, target in forward]
        low = lax.ppermute(
            lax.slice_in_dim(block, block.shape[dim] - width, None, axis=dim), axis, forward
        )
        high = lax.ppermute(lax.slice_in_dim(block, 0, width, axis=dim), axis, backward)
        block = jnp.concatenate([low, block, high], axis=dim)
    return block


def smooth(source):
    return jax.nn.gelu(source, approximate=True)


def smooth_back(pre_value, gradient):
    _, pull_back = jax.vjp(smooth, pre_value)
    return pull_back(gradient)[0]


def widened_field(source):
    return with_halo(source, (("ha", 1), ("wa", 2)), 1)


def conv_taps(padded, weight):
    kernel = weight.reshape(3, 3, padded.shape[3], weight.shape[1])
    return lax.conv_general_dilated(
        padded,
        kernel,
        (1, 1),
        "VALID",
        dimension_numbers=("NHWC", "HWIO", "NHWC"),
        preferred_element_type=jnp.float32,
    )


def conv_back(padded, grad_out, weight, back_chan):
    in_chan = padded.shape[3]
    weight_grad = lax.conv_general_dilated(
        padded,
        grad_out,
        (1, 1),
        "VALID",
        dimension_numbers=("CHWN", "IHWO", "HWNC"),
        preferred_element_type=jnp.float32,
    ).reshape(9 * in_chan, grad_out.shape[3])
    if not back_chan:
        return (weight_grad, None)
    grad_padded = widened_field(grad_out)
    kernel = weight.reshape(3, 3, in_chan, weight.shape[1])[::-1, ::-1, :back_chan]
    source_grad = lax.conv_general_dilated(
        grad_padded,
        kernel,
        (1, 1),
        "VALID",
        dimension_numbers=("NHWC", "HWOI", "NHWC"),
        preferred_element_type=jnp.float32,
    )
    return (weight_grad, source_grad)


def upsample(source, weight):
    slices, row_count, col_count, _ = source.shape
    flattened = jnp.einsum("shwc,cq->shwq", source, weight, preferred_element_type=jnp.float32)
    blocks = flattened.reshape(slices, row_count, col_count, 2, 2, -1).transpose(0, 1, 3, 2, 4, 5)
    return blocks.reshape(slices, 2 * row_count, 2 * col_count, -1)


def upsample_back(source, grad_up, weight):
    slices, row_count, col_count, _ = source.shape
    blocks = grad_up.reshape(slices, row_count, 2, col_count, 2, -1).transpose(0, 1, 3, 2, 4, 5)
    flattened = blocks.reshape(slices, row_count, col_count, -1)
    weight_grad = jnp.einsum("shwc,shwq->cq", source, flattened, preferred_element_type=jnp.float32)
    source_grad = jnp.einsum("shwq,cq->shwc", flattened, weight, preferred_element_type=jnp.float32)
    return (weight_grad, source_grad)


def forward(gathered, bottom, skipped):
    weight_one, weight_two, weight_up, weight_three, weight_head = gathered
    pad_zero = widened_field(bottom)
    pre_one = conv_taps(pad_zero, weight_one)
    hidden_one = smooth(pre_one).astype(jnp.bfloat16)
    pad_one = widened_field(hidden_one)
    pre_two = conv_taps(pad_one, weight_two)
    hidden_two = smooth(pre_two).astype(jnp.bfloat16)
    upsampled = upsample(hidden_two, weight_up).astype(jnp.bfloat16)
    joined = jnp.concatenate([upsampled, skipped], axis=3)
    pad_two = widened_field(joined)
    pre_three = conv_taps(pad_two, weight_three)
    hidden_three = smooth(pre_three).astype(jnp.bfloat16)
    logits = jnp.einsum(
        "shwc,ck->shwk", hidden_three, weight_head, preferred_element_type=jnp.float32
    )
    return (
        pad_zero,
        pre_one,
        pad_one,
        pre_two,
        hidden_two,
        pad_two,
        pre_three,
        hidden_three,
        logits,
    )


def pixel_terms(logits, pixel_mask, labels):
    probability = jax.nn.softmax(logits, axis=-1)
    classes = jnp.arange(logits.shape[-1])
    target = (labels[..., None] == classes[None, None, None, :]).astype(jnp.float32)
    weighted = pixel_mask[..., None].astype(jnp.float32)
    return (probability, target, weighted)


def dice_terms(logits, pixel_mask, labels, member):
    probability, target, weighted = pixel_terms(logits, pixel_mask, labels)
    per_slice = jnp.stack(
        [
            jnp.sum(weighted * probability * target, axis=(1, 2)),
            jnp.sum(weighted * probability, axis=(1, 2)),
            jnp.sum(weighted * target, axis=(1, 2)),
        ],
        axis=-1,
    )
    return jnp.einsum("skj,sg->gkj", per_slice, member, precision=HIGHEST)


def dice_back(logits, pixel_mask, labels, member, totals):
    probability, target, weighted = pixel_terms(logits, pixel_mask, labels)
    union_sum = totals[..., 1] + totals[..., 2] + SMOOTHING
    numerator = 2.0 * totals[..., 0] + SMOOTHING
    dice_score = numerator / union_sum
    loss_value = 1.0 - jnp.mean(dice_score)
    entry_count = float(dice_score.size)
    coef_common = -2.0 / (entry_count * union_sum)
    coef_prob = numerator / (entry_count * union_sum * union_sum)
    slice_common = jnp.einsum("sg,gk->sk", member, coef_common, precision=HIGHEST)
    slice_prob = jnp.einsum("sg,gk->sk", member, coef_prob, precision=HIGHEST)
    grad_prob = weighted * (target * slice_common[:, None, None, :] + slice_prob[:, None, None, :])
    inner = jnp.sum(probability * grad_prob, axis=-1, keepdims=True)
    grad_logits = (probability * (grad_prob - inner)).astype(jnp.bfloat16)
    return (loss_value, grad_logits)


def renew_state(weight, moment, average, gradient, rate):
    moment_new = MOMENTUM * moment + gradient
    weight_new = weight - rate * (gradient + MOMENTUM * moment_new)
    average_new = AVERAGE_DECAY * average + (1.0 - AVERAGE_DECAY) * weight_new
    return (weight_new, moment_new, average_new)


def tiled_grads(
    bottom, skipped, groups, pixel_mask, labels, conv1_weight, conv2_weight, up_weight, conv3_weight,
    head_weight,
):
    gathered = (
        lax.all_gather(conv1_weight.astype(jnp.bfloat16), ("ha", "wa"), axis=0, tiled=True),
        lax.all_gather(conv2_weight.astype(jnp.bfloat16), ("ha", "wa"), axis=0, tiled=True),
        lax.all_gather(up_weight.astype(jnp.bfloat16), ("ha", "wa"), axis=0, tiled=True),
        lax.all_gather(conv3_weight.astype(jnp.bfloat16), ("ha", "wa"), axis=0, tiled=True),
        lax.all_gather(head_weight.astype(jnp.bfloat16), ("ha", "wa"), axis=0, tiled=True),
    )
    member = (groups[:, None] == jnp.arange(GROUPS)[None, :]).astype(jnp.float32)
    kept = forward(gathered, bottom, skipped)
    partial_sums = dice_terms(kept[8], pixel_mask, labels, member)
    totals = lax.psum(partial_sums, ("ha", "wa"))
    pad_zero, pre_one, pad_one, pre_two, hidden_two, pad_two, pre_three, hidden_three, logits = kept
    weight_one, weight_two, weight_up, weight_three, weight_head = gathered
    loss_value, grad_logits = dice_back(logits, pixel_mask, labels, member, totals)
    head_grad = jnp.einsum(
        "shwc,shwk->ck", hidden_three, grad_logits, preferred_element_type=jnp.float32
    )
    grad_hidden = jnp.einsum(
        "shwk,ck->shwc", grad_logits, weight_head, preferred_element_type=jnp.float32
    )
    grad_pre_three = smooth_back(pre_three, grad_hidden).astype(jnp.bfloat16)
    conv3_grad, grad_joined = conv_back(pad_two, grad_pre_three, weight_three, weight_up.shape[1] // 4)
    grad_upsampled = grad_joined.astype(jnp.bfloat16)
    up_grad, grad_hidden_two = upsample_back(hidden_two, grad_upsampled, weight_up)
    grad_pre_two = smooth_back(pre_two, grad_hidden_two).astype(jnp.bfloat16)
    conv2_grad, grad_hidden_one = conv_back(pad_one, grad_pre_two, weight_two, pad_one.shape[3])
    grad_pre_one = smooth_back(pre_one, grad_hidden_one).astype(jnp.bfloat16)
    conv1_grad, _ = conv_back(pad_zero, grad_pre_one, weight_one, 0)
    sums = (
        lax.psum_scatter(conv1_grad.astype(jnp.bfloat16), ("ha", "wa"), scatter_dimension=0, tiled=True),
        lax.psum_scatter(conv2_grad.astype(jnp.bfloat16), ("ha", "wa"), scatter_dimension=0, tiled=True),
        lax.psum_scatter(up_grad.astype(jnp.bfloat16), ("ha", "wa"), scatter_dimension=0, tiled=True),
        lax.psum_scatter(conv3_grad.astype(jnp.bfloat16), ("ha", "wa"), scatter_dimension=0, tiled=True),
        lax.psum_scatter(head_grad.astype(jnp.bfloat16), ("ha", "wa"), scatter_dimension=0, tiled=True),
    )
    return (loss_value, *[s.astype(jnp.float32) for s in sums])


MESH = pl.DeviceIdType.MESH
FLOAT = jnp.float32
HALF = jnp.bfloat16


def place():
    row, col = (lax.axis_index("ha"), lax.axis_index("wa"))
    return (row // 2, row % 2, col // 2, col % 2)


def spot(z, x, y, c):
    return (2 * z + x, 2 * y + c)


def greet_all():
    row, col = (lax.axis_index("ha"), lax.axis_index("wa"))
    rows, cols = (lax.axis_size("ha"), lax.axis_size("wa"))
    barrier = pltpu.get_barrier_semaphore()
    for step in range(1, rows * cols):
        other = lax.rem(row * cols + col + step, rows * cols)
        pl.semaphore_signal(
            barrier, inc=1, device_id=(other // cols, lax.rem(other, cols)), device_id_type=MESH
        )
    pl.semaphore_wait(barrier, rows * cols - 1)


def remote(source, target, send_sem, recv_sem, device):
    return pltpu.make_async_remote_copy(
        src_ref=source,
        dst_ref=target,
        send_sem=send_sem,
        recv_sem=recv_sem,
        device_id=device,
        device_id_type=MESH,
    )


def gelu_of(value):
    inner = 0.7978845608028654 * (value + 0.044715 * value * value * value)
    return 0.5 * value * (1.0 + jnp.tanh(inner))


def conv_slice(source, weight, parts, index, chan):
    parts[...] = jnp.zeros_like(parts)

    def row_tap(r, carry):
        window = source[index, pl.ds(r, 16)].reshape(512, chan)
        for c in range(3):
            start = pl.multiple_of((3 * r + c) * chan, chan)
            parts[c] += jnp.dot(
                window, weight[pl.ds(start, chan), :], preferred_element_type=FLOAT
            )
        return carry

    lax.fori_loop(0, 3, row_tap, 0)
    shape = (16, 32, 256)
    column = lax.broadcasted_iota(jnp.int32, shape, 1)
    low = jnp.where(column > 0, pltpu.roll(parts[0].reshape(shape), 1, 1), 0.0)
    high = jnp.where(column < 31, pltpu.roll(parts[2].reshape(shape), 31, 1), 0.0)
    return parts[1].reshape(shape) + low + high


def put_shifts(target, lanes, s, value, left, right):
    column = lax.broadcasted_iota(jnp.int32, value.shape, 1)
    last = value.shape[1] - 1
    rows = pl.ds(1, value.shape[0])
    low = jnp.where(column > 0, pltpu.roll(value, 1, 1), left)
    target[0, s, rows, :, lanes] = low.astype(HALF)
    target[1, s, rows, :, lanes] = value.astype(HALF)
    high = jnp.where(column < last, pltpu.roll(value, last, 1), right)
    target[2, s, rows, :, lanes] = high.astype(HALF)


def put_tile(target, first, s, value, left, right):
    column = lax.broadcasted_iota(jnp.int32, value.shape, 1)
    last = value.shape[1] - 1
    rows = pl.ds(1, value.shape[0])
    low = jnp.where(column > 0, pltpu.roll(value, 1, 1), left)
    high = jnp.where(column < last, pltpu.roll(value, last, 1), right)
    for shift, part in enumerate((low, value, high)):
        target[s, rows, :, pl.ds(1024 * shift + first, 512)] = part.astype(HALF)


def front_kernel(
    compute,
    bot, skip, code, w1, w2, wu, w3, wh,
    x0_out, h1_out, h2_out, joined_out, w2_out, wu_out, w3_out, pre1_out, pre2_out, pre3_out,
    hidden_out, logit_out, code_out, sums_out, head_out,
    xr, x0, w1q, w2q, h1s, h1, parts, h2s, h2v, wuv, w3v, skv, rims, rims_got, tiles, whv,
    pre1, pre2, pre3, hidden_all,
    send, here, r_bot, r_grp, r_w1, r_w2, r_h1, r_h2, r_skip, r_wh, r_w3, r_wu,
    r_code, r_rim, r_sum,
):
    z, x, y, c = place()
    ha, wa = (2 * z + x, 2 * y + c)
    x_peer, y_peer, c_peer = (spot(z, 1 - x, y, c), spot(z, x, 1 - y, c), spot(z, x, y, 1 - c))
    mine = ha * 4 + wa
    greet_all()
    sends = []
    stays = []

    def go(source, target, recv_sem, device):
        copy = remote(source, target, send.at[len(sends)], recv_sem, device)
        copy.start()
        sends.append((copy, None))
        return copy

    def stay(source, target):
        copy = pltpu.make_async_copy(source, target, here.at[len(stays)])
        copy.start()
        stays.append([copy, False])
        return stays[-1]

    def settle(*entries):
        for entry in entries:
            entry[0].wait()
            entry[1] = True

    def arrive(*copies):
        for copy in copies:
            copy.wait_recv()

    def go_if(when, source, target, recv_sem, device):
        copy = remote(source, target, send.at[len(sends)], recv_sem, device)
        pl.when(when)(lambda: copy.start())
        sends.append((copy, when))
        return (copy, when)

    def arrive_if(copy, when):
        pl.when(when)(lambda: copy.wait_recv())

    above, below = (spot(lax.rem(z + 1, 4), x, y, c), spot(lax.rem(z + 3, 4), x, y, c))

    def line_start(part, line):
        go_if(z < 3, part(z), part(z), line.at[0], above)
        go_if(z > 0, part(z), part(z), line.at[3], below)

    def line_hop(part, line, j, passes):
        for first, other, more, last, neighbour in (
            (0, lax.rem(z + 3 - j, 4), z >= j + 1, z < 3, above),
            (3, lax.rem(z + 1 + j, 4), z <= 2 - j, z > 0, below),
        ):
            piece = part(other)
            arrive_if(remote(piece, piece, send.at[0], line.at[first + j], x_peer), more)
            if j < 2:
                go_if(
                    jnp.logical_and(more, last), piece, piece, line.at[first + j + 1], neighbour
                )
            for recv, got, device in passes:
                got.append(go_if(more, piece, piece, recv.at[1 + first + j], device))

    def swap(shard, whole, first, count, recv):
        source_rows = pl.ds(first, count)
        target = whole.at[ha, wa, source_rows]
        lanes = [pl.ds(pl.multiple_of(lax.rem(wa + dw, 4) * 256, 256), 256) for dw in range(4)]
        own = stay(shard.at[source_rows, lanes[0]], target)
        copies = [
            go(shard.at[source_rows, lanes[dw]], target, recv.at[dw], (ha, lax.rem(wa + dw, 4)))
            for dw in range(1, 4)
        ]
        return (own, copies)

    class Quarter:
        def __init__(self, shard, whole, first, count, line, recv):
            self.line, self.recv, self.got = (line, recv, [])
            self.part = lambda bz: whole.at[bz * 2 + x, :, pl.ds(first, count)]
            self.swapped = swap(shard, whole, first, count, recv.at[1])

        def start(self):
            settle(self.swapped[0])
            arrive(*self.swapped[1])
            line_start(self.part, self.line)
            own = self.part(z)
            self.got.append((go(own, own, self.recv.at[0, 0], x_peer), None))

        def hop(self, j):
            line_hop(self.part, self.line, j, [(self.recv.at[0], self.got, x_peer)])

        def done(self):
            for copy, when in self.got:
                if when is None:
                    copy.wait_recv()
                else:
                    arrive_if(copy, when)

    class Whole:
        def __init__(self, shard, whole, line, recv):
            self.whole, self.line, self.recv = (whole, line, recv)
            self.part = lambda bz: whole.at[bz, x, y, c]
            self.own = stay(shard, self.part(z))
            self.along_x, self.along_y, self.core = ([], [], [])

        def start(self):
            settle(self.own)
            line_start(self.part, self.line)
            own = self.part(z)
            self.along_x.append((go(own, own, self.recv.at[0, 0], x_peer), None))
            self.along_y.append((go(own, own, self.recv.at[1, 0], y_peer), None))
            self.core.append((go(own, own, self.recv.at[2, 0], c_peer), None))

        def hop(self, j):
            passes = [
                (self.recv.at[0], self.along_x, x_peer),
                (self.recv.at[1], self.along_y, y_peer),
                (self.recv.at[2], self.core, c_peer),
            ]
            line_hop(self.part, self.line, j, passes)

        def wait(self, got):
            for copy, when in got:
                if when is None:
                    copy.wait_recv()
                else:
                    arrive_if(copy, when)

        def turn(self):
            self.wait(self.along_x)
            part = self.whole.at[:, 1 - x, y, c]
            self.last = go(part, part, self.recv.at[1, 7], y_peer)
            self.core.append((go(part, part, self.recv.at[2, 7], c_peer), None))

        def finish(self):
            self.wait(self.along_y)
            part = self.whole.at[:, x, 1 - y, c]
            self.core.append((go(part, part, self.recv.at[0, 7], c_peer), None))
            arrive(self.last)
            part = self.whole.at[:, 1 - x, 1 - y, c]
            self.core.append((go(part, part, self.recv.at[3, 0], c_peer), None))

        def done(self):
            self.wait(self.core)

    own_bot = stay(bot.at[ha], xr.at[ha, wa])
    bots = [
        go(bot.at[lax.rem(ha + d, 8)], xr.at[ha, wa], r_bot.at[d - 1], (lax.rem(ha + d, 8), wa))
        for d in range(1, 8)
    ]
    whole_three = Whole(w3, w3v, r_w3.at[4, pl.ds(0, 6)], r_w3)
    whole_up = Whole(wu, wuv, r_wu.at[4, pl.ds(0, 6)], r_wu)
    one_part = Quarter(w1, w1q, 0, 144, r_w1.at[2], r_w1)
    two_low = Quarter(w2, w2q, 0, 144, r_w2.at[0, 2], r_w2.at[0])
    two_high = Quarter(w2, w2q, 144, 144, r_w2.at[1, 2], r_w2.at[1])
    whole_three.start()
    whole_up.start()
    settle(own_bot)
    arrive(*bots)
    to_c = go(xr.at[:, wa], xr.at[:, wa], r_grp.at[0], c_peer)
    to_y = go(xr.at[:, wa], xr.at[:, wa], r_grp.at[1], y_peer)
    whole_three.hop(0)
    whole_up.hop(0)
    one_part.start()
    whole_three.hop(1)
    whole_up.hop(1)
    own_code = stay(code.at[ha], code_out.at[ha])
    codes = [
        go(code.at[lax.rem(ha + d, 8)], code_out.at[ha], r_code.at[d - 1], (lax.rem(ha + d, 8), wa))
        for d in range(1, 8)
    ]
    own_head = stay(wh, whv.at[mine])
    heads = []
    for step in range(1, 32):
        other = lax.rem(mine + step, 32)
        heads.append(go(wh, whv.at[mine], r_wh.at[step - 1], (other // 4, lax.rem(other, 4))))
    if compute:
        x0[:, 0] = jnp.zeros((3, 32, 512), HALF)
        x0[:, 17] = jnp.zeros((3, 32, 512), HALF)
        h1[:, 0] = jnp.zeros((3, 32, 1024), HALF)
        h1[:, 17] = jnp.zeros((3, 32, 1024), HALF)
        tiles[:, 0] = jnp.zeros((3, 16, 3072), HALF)
        tiles[:, 33] = jnp.zeros((3, 16, 3072), HALF)
    whole_three.hop(2)
    two_low.start()
    whole_up.hop(2)
    one_part.hop(0)
    two_high.start()
    arrive(to_y)
    part = xr.at[:, 2 * (1 - y) + c]
    on_c = go(part, part, r_grp.at[2], c_peer)
    arrive(to_c, on_c)

    if compute:

        def reorder(h, carry):
            block = xr[h].astype(FLOAT).reshape(4, 3, 2, 8, 512)
            for s in range(3):
                for r in range(2):
                    row = jnp.concatenate([block[w, s, r] for w in range(4)], axis=0)
                    x0[s, 2 * h + 1 + r] = row.astype(HALF)
            return carry

        lax.fori_loop(0, 8, reorder, 0)
    stay(x0.at[:, pl.ds(1, 16)], x0_out)
    one_part.hop(1)
    two_low.hop(0)
    one_part.hop(2)
    two_high.hop(0)
    whole_three.turn()
    two_low.hop(1)
    two_high.hop(1)
    whole_up.turn()
    own_skip = stay(skip.at[ha], skv.at[ha])
    skips = [
        go(skip.at[lax.rem(ha + d, 8)], skv.at[ha], r_skip.at[d - 1], (lax.rem(ha + d, 8), wa))
        for d in range(1, 8)
    ]
    two_low.hop(2)
    one_part.done()
    if compute:

        def one(s, carry):
            value = conv_slice(x0, w1q.reshape(4608, 256), parts, s, 512)
            pre1[s] = value
            h1s[s] = gelu_of(value).astype(HALF)
            return carry

        lax.fori_loop(0, 3, one, 0)

    def lanes(col):
        return h1.at[:, pl.ds(1, 16), :, pl.ds(pl.multiple_of(col * 256, 256), 256)]

    own_h1 = stay(h1s, lanes(wa))
    stay(pre1, pre1_out)
    h1_c = go(h1s, lanes(wa), r_h1.at[0], c_peer)
    h1_y = go(h1s, lanes(wa), r_h1.at[1], y_peer)

    two_high.hop(2)
    whole_three.finish()
    whole_up.finish()
    arrive(h1_y)
    h1_on = go(lanes(2 * (1 - y) + c), lanes(2 * (1 - y) + c), r_h1.at[2], c_peer)
    settle(own_h1)
    arrive(h1_c, h1_on)
    stay(h1.at[:, pl.ds(1, 16)], h1_out)
    two_low.done()
    two_high.done()
    stay(w2q, w2_out)
    if compute:

        def two(s, carry):
            value = conv_slice(h1, w2q.reshape(9216, 256), parts, s, 1024)
            pre2[s] = value
            hidden = gelu_of(value)
            for w in range(4):
                tile = hidden[:, 8 * w : 8 * w + 8].reshape(128, 256)
                h2s[w, pl.ds(pl.multiple_of(s * 128, 128), 128)] = tile.astype(HALF)
                left = hidden[:, 8 * w - 1] if w > 0 else jnp.zeros((16, 256), FLOAT)
                h2s[w, pl.ds(pl.multiple_of(384 + s * 16, 16), 16)] = left.astype(HALF)
                right = hidden[:, 8 * w + 8] if w < 3 else jnp.zeros((16, 256), FLOAT)
                h2s[w, pl.ds(pl.multiple_of(432 + s * 16, 16), 16)] = right.astype(HALF)
            return carry

        lax.fori_loop(0, 3, two, 0)
    h2_lanes = h2v.at[:, pl.ds(pl.multiple_of(wa * 256, 256), 256)]
    own_h2 = stay(h2s.at[wa], h2_lanes)
    stay(pre2, pre2_out)
    h2_got = [
        go(h2s.at[lax.rem(wa + d, 4)], h2_lanes, r_h2.at[d - 1], (ha, lax.rem(wa + d, 4)))
        for d in range(1, 4)
    ]

    settle(own_skip)
    arrive(*skips)

    def skip_slice(s):
        return skv[:, 64 * s : 64 * s + 64].astype(FLOAT).reshape(32, 16, 512)

    if compute:
        for s in range(3):
            value = skip_slice(s)
            rims[0, s] = value[:, 0].astype(HALF)
            rims[1, s] = value[:, 15].astype(HALF)
    before = (ha, lax.rem(wa + 3, 4))
    after = (ha, lax.rem(wa + 1, 4))
    rim_right = go(rims.at[0], rims_got.at[1], r_rim.at[1], before)
    rim_left = go(rims.at[1], rims_got.at[0], r_rim.at[0], after)
    arrive(rim_right, rim_left)
    if compute:
        for s in range(3):
            left = jnp.where(wa > 0, rims_got[0, s].astype(FLOAT), 0.0)
            right = jnp.where(wa < 3, rims_got[1, s].astype(FLOAT), 0.0)
            put_tile(tiles, 512, s, skip_slice(s), left[:, None, :], right[:, None, :])
    whole_three.done()
    stay(w3v, w3_out)
    settle(own_h2)
    arrive(*h2_got)
    stay(h2v, h2_out)
    whole_up.done()
    stay(wuv, wu_out)
    if compute:
        order = lax.broadcasted_iota(jnp.int32, (256, 256), 1)
        inner = order % 128
        pick = (inner // 8) * 16 + (inner % 8) * 2 + order // 128
        woven = jnp.where(lax.broadcasted_iota(jnp.int32, (256, 256), 0) == pick, 1.0, 0.0)
        woven = woven.astype(HALF)
        wide = wuv.reshape(1024, 2048)
        for s in range(3):
            fine, sides = ([], ([], []))
            for a in range(2):
                weight = wide[:, 1024 * a : 1024 * a + 1024]
                flat = jnp.dot(
                    h2v[128 * s : 128 * s + 128], weight, preferred_element_type=FLOAT
                ).astype(HALF)
                flat = jnp.concatenate([flat[:, :512], flat[:, 512:]], axis=0)
                flat = jnp.dot(woven, flat, preferred_element_type=FLOAT)
                fine.append(flat.reshape(16, 16, 512))
                for side in range(2):
                    start = 384 + 48 * side + 16 * s
                    rim = jnp.dot(
                        h2v[start : start + 16],
                        weight[:, 512 * (1 - side) : 512 * (1 - side) + 512],
                        preferred_element_type=FLOAT,
                    )
                    sides[side].append(rim.astype(HALF).astype(FLOAT)[:, None, :])
            value = jnp.stack(fine, axis=1).reshape(32, 16, 512)
            left, right = [jnp.stack(side, axis=1).reshape(32, 1, 512) for side in sides]
            put_tile(tiles, 0, s, value, left, right)

    stay(tiles.at[:, pl.ds(1, 32), :, pl.ds(1024, 1024)], joined_out)
    settle(own_head)
    arrive(*heads)
    settle(own_code)
    arrive(*codes)
    if compute:
        head = whv.reshape(512, 128)[...].astype(FLOAT).T[:16].astype(HALF)
        head_out[...] = head
        row = lax.broadcasted_iota(jnp.int32, (8, 128), 0)
        lane = lax.broadcasted_iota(jnp.int32, (8, 128), 1)
        sums_out[0] = jnp.zeros((8, 128), FLOAT)

        rows = w3v.reshape(9216, 512)

        def three(s, carry):
            for r in range(3):
                window = tiles[s, r : r + 32].reshape(512, 3072)
                value = jnp.dot(
                    window, rows[3072 * r : 3072 * r + 3072, :], preferred_element_type=FLOAT
                )
                if r == 0:
                    pre3[s] = value
                else:
                    pre3[s] += value
            hidden = gelu_of(pre3[s]).astype(HALF)
            hidden_all[s] = hidden
            logits = lax.dot_general(
                head, hidden, (((1,), (1,)), ((), ())), preferred_element_type=FLOAT
            )
            logit_out[s] = logits
            return carry

        lax.fori_loop(0, 3, three, 0)
        stay(pre3, pre3_out)
        stay(hidden_all, hidden_out)
        total = jnp.zeros((8, 128), FLOAT)
        for s in range(3):
            probability, target, weighted = class_terms(logit_out, code_out, s)
            for k in range(2):
                terms = (
                    weighted * probability[k] * target[k],
                    weighted * probability[k],
                    weighted * target[k],
                )
                for j, term in enumerate(terms):
                    value = jnp.sum(term, axis=1, keepdims=True)
                    here_is = jnp.logical_and(row == s, lane == 3 * k + j)
                    total = total + jnp.where(here_is, value, 0.0)
        sums_out[0] = total
    sums = []
    for step in range(1, 32):
        other = lax.rem(mine + step, 32)
        sums.append(
            go(
                sums_out.at[0],
                sums_out.at[step],
                r_sum.at[step - 1],
                (other // 4, lax.rem(other, 4)),
            )
        )
    arrive(*sums)
    for entry in stays:
        if not entry[1]:
            settle(entry)
    for copy, when in sends:
        if when is None:
            copy.wait_send()
        else:
            pl.when(when)(copy.wait_send)


def class_terms(logits, codes, s):
    pieces = [codes[2 * q, s : s + 1] + codes[2 * q + 1, s : s + 1] for q in range(4)]
    both = jnp.concatenate(pieces, axis=1)
    label = jnp.where(both >= 2.0, 1.0, 0.0)
    weighted = both - 2.0 * label
    first, second = (logits[s, 0:1], logits[s, 1:2])
    top = jnp.maximum(first, second)
    first, second = (jnp.exp(first - top), jnp.exp(second - top))
    scale = 1.0 / (first + second)
    return ((first * scale, second * scale), (1.0 - label, label), weighted)


def front(bot, skip, code, w1, w2, wu, w3, wh, compute=True):
    anywhere = pl.BlockSpec(memory_space=pl.ANY)
    inside = pl.BlockSpec(memory_space=pltpu.VMEM)
    shape = jax.ShapeDtypeStruct
    dma = pltpu.SemaphoreType.DMA

    def room(*dims):
        return pltpu.VMEM(dims, HALF)

    return pl.pallas_call(
        functools.partial(front_kernel, compute),
        name="front",
        out_shape=(
            shape((3, 16, 32, 512), HALF),
            shape((3, 16, 32, 1024), HALF),
            shape((480, 1024), HALF),
            shape((3, 32, 16, 1024), HALF),
            shape((8, 4, 288, 256), HALF),
            shape((4, 2, 2, 2, 32, 2048), HALF),
            shape((4, 2, 2, 2, 288, 512), HALF),
            shape((3, 16, 32, 256), FLOAT),
            shape((3, 16, 32, 256), FLOAT),
            shape((3, 512, 512), FLOAT),
            shape((3, 512, 512), HALF),
            shape((3, 16, 512), FLOAT),
            shape((8, 8, 128), FLOAT),
            shape((32, 8, 128), FLOAT),
            shape((16, 512), HALF),
        ),
        in_specs=[anywhere] * 8,
        out_specs=[anywhere] * 11 + [inside] * 4,
        scratch_shapes=[
            room(8, 4, 48, 512),
            room(3, 18, 32, 512),
            room(8, 4, 144, 256),
            room(8, 4, 288, 256),
            room(3, 16, 32, 256),
            room(3, 18, 32, 1024),
            pltpu.VMEM((3, 512, 256), FLOAT),
            room(4, 480, 256),
            room(480, 1024),
            room(4, 2, 2, 2, 32, 2048),
            room(4, 2, 2, 2, 288, 512),
            room(8, 192, 512),
            room(2, 3, 32, 512),
            room(2, 3, 32, 512),
            room(3, 34, 16, 3072),
            room(32, 16, 128),
            pltpu.VMEM((3, 16, 32, 256), FLOAT),
            pltpu.VMEM((3, 16, 32, 256), FLOAT),
            pltpu.VMEM((3, 512, 512), FLOAT),
            room(3, 512, 512),
            dma((256,)),
            dma((24,)),
            dma((7,)),
            dma((3,)),
            dma((3, 8)),
            dma((2, 3, 8)),
            dma((3,)),
            dma((3,)),
            dma((7,)),
            dma((31,)),
            dma((5, 8)),
            dma((5, 8)),
            dma((7,)),
            dma((2,)),
            dma((31,)),
        ],
        compiler_params=pltpu.CompilerParams(
            collective_id=0, has_side_effects=True, vmem_limit_bytes=64 * 1024 * 1024
        ),
    )(bot, skip, code, w1, w2, wu, w3, wh)


def gelu_slope(value):
    square = value * value
    bend = jnp.tanh(0.7978845608028654 * value * (1.0 + 0.044715 * square))
    rise = 0.7978845608028654 * (1.0 + 3.0 * 0.044715 * square)
    return 0.5 * (1.0 + bend) + 0.5 * value * (1.0 - bend * bend) * rise


def across(source, window):
    return lax.dot_general(source, window, (((0,), (0,)), ((), ())), preferred_element_type=FLOAT)


def against(window, weight):
    return lax.dot_general(window, weight, (((1,), (1,)), ((), ())), preferred_element_type=FLOAT)


def add_rows(total, start, term, rows):
    where = pl.ds(pl.multiple_of(start, 16), rows)
    total[where] = (total[where].astype(FLOAT) + term.astype(FLOAT)).astype(HALF)


def back_kernel(
    w3_in, wu_in, w2_in, joined_in, h2_in, h1_in, x0_in, pre1_in, pre2_in, pre3_in, hidden_in,
    logits, codes, slopes, head,
    g3, gu, g2, g1, gh,
    gs3, rims, rims_got, dh, joined, slot, acc, flat, wu, h2, gh2, from_wa, pre, gs2, d_core, d_y,
    du_c, du_y, du_x, du_z, d3, d3_c, d3_y, d3_x, d3_z, d2, d2_x, d2_z, d1_x, d1_z, hh,
    send, here, r_rim, r_wa, r_d, r_u, r_3, r_2, r_1, r_h, free,
):
    z, x, y, c = place()
    ha, wa = (2 * z + x, 2 * y + c)
    x_peer, y_peer, c_peer = (spot(z, 1 - x, y, c), spot(z, x, 1 - y, c), spot(z, x, y, 1 - c))
    mine = ha * 4 + wa
    sends = []
    stays = []

    def go(source, target, recv_sem, device):
        copy = remote(source, target, send.at[len(sends)], recv_sem, device)
        copy.start()
        sends.append(copy)
        return copy

    def stay(source, target):
        copy = pltpu.make_async_copy(source, target, here.at[len(stays)])
        copy.start()
        stays.append([copy, False])
        return stays[-1]

    def settle(*entries):
        for entry in entries:
            entry[0].wait()
            entry[1] = True

    got_hidden = stay(hidden_in, d3.at[pl.ds(0, 1536)])
    got_pre3 = stay(pre3_in.at[0], acc)
    got_w3 = [
        stay(w3_in.at[pl.ds(1024 * t, 512)], d3.at[pl.ds(4608 + 512 * t, 512)]) for t in range(9)
    ]
    got_w2 = stay(w2_in, slot)
    got_wu = stay(wu_in, wu)
    got_h2 = stay(h2_in.at[pl.ds(0, 384)], h2)
    got_h1 = stay(h1_in, joined)
    greet_all()

    settle(got_hidden)
    head_sum = jnp.zeros((16, 512), FLOAT)
    class_row = lax.broadcasted_iota(jnp.int32, (16, 512), 0)
    for e in range(3):
        gs3[e, :, 0] = jnp.zeros((3, 16, 512), HALF)
        gs3[e, :, 33] = jnp.zeros((3, 16, 512), HALF)
    for s in range(3):
        probability, target, weighted = class_terms(logits, codes, s)
        grads = [
            weighted * (target[k] * slopes[s : s + 1, k : k + 1] + slopes[s : s + 1, 2 + k : 3 + k])
            for k in range(2)
        ]
        inner = probability[0] * grads[0] + probability[1] * grads[1]
        grads = [probability[k] * (grads[k] - inner) for k in range(2)]
        grads = jnp.where(class_row == 0, grads[0], jnp.where(class_row == 1, grads[1], 0.0))
        grads = grads.astype(HALF)
        hidden = d3[512 * s : 512 * s + 512]
        head_sum = head_sum + jnp.dot(grads, hidden, preferred_element_type=FLOAT)
        settle(got_pre3)
        value = (across(grads, head[...]) * gelu_slope(acc[...])).astype(HALF)
        if s < 2:
            got_pre3 = stay(pre3_in.at[s + 1], acc)
        gs3[1, s, 1:33] = value.reshape(32, 16, 512)
        value = value.astype(FLOAT).reshape(32, 16, 512)
        rims[0, s] = value[:, 0].astype(HALF)
        rims[1, s] = value[:, 15].astype(HALF)
    before = (ha, lax.rem(wa + 3, 4))
    after = (ha, lax.rem(wa + 1, 4))
    rim_right = go(rims.at[0], rims_got.at[1], r_rim.at[1], before)
    rim_left = go(rims.at[1], rims_got.at[0], r_rim.at[0], after)
    rows = jnp.concatenate([head_sum, jnp.zeros((112, 512), FLOAT)], axis=0)
    dh[...] = rows.T.reshape(32, 16, 128)
    own_head = stay(dh.at[mine], hh.at[0])
    heads = []
    for step in range(1, 32):
        other = lax.rem(mine + step, 32)
        heads.append(
            go(dh.at[other], hh.at[step], r_h.at[step - 1], (other // 4, lax.rem(other, 4)))
        )
    rim_right.wait_recv()
    rim_left.wait_recv()
    for s in range(3):
        left = jnp.where(wa > 0, rims_got[0, s].astype(FLOAT), 0.0)
        right = jnp.where(wa < 3, rims_got[1, s].astype(FLOAT), 0.0)
        value = gs3[1, s, 1:33].astype(FLOAT)
        put_shifts(gs3, pl.ds(0, 512), s, value, left[:, None, :], right[:, None, :])

    order = lax.broadcasted_iota(jnp.int32, (256, 256), 0)
    inner = order % 128
    pick = (inner // 8) * 16 + (inner % 8) * 2 + order // 128
    apart = jnp.where(lax.broadcasted_iota(jnp.int32, (256, 256), 1) == pick, 1.0, 0.0).astype(HALF)
    settle(*got_w3)

    def three_source(s, carry):
        acc[...] = jnp.zeros_like(acc)

        def tap(t, inner_carry):
            window = gs3[2 - t % 3, s, pl.ds(2 - t // 3, 32)].reshape(512, 512)
            acc[...] += against(window, d3[pl.ds(pl.multiple_of(4608 + 512 * t, 512), 512)])
            return inner_carry

        lax.fori_loop(0, 9, tap, 0)
        fine = acc[...].astype(HALF).reshape(16, 2, 16, 512)
        for a in range(2):
            parted = jnp.dot(
                apart, fine[:, a].reshape(256, 512), preferred_element_type=FLOAT
            ).astype(HALF)
            for b in range(2):
                rows = pl.ds(pl.multiple_of(128 * s, 128), 128)
                flat[rows, pl.ds(512 * (2 * a + b), 512)] = parted[128 * b : 128 * b + 128]
        return carry

    lax.fori_loop(0, 3, three_source, 0)
    settle(got_wu, got_h2)
    for part in range(4):
        lanes = slice(256 * part, 256 * part + 256)
        gh2[:, lanes] = against(flat[...], wu[lanes, :]).astype(HALF)

    def wa_lanes(col):
        return gh2.at[:, pl.ds(pl.multiple_of(col * 256, 256), 256)]

    own_wa = stay(wa_lanes(wa), from_wa.at[wa])
    got_wa = [
        go(
            wa_lanes(lax.rem(wa + d, 4)),
            from_wa.at[wa],
            r_wa.at[d - 1],
            (ha, lax.rem(wa + d, 4)),
        )
        for d in range(1, 4)
    ]
    for part in range(4):
        lanes = slice(512 * part, 512 * part + 512)
        wu[:, lanes] = across(h2[...], flat[:, lanes]).astype(HALF)

    def block(grad, rows, bz, bx, by, bc):
        number = ((bz * 2 + bx) * 2 + by) * 2 + bc
        return grad.at[pl.ds(pl.multiple_of(number * rows, 16), rows)]

    def all_core(grad, rows, core, recv, some):
        return [
            go(
                block(grad, rows, bz, bx, by, 1 - c),
                core.at[((bz - some[0]) * 2 + bx) * 2 + by],
                recv.at[((bz - some[0]) * 2 + bx) * 2 + by],
                c_peer,
            )
            for bz in some
            for bx in range(2)
            for by in range(2)
        ]

    def all_y(grad, rows, core, along_y, recv, some, got):
        for copy in got:
            copy.wait_recv()

        def step(by):
            def add(i, carry):
                number = (((some[0] * 2 + i) * 2) + by) * 2 + c
                add_rows(grad, number * rows, core[i * 2 + by], rows)
                return carry

            lax.fori_loop(0, 2 * len(some), add, 0)

        step(1 - y)
        copies = [
            go(
                block(grad, rows, bz, bx, 1 - y, c),
                along_y.at[bz * 2 + bx],
                recv.at[16 + bz * 2 + bx],
                y_peer,
            )
            for bz in some
            for bx in range(2)
        ]
        step(y)
        return copies

    def all_x(grad, rows, along_y, along_x, recv, some, got):
        for copy in got:
            copy.wait_recv()

        def step(bx):
            def add(bz, carry):
                number = ((bz * 2 + bx) * 2 + y) * 2 + c
                add_rows(grad, number * rows, along_y[bz * 2 + bx], rows)
                return carry

            lax.fori_loop(some[0], some[-1] + 1, add, 0)

        step(1 - x)
        copies = [
            go(block(grad, rows, bz, 1 - x, y, c), along_x.at[bz], recv.at[24 + bz], x_peer)
            for bz in some
        ]
        step(x)
        return copies

    def all_z(grad, rows, along_x, along_z, recv, got):
        for copy in got:
            copy.wait_recv()

        def add(bz, carry):
            number = ((bz * 2 + x) * 2 + y) * 2 + c
            add_rows(grad, number * rows, along_x[bz], rows)
            return carry

        lax.fori_loop(0, 4, add, 0)
        return [
            go(
                block(grad, rows, lax.rem(z + d, 4), x, y, c),
                along_z.at[d - 1],
                recv.at[27 + d],
                spot(lax.rem(z + d, 4), x, y, c),
            )
            for d in range(1, 4)
        ]

    def all_end(grad, rows, along_z, out, got):
        total = grad[pl.ds(pl.multiple_of(mine * rows, 16), rows)].astype(FLOAT)
        for d in range(3):
            got[d].wait_recv()
            total = total + along_z[d].astype(FLOAT)
        out[...] = total

    def quarter_rows(rows, bz, bx):
        return pl.ds(pl.multiple_of((bz * 2 + bx) * 4 * rows, 16), 4 * rows)

    def quarter_x(grad, rows, along_x, recv, d):
        bz = lax.rem(z + d, 4)
        return go(grad.at[quarter_rows(rows, bz, 1 - x)], along_x.at[d - 1], recv.at[d - 1], x_peer)

    def quarter_z(grad, rows, along_x, along_z, recv, got, d):
        got[d - 1].wait_recv()
        bz = lax.rem(z + d, 4)
        add_rows(grad, (bz * 2 + x) * 4 * rows, along_x[d - 1], 4 * rows)
        if d == 4:
            return None
        return go(
            grad.at[quarter_rows(rows, bz, x)],
            along_z.at[d - 1],
            recv.at[3 + d],
            spot(bz, x, y, c),
        )

    def quarter_taps(taps):
        first = 2 * lax.rem(z + 1, 4)
        return [
            (d + 1, span, lambda i, carry: taps(lax.rem(first + i, 9), carry))
            for d, span in enumerate(((0, 3), (3, 6), (6, 8), (8, 9)))
        ]

    def quarter_w(grad, rows, along_z, out, recv, got):
        for copy in got:
            copy.wait_recv()

        own = pl.ds(pl.multiple_of(ha * 4 * rows, 16), 4 * rows)
        value = grad[own].astype(FLOAT)
        for d in range(3):
            value = value + along_z[d].astype(FLOAT)
        grad[own] = value.astype(HALF)
        target = out.at[:, pl.ds(pl.multiple_of(wa * 256, 256), 256)]

        def piece(col):
            return grad.at[pl.ds(pl.multiple_of((ha * 4 + col) * rows, 16), rows)]

        stay(piece(wa), target)
        return [
            go(
                piece(lax.rem(wa + d, 4)),
                target,
                recv.at[6 + d],
                (ha, lax.rem(wa + d, 4)),
            )
            for d in range(1, 4)
        ]

    su = all_core(wu, 32, du_c, r_u, (0, 1, 2, 3))
    su = all_y(wu, 32, du_c, du_y, r_u, (0, 1, 2, 3), su)

    def put_columns(target, s, value):
        put_shifts(target, pl.ds(0, 256), s, value, 0.0, 0.0)

    for e in range(3):
        gs2[e, :, 0] = jnp.zeros((3, 32, 256), HALF)
        gs2[e, :, 17] = jnp.zeros((3, 32, 256), HALF)
    settle(stay(pre2_in, pre))
    settle(own_wa)
    for copy in got_wa:
        copy.wait_recv()

    def two_grad(s, carry):
        rows = pl.ds(pl.multiple_of(128 * s, 128), 128)
        parts = [from_wa[w, rows].astype(FLOAT).reshape(16, 8, 256) for w in range(4)]
        put_columns(gs2, s, jnp.concatenate(parts, axis=1) * gelu_slope(pre[s]))
        return carry

    lax.fori_loop(0, 3, two_grad, 0)
    got_pre1 = stay(pre1_in, pre)
    settle(got_h1)

    def two_weight(t, carry):
        window = gs2[2 - t % 3, :, pl.ds(2 - t // 3, 16)].reshape(1536, 256)
        rows = pl.ds(pl.multiple_of(1024 * t, 1024), 1024)
        d2[rows] = across(joined[...], window).astype(HALF)
        return carry

    s2 = []
    for d, (first, last), taps in quarter_taps(two_weight):
        lax.fori_loop(first, last, taps, 0)
        s2.append(quarter_x(d2, 288, d2_x, r_2, d))
    settle(stay(joined_in, joined))

    def three_weight(t, carry):
        window = gs3[2 - t % 3, :, pl.ds(2 - t // 3, 32)].reshape(1536, 512)
        rows = pl.ds(pl.multiple_of(1024 * t, 1024), 1024)
        d3[rows] = across(joined[...], window).astype(HALF)
        return carry

    lax.fori_loop(0, 5, three_weight, 0)
    s3 = all_core(d3, 288, d3_c, r_3, (0, 1))
    z2 = [quarter_z(d2, 288, d2_x, d2_z, r_2, s2, 1)]
    s3_low = all_y(d3, 288, d3_c, d3_y, r_3, (0, 1), s3)
    pl.semaphore_signal(free, inc=1, device_id=c_peer, device_id_type=MESH)
    lax.fori_loop(5, 9, three_weight, 0)
    pl.semaphore_wait(free, 1)
    s3 = all_core(d3, 288, d3_c, r_3, (2, 3))
    got_x0 = stay(x0_in, joined.at[:, pl.ds(0, 512)])
    z2.append(quarter_z(d2, 288, d2_x, d2_z, r_2, s2, 2))
    settle(got_w2)

    def source_two(s):
        for half in range(2):
            acc[...] = jnp.zeros_like(acc)

            def tap(t, inner_carry):
                window = gs2[2 - t % 3, s, pl.ds(2 - t // 3, 16)].reshape(512, 256)
                rows = pl.ds(pl.multiple_of(1024 * t + 512 * half, 512), 512)
                acc[...] += against(window, slot[rows])
                return inner_carry

            lax.fori_loop(0, 9, tap, 0)
            gs3[half, s, pl.ds(0, 32)] = acc[...].astype(HALF).reshape(32, 16, 512)

    def d_lanes(halves, s, core):
        return gs3.at[halves, s, pl.ds(0, 32), :, pl.ds(pl.multiple_of(256 * core, 256), 256)]

    own_lanes = pl.ds(pl.multiple_of(256 * c, 256), 256)

    def d_pass(s):
        sd[s].wait_recv()
        for half in range(2):
            value = gs3[half, s, pl.ds(0, 32), :, own_lanes].astype(FLOAT)
            value = value + d_core[s, half].astype(FLOAT)
            gs3[half, s, pl.ds(0, 32), :, own_lanes] = value.astype(HALF)
        return go(d_lanes(1 - y, s, c), d_y.at[s], r_d.at[3 + s], y_peer)

    sd = []
    sy = []
    for s in range(3):
        source_two(s)
        sd.append(go(d_lanes(pl.ds(0, 2), s, 1 - c), d_core.at[s], r_d.at[s], c_peer))
        if s > 0:
            sy.append(d_pass(s - 1))
    sy.append(d_pass(2))
    s3_high = all_y(d3, 288, d3_c, d3_y, r_3, (2, 3), s3)
    z2.append(quarter_z(d2, 288, d2_x, d2_z, r_2, s2, 3))
    su = all_x(wu, 32, du_y, du_x, r_u, (0, 1, 2, 3), su)
    settle(got_pre1)
    for s in range(3):
        sy[s].wait_recv()
        value = gs3[y, s, pl.ds(0, 32), :, own_lanes].astype(FLOAT) + d_y[s].astype(FLOAT)
        put_columns(gs2, s, value.reshape(16, 32, 256) * gelu_slope(pre[s]))
    settle(got_x0)

    def one_weight(t, carry):
        window = gs2[2 - t % 3, :, pl.ds(2 - t // 3, 16)].reshape(1536, 256)
        rows = pl.ds(pl.multiple_of(512 * t, 512), 512)
        slot[rows] = across(joined[:, 0:512], window).astype(HALF)
        return carry

    s1 = []
    for d, (first, last), taps in quarter_taps(one_weight):
        lax.fori_loop(first, last, taps, 0)
        s1.append(quarter_x(slot, 144, d1_x, r_1, d))

    quarter_z(d2, 288, d2_x, d2_z, r_2, s2, 4)
    x3 = all_x(d3, 288, d3_y, d3_x, r_3, (0, 1), s3_low)
    su = all_z(wu, 32, du_x, du_z, r_u, su)
    z1 = [quarter_z(slot, 144, d1_x, d1_z, r_1, s1, d) for d in range(1, 4)]
    x3 += all_x(d3, 288, d3_y, d3_x, r_3, (2, 3), s3_high)
    s2 = quarter_w(d2, 288, d2_z, g2, r_2, z2)
    quarter_z(slot, 144, d1_x, d1_z, r_1, s1, 4)
    settle(own_head)
    total = hh[0]
    for step in range(1, 32):
        heads[step - 1].wait_recv()
        total = total + hh[step]
    gh[...] = total
    s3 = all_z(d3, 288, d3_x, d3_z, r_3, x3)
    all_end(wu, 32, du_z, gu, su)
    s1 = quarter_w(slot, 144, d1_z, g1, r_1, z1)
    all_end(d3, 288, d3_z, g3, s3)
    for copy in s2 + s1:
        copy.wait_recv()
    for entry in stays:
        if not entry[1]:
            settle(entry)
    for copy in sends:
        copy.wait_send()


def back(*args):
    anywhere = pl.BlockSpec(memory_space=pl.ANY)
    inside = pl.BlockSpec(memory_space=pltpu.VMEM)
    shape = jax.ShapeDtypeStruct
    dma = pltpu.SemaphoreType.DMA

    def room(*dims):
        return pltpu.VMEM(dims, HALF)

    return pl.pallas_call(
        back_kernel,
        name="back",
        out_shape=(
            shape((288, 512), FLOAT),
            shape((32, 2048), FLOAT),
            shape((288, 1024), HALF),
            shape((144, 1024), HALF),
            shape((16, 128), FLOAT),
        ),
        in_specs=[anywhere] * 11 + [inside] * 4,
        out_specs=[inside, inside, anywhere, anywhere, inside],
        scratch_shapes=[
            room(3, 3, 34, 16, 512),
            room(2, 3, 32, 512),
            room(2, 3, 32, 512),
            pltpu.VMEM((32, 16, 128), FLOAT),
            room(1536, 1024),
            room(9216, 256),
            pltpu.VMEM((512, 512), FLOAT),
            room(384, 2048),
            room(1024, 2048),
            room(384, 1024),
            room(384, 1024),
            room(4, 384, 256),
            pltpu.VMEM((3, 16, 32, 256), FLOAT),
            room(3, 3, 18, 32, 256),
            room(3, 2, 32, 16, 256),
            room(3, 32, 16, 256),
            room(16, 32, 2048),
            room(8, 32, 2048),
            room(4, 32, 2048),
            room(3, 32, 2048),
            room(9216, 512),
            room(8, 288, 512),
            room(8, 288, 512),
            room(4, 288, 512),
            room(3, 288, 512),
            room(9216, 256),
            room(4, 1152, 256),
            room(3, 1152, 256),
            room(4, 576, 256),
            room(3, 576, 256),
            pltpu.VMEM((32, 16, 128), FLOAT),
            dma((144,)),
            dma((40,)),
            dma((2,)),
            dma((3,)),
            dma((6,)),
            dma((31,)),
            dma((31,)),
            dma((10,)),
            dma((10,)),
            dma((31,)),
            pltpu.SemaphoreType.REGULAR,
        ],
        compiler_params=pltpu.CompilerParams(
            collective_id=2, has_side_effects=True, vmem_limit_bytes=64 * 1024 * 1024
        ),
    )(*args)


def dice_slopes(totals):
    union_sum = totals[..., 1] + totals[..., 2] + SMOOTHING
    numerator = 2.0 * totals[..., 0] + SMOOTHING
    dice_score = numerator / union_sum
    loss_value = 1.0 - jnp.mean(dice_score)
    entry_count = float(dice_score.size)
    common = -2.0 / (entry_count * union_sum)
    return (loss_value, jnp.concatenate([common, numerator / (entry_count * union_sum**2)], axis=1))


def sliced_grads(
    bottom, skipped, groups, pixel_mask, labels, weight_one, weight_two, weight_up, weight_three,
    weight_head,
):
    ha = lax.axis_index("ha")
    code = (pixel_mask + 2 * labels).astype(FLOAT).reshape(8, 3, 64)
    pads = [jnp.pad(code, ((0, 0), (0, 5), (64 * odd, 64 - 64 * odd))) for odd in range(2)]
    code = jnp.where(ha % 2 == 0, *pads)
    head_rows = jnp.pad(weight_head.astype(HALF), ((0, 0), (0, 126)))
    x0, h1, h2, joined, w2, wu, w3, pre_one, pre_two, pre_three, hidden_three, logits, code, sums, head = front(
        bottom.reshape(8, 48, 512),
        skipped.reshape(8, 192, 512),
        code,
        weight_one.astype(HALF),
        weight_two.astype(HALF),
        weight_up.astype(HALF),
        weight_three.astype(HALF),
        head_rows,
    )
    wu = wu.reshape(1024, 2048)
    w3 = w3.reshape(9216, 512)
    w2 = w2.reshape(9216, 256)
    member = (groups[:, None] == jnp.arange(GROUPS)[None, :]).astype(FLOAT)
    step = lax.axis_index("ha") * 4 + lax.axis_index("wa")
    origin = (step - jnp.arange(32)) % 32
    at_group = jnp.einsum(
        "dh,hsg->dsg",
        (origin[:, None] // 4 == jnp.arange(8)[None, :]).astype(FLOAT),
        member.reshape(8, 3, GROUPS),
        precision=HIGHEST,
    )
    totals = jnp.einsum("dsg,dsq->gq", at_group, sums[:, :3, :6], precision=HIGHEST)
    totals = totals.reshape(GROUPS, 2, 3)
    loss_value, slopes = dice_slopes(totals)
    member = lax.dynamic_slice_in_dim(member, 3 * ha, 3, axis=0)
    slopes = jnp.einsum("sg,gq->sq", member, slopes, precision=HIGHEST)
    g3, gu, g2, g1, gh = back(
        w3,
        wu,
        w2,
        joined.reshape(1536, 1024),
        h2,
        h1.reshape(1536, 1024),
        x0.reshape(1536, 512),
        pre_one,
        pre_two,
        pre_three,
        hidden_three.reshape(1536, 512),
        logits,
        code,
        jnp.pad(slopes, ((0, 5), (0, 124))),
        head,
    )
    return (loss_value, g1.astype(FLOAT), g2.astype(FLOAT), gu, g3, gh[:, :2])


def body(
    bottom,
    skipped,
    groups,
    pixel_mask,
    labels,
    conv1_weight,
    conv1_momentum,
    conv1_average,
    conv2_weight,
    conv2_momentum,
    conv2_average,
    up_weight,
    up_momentum,
    up_average,
    conv3_weight,
    conv3_momentum,
    conv3_average,
    head_weight,
    head_momentum,
    head_average,
):
    split = bottom.shape[0] == 24 and bottom.shape[1:3] == (2, 8) and bottom.shape[3] == 512
    split = split and (lax.axis_size("ha"), lax.axis_size("wa")) == (8, 4)
    grads = sliced_grads if split else tiled_grads
    loss_value, conv1_grad, conv2_grad, up_grad, conv3_grad, head_grad = grads(
        bottom,
        skipped,
        groups,
        pixel_mask,
        labels,
        conv1_weight,
        conv2_weight,
        up_weight,
        conv3_weight,
        head_weight,
    )
    first = renew_state(conv1_weight, conv1_momentum, conv1_average, conv1_grad, RATE_CONV)
    second = renew_state(conv2_weight, conv2_momentum, conv2_average, conv2_grad, RATE_CONV)
    upward = renew_state(up_weight, up_momentum, up_average, up_grad, RATE_CONV)
    third = renew_state(conv3_weight, conv3_momentum, conv3_average, conv3_grad, RATE_CONV)
    header = renew_state(head_weight, head_momentum, head_average, head_grad, RATE_HEAD)
    return (
        loss_value,
        first[0],
        first[1],
        first[2],
        second[0],
        second[1],
        second[2],
        upward[0],
        upward[1],
        upward[2],
        third[0],
        third[1],
        third[2],
        header[0],
        header[1],
        header[2],
    )


def solution(mesh):
    in_specs = (
        P(None, "ha", "wa", None),
        P(None, "ha", "wa", None),
        P(),
        P(None, "ha", "wa"),
        P(None, "ha", "wa"),
        P(("ha", "wa"), None),
        P(("ha", "wa"), None),
        P(("ha", "wa"), None),
        P(("ha", "wa"), None),
        P(("ha", "wa"), None),
        P(("ha", "wa"), None),
        P(("ha", "wa"), None),
        P(("ha", "wa"), None),
        P(("ha", "wa"), None),
        P(("ha", "wa"), None),
        P(("ha", "wa"), None),
        P(("ha", "wa"), None),
        P(("ha", "wa"), None),
        P(("ha", "wa"), None),
        P(("ha", "wa"), None),
    )
    out_specs = (
        P(),
        P(("ha", "wa"), None),
        P(("ha", "wa"), None),
        P(("ha", "wa"), None),
        P(("ha", "wa"), None),
        P(("ha", "wa"), None),
        P(("ha", "wa"), None),
        P(("ha", "wa"), None),
        P(("ha", "wa"), None),
        P(("ha", "wa"), None),
        P(("ha", "wa"), None),
        P(("ha", "wa"), None),
        P(("ha", "wa"), None),
        P(("ha", "wa"), None),
        P(("ha", "wa"), None),
        P(("ha", "wa"), None),
    )
    return jax.shard_map(body, mesh=mesh, in_specs=in_specs, out_specs=out_specs, check_vma=False)
```

```python
import functools

import jax
import jax.numpy as jnp
from jax import lax
from jax.experimental import pallas as pl
from jax.experimental.pallas import tpu as pltpu
from jax.sharding import PartitionSpec as P

GROUPS = 5


MOMENTUM = 0.9
RATE_CONV = 600.0
RATE_HEAD = 25.0
AVERAGE_DECAY = 0.5
SMOOTHING = 1.0
HIGHEST = lax.Precision.HIGHEST


def with_halo(block, sides, width):
    for axis, dim in sides:
        count = lax.axis_size(axis)
        forward = [(i, i + 1) for i in range(count - 1)]
        backward = [(target, source) for source, target in forward]
        low = lax.ppermute(
            lax.slice_in_dim(block, block.shape[dim] - width, None, axis=dim), axis, forward
        )
        high = lax.ppermute(lax.slice_in_dim(block, 0, width, axis=dim), axis, backward)
        block = jnp.concatenate([low, block, high], axis=dim)
    return block


def smooth(source):
    return jax.nn.gelu(source, approximate=True)


def smooth_back(pre_value, gradient):
    _, pull_back = jax.vjp(smooth, pre_value)
    return pull_back(gradient)[0]


def widened_field(source):
    return with_halo(source, (("ha", 1), ("wa", 2)), 1)


def conv_taps(padded, weight):
    kernel = weight.reshape(3, 3, padded.shape[3], weight.shape[1])
    return lax.conv_general_dilated(
        padded,
        kernel,
        (1, 1),
        "VALID",
        dimension_numbers=("NHWC", "HWIO", "NHWC"),
        preferred_element_type=jnp.float32,
    )


def conv_back(padded, grad_out, weight, back_chan):
    in_chan = padded.shape[3]
    weight_grad = lax.conv_general_dilated(
        padded,
        grad_out,
        (1, 1),
        "VALID",
        dimension_numbers=("CHWN", "IHWO", "HWNC"),
        preferred_element_type=jnp.float32,
    ).reshape(9 * in_chan, grad_out.shape[3])
    if not back_chan:
        return (weight_grad, None)
    grad_padded = widened_field(grad_out)
    kernel = weight.reshape(3, 3, in_chan, weight.shape[1])[::-1, ::-1, :back_chan]
    source_grad = lax.conv_general_dilated(
        grad_padded,
        kernel,
        (1, 1),
        "VALID",
        dimension_numbers=("NHWC", "HWOI", "NHWC"),
        preferred_element_type=jnp.float32,
    )
    return (weight_grad, source_grad)


def upsample(source, weight):
    slices, row_count, col_count, _ = source.shape
    flattened = jnp.einsum("shwc,cq->shwq", source, weight, preferred_element_type=jnp.float32)
    blocks = flattened.reshape(slices, row_count, col_count, 2, 2, -1).transpose(0, 1, 3, 2, 4, 5)
    return blocks.reshape(slices, 2 * row_count, 2 * col_count, -1)


def upsample_back(source, grad_up, weight):
    slices, row_count, col_count, _ = source.shape
    blocks = grad_up.reshape(slices, row_count, 2, col_count, 2, -1).transpose(0, 1, 3, 2, 4, 5)
    flattened = blocks.reshape(slices, row_count, col_count, -1)
    weight_grad = jnp.einsum("shwc,shwq->cq", source, flattened, preferred_element_type=jnp.float32)
    source_grad = jnp.einsum("shwq,cq->shwc", flattened, weight, preferred_element_type=jnp.float32)
    return (weight_grad, source_grad)


def forward(gathered, bottom, skipped):
    weight_one, weight_two, weight_up, weight_three, weight_head = gathered
    pad_zero = widened_field(bottom)
    pre_one = conv_taps(pad_zero, weight_one)
    hidden_one = smooth(pre_one).astype(jnp.bfloat16)
    pad_one = widened_field(hidden_one)
    pre_two = conv_taps(pad_one, weight_two)
    hidden_two = smooth(pre_two).astype(jnp.bfloat16)
    upsampled = upsample(hidden_two, weight_up).astype(jnp.bfloat16)
    joined = jnp.concatenate([upsampled, skipped], axis=3)
    pad_two = widened_field(joined)
    pre_three = conv_taps(pad_two, weight_three)
    hidden_three = smooth(pre_three).astype(jnp.bfloat16)
    logits = jnp.einsum(
        "shwc,ck->shwk", hidden_three, weight_head, preferred_element_type=jnp.float32
    )
    return (
        pad_zero,
        pre_one,
        pad_one,
        pre_two,
        hidden_two,
        pad_two,
        pre_three,
        hidden_three,
        logits,
    )


def pixel_terms(logits, pixel_mask, labels):
    probability = jax.nn.softmax(logits, axis=-1)
    classes = jnp.arange(logits.shape[-1])
    target = (labels[..., None] == classes[None, None, None, :]).astype(jnp.float32)
    weighted = pixel_mask[..., None].astype(jnp.float32)
    return (probability, target, weighted)


def dice_terms(logits, pixel_mask, labels, member):
    probability, target, weighted = pixel_terms(logits, pixel_mask, labels)
    per_slice = jnp.stack(
        [
            jnp.sum(weighted * probability * target, axis=(1, 2)),
            jnp.sum(weighted * probability, axis=(1, 2)),
            jnp.sum(weighted * target, axis=(1, 2)),
        ],
        axis=-1,
    )
    return jnp.einsum("skj,sg->gkj", per_slice, member, precision=HIGHEST)


def dice_back(logits, pixel_mask, labels, member, totals):
    probability, target, weighted = pixel_terms(logits, pixel_mask, labels)
    union_sum = totals[..., 1] + totals[..., 2] + SMOOTHING
    numerator = 2.0 * totals[..., 0] + SMOOTHING
    dice_score = numerator / union_sum
    loss_value = 1.0 - jnp.mean(dice_score)
    entry_count = float(dice_score.size)
    coef_common = -2.0 / (entry_count * union_sum)
    coef_prob = numerator / (entry_count * union_sum * union_sum)
    slice_common = jnp.einsum("sg,gk->sk", member, coef_common, precision=HIGHEST)
    slice_prob = jnp.einsum("sg,gk->sk", member, coef_prob, precision=HIGHEST)
    grad_prob = weighted * (target * slice_common[:, None, None, :] + slice_prob[:, None, None, :])
    inner = jnp.sum(probability * grad_prob, axis=-1, keepdims=True)
    grad_logits = (probability * (grad_prob - inner)).astype(jnp.bfloat16)
    return (loss_value, grad_logits)


def renew_state(weight, moment, average, gradient, rate):
    moment_new = MOMENTUM * moment + gradient
    weight_new = weight - rate * (gradient + MOMENTUM * moment_new)
    average_new = AVERAGE_DECAY * average + (1.0 - AVERAGE_DECAY) * weight_new
    return (weight_new, moment_new, average_new)


def tiled_grads(
    bottom, skipped, groups, pixel_mask, labels, conv1_weight, conv2_weight, up_weight, conv3_weight,
    head_weight,
):
    gathered = (
        lax.all_gather(conv1_weight.astype(jnp.bfloat16), ("ha", "wa"), axis=0, tiled=True),
        lax.all_gather(conv2_weight.astype(jnp.bfloat16), ("ha", "wa"), axis=0, tiled=True),
        lax.all_gather(up_weight.astype(jnp.bfloat16), ("ha", "wa"), axis=0, tiled=True),
        lax.all_gather(conv3_weight.astype(jnp.bfloat16), ("ha", "wa"), axis=0, tiled=True),
        lax.all_gather(head_weight.astype(jnp.bfloat16), ("ha", "wa"), axis=0, tiled=True),
    )
    member = (groups[:, None] == jnp.arange(GROUPS)[None, :]).astype(jnp.float32)
    kept = forward(gathered, bottom, skipped)
    partial_sums = dice_terms(kept[8], pixel_mask, labels, member)
    totals = lax.psum(partial_sums, ("ha", "wa"))
    pad_zero, pre_one, pad_one, pre_two, hidden_two, pad_two, pre_three, hidden_three, logits = kept
    weight_one, weight_two, weight_up, weight_three, weight_head = gathered
    loss_value, grad_logits = dice_back(logits, pixel_mask, labels, member, totals)
    head_grad = jnp.einsum(
        "shwc,shwk->ck", hidden_three, grad_logits, preferred_element_type=jnp.float32
    )
    grad_hidden = jnp.einsum(
        "shwk,ck->shwc", grad_logits, weight_head, preferred_element_type=jnp.float32
    )
    grad_pre_three = smooth_back(pre_three, grad_hidden).astype(jnp.bfloat16)
    conv3_grad, grad_joined = conv_back(pad_two, grad_pre_three, weight_three, weight_up.shape[1] // 4)
    grad_upsampled = grad_joined.astype(jnp.bfloat16)
    up_grad, grad_hidden_two = upsample_back(hidden_two, grad_upsampled, weight_up)
    grad_pre_two = smooth_back(pre_two, grad_hidden_two).astype(jnp.bfloat16)
    conv2_grad, grad_hidden_one = conv_back(pad_one, grad_pre_two, weight_two, pad_one.shape[3])
    grad_pre_one = smooth_back(pre_one, grad_hidden_one).astype(jnp.bfloat16)
    conv1_grad, _ = conv_back(pad_zero, grad_pre_one, weight_one, 0)
    sums = (
        lax.psum_scatter(conv1_grad.astype(jnp.bfloat16), ("ha", "wa"), scatter_dimension=0, tiled=True),
        lax.psum_scatter(conv2_grad.astype(jnp.bfloat16), ("ha", "wa"), scatter_dimension=0, tiled=True),
        lax.psum_scatter(up_grad.astype(jnp.bfloat16), ("ha", "wa"), scatter_dimension=0, tiled=True),
        lax.psum_scatter(conv3_grad.astype(jnp.bfloat16), ("ha", "wa"), scatter_dimension=0, tiled=True),
        lax.psum_scatter(head_grad.astype(jnp.bfloat16), ("ha", "wa"), scatter_dimension=0, tiled=True),
    )
    return (loss_value, *[s.astype(jnp.float32) for s in sums])


MESH = pl.DeviceIdType.MESH
FLOAT = jnp.float32
HALF = jnp.bfloat16


def place():
    row, col = (lax.axis_index("ha"), lax.axis_index("wa"))
    return (row // 2, row % 2, col // 2, col % 2)


def spot(z, x, y, c):
    return (2 * z + x, 2 * y + c)


def greet_all():
    row, col = (lax.axis_index("ha"), lax.axis_index("wa"))
    rows, cols = (lax.axis_size("ha"), lax.axis_size("wa"))
    barrier = pltpu.get_barrier_semaphore()
    for step in range(1, rows * cols):
        other = lax.rem(row * cols + col + step, rows * cols)
        pl.semaphore_signal(
            barrier, inc=1, device_id=(other // cols, lax.rem(other, cols)), device_id_type=MESH
        )
    pl.semaphore_wait(barrier, rows * cols - 1)


def remote(source, target, send_sem, recv_sem, device):
    return pltpu.make_async_remote_copy(
        src_ref=source,
        dst_ref=target,
        send_sem=send_sem,
        recv_sem=recv_sem,
        device_id=device,
        device_id_type=MESH,
    )


def gelu_of(value):
    inner = 0.7978845608028654 * (value + 0.044715 * value * value * value)
    return 0.5 * value * (1.0 + jnp.tanh(inner))


def conv_slice(source, weight, parts, index, chan):
    parts[...] = jnp.zeros_like(parts)

    def row_tap(r, carry):
        window = source[index, pl.ds(r, 16)].reshape(512, chan)
        for c in range(3):
            start = pl.multiple_of((3 * r + c) * chan, chan)
            parts[c] += jnp.dot(
                window, weight[pl.ds(start, chan), :], preferred_element_type=FLOAT
            )
        return carry

    lax.fori_loop(0, 3, row_tap, 0)
    shape = (16, 32, 256)
    column = lax.broadcasted_iota(jnp.int32, shape, 1)
    low = jnp.where(column > 0, pltpu.roll(parts[0].reshape(shape), 1, 1), 0.0)
    high = jnp.where(column < 31, pltpu.roll(parts[2].reshape(shape), 31, 1), 0.0)
    return parts[1].reshape(shape) + low + high


def put_shifts(target, lanes, s, value, left, right):
    column = lax.broadcasted_iota(jnp.int32, value.shape, 1)
    last = value.shape[1] - 1
    rows = pl.ds(1, value.shape[0])
    low = jnp.where(column > 0, pltpu.roll(value, 1, 1), left)
    target[0, s, rows, :, lanes] = low.astype(HALF)
    target[1, s, rows, :, lanes] = value.astype(HALF)
    high = jnp.where(column < last, pltpu.roll(value, last, 1), right)
    target[2, s, rows, :, lanes] = high.astype(HALF)


def put_tile(target, first, s, value, left, right):
    column = lax.broadcasted_iota(jnp.int32, value.shape, 1)
    last = value.shape[1] - 1
    rows = pl.ds(1, value.shape[0])
    low = jnp.where(column > 0, pltpu.roll(value, 1, 1), left)
    high = jnp.where(column < last, pltpu.roll(value, last, 1), right)
    for shift, part in enumerate((low, value, high)):
        target[s, rows, :, pl.ds(1024 * shift + first, 512)] = part.astype(HALF)


def front_kernel(
    compute,
    bot, skip, code, w1, w2, wu, w3, wh,
    x0_out, h1_out, h2_out, joined_out, w2_out, wu_out, w3_out, pre1_out, pre2_out, pre3_out,
    hidden_out, logit_out, code_out, sums_out, head_out,
    xr, x0, w1q, w2q, h1s, h1, parts, h2s, h2v, wuv, w3v, skv, rims, rims_got, tiles, whv,
    pre1, pre2, pre3, hidden_all,
    send, here, r_bot, r_grp, r_w1, r_w2, r_h1, r_h2, r_skip, r_wh, r_w3, r_wu,
    r_code, r_rim, r_sum,
):
    z, x, y, c = place()
    ha, wa = (2 * z + x, 2 * y + c)
    x_peer, y_peer, c_peer = (spot(z, 1 - x, y, c), spot(z, x, 1 - y, c), spot(z, x, y, 1 - c))
    mine = ha * 4 + wa
    greet_all()
    sends = []
    stays = []

    def go(source, target, recv_sem, device):
        copy = remote(source, target, send.at[len(sends)], recv_sem, device)
        copy.start()
        sends.append((copy, None))
        return copy

    def stay(source, target):
        copy = pltpu.make_async_copy(source, target, here.at[len(stays)])
        copy.start()
        stays.append([copy, False])
        return stays[-1]

    def settle(*entries):
        for entry in entries:
            entry[0].wait()
            entry[1] = True

    def arrive(*copies):
        for copy in copies:
            copy.wait_recv()

    def go_if(when, source, target, recv_sem, device):
        copy = remote(source, target, send.at[len(sends)], recv_sem, device)
        pl.when(when)(lambda: copy.start())
        sends.append((copy, when))
        return (copy, when)

    def arrive_if(copy, when):
        pl.when(when)(lambda: copy.wait_recv())

    above, below = (spot(lax.rem(z + 1, 4), x, y, c), spot(lax.rem(z + 3, 4), x, y, c))

    def line_start(part, line):
        go_if(z < 3, part(z), part(z), line.at[0], above)
        go_if(z > 0, part(z), part(z), line.at[3], below)

    def line_hop(part, line, j, passes):
        for first, other, more, last, neighbour in (
            (0, lax.rem(z + 3 - j, 4), z >= j + 1, z < 3, above),
            (3, lax.rem(z + 1 + j, 4), z <= 2 - j, z > 0, below),
        ):
            piece = part(other)
            arrive_if(remote(piece, piece, send.at[0], line.at[first + j], x_peer), more)
            if j < 2:
                go_if(
                    jnp.logical_and(more, last), piece, piece, line.at[first + j + 1], neighbour
                )
            for recv, got, device in passes:
                got.append(go_if(more, piece, piece, recv.at[1 + first + j], device))

    def swap(shard, whole, first, count, recv):
        source_rows = pl.ds(first, count)
        target = whole.at[ha, wa, source_rows]
        lanes = [pl.ds(pl.multiple_of(lax.rem(wa + dw, 4) * 256, 256), 256) for dw in range(4)]
        own = stay(shard.at[source_rows, lanes[0]], target)
        copies = [
            go(shard.at[source_rows, lanes[dw]], target, recv.at[dw], (ha, lax.rem(wa + dw, 4)))
            for dw in range(1, 4)
        ]
        return (own, copies)

    class Quarter:
        def __init__(self, shard, whole, first, count, line, recv):
            self.line, self.recv, self.got = (line, recv, [])
            self.part = lambda bz: whole.at[bz * 2 + x, :, pl.ds(first, count)]
            self.swapped = swap(shard, whole, first, count, recv.at[1])

        def start(self):
            settle(self.swapped[0])
            arrive(*self.swapped[1])
            line_start(self.part, self.line)
            own = self.part(z)
            self.got.append((go(own, own, self.recv.at[0, 0], x_peer), None))

        def hop(self, j):
            line_hop(self.part, self.line, j, [(self.recv.at[0], self.got, x_peer)])

        def done(self):
            for copy, when in self.got:
                if when is None:
                    copy.wait_recv()
                else:
                    arrive_if(copy, when)

    class Whole:
        def __init__(self, shard, whole, line, recv):
            self.whole, self.line, self.recv = (whole, line, recv)
            self.part = lambda bz: whole.at[bz, x, y, c]
            self.own = stay(shard, self.part(z))
            self.along_x, self.along_y, self.core = ([], [], [])

        def start(self):
            settle(self.own)
            line_start(self.part, self.line)
            own = self.part(z)
            self.along_x.append((go(own, own, self.recv.at[0, 0], x_peer), None))
            self.along_y.append((go(own, own, self.recv.at[1, 0], y_peer), None))
            self.core.append((go(own, own, self.recv.at[2, 0], c_peer), None))

        def hop(self, j):
            passes = [
                (self.recv.at[0], self.along_x, x_peer),
                (self.recv.at[1], self.along_y, y_peer),
                (self.recv.at[2], self.core, c_peer),
            ]
            line_hop(self.part, self.line, j, passes)

        def wait(self, got):
            for copy, when in got:
                if when is None:
                    copy.wait_recv()
                else:
                    arrive_if(copy, when)

        def turn(self):
            self.wait(self.along_x)
            part = self.whole.at[:, 1 - x, y, c]
            self.last = go(part, part, self.recv.at[1, 7], y_peer)
            self.core.append((go(part, part, self.recv.at[2, 7], c_peer), None))

        def finish(self):
            self.wait(self.along_y)
            part = self.whole.at[:, x, 1 - y, c]
            self.core.append((go(part, part, self.recv.at[0, 7], c_peer), None))
            arrive(self.last)
            part = self.whole.at[:, 1 - x, 1 - y, c]
            self.core.append((go(part, part, self.recv.at[3, 0], c_peer), None))

        def done(self):
            self.wait(self.core)

    own_bot = stay(bot.at[ha], xr.at[ha, wa])
    bots = [
        go(bot.at[lax.rem(ha + d, 8)], xr.at[ha, wa], r_bot.at[d - 1], (lax.rem(ha + d, 8), wa))
        for d in range(1, 8)
    ]
    whole_three = Whole(w3, w3v, r_w3.at[4, pl.ds(0, 6)], r_w3)
    whole_up = Whole(wu, wuv, r_wu.at[4, pl.ds(0, 6)], r_wu)
    one_part = Quarter(w1, w1q, 0, 144, r_w1.at[2], r_w1)
    two_low = Quarter(w2, w2q, 0, 144, r_w2.at[0, 2], r_w2.at[0])
    two_high = Quarter(w2, w2q, 144, 144, r_w2.at[1, 2], r_w2.at[1])
    whole_three.start()
    whole_up.start()
    settle(own_bot)
    arrive(*bots)
    to_c = go(xr.at[:, wa], xr.at[:, wa], r_grp.at[0], c_peer)
    to_y = go(xr.at[:, wa], xr.at[:, wa], r_grp.at[1], y_peer)
    whole_three.hop(0)
    whole_up.hop(0)
    one_part.start()
    whole_three.hop(1)
    whole_up.hop(1)
    if compute:
        x0[:, 0] = jnp.zeros((3, 32, 512), HALF)
        x0[:, 17] = jnp.zeros((3, 32, 512), HALF)
        h1[:, 0] = jnp.zeros((3, 32, 1024), HALF)
        h1[:, 17] = jnp.zeros((3, 32, 1024), HALF)
        tiles[:, 0] = jnp.zeros((3, 16, 3072), HALF)
        tiles[:, 33] = jnp.zeros((3, 16, 3072), HALF)
    whole_three.hop(2)
    two_low.start()
    whole_up.hop(2)
    one_part.hop(0)
    two_high.start()
    arrive(to_y)
    part = xr.at[:, 2 * (1 - y) + c]
    on_c = go(part, part, r_grp.at[2], c_peer)
    arrive(to_c, on_c)

    if compute:

        def reorder(h, carry):
            block = xr[h].astype(FLOAT).reshape(4, 3, 2, 8, 512)
            for s in range(3):
                for r in range(2):
                    row = jnp.concatenate([block[w, s, r] for w in range(4)], axis=0)
                    x0[s, 2 * h + 1 + r] = row.astype(HALF)
            return carry

        lax.fori_loop(0, 8, reorder, 0)
    stay(x0.at[:, pl.ds(1, 16)], x0_out)
    one_part.hop(1)
    two_low.hop(0)
    one_part.hop(2)
    two_high.hop(0)
    whole_three.turn()
    two_low.hop(1)
    two_high.hop(1)
    whole_up.turn()
    own_skip = stay(skip.at[ha], skv.at[ha])
    skips = [
        go(skip.at[lax.rem(ha + d, 8)], skv.at[ha], r_skip.at[d - 1], (lax.rem(ha + d, 8), wa))
        for d in range(1, 8)
    ]
    two_low.hop(2)
    one_part.done()
    if compute:

        def one(s, carry):
            value = conv_slice(x0, w1q.reshape(4608, 256), parts, s, 512)
            pre1[s] = value
            h1s[s] = gelu_of(value).astype(HALF)
            return carry

        lax.fori_loop(0, 3, one, 0)

    def lanes(col):
        return h1.at[:, pl.ds(1, 16), :, pl.ds(pl.multiple_of(col * 256, 256), 256)]

    own_h1 = stay(h1s, lanes(wa))
    stay(pre1, pre1_out)
    h1_c = go(h1s, lanes(wa), r_h1.at[0], c_peer)
    h1_y = go(h1s, lanes(wa), r_h1.at[1], y_peer)

    own_code = stay(code.at[ha], code_out.at[ha])
    codes = [
        go(code.at[lax.rem(ha + d, 8)], code_out.at[ha], r_code.at[d - 1], (lax.rem(ha + d, 8), wa))
        for d in range(1, 8)
    ]
    own_head = stay(wh, whv.at[mine])
    heads = []
    for step in range(1, 32):
        other = lax.rem(mine + step, 32)
        heads.append(go(wh, whv.at[mine], r_wh.at[step - 1], (other // 4, lax.rem(other, 4))))
    two_high.hop(2)
    whole_three.finish()
    whole_up.finish()
    arrive(h1_y)
    h1_on = go(lanes(2 * (1 - y) + c), lanes(2 * (1 - y) + c), r_h1.at[2], c_peer)
    settle(own_h1)
    arrive(h1_c, h1_on)
    stay(h1.at[:, pl.ds(1, 16)], h1_out)
    two_low.done()
    two_high.done()
    stay(w2q, w2_out)
    if compute:

        def two(s, carry):
            value = conv_slice(h1, w2q.reshape(9216, 256), parts, s, 1024)
            pre2[s] = value
            hidden = gelu_of(value)
            for w in range(4):
                tile = hidden[:, 8 * w : 8 * w + 8].reshape(128, 256)
                h2s[w, pl.ds(pl.multiple_of(s * 128, 128), 128)] = tile.astype(HALF)
                left = hidden[:, 8 * w - 1] if w > 0 else jnp.zeros((16, 256), FLOAT)
                h2s[w, pl.ds(pl.multiple_of(384 + s * 16, 16), 16)] = left.astype(HALF)
                right = hidden[:, 8 * w + 8] if w < 3 else jnp.zeros((16, 256), FLOAT)
                h2s[w, pl.ds(pl.multiple_of(432 + s * 16, 16), 16)] = right.astype(HALF)
            return carry

        lax.fori_loop(0, 3, two, 0)
    h2_lanes = h2v.at[:, pl.ds(pl.multiple_of(wa * 256, 256), 256)]
    own_h2 = stay(h2s.at[wa], h2_lanes)
    stay(pre2, pre2_out)
    h2_got = [
        go(h2s.at[lax.rem(wa + d, 4)], h2_lanes, r_h2.at[d - 1], (ha, lax.rem(wa + d, 4)))
        for d in range(1, 4)
    ]

    settle(own_skip)
    arrive(*skips)

    def skip_slice(s):
        return skv[:, 64 * s : 64 * s + 64].astype(FLOAT).reshape(32, 16, 512)

    if compute:
        for s in range(3):
            value = skip_slice(s)
            rims[0, s] = value[:, 0].astype(HALF)
            rims[1, s] = value[:, 15].astype(HALF)
    before = (ha, lax.rem(wa + 3, 4))
    after = (ha, lax.rem(wa + 1, 4))
    rim_right = go(rims.at[0], rims_got.at[1], r_rim.at[1], before)
    rim_left = go(rims.at[1], rims_got.at[0], r_rim.at[0], after)
    arrive(rim_right, rim_left)
    if compute:
        for s in range(3):
            left = jnp.where(wa > 0, rims_got[0, s].astype(FLOAT), 0.0)
            right = jnp.where(wa < 3, rims_got[1, s].astype(FLOAT), 0.0)
            put_tile(tiles, 512, s, skip_slice(s), left[:, None, :], right[:, None, :])
    whole_three.done()
    stay(w3v, w3_out)
    settle(own_h2)
    arrive(*h2_got)
    stay(h2v, h2_out)
    whole_up.done()
    stay(wuv, wu_out)
    if compute:
        order = lax.broadcasted_iota(jnp.int32, (256, 256), 1)
        inner = order % 128
        pick = (inner // 8) * 16 + (inner % 8) * 2 + order // 128
        woven = jnp.where(lax.broadcasted_iota(jnp.int32, (256, 256), 0) == pick, 1.0, 0.0)
        woven = woven.astype(HALF)
        wide = wuv.reshape(1024, 2048)
        for s in range(3):
            fine, sides = ([], ([], []))
            for a in range(2):
                weight = wide[:, 1024 * a : 1024 * a + 1024]
                flat = jnp.dot(
                    h2v[128 * s : 128 * s + 128], weight, preferred_element_type=FLOAT
                ).astype(HALF)
                flat = jnp.concatenate([flat[:, :512], flat[:, 512:]], axis=0)
                flat = jnp.dot(woven, flat, preferred_element_type=FLOAT)
                fine.append(flat.reshape(16, 16, 512))
                for side in range(2):
                    start = 384 + 48 * side + 16 * s
                    rim = jnp.dot(
                        h2v[start : start + 16],
                        weight[:, 512 * (1 - side) : 512 * (1 - side) + 512],
                        preferred_element_type=FLOAT,
                    )
                    sides[side].append(rim.astype(HALF).astype(FLOAT)[:, None, :])
            value = jnp.stack(fine, axis=1).reshape(32, 16, 512)
            left, right = [jnp.stack(side, axis=1).reshape(32, 1, 512) for side in sides]
            put_tile(tiles, 0, s, value, left, right)

    stay(tiles.at[:, pl.ds(1, 32), :, pl.ds(1024, 1024)], joined_out)
    settle(own_head)
    arrive(*heads)
    settle(own_code)
    arrive(*codes)
    if compute:
        head = whv.reshape(512, 128)[...].astype(FLOAT).T[:16].astype(HALF)
        head_out[...] = head
        row = lax.broadcasted_iota(jnp.int32, (8, 128), 0)
        lane = lax.broadcasted_iota(jnp.int32, (8, 128), 1)
        sums_out[0] = jnp.zeros((8, 128), FLOAT)

        rows = w3v.reshape(9216, 512)

        def three(s, carry):
            for r in range(3):
                window = tiles[s, r : r + 32].reshape(512, 3072)
                value = jnp.dot(
                    window, rows[3072 * r : 3072 * r + 3072, :], preferred_element_type=FLOAT
                )
                if r == 0:
                    pre3[s] = value
                else:
                    pre3[s] += value
            hidden = gelu_of(pre3[s]).astype(HALF)
            hidden_all[s] = hidden
            logits = lax.dot_general(
                head, hidden, (((1,), (1,)), ((), ())), preferred_element_type=FLOAT
            )
            logit_out[s] = logits
            return carry

        lax.fori_loop(0, 3, three, 0)
        stay(pre3, pre3_out)
        stay(hidden_all, hidden_out)
        total = jnp.zeros((8, 128), FLOAT)
        for s in range(3):
            probability, target, weighted = class_terms(logit_out, code_out, s)
            for k in range(2):
                terms = (
                    weighted * probability[k] * target[k],
                    weighted * probability[k],
                    weighted * target[k],
                )
                for j, term in enumerate(terms):
                    value = jnp.sum(term, axis=1, keepdims=True)
                    here_is = jnp.logical_and(row == s, lane == 3 * k + j)
                    total = total + jnp.where(here_is, value, 0.0)
        sums_out[0] = total
    sums = []
    for step in range(1, 32):
        other = lax.rem(mine + step, 32)
        sums.append(
            go(
                sums_out.at[0],
                sums_out.at[step],
                r_sum.at[step - 1],
                (other // 4, lax.rem(other, 4)),
            )
        )
    arrive(*sums)
    for entry in stays:
        if not entry[1]:
            settle(entry)
    for copy, when in sends:
        if when is None:
            copy.wait_send()
        else:
            pl.when(when)(copy.wait_send)


def class_terms(logits, codes, s):
    pieces = [codes[2 * q, s : s + 1] + codes[2 * q + 1, s : s + 1] for q in range(4)]
    both = jnp.concatenate(pieces, axis=1)
    label = jnp.where(both >= 2.0, 1.0, 0.0)
    weighted = both - 2.0 * label
    first, second = (logits[s, 0:1], logits[s, 1:2])
    top = jnp.maximum(first, second)
    first, second = (jnp.exp(first - top), jnp.exp(second - top))
    scale = 1.0 / (first + second)
    return ((first * scale, second * scale), (1.0 - label, label), weighted)


def front(bot, skip, code, w1, w2, wu, w3, wh, compute=True):
    anywhere = pl.BlockSpec(memory_space=pl.ANY)
    inside = pl.BlockSpec(memory_space=pltpu.VMEM)
    shape = jax.ShapeDtypeStruct
    dma = pltpu.SemaphoreType.DMA

    def room(*dims):
        return pltpu.VMEM(dims, HALF)

    return pl.pallas_call(
        functools.partial(front_kernel, compute),
        name="front",
        out_shape=(
            shape((3, 16, 32, 512), HALF),
            shape((3, 16, 32, 1024), HALF),
            shape((480, 1024), HALF),
            shape((3, 32, 16, 1024), HALF),
            shape((8, 4, 288, 256), HALF),
            shape((4, 2, 2, 2, 32, 2048), HALF),
            shape((4, 2, 2, 2, 288, 512), HALF),
            shape((3, 16, 32, 256), FLOAT),
            shape((3, 16, 32, 256), FLOAT),
            shape((3, 512, 512), FLOAT),
            shape((3, 512, 512), HALF),
            shape((3, 16, 512), FLOAT),
            shape((8, 8, 128), FLOAT),
            shape((32, 8, 128), FLOAT),
            shape((16, 512), HALF),
        ),
        in_specs=[anywhere] * 8,
        out_specs=[anywhere] * 11 + [inside] * 4,
        scratch_shapes=[
            room(8, 4, 48, 512),
            room(3, 18, 32, 512),
            room(8, 4, 144, 256),
            room(8, 4, 288, 256),
            room(3, 16, 32, 256),
            room(3, 18, 32, 1024),
            pltpu.VMEM((3, 512, 256), FLOAT),
            room(4, 480, 256),
            room(480, 1024),
            room(4, 2, 2, 2, 32, 2048),
            room(4, 2, 2, 2, 288, 512),
            room(8, 192, 512),
            room(2, 3, 32, 512),
            room(2, 3, 32, 512),
            room(3, 34, 16, 3072),
            room(32, 16, 128),
            pltpu.VMEM((3, 16, 32, 256), FLOAT),
            pltpu.VMEM((3, 16, 32, 256), FLOAT),
            pltpu.VMEM((3, 512, 512), FLOAT),
            room(3, 512, 512),
            dma((256,)),
            dma((24,)),
            dma((7,)),
            dma((3,)),
            dma((3, 8)),
            dma((2, 3, 8)),
            dma((3,)),
            dma((3,)),
            dma((7,)),
            dma((31,)),
            dma((5, 8)),
            dma((5, 8)),
            dma((7,)),
            dma((2,)),
            dma((31,)),
        ],
        compiler_params=pltpu.CompilerParams(
            collective_id=0, has_side_effects=True, vmem_limit_bytes=64 * 1024 * 1024
        ),
    )(bot, skip, code, w1, w2, wu, w3, wh)


def gelu_slope(value):
    square = value * value
    bend = jnp.tanh(0.7978845608028654 * value * (1.0 + 0.044715 * square))
    rise = 0.7978845608028654 * (1.0 + 3.0 * 0.044715 * square)
    return 0.5 * (1.0 + bend) + 0.5 * value * (1.0 - bend * bend) * rise


def across(source, window):
    return lax.dot_general(source, window, (((0,), (0,)), ((), ())), preferred_element_type=FLOAT)


def against(window, weight):
    return lax.dot_general(window, weight, (((1,), (1,)), ((), ())), preferred_element_type=FLOAT)


def add_rows(total, start, term, rows):
    where = pl.ds(pl.multiple_of(start, 16), rows)
    total[where] = (total[where].astype(FLOAT) + term.astype(FLOAT)).astype(HALF)


def back_kernel(
    w3_in, wu_in, w2_in, joined_in, h2_in, h1_in, x0_in, pre1_in, pre2_in, pre3_in, hidden_in,
    logits, codes, slopes, head,
    g3, gu, g2, g1, gh,
    gs3, rims, rims_got, dh, joined, slot, acc, flat, wu, h2, gh2, from_wa, pre, gs2, d_core, d_y,
    du_c, du_y, du_x, du_z, d3, d3_c, d3_y, d3_x, d3_z, d2, d2_x, d2_z, d1_x, d1_z, hh,
    send, here, r_rim, r_wa, r_d, r_u, r_3, r_2, r_1, r_h, free,
):
    z, x, y, c = place()
    ha, wa = (2 * z + x, 2 * y + c)
    x_peer, y_peer, c_peer = (spot(z, 1 - x, y, c), spot(z, x, 1 - y, c), spot(z, x, y, 1 - c))
    mine = ha * 4 + wa
    sends = []
    stays = []

    def go(source, target, recv_sem, device):
        copy = remote(source, target, send.at[len(sends)], recv_sem, device)
        copy.start()
        sends.append(copy)
        return copy

    def stay(source, target):
        copy = pltpu.make_async_copy(source, target, here.at[len(stays)])
        copy.start()
        stays.append([copy, False])
        return stays[-1]

    def settle(*entries):
        for entry in entries:
            entry[0].wait()
            entry[1] = True

    got_hidden = stay(hidden_in, d3.at[pl.ds(0, 1536)])
    got_pre3 = stay(pre3_in.at[0], acc)
    got_w3 = [
        stay(w3_in.at[pl.ds(1024 * t, 512)], d3.at[pl.ds(4608 + 512 * t, 512)]) for t in range(9)
    ]
    got_w2 = stay(w2_in, slot)
    got_wu = stay(wu_in, wu)
    got_h2 = stay(h2_in.at[pl.ds(0, 384)], h2)
    got_h1 = stay(h1_in, joined)
    greet_all()

    settle(got_hidden)
    head_sum = jnp.zeros((16, 512), FLOAT)
    class_row = lax.broadcasted_iota(jnp.int32, (16, 512), 0)
    for e in range(3):
        gs3[e, :, 0] = jnp.zeros((3, 16, 512), HALF)
        gs3[e, :, 33] = jnp.zeros((3, 16, 512), HALF)
    for s in range(3):
        probability, target, weighted = class_terms(logits, codes, s)
        grads = [
            weighted * (target[k] * slopes[s : s + 1, k : k + 1] + slopes[s : s + 1, 2 + k : 3 + k])
            for k in range(2)
        ]
        inner = probability[0] * grads[0] + probability[1] * grads[1]
        grads = [probability[k] * (grads[k] - inner) for k in range(2)]
        grads = jnp.where(class_row == 0, grads[0], jnp.where(class_row == 1, grads[1], 0.0))
        grads = grads.astype(HALF)
        hidden = d3[512 * s : 512 * s + 512]
        head_sum = head_sum + jnp.dot(grads, hidden, preferred_element_type=FLOAT)
        settle(got_pre3)
        value = (across(grads, head[...]) * gelu_slope(acc[...])).astype(HALF)
        if s < 2:
            got_pre3 = stay(pre3_in.at[s + 1], acc)
        gs3[1, s, 1:33] = value.reshape(32, 16, 512)
        value = value.astype(FLOAT).reshape(32, 16, 512)
        rims[0, s] = value[:, 0].astype(HALF)
        rims[1, s] = value[:, 15].astype(HALF)
    before = (ha, lax.rem(wa + 3, 4))
    after = (ha, lax.rem(wa + 1, 4))
    rim_right = go(rims.at[0], rims_got.at[1], r_rim.at[1], before)
    rim_left = go(rims.at[1], rims_got.at[0], r_rim.at[0], after)
    rows = jnp.concatenate([head_sum, jnp.zeros((112, 512), FLOAT)], axis=0)
    dh[...] = rows.T.reshape(32, 16, 128)
    own_head = stay(dh.at[mine], hh.at[0])
    heads = []
    for step in range(1, 32):
        other = lax.rem(mine + step, 32)
        heads.append(
            go(dh.at[other], hh.at[step], r_h.at[step - 1], (other // 4, lax.rem(other, 4)))
        )
    rim_right.wait_recv()
    rim_left.wait_recv()
    for s in range(3):
        left = jnp.where(wa > 0, rims_got[0, s].astype(FLOAT), 0.0)
        right = jnp.where(wa < 3, rims_got[1, s].astype(FLOAT), 0.0)
        value = gs3[1, s, 1:33].astype(FLOAT)
        put_shifts(gs3, pl.ds(0, 512), s, value, left[:, None, :], right[:, None, :])

    order = lax.broadcasted_iota(jnp.int32, (256, 256), 0)
    inner = order % 128
    pick = (inner // 8) * 16 + (inner % 8) * 2 + order // 128
    apart = jnp.where(lax.broadcasted_iota(jnp.int32, (256, 256), 1) == pick, 1.0, 0.0).astype(HALF)
    settle(*got_w3)

    def three_source(s, carry):
        acc[...] = jnp.zeros_like(acc)

        def tap(t, inner_carry):
            window = gs3[2 - t % 3, s, pl.ds(2 - t // 3, 32)].reshape(512, 512)
            acc[...] += against(window, d3[pl.ds(pl.multiple_of(4608 + 512 * t, 512), 512)])
            return inner_carry

        lax.fori_loop(0, 9, tap, 0)
        fine = acc[...].astype(HALF).reshape(16, 2, 16, 512)
        for a in range(2):
            parted = jnp.dot(
                apart, fine[:, a].reshape(256, 512), preferred_element_type=FLOAT
            ).astype(HALF)
            for b in range(2):
                rows = pl.ds(pl.multiple_of(128 * s, 128), 128)
                flat[rows, pl.ds(512 * (2 * a + b), 512)] = parted[128 * b : 128 * b + 128]
        return carry

    lax.fori_loop(0, 3, three_source, 0)
    settle(got_wu, got_h2)
    for part in range(4):
        lanes = slice(256 * part, 256 * part + 256)
        gh2[:, lanes] = against(flat[...], wu[lanes, :]).astype(HALF)

    def wa_lanes(col):
        return gh2.at[:, pl.ds(pl.multiple_of(col * 256, 256), 256)]

    own_wa = stay(wa_lanes(wa), from_wa.at[wa])
    got_wa = [
        go(
            wa_lanes(lax.rem(wa + d, 4)),
            from_wa.at[wa],
            r_wa.at[d - 1],
            (ha, lax.rem(wa + d, 4)),
        )
        for d in range(1, 4)
    ]
    for part in range(4):
        lanes = slice(512 * part, 512 * part + 512)
        wu[:, lanes] = across(h2[...], flat[:, lanes]).astype(HALF)

    def block(grad, rows, bz, bx, by, bc):
        number = ((bz * 2 + bx) * 2 + by) * 2 + bc
        return grad.at[pl.ds(pl.multiple_of(number * rows, 16), rows)]

    def all_core(grad, rows, core, recv, some):
        return [
            go(
                block(grad, rows, bz, bx, by, 1 - c),
                core.at[((bz - some[0]) * 2 + bx) * 2 + by],
                recv.at[((bz - some[0]) * 2 + bx) * 2 + by],
                c_peer,
            )
            for bz in some
            for bx in range(2)
            for by in range(2)
        ]

    def all_y(grad, rows, core, along_y, recv, some, got):
        for copy in got:
            copy.wait_recv()

        def step(by):
            def add(i, carry):
                number = (((some[0] * 2 + i) * 2) + by) * 2 + c
                add_rows(grad, number * rows, core[i * 2 + by], rows)
                return carry

            lax.fori_loop(0, 2 * len(some), add, 0)

        step(1 - y)
        copies = [
            go(
                block(grad, rows, bz, bx, 1 - y, c),
                along_y.at[bz * 2 + bx],
                recv.at[16 + bz * 2 + bx],
                y_peer,
            )
            for bz in some
            for bx in range(2)
        ]
        step(y)
        return copies

    def all_x(grad, rows, along_y, along_x, recv, some, got):
        for copy in got:
            copy.wait_recv()

        def step(bx):
            def add(bz, carry):
                number = ((bz * 2 + bx) * 2 + y) * 2 + c
                add_rows(grad, number * rows, along_y[bz * 2 + bx], rows)
                return carry

            lax.fori_loop(some[0], some[-1] + 1, add, 0)

        step(1 - x)
        copies = [
            go(block(grad, rows, bz, 1 - x, y, c), along_x.at[bz], recv.at[24 + bz], x_peer)
            for bz in some
        ]
        step(x)
        return copies

    def all_z(grad, rows, along_x, along_z, recv, got):
        for copy in got:
            copy.wait_recv()

        def add(bz, carry):
            number = ((bz * 2 + x) * 2 + y) * 2 + c
            add_rows(grad, number * rows, along_x[bz], rows)
            return carry

        lax.fori_loop(0, 4, add, 0)
        return [
            go(
                block(grad, rows, lax.rem(z + d, 4), x, y, c),
                along_z.at[d - 1],
                recv.at[27 + d],
                spot(lax.rem(z + d, 4), x, y, c),
            )
            for d in range(1, 4)
        ]

    def all_end(grad, rows, along_z, out, got):
        total = grad[pl.ds(pl.multiple_of(mine * rows, 16), rows)].astype(FLOAT)
        for d in range(3):
            got[d].wait_recv()
            total = total + along_z[d].astype(FLOAT)
        out[...] = total

    def quarter_rows(rows, bz, bx):
        return pl.ds(pl.multiple_of((bz * 2 + bx) * 4 * rows, 16), 4 * rows)

    def quarter_x(grad, rows, along_x, recv, d):
        bz = lax.rem(z + d, 4)
        return go(grad.at[quarter_rows(rows, bz, 1 - x)], along_x.at[d - 1], recv.at[d - 1], x_peer)

    def quarter_z(grad, rows, along_x, along_z, recv, got, d):
        got[d - 1].wait_recv()
        bz = lax.rem(z + d, 4)
        add_rows(grad, (bz * 2 + x) * 4 * rows, along_x[d - 1], 4 * rows)
        if d == 4:
            return None
        return go(
            grad.at[quarter_rows(rows, bz, x)],
            along_z.at[d - 1],
            recv.at[3 + d],
            spot(bz, x, y, c),
        )

    def quarter_taps(taps):
        first = 2 * lax.rem(z + 1, 4)
        return [
            (d + 1, span, lambda i, carry: taps(lax.rem(first + i, 9), carry))
            for d, span in enumerate(((0, 3), (3, 6), (6, 8), (8, 9)))
        ]

    def quarter_w(grad, rows, along_z, out, recv, got):
        for copy in got:
            copy.wait_recv()

        own = pl.ds(pl.multiple_of(ha * 4 * rows, 16), 4 * rows)
        value = grad[own].astype(FLOAT)
        for d in range(3):
            value = value + along_z[d].astype(FLOAT)
        grad[own] = value.astype(HALF)
        target = out.at[:, pl.ds(pl.multiple_of(wa * 256, 256), 256)]

        def piece(col):
            return grad.at[pl.ds(pl.multiple_of((ha * 4 + col) * rows, 16), rows)]

        stay(piece(wa), target)
        return [
            go(
                piece(lax.rem(wa + d, 4)),
                target,
                recv.at[6 + d],
                (ha, lax.rem(wa + d, 4)),
            )
            for d in range(1, 4)
        ]

    su = all_core(wu, 32, du_c, r_u, (0, 1, 2, 3))
    su = all_y(wu, 32, du_c, du_y, r_u, (0, 1, 2, 3), su)

    def put_columns(target, s, value):
        put_shifts(target, pl.ds(0, 256), s, value, 0.0, 0.0)

    for e in range(3):
        gs2[e, :, 0] = jnp.zeros((3, 32, 256), HALF)
        gs2[e, :, 17] = jnp.zeros((3, 32, 256), HALF)
    settle(stay(pre2_in, pre))
    settle(own_wa)
    for copy in got_wa:
        copy.wait_recv()

    def two_grad(s, carry):
        rows = pl.ds(pl.multiple_of(128 * s, 128), 128)
        parts = [from_wa[w, rows].astype(FLOAT).reshape(16, 8, 256) for w in range(4)]
        put_columns(gs2, s, jnp.concatenate(parts, axis=1) * gelu_slope(pre[s]))
        return carry

    lax.fori_loop(0, 3, two_grad, 0)
    got_pre1 = stay(pre1_in, pre)
    settle(got_h1)

    def two_weight(t, carry):
        window = gs2[2 - t % 3, :, pl.ds(2 - t // 3, 16)].reshape(1536, 256)
        rows = pl.ds(pl.multiple_of(1024 * t, 1024), 1024)
        d2[rows] = across(joined[...], window).astype(HALF)
        return carry

    s2 = []
    for d, (first, last), taps in quarter_taps(two_weight):
        lax.fori_loop(first, last, taps, 0)
        s2.append(quarter_x(d2, 288, d2_x, r_2, d))
    settle(stay(joined_in, joined))

    def three_weight(t, carry):
        window = gs3[2 - t % 3, :, pl.ds(2 - t // 3, 32)].reshape(1536, 512)
        rows = pl.ds(pl.multiple_of(1024 * t, 1024), 1024)
        d3[rows] = across(joined[...], window).astype(HALF)
        return carry

    lax.fori_loop(0, 5, three_weight, 0)
    s3 = all_core(d3, 288, d3_c, r_3, (0, 1))
    z2 = [quarter_z(d2, 288, d2_x, d2_z, r_2, s2, 1)]
    s3_low = all_y(d3, 288, d3_c, d3_y, r_3, (0, 1), s3)
    pl.semaphore_signal(free, inc=1, device_id=c_peer, device_id_type=MESH)
    lax.fori_loop(5, 9, three_weight, 0)
    pl.semaphore_wait(free, 1)
    s3 = all_core(d3, 288, d3_c, r_3, (2, 3))
    got_x0 = stay(x0_in, joined.at[:, pl.ds(0, 512)])
    z2.append(quarter_z(d2, 288, d2_x, d2_z, r_2, s2, 2))
    settle(got_w2)

    def source_two(s):
        for half in range(2):
            acc[...] = jnp.zeros_like(acc)

            def tap(t, inner_carry):
                window = gs2[2 - t % 3, s, pl.ds(2 - t // 3, 16)].reshape(512, 256)
                rows = pl.ds(pl.multiple_of(1024 * t + 512 * half, 512), 512)
                acc[...] += against(window, slot[rows])
                return inner_carry

            lax.fori_loop(0, 9, tap, 0)
            gs3[half, s, pl.ds(0, 32)] = acc[...].astype(HALF).reshape(32, 16, 512)

    def d_lanes(halves, s, core):
        return gs3.at[halves, s, pl.ds(0, 32), :, pl.ds(pl.multiple_of(256 * core, 256), 256)]

    own_lanes = pl.ds(pl.multiple_of(256 * c, 256), 256)

    def d_pass(s):
        sd[s].wait_recv()
        for half in range(2):
            value = gs3[half, s, pl.ds(0, 32), :, own_lanes].astype(FLOAT)
            value = value + d_core[s, half].astype(FLOAT)
            gs3[half, s, pl.ds(0, 32), :, own_lanes] = value.astype(HALF)
        return go(d_lanes(1 - y, s, c), d_y.at[s], r_d.at[3 + s], y_peer)

    sd = []
    sy = []
    for s in range(3):
        source_two(s)
        sd.append(go(d_lanes(pl.ds(0, 2), s, 1 - c), d_core.at[s], r_d.at[s], c_peer))
        if s > 0:
            sy.append(d_pass(s - 1))
    sy.append(d_pass(2))
    s3_high = all_y(d3, 288, d3_c, d3_y, r_3, (2, 3), s3)
    z2.append(quarter_z(d2, 288, d2_x, d2_z, r_2, s2, 3))
    su = all_x(wu, 32, du_y, du_x, r_u, (0, 1, 2, 3), su)
    settle(got_pre1)
    for s in range(3):
        sy[s].wait_recv()
        value = gs3[y, s, pl.ds(0, 32), :, own_lanes].astype(FLOAT) + d_y[s].astype(FLOAT)
        put_columns(gs2, s, value.reshape(16, 32, 256) * gelu_slope(pre[s]))
    settle(got_x0)

    def one_weight(t, carry):
        window = gs2[2 - t % 3, :, pl.ds(2 - t // 3, 16)].reshape(1536, 256)
        rows = pl.ds(pl.multiple_of(512 * t, 512), 512)
        slot[rows] = across(joined[:, 0:512], window).astype(HALF)
        return carry

    s1 = []
    for d, (first, last), taps in quarter_taps(one_weight):
        lax.fori_loop(first, last, taps, 0)
        s1.append(quarter_x(slot, 144, d1_x, r_1, d))

    quarter_z(d2, 288, d2_x, d2_z, r_2, s2, 4)
    x3 = all_x(d3, 288, d3_y, d3_x, r_3, (0, 1), s3_low)
    su = all_z(wu, 32, du_x, du_z, r_u, su)
    z1 = [quarter_z(slot, 144, d1_x, d1_z, r_1, s1, d) for d in range(1, 4)]
    x3 += all_x(d3, 288, d3_y, d3_x, r_3, (2, 3), s3_high)
    s2 = quarter_w(d2, 288, d2_z, g2, r_2, z2)
    quarter_z(slot, 144, d1_x, d1_z, r_1, s1, 4)
    settle(own_head)
    total = hh[0]
    for step in range(1, 32):
        heads[step - 1].wait_recv()
        total = total + hh[step]
    gh[...] = total
    s3 = all_z(d3, 288, d3_x, d3_z, r_3, x3)
    all_end(wu, 32, du_z, gu, su)
    s1 = quarter_w(slot, 144, d1_z, g1, r_1, z1)
    all_end(d3, 288, d3_z, g3, s3)
    for copy in s2 + s1:
        copy.wait_recv()
    for entry in stays:
        if not entry[1]:
            settle(entry)
    for copy in sends:
        copy.wait_send()


def back(*args):
    anywhere = pl.BlockSpec(memory_space=pl.ANY)
    inside = pl.BlockSpec(memory_space=pltpu.VMEM)
    shape = jax.ShapeDtypeStruct
    dma = pltpu.SemaphoreType.DMA

    def room(*dims):
        return pltpu.VMEM(dims, HALF)

    return pl.pallas_call(
        back_kernel,
        name="back",
        out_shape=(
            shape((288, 512), FLOAT),
            shape((32, 2048), FLOAT),
            shape((288, 1024), HALF),
            shape((144, 1024), HALF),
            shape((16, 128), FLOAT),
        ),
        in_specs=[anywhere] * 11 + [inside] * 4,
        out_specs=[inside, inside, anywhere, anywhere, inside],
        scratch_shapes=[
            room(3, 3, 34, 16, 512),
            room(2, 3, 32, 512),
            room(2, 3, 32, 512),
            pltpu.VMEM((32, 16, 128), FLOAT),
            room(1536, 1024),
            room(9216, 256),
            pltpu.VMEM((512, 512), FLOAT),
            room(384, 2048),
            room(1024, 2048),
            room(384, 1024),
            room(384, 1024),
            room(4, 384, 256),
            pltpu.VMEM((3, 16, 32, 256), FLOAT),
            room(3, 3, 18, 32, 256),
            room(3, 2, 32, 16, 256),
            room(3, 32, 16, 256),
            room(16, 32, 2048),
            room(8, 32, 2048),
            room(4, 32, 2048),
            room(3, 32, 2048),
            room(9216, 512),
            room(8, 288, 512),
            room(8, 288, 512),
            room(4, 288, 512),
            room(3, 288, 512),
            room(9216, 256),
            room(4, 1152, 256),
            room(3, 1152, 256),
            room(4, 576, 256),
            room(3, 576, 256),
            pltpu.VMEM((32, 16, 128), FLOAT),
            dma((144,)),
            dma((40,)),
            dma((2,)),
            dma((3,)),
            dma((6,)),
            dma((31,)),
            dma((31,)),
            dma((10,)),
            dma((10,)),
            dma((31,)),
            pltpu.SemaphoreType.REGULAR,
        ],
        compiler_params=pltpu.CompilerParams(
            collective_id=2, has_side_effects=True, vmem_limit_bytes=64 * 1024 * 1024
        ),
    )(*args)


def dice_slopes(totals):
    union_sum = totals[..., 1] + totals[..., 2] + SMOOTHING
    numerator = 2.0 * totals[..., 0] + SMOOTHING
    dice_score = numerator / union_sum
    loss_value = 1.0 - jnp.mean(dice_score)
    entry_count = float(dice_score.size)
    common = -2.0 / (entry_count * union_sum)
    return (loss_value, jnp.concatenate([common, numerator / (entry_count * union_sum**2)], axis=1))


def sliced_grads(
    bottom, skipped, groups, pixel_mask, labels, weight_one, weight_two, weight_up, weight_three,
    weight_head,
):
    ha = lax.axis_index("ha")
    code = (pixel_mask + 2 * labels).astype(FLOAT).reshape(8, 3, 64)
    pads = [jnp.pad(code, ((0, 0), (0, 5), (64 * odd, 64 - 64 * odd))) for odd in range(2)]
    code = jnp.where(ha % 2 == 0, *pads)
    head_rows = jnp.pad(weight_head.astype(HALF), ((0, 0), (0, 126)))
    x0, h1, h2, joined, w2, wu, w3, pre_one, pre_two, pre_three, hidden_three, logits, code, sums, head = front(
        bottom.reshape(8, 48, 512),
        skipped.reshape(8, 192, 512),
        code,
        weight_one.astype(HALF),
        weight_two.astype(HALF),
        weight_up.astype(HALF),
        weight_three.astype(HALF),
        head_rows,
    )
    wu = wu.reshape(1024, 2048)
    w3 = w3.reshape(9216, 512)
    w2 = w2.reshape(9216, 256)
    member = (groups[:, None] == jnp.arange(GROUPS)[None, :]).astype(FLOAT)
    step = lax.axis_index("ha") * 4 + lax.axis_index("wa")
    origin = (step - jnp.arange(32)) % 32
    at_group = jnp.einsum(
        "dh,hsg->dsg",
        (origin[:, None] // 4 == jnp.arange(8)[None, :]).astype(FLOAT),
        member.reshape(8, 3, GROUPS),
        precision=HIGHEST,
    )
    totals = jnp.einsum("dsg,dsq->gq", at_group, sums[:, :3, :6], precision=HIGHEST)
    totals = totals.reshape(GROUPS, 2, 3)
    loss_value, slopes = dice_slopes(totals)
    member = lax.dynamic_slice_in_dim(member, 3 * ha, 3, axis=0)
    slopes = jnp.einsum("sg,gq->sq", member, slopes, precision=HIGHEST)
    g3, gu, g2, g1, gh = back(
        w3,
        wu,
        w2,
        joined.reshape(1536, 1024),
        h2,
        h1.reshape(1536, 1024),
        x0.reshape(1536, 512),
        pre_one,
        pre_two,
        pre_three,
        hidden_three.reshape(1536, 512),
        logits,
        code,
        jnp.pad(slopes, ((0, 5), (0, 124))),
        head,
    )
    return (loss_value, g1.astype(FLOAT), g2.astype(FLOAT), gu, g3, gh[:, :2])


def body(
    bottom,
    skipped,
    groups,
    pixel_mask,
    labels,
    conv1_weight,
    conv1_momentum,
    conv1_average,
    conv2_weight,
    conv2_momentum,
    conv2_average,
    up_weight,
    up_momentum,
    up_average,
    conv3_weight,
    conv3_momentum,
    conv3_average,
    head_weight,
    head_momentum,
    head_average,
):
    split = bottom.shape[0] == 24 and bottom.shape[1:3] == (2, 8) and bottom.shape[3] == 512
    split = split and (lax.axis_size("ha"), lax.axis_size("wa")) == (8, 4)
    grads = sliced_grads if split else tiled_grads
    loss_value, conv1_grad, conv2_grad, up_grad, conv3_grad, head_grad = grads(
        bottom,
        skipped,
        groups,
        pixel_mask,
        labels,
        conv1_weight,
        conv2_weight,
        up_weight,
        conv3_weight,
        head_weight,
    )
    first = renew_state(conv1_weight, conv1_momentum, conv1_average, conv1_grad, RATE_CONV)
    second = renew_state(conv2_weight, conv2_momentum, conv2_average, conv2_grad, RATE_CONV)
    upward = renew_state(up_weight, up_momentum, up_average, up_grad, RATE_CONV)
    third = renew_state(conv3_weight, conv3_momentum, conv3_average, conv3_grad, RATE_CONV)
    header = renew_state(head_weight, head_momentum, head_average, head_grad, RATE_HEAD)
    return (
        loss_value,
        first[0],
        first[1],
        first[2],
        second[0],
        second[1],
        second[2],
        upward[0],
        upward[1],
        upward[2],
        third[0],
        third[1],
        third[2],
        header[0],
        header[1],
        header[2],
    )


def solution(mesh):
    in_specs = (
        P(None, "ha", "wa", None),
        P(None, "ha", "wa", None),
        P(),
        P(None, "ha", "wa"),
        P(None, "ha", "wa"),
        P(("ha", "wa"), None),
        P(("ha", "wa"), None),
        P(("ha", "wa"), None),
        P(("ha", "wa"), None),
        P(("ha", "wa"), None),
        P(("ha", "wa"), None),
        P(("ha", "wa"), None),
        P(("ha", "wa"), None),
        P(("ha", "wa"), None),
        P(("ha", "wa"), None),
        P(("ha", "wa"), None),
        P(("ha", "wa"), None),
        P(("ha", "wa"), None),
        P(("ha", "wa"), None),
        P(("ha", "wa"), None),
    )
    out_specs = (
        P(),
        P(("ha", "wa"), None),
        P(("ha", "wa"), None),
        P(("ha", "wa"), None),
        P(("ha", "wa"), None),
        P(("ha", "wa"), None),
        P(("ha", "wa"), None),
        P(("ha", "wa"), None),
        P(("ha", "wa"), None),
        P(("ha", "wa"), None),
        P(("ha", "wa"), None),
        P(("ha", "wa"), None),
        P(("ha", "wa"), None),
        P(("ha", "wa"), None),
        P(("ha", "wa"), None),
        P(("ha", "wa"), None),
    )
    return jax.shard_map(body, mesh=mesh, in_specs=in_specs, out_specs=out_specs, check_vma=False)
```
